256 devices in a mesh: chain: 32 (over y, z_hi, x), head: 8 (over z_lo, core).
Axes of the slice: x: 4, y: 4, z: 8 (z_hi: 2, z_lo: 4; z = z_hi * 4 + z_lo), core: 2. Of those that a mesh axis runs over, the one named last changes fastest.
Arguments:
- latent: bfloat16 [8192, 5120], P(('chain', 'head')), may hold values from -3 to 3
- query_in: bfloat16 [8192, 5120], P(('chain', 'head')), may hold values from -64 to 64
- key_in: bfloat16 [8192, 5120], P(('chain', 'head')), may hold values from -64 to 64
- value_in: bfloat16 [8192, 5120], P(('chain', 'head')), may hold values from -6 to 6
- cache_keys: bfloat16 [1024, 5120], P('chain', 'head'), may hold values from -6 to 6
- cache_values: bfloat16 [1024, 5120], P('chain', 'head'), may hold values from -6 to 6
- levels: int32 [4], replicated, may hold values from 0 to 49
- timesteps: int32 [50], replicated, may hold values from 1 to 999
- cache_mask: int32 [4, 32], replicated, may hold values 0 or 1
- time_weight: bfloat16 [256, 5120], replicated, may hold values from -8 to 8
Outputs:
- advanced: bfloat16 [8192, 5120], P(('chain', 'head'))
The draws below stay inside these ranges and needn't reach their ends.
All inputs are finite; a program needn't handle non-finite values.
Results may differ from the reference program's by a relative error of at most 0.012.
Values may be sent and summed in bfloat16 or wider, within the bound.
A program may use at most 128 MiB of HBM per device.

```python
import math
import jax
import jax.numpy as jnp
from jax import lax

D = 5120
HEADS = 40
HEAD_DIM = 128
FREQ = 256
CACHE_ROWS = 32
SPANS = 4
LEVELS = 50
TOKENS = 8192
CACHE = 1024
N_CHAIN = 32


def shared_base(key):
    return jax.random.normal(key, (TOKENS, D), jnp.float32)


def draw_key_in(key, part):
    base = shared_base(key)
    return jnp.clip(base, -6.0, 6.0).astype(jnp.bfloat16)


def draw_query_in(key, part):
    key = jax.random.fold_in(key, 5)
    return jnp.clip(jax.random.normal(key, (TOKENS, D), jnp.float32), -6.0, 6.0).astype(jnp.bfloat16)


def place_ends(drawn, rng, smallest, top_value):
    longest = drawn.shape.index(max(drawn.shape))
    spots = []
    for shift in (0, 1):
        where = [jax.random.randint(jax.random.fold_in(rng, axis), (), 0, length) for axis, length in enumerate(drawn.shape)]
        where[longest] = (where[longest] + shift) % drawn.shape[longest]
        spots.append(tuple(where))
    return drawn.at[spots[0]].set(smallest).at[spots[1]].set(top_value)


def steps_of(key, extent, shards, least, largest):
    level, own = 1.0, jax.random.fold_in(key, 6)
    for dim, blocks in shards:
        steps = jnp.exp(jax.random.uniform(jax.random.fold_in(own, dim), (blocks,), jnp.float32, least / len(shards), largest / len(shards)))
        level = level * jnp.repeat(steps, extent[dim] // blocks).reshape([-1 if axis == dim else 1 for axis in range(len(extent))])
    return level


def scatter_about(rng, dims, scale, limit, shards=(), kind=jnp.bfloat16):
    result = scale * jax.random.normal(rng, dims, jnp.float32)
    if shards:
        result = result * steps_of(rng, dims, shards, -0.22, 0.18)
    return jnp.clip(result, -limit, limit).astype(kind)


def setup_inputs(seed: int = 0) -> dict:
    key_of = jax.random.split(jax.random.key(seed), 11)
    return {
        "latent": scatter_about(key_of[0], (TOKENS, D), 0.5, 3.0, ((0, 256),)),
        "query_in": draw_query_in(jax.random.fold_in(key_of[10], 71), 0),
        "key_in": draw_key_in(jax.random.fold_in(key_of[10], 71), 0),
        "value_in": scatter_about(key_of[3], (TOKENS, D), 1.0, 6.0, ((0, 256),)),
        "cache_keys": scatter_about(key_of[4], (CACHE, D), 1.0, 6.0, ((0, 32), (1, 8))),
        "cache_values": scatter_about(key_of[5], (CACHE, D), 1.0, 6.0, ((0, 32), (1, 8))),
        "levels": place_ends(jax.random.randint(key_of[6], (SPANS,), 0, LEVELS), jax.random.fold_in(key_of[6], 1), 0, LEVELS - 1).astype(jnp.int32),
        "timesteps": place_ends(jax.random.randint(key_of[7], (LEVELS,), 1, 1000), jax.random.fold_in(key_of[7], 1), 1, 999).astype(jnp.int32),
        "cache_mask": place_ends((jax.random.randint(key_of[8], (SPANS, N_CHAIN), 0, 4) < 3).astype(jnp.int32), jax.random.fold_in(key_of[8], 1), 0, 1),
        "time_weight": scatter_about(key_of[9], (FREQ, D), 2.0, 8.0),
    }


def timestep_gates(levels, timesteps, time_weight):
    half = FREQ // 2
    freqs = jnp.exp(-math.log(10000.0) * jnp.arange(half, dtype=jnp.float32) / half)
    stamps = timesteps[levels].astype(jnp.float32)
    phase = stamps[:, None] * freqs[None, :]
    embed = jnp.concatenate([jnp.cos(phase), jnp.sin(phase)], axis=1).astype(jnp.bfloat16)
    return jnp.dot(embed, time_weight, preferred_element_type=jnp.float32)

def reference(latent, query_in, key_in, value_in, cache_keys, cache_values, levels, timesteps, cache_mask, time_weight):
    gate = timestep_gates(levels, timesteps, time_weight)
    span_tokens = TOKENS // SPANS
    scale = 1.0 / math.sqrt(HEAD_DIM)
    blocks = jnp.arange(CACHE, dtype=jnp.int32) // CACHE_ROWS
    pieces = []
    for span in range(SPANS):
        lower = span * span_tokens
        upper = lower + span_tokens
        cache_seen = cache_mask[span][blocks] == 1
        visible = jnp.concatenate([jnp.ones((span_tokens,), dtype=bool), cache_seen])
        keys = jnp.concatenate([key_in[lower:upper], cache_keys], axis=0)
        values = jnp.concatenate([value_in[lower:upper], cache_values], axis=0)
        count = keys.shape[0]
        query_heads = query_in[lower:upper].reshape(span_tokens, HEADS, HEAD_DIM).transpose(1, 0, 2)
        key_heads = keys.reshape(count, HEADS, HEAD_DIM).transpose(1, 0, 2)
        value_heads = values.reshape(count, HEADS, HEAD_DIM).transpose(1, 0, 2)

        def one_head(operands):
            query, key_rows, value_rows = operands
            scores = jnp.dot(query, key_rows.T, preferred_element_type=jnp.float32) * scale
            scores = jnp.where(visible[None, :], scores, -jnp.inf)
            peak = lax.optimization_barrier(jnp.max(scores, axis=1, keepdims=True))
            weights = jnp.exp(scores - peak)
            total = lax.optimization_barrier(jnp.sum(weights, axis=1, keepdims=True))
            summed = jnp.dot(weights.astype(jnp.bfloat16), value_rows, preferred_element_type=jnp.float32)
            return (summed / total).astype(jnp.bfloat16)
        attended = lax.map(one_head, (query_heads, key_heads, value_heads))
        attended = attended.transpose(1, 0, 2).reshape(span_tokens, D)
        updated = latent[lower:upper].astype(jnp.float32) + gate[span][None, :] * attended.astype(jnp.float32)
        pieces.append(updated.astype(jnp.bfloat16))
    updated_all = jnp.concatenate(pieces, axis=0)
    return jnp.concatenate([updated_all[span_tokens:], updated_all[:span_tokens]], axis=0)
```

```python
import functools
import math

import jax
import jax.numpy as jnp
from jax import lax
from jax.experimental import pallas as pl
from jax.experimental.pallas import tpu as pltpu
from jax.sharding import PartitionSpec as P

MESH = pl.DeviceIdType.MESH
HEAD_DIM = 128
SPANS = 4
NY, NX, NZ = 4, 4, 8
GROUP = 5
WIDTH = GROUP * HEAD_DIM
ROWS = 32
HOPS = (0, 1, 7, 2, 6, 3, 5, 4)
CHUNKS = 12
FIRST_Z = 2
X_CHUNKS = 9
KEYS = 8 * ROWS
LOG2E = 1.4426950408889634
HIDDEN = -1e30


def device(y, z, x, core):
    return {"chain": (y * 2 + z // 4) * NX + x, "head": (z % 4) * 2 + core}


def group_columns(z):
    group = (z % 4) * 2 + z // 4
    return pl.ds(pl.multiple_of(group * WIDTH, 128), WIDTH)


def kernel(
    levels, timesteps, cache_mask, latent, query_in, key_in, value_in, cache_keys, cache_values, time_weight,
    out,
    query, kv, attended, returned, shifted, weight, gate, peak, total, summed, bias,
    send_z, send_x, send_y, send_o, recv_q, recv_k, recv_v, recv_x, recv_y, recv_o, local,
):
    chain, head = lax.axis_index("chain"), lax.axis_index("head")
    y, x = chain // 8, chain % 4
    zh, zl, core = (chain // 4) % 2, head // 2, head % 2
    z = zh * 4 + zl
    up, down = (y + 1) % 4, (y + 3) % 4
    right, left = (x + 1) % 4, (x + 3) % 4
    sibling = device(y, z, x, 1 - core)
    across = device(y, (z + 4) % 8, x, 1 - core)

    def remote(src, dst, send, recv, to):
        return pltpu.make_async_remote_copy(
            src_ref=src, dst_ref=dst, send_sem=send, recv_sem=recv, device_id=to, device_id_type=MESH
        )

    mine = group_columns(z)
    own = [
        pltpu.make_async_copy(key_in.at[:, mine], kv.at[0, 0, 0], recv_k.at[0]),
        pltpu.make_async_copy(value_in.at[:, mine], kv.at[0, 1, 0], recv_v.at[0]),
        pltpu.make_async_copy(query_in.at[:, mine], query.at[0], recv_q.at[0]),
    ]
    for copy in own:
        copy.start()
    weight_copy = pltpu.make_async_copy(time_weight, weight, local.at[0])
    weight_copy.start()

    @pl.when(core == zh)
    def _():
        pltpu.make_async_copy(cache_keys, kv.at[1, 0, 0], recv_k.at[1]).start()
        pltpu.make_async_copy(cache_values, kv.at[1, 1, 0], recv_v.at[1]).start()

    barrier = pltpu.get_barrier_semaphore()
    partners = [sibling, across, device(y, z, right, core), device(y, z, left, core)]
    partners += [device(up, z, x, core), device(down, z, x, core)]
    for hop in HOPS[1:]:
        partners += [device(row, (z + hop) % 8, x, core) for row in (y, up, down)]
    for partner in partners:
        pl.semaphore_signal(barrier, inc=1, device_id=partner, device_id_type=MESH)
    pl.semaphore_wait(barrier, len(partners))

    def cache_across(which, source, recv):
        return remote(source, kv.at[1, which, 0], send_z.at[0, which], recv.at[1], across)

    def query_over_z(j):
        to = (z + HOPS[j]) % 8
        return remote(
            query_in.at[:, group_columns(to)], query.at[j], send_z.at[j, 2], recv_q.at[j], device(y, to, x, core)
        )

    def kv_over_z(j, which, source, recv):
        to = (z + HOPS[j]) % 8
        return remote(
            source.at[:, group_columns(to)],
            kv.at[j + 1, which, 0],
            send_z.at[j, which],
            recv.at[j + 1],
            device(y, to, x, core),
        )

    def over_x(i):
        own_kv = kv.at[i, :, 0]
        return (
            remote(own_kv, kv.at[i, :, 1], send_x.at[i, 0], recv_x.at[i, 0], device(y, z, right, core)),
            remote(own_kv, kv.at[i, :, 3], send_x.at[i, 1], recv_x.at[i, 1], device(y, z, left, core)),
            remote(kv.at[i, 0, 1], kv.at[i, 0, 2], send_x.at[i, 2], recv_x.at[i, 2], device(y, z, right, core)),
            remote(kv.at[i, 1, 3], kv.at[i, 1, 2], send_x.at[i, 3], recv_x.at[i, 3], device(y, z, left, core)),
        )

    def to_sibling(i, send, recv):
        return remote(kv.at[i, :, 0:4], kv.at[i, :, 4:8], send, recv, sibling)

    def sibling_x(i):
        return to_sibling(i, send_x.at[i, 4], recv_x.at[i, 4])

    half = slice(0, 4)
    to_up, to_down = device(up, z, x, core), device(down, z, x, core)
    y_up = remote(kv.at[1, :, half], kv.at[9, :, half], send_y.at[0], recv_y.at[0], to_up)
    y_down = remote(kv.at[1, :, half], kv.at[10, :, half], send_y.at[1], recv_y.at[1], to_down)
    y_on_up = remote(kv.at[9, 0, half], kv.at[11, 0, half], send_y.at[2], recv_y.at[2], to_up)
    y_on_down = remote(kv.at[10, 1, half], kv.at[11, 1, half], send_y.at[3], recv_y.at[3], to_down)
    latent_down = remote(latent, shifted, send_y.at[7], recv_y.at[7], to_down)

    def sibling_y(i):
        return to_sibling(i, send_y.at[i - 5], recv_y.at[i - 5])

    def back(j):
        to = (z - HOPS[j] + 8) % 8
        return remote(attended.at[j], returned.at[:, mine], send_o.at[j], recv_o.at[j], device(down, to, x, core))

    @pl.when(core != zh)
    def _():
        cache_across(0, cache_keys, recv_k).start()
        cache_across(1, cache_values, recv_v).start()

    for j in range(1, 8):
        if j == 3:
            for early in range(1, 8):
                query_over_z(early).start()
        kv_over_z(j, 0, key_in, recv_k).start()
        kv_over_z(j, 1, value_in, recv_v).start()
    latent_down.start()

    for i in range(CHUNKS):
        for slot in range(8):
            if i == 1 or i >= 9:
                plane = {1: y, 9: down, 10: up, 11: (y + 2) % 4}[i]
                side = core if slot < 4 else 1 - core
                block = plane * 8 + side * 4 + (x + (0, 3, 2, 1)[slot % 4]) % 4
                bias[i * 8 + slot] = jnp.where(cache_mask[y, block] == 1, 0.0, HIDDEN).astype(jnp.float32)
            else:
                bias[i * 8 + slot] = jnp.float32(0.0)

    stamp = timesteps[levels[up]].astype(jnp.float32)
    count = 128
    index = lax.broadcasted_iota(jnp.int32, (8, count), 1).astype(jnp.float32)
    phase = stamp * jnp.exp(-math.log(10000.0) * index / count)
    embed = jnp.concatenate([jnp.cos(phase), jnp.sin(phase)], axis=1).astype(jnp.bfloat16)
    weight_copy.wait()

    def gate_columns(c, carry):
        columns = pl.ds(pl.multiple_of(c * WIDTH, 128), WIDTH)
        gate[:, columns] = jnp.dot(embed, weight[:, columns], preferred_element_type=jnp.float32)
        return carry

    lax.fori_loop(0, 8, gate_columns, 0)

    peak[...] = jnp.full_like(peak, HIDDEN)
    total[...] = jnp.zeros_like(total)
    summed[...] = jnp.zeros_like(summed)
    own[2].wait()
    for j in range(1, 8):
        query_over_z(j).wait_recv()

    def attend(i):
        for h in range(GROUP):
            columns = slice(h * HEAD_DIM, (h + 1) * HEAD_DIM)
            keys = kv[i, 0, :, :, columns].reshape(KEYS, HEAD_DIM)
            values = kv[i, 1, :, :, columns].reshape(KEYS, HEAD_DIM)
            queries = query[:, :, columns].reshape(KEYS, HEAD_DIM)
            scores = lax.dot_general(keys, queries, (((1,), (1,)), ((), ())), preferred_element_type=jnp.float32)
            scores = scores * (LOG2E / math.sqrt(HEAD_DIM))
            scores = jnp.concatenate(
                [scores[slot * ROWS : (slot + 1) * ROWS] + bias[i * 8 + slot] for slot in range(8)], axis=0
            )
            old = peak[h]
            new = jnp.maximum(old, jnp.max(scores, axis=0, keepdims=True))
            weights = jnp.exp2(scores - new)
            factor = jnp.exp2(old - new)
            peak[h] = new
            total[h] = factor * total[h] + jnp.sum(weights, axis=0, keepdims=True)
            added = lax.dot_general(
                values, weights.astype(jnp.bfloat16), (((0,), (0,)), ((), ())), preferred_element_type=jnp.float32
            )
            summed[h] = factor * summed[h] + added

    def turn(t, carry):
        @pl.when(t < X_CHUNKS)
        def _():
            pltpu.make_async_copy(kv.at[t, 0, 0], kv.at[t, 0, 0], recv_k.at[t]).wait()
            pltpu.make_async_copy(kv.at[t, 1, 0], kv.at[t, 1, 0], recv_v.at[t]).wait()
            over_x(t)[0].start()
            over_x(t)[1].start()

        @pl.when((t >= 1) & (t < X_CHUNKS + 1))
        def _():
            copies = over_x(t - 1)
            copies[0].wait_recv()
            copies[2].start()
            copies[1].wait_recv()
            copies[3].start()

        @pl.when((t >= 2) & (t < X_CHUNKS + 2))
        def _():
            copies = over_x(t - 2)
            copies[2].wait_recv()
            copies[3].wait_recv()
            sibling_x(t - 2).start()

        @pl.when(t == 3)
        def _():
            y_up.start()
            y_down.start()

        @pl.when(t == 6)
        def _():
            y_up.wait_recv()
            y_on_up.start()
            y_down.wait_recv()
            y_on_down.start()
            sibling_y(9).start()
            sibling_y(10).start()

        @pl.when(t == 8)
        def _():
            y_on_up.wait_recv()
            y_on_down.wait_recv()
            sibling_y(11).start()

        @pl.when(t >= 3)
        def _():
            sibling_x(t - 3).wait_recv()

        @pl.when(t == 8)
        def _():
            sibling_y(9).wait_recv()

        @pl.when(t == 9)
        def _():
            sibling_y(10).wait_recv()

        @pl.when(t == 10)
        def _():
            sibling_y(11).wait_recv()

        def ready(e, carry):
            attend(jnp.where(e == 0, t - 3, t + 1))
            return carry

        ready_count = jnp.where(t < 3, 0, jnp.where((t >= 8) & (t <= 10), 2, 1))
        lax.fori_loop(0, ready_count, ready, 0)
        return carry

    lax.fori_loop(0, X_CHUNKS + 3, turn, 0)

    for h in range(GROUP):
        result = summed[h] * (1.0 / total[h])
        attended[:, :, h * HEAD_DIM : (h + 1) * HEAD_DIM] = result.T.astype(jnp.bfloat16).reshape(8, ROWS, HEAD_DIM)
    for j in range(8):
        back(j).start()

    latent_down.wait_recv()
    for j in range(8):
        back(j).wait_recv()
        columns = group_columns((z + HOPS[j]) % 8)
        out[:, columns] = (
            shifted[:, columns].astype(jnp.float32) + gate[0:1, columns] * returned[:, columns].astype(jnp.float32)
        ).astype(jnp.bfloat16)

    @pl.when(core != zh)
    def _():
        cache_across(0, cache_keys, recv_k).wait_send()
        cache_across(1, cache_values, recv_v).wait_send()

    for j in range(1, 8):
        query_over_z(j).wait_send()
        kv_over_z(j, 0, key_in, recv_k).wait_send()
        kv_over_z(j, 1, value_in, recv_v).wait_send()

    def sent(i, carry):
        for copy in over_x(i):
            copy.wait_send()
        sibling_x(i).wait_send()
        return carry

    lax.fori_loop(0, X_CHUNKS, sent, 0)
    for copy in (y_up, y_down, y_on_up, y_on_down, sibling_y(9), sibling_y(10), sibling_y(11), latent_down):
        copy.wait_send()
    for j in range(8):
        back(j).wait_send()


def shards(
    latent, query_in, key_in, value_in, cache_keys, cache_values, levels, timesteps, cache_mask, time_weight
):
    anywhere = pl.BlockSpec(memory_space=pl.ANY)
    scalars = pl.BlockSpec(memory_space=pltpu.SMEM)
    bf16, f32 = jnp.bfloat16, jnp.float32
    dma = pltpu.SemaphoreType.DMA
    return pl.pallas_call(
        kernel,
        out_shape=jax.ShapeDtypeStruct(latent.shape, latent.dtype),
        in_specs=[scalars] * 3 + [anywhere] * 7,
        out_specs=pl.BlockSpec(memory_space=pltpu.VMEM),
        scratch_shapes=[
            pltpu.VMEM((8, ROWS, WIDTH), bf16),
            pltpu.VMEM((CHUNKS, 2, 8, ROWS, WIDTH), bf16),
            pltpu.VMEM((8, ROWS, WIDTH), bf16),
            pltpu.VMEM(latent.shape, bf16),
            pltpu.VMEM(latent.shape, bf16),
            pltpu.VMEM(time_weight.shape, bf16),
            pltpu.VMEM((8, latent.shape[1]), f32),
            pltpu.VMEM((GROUP, 1, KEYS), f32),
            pltpu.VMEM((GROUP, 1, KEYS), f32),
            pltpu.VMEM((GROUP, HEAD_DIM, KEYS), f32),
            pltpu.SMEM((CHUNKS * 8,), f32),
            dma((8, 3)),
            dma((X_CHUNKS, 5)),
            dma((8,)),
            dma((8,)),
            dma((8,)),
            dma((X_CHUNKS,)),
            dma((X_CHUNKS,)),
            dma((X_CHUNKS, 5)),
            dma((8,)),
            dma((8,)),
            dma((1,)),
        ],
        compiler_params=pltpu.CompilerParams(
            collective_id=0, has_side_effects=True, vmem_limit_bytes=40 * 1024 * 1024
        ),
        cost_estimate=pl.CostEstimate(flops=2 * 10**9, bytes_accessed=5 * 10**6, transcendentals=4 * 10**6),
    )(
        levels, timesteps, cache_mask, latent, query_in, key_in, value_in, cache_keys, cache_values, time_weight
    )


def solution(mesh):
    return jax.shard_map(
        shards,
        mesh=mesh,
        in_specs=(
            P(("chain", "head"), None),
            P(("chain", "head"), None),
            P(("chain", "head"), None),
            P(("chain", "head"), None),
            P("chain", "head"),
            P("chain", "head"),
            P(),
            P(),
            P(),
            P(),
        ),
        out_specs=P(("chain", "head"), None),
        check_vma=False,
    )
```

```python
import functools
import math

import jax
import jax.numpy as jnp
from jax import lax
from jax.experimental import pallas as pl
from jax.experimental.pallas import tpu as pltpu
from jax.sharding import PartitionSpec as P

MESH = pl.DeviceIdType.MESH
HEAD_DIM = 128
SPANS = 4
NY, NX, NZ = 4, 4, 8
GROUP = 5
WIDTH = GROUP * HEAD_DIM
ROWS = 32
HOPS = (0, 1, 7, 2, 6, 3, 5, 4)
CHUNKS = 12
FIRST_Z = 2
X_CHUNKS = 9
KEYS = 8 * ROWS
LOG2E = 1.4426950408889634
HIDDEN = -1e30


def device(y, z, x, core):
    return {"chain": (y * 2 + z // 4) * NX + x, "head": (z % 4) * 2 + core}


def group_columns(z):
    group = (z % 4) * 2 + z // 4
    return pl.ds(pl.multiple_of(group * WIDTH, 128), WIDTH)


def kernel(
    levels, timesteps, cache_mask, latent, query_in, key_in, value_in, cache_keys, cache_values, time_weight,
    out,
    query, kv, attended, returned, shifted, weight, gate, peak, total, summed, bias,
    send_z, send_x, send_y, send_o, recv_q, recv_k, recv_v, recv_x, recv_y, recv_o, local,
):
    chain, head = lax.axis_index("chain"), lax.axis_index("head")
    y, x = chain // 8, chain % 4
    zh, zl, core = (chain // 4) % 2, head // 2, head % 2
    z = zh * 4 + zl
    up, down = (y + 1) % 4, (y + 3) % 4
    right, left = (x + 1) % 4, (x + 3) % 4
    sibling = device(y, z, x, 1 - core)
    across = device(y, (z + 4) % 8, x, 1 - core)

    def remote(src, dst, send, recv, to):
        return pltpu.make_async_remote_copy(
            src_ref=src, dst_ref=dst, send_sem=send, recv_sem=recv, device_id=to, device_id_type=MESH
        )

    mine = group_columns(z)
    own = [
        pltpu.make_async_copy(key_in.at[:, mine], kv.at[0, 0, 0], recv_k.at[0]),
        pltpu.make_async_copy(value_in.at[:, mine], kv.at[0, 1, 0], recv_v.at[0]),
        pltpu.make_async_copy(query_in.at[:, mine], query.at[0], recv_q.at[0]),
    ]
    for copy in own:
        copy.start()
    weight_copy = pltpu.make_async_copy(time_weight, weight, local.at[0])
    weight_copy.start()

    @pl.when(core == zh)
    def _():
        pltpu.make_async_copy(cache_keys, kv.at[1, 0, 0], recv_k.at[1]).start()
        pltpu.make_async_copy(cache_values, kv.at[1, 1, 0], recv_v.at[1]).start()

    barrier = pltpu.get_barrier_semaphore()
    partners = [sibling, across, device(y, z, right, core), device(y, z, left, core)]
    partners += [device(up, z, x, core), device(down, z, x, core)]
    for hop in HOPS[1:]:
        partners += [device(row, (z + hop) % 8, x, core) for row in (y, up, down)]
    for partner in partners:
        pl.semaphore_signal(barrier, inc=1, device_id=partner, device_id_type=MESH)
    pl.semaphore_wait(barrier, len(partners))

    def cache_across(which, source, recv):
        return remote(source, kv.at[1, which, 0], send_z.at[0, which], recv.at[1], across)

    def query_over_z(j):
        to = (z + HOPS[j]) % 8
        return remote(
            query_in.at[:, group_columns(to)], query.at[j], send_z.at[j, 2], recv_q.at[j], device(y, to, x, core)
        )

    def kv_over_z(j, which, source, recv):
        to = (z + HOPS[j]) % 8
        return remote(
            source.at[:, group_columns(to)],
            kv.at[j + 1, which, 0],
            send_z.at[j, which],
            recv.at[j + 1],
            device(y, to, x, core),
        )

    def over_x(i):
        own_kv = kv.at[i, :, 0]
        return (
            remote(own_kv, kv.at[i, :, 1], send_x.at[i, 0], recv_x.at[i, 0], device(y, z, right, core)),
            remote(own_kv, kv.at[i, :, 3], send_x.at[i, 1], recv_x.at[i, 1], device(y, z, left, core)),
            remote(kv.at[i, 0, 1], kv.at[i, 0, 2], send_x.at[i, 2], recv_x.at[i, 2], device(y, z, right, core)),
            remote(kv.at[i, 1, 3], kv.at[i, 1, 2], send_x.at[i, 3], recv_x.at[i, 3], device(y, z, left, core)),
        )

    def to_sibling(i, send, recv):
        return remote(kv.at[i, :, 0:4], kv.at[i, :, 4:8], send, recv, sibling)

    def sibling_x(i):
        return to_sibling(i, send_x.at[i, 4], recv_x.at[i, 4])

    half = slice(0, 4)
    to_up, to_down = device(up, z, x, core), device(down, z, x, core)
    y_up = remote(kv.at[1, :, half], kv.at[9, :, half], send_y.at[0], recv_y.at[0], to_up)
    y_down = remote(kv.at[1, :, half], kv.at[10, :, half], send_y.at[1], recv_y.at[1], to_down)
    y_on_up = remote(kv.at[9, 0, half], kv.at[11, 0, half], send_y.at[2], recv_y.at[2], to_up)
    y_on_down = remote(kv.at[10, 1, half], kv.at[11, 1, half], send_y.at[3], recv_y.at[3], to_down)
    latent_down = remote(latent, shifted, send_y.at[7], recv_y.at[7], to_down)

    def sibling_y(i):
        return to_sibling(i, send_y.at[i - 5], recv_y.at[i - 5])

    def back(j):
        to = (z - HOPS[j] + 8) % 8
        return remote(attended.at[j], returned.at[:, mine], send_o.at[j], recv_o.at[j], device(down, to, x, core))

    @pl.when(core != zh)
    def _():
        cache_across(0, cache_keys, recv_k).start()
        cache_across(1, cache_values, recv_v).start()

    def start_kv(j):
        kv_over_z(j, 0, key_in, recv_k).start()
        kv_over_z(j, 1, value_in, recv_v).start()

    start_kv(1)
    start_kv(2)
    for j in range(1, 8):
        query_over_z(j).start()
    latent_down.start()

    for i in range(CHUNKS):
        for slot in range(8):
            if i == 1 or i >= 9:
                plane = {1: y, 9: down, 10: up, 11: (y + 2) % 4}[i]
                side = core if slot < 4 else 1 - core
                block = plane * 8 + side * 4 + (x + (0, 3, 2, 1)[slot % 4]) % 4
                bias[i * 8 + slot] = jnp.where(cache_mask[y, block] == 1, 0.0, HIDDEN).astype(jnp.float32)
            else:
                bias[i * 8 + slot] = jnp.float32(0.0)

    stamp = timesteps[levels[up]].astype(jnp.float32)
    count = 128
    index = lax.broadcasted_iota(jnp.int32, (8, count), 1).astype(jnp.float32)
    phase = stamp * jnp.exp(-math.log(10000.0) * index / count)
    embed = jnp.concatenate([jnp.cos(phase), jnp.sin(phase)], axis=1).astype(jnp.bfloat16)
    weight_copy.wait()

    def gate_columns(c, carry):
        columns = pl.ds(pl.multiple_of(c * WIDTH, 128), WIDTH)
        gate[:, columns] = jnp.dot(embed, weight[:, columns], preferred_element_type=jnp.float32)
        return carry

    lax.fori_loop(0, 8, gate_columns, 0)

    peak[...] = jnp.full_like(peak, HIDDEN)
    total[...] = jnp.zeros_like(total)
    summed[...] = jnp.zeros_like(summed)

    def attend(i):
        for h in range(GROUP):
            columns = slice(h * HEAD_DIM, (h + 1) * HEAD_DIM)
            keys = kv[i, 0, :, :, columns].reshape(KEYS, HEAD_DIM)
            values = kv[i, 1, :, :, columns].reshape(KEYS, HEAD_DIM)
            queries = query[:, :, columns].reshape(KEYS, HEAD_DIM)
            scores = lax.dot_general(keys, queries, (((1,), (1,)), ((), ())), preferred_element_type=jnp.float32)
            scores = scores * (LOG2E / math.sqrt(HEAD_DIM))
            scores = jnp.concatenate(
                [scores[slot * ROWS : (slot + 1) * ROWS] + bias[i * 8 + slot] for slot in range(8)], axis=0
            )
            old = peak[h]
            new = jnp.maximum(old, jnp.max(scores, axis=0, keepdims=True))
            weights = jnp.exp2(scores - new)
            factor = jnp.exp2(old - new)
            peak[h] = new
            total[h] = factor * total[h] + jnp.sum(weights, axis=0, keepdims=True)
            added = lax.dot_general(
                values, weights.astype(jnp.bfloat16), (((0,), (0,)), ((), ())), preferred_element_type=jnp.float32
            )
            summed[h] = factor * summed[h] + added

    def turn(t, carry):
        @pl.when(t < X_CHUNKS)
        def _():
            pltpu.make_async_copy(kv.at[t, 0, 0], kv.at[t, 0, 0], recv_k.at[t]).wait()
            pltpu.make_async_copy(kv.at[t, 1, 0], kv.at[t, 1, 0], recv_v.at[t]).wait()
            over_x(t)[0].start()
            over_x(t)[1].start()

        for turn_of, hops in ((1, (3, 4)), (3, (5, 6)), (5, (7,))):

            @pl.when(t == turn_of)
            def _(hops=hops):
                for j in hops:
                    start_kv(j)

        @pl.when((t >= 1) & (t < X_CHUNKS + 1))
        def _():
            copies = over_x(t - 1)
            copies[0].wait_recv()
            copies[2].start()
            copies[1].wait_recv()
            copies[3].start()

        @pl.when((t >= 2) & (t < X_CHUNKS + 2))
        def _():
            copies = over_x(t - 2)
            copies[2].wait_recv()
            copies[3].wait_recv()
            sibling_x(t - 2).start()

        @pl.when(t == 3)
        def _():
            y_up.start()
            y_down.start()
            own[2].wait()
            for j in range(1, 8):
                query_over_z(j).wait_recv()

        @pl.when(t == 6)
        def _():
            y_up.wait_recv()
            y_on_up.start()
            y_down.wait_recv()
            y_on_down.start()
            sibling_y(9).start()
            sibling_y(10).start()

        @pl.when(t == 8)
        def _():
            y_on_up.wait_recv()
            y_on_down.wait_recv()
            sibling_y(11).start()

        @pl.when(t >= 3)
        def _():
            sibling_x(t - 3).wait_recv()

        @pl.when(t == 8)
        def _():
            sibling_y(9).wait_recv()

        @pl.when(t == 9)
        def _():
            sibling_y(10).wait_recv()

        @pl.when(t == 10)
        def _():
            sibling_y(11).wait_recv()

        def ready(e, carry):
            attend(jnp.where(e == 0, t - 3, t + 1))
            return carry

        ready_count = jnp.where(t < 3, 0, jnp.where((t >= 8) & (t <= 10), 2, 1))
        lax.fori_loop(0, ready_count, ready, 0)
        return carry

    lax.fori_loop(0, X_CHUNKS + 3, turn, 0)

    for h in range(GROUP):
        result = summed[h] * (1.0 / total[h])
        attended[:, :, h * HEAD_DIM : (h + 1) * HEAD_DIM] = result.T.astype(jnp.bfloat16).reshape(8, ROWS, HEAD_DIM)
    for j in range(8):
        back(j).start()

    latent_down.wait_recv()
    for j in range(8):
        back(j).wait_recv()
        columns = group_columns((z + HOPS[j]) % 8)
        out[:, columns] = (
            shifted[:, columns].astype(jnp.float32) + gate[0:1, columns] * returned[:, columns].astype(jnp.float32)
        ).astype(jnp.bfloat16)

    @pl.when(core != zh)
    def _():
        cache_across(0, cache_keys, recv_k).wait_send()
        cache_across(1, cache_values, recv_v).wait_send()

    for j in range(1, 8):
        query_over_z(j).wait_send()
        kv_over_z(j, 0, key_in, recv_k).wait_send()
        kv_over_z(j, 1, value_in, recv_v).wait_send()

    def sent(i, carry):
        for copy in over_x(i):
            copy.wait_send()
        sibling_x(i).wait_send()
        return carry

    lax.fori_loop(0, X_CHUNKS, sent, 0)
    for copy in (y_up, y_down, y_on_up, y_on_down, sibling_y(9), sibling_y(10), sibling_y(11), latent_down):
        copy.wait_send()
    for j in range(8):
        back(j).wait_send()


def shards(
    latent, query_in, key_in, value_in, cache_keys, cache_values, levels, timesteps, cache_mask, time_weight
):
    anywhere = pl.BlockSpec(memory_space=pl.ANY)
    scalars = pl.BlockSpec(memory_space=pltpu.SMEM)
    bf16, f32 = jnp.bfloat16, jnp.float32
    dma = pltpu.SemaphoreType.DMA
    return pl.pallas_call(
        kernel,
        out_shape=jax.ShapeDtypeStruct(latent.shape, latent.dtype),
        in_specs=[scalars] * 3 + [anywhere] * 7,
        out_specs=pl.BlockSpec(memory_space=pltpu.VMEM),
        scratch_shapes=[
            pltpu.VMEM((8, ROWS, WIDTH), bf16),
            pltpu.VMEM((CHUNKS, 2, 8, ROWS, WIDTH), bf16),
            pltpu.VMEM((8, ROWS, WIDTH), bf16),
            pltpu.VMEM(latent.shape, bf16),
            pltpu.VMEM(latent.shape, bf16),
            pltpu.VMEM(time_weight.shape, bf16),
            pltpu.VMEM((8, latent.shape[1]), f32),
            pltpu.VMEM((GROUP, 1, KEYS), f32),
            pltpu.VMEM((GROUP, 1, KEYS), f32),
            pltpu.VMEM((GROUP, HEAD_DIM, KEYS), f32),
            pltpu.SMEM((CHUNKS * 8,), f32),
            dma((8, 3)),
            dma((X_CHUNKS, 5)),
            dma((8,)),
            dma((8,)),
            dma((8,)),
            dma((X_CHUNKS,)),
            dma((X_CHUNKS,)),
            dma((X_CHUNKS, 5)),
            dma((8,)),
            dma((8,)),
            dma((1,)),
        ],
        compiler_params=pltpu.CompilerParams(
            collective_id=0, has_side_effects=True, vmem_limit_bytes=64 * 1024 * 1024
        ),
        cost_estimate=pl.CostEstimate(flops=2 * 10**9, bytes_accessed=5 * 10**6, transcendentals=4 * 10**6),
    )(
        levels, timesteps, cache_mask, latent, query_in, key_in, value_in, cache_keys, cache_values, time_weight
    )


def solution(mesh):
    return jax.shard_map(
        shards,
        mesh=mesh,
        in_specs=(
            P(("chain", "head"), None),
            P(("chain", "head"), None),
            P(("chain", "head"), None),
            P(("chain", "head"), None),
            P("chain", "head"),
            P("chain", "head"),
            P(),
            P(),
            P(),
            P(),
        ),
        out_specs=P(("chain", "head"), None),
        check_vma=False,
    )
```

```python
import functools
import math

import jax
import jax.numpy as jnp
from jax import lax
from jax.experimental import pallas as pl
from jax.experimental.pallas import tpu as pltpu
from jax.sharding import PartitionSpec as P

MESH = pl.DeviceIdType.MESH
HEAD_DIM = 128
SPANS = 4
NY, NX, NZ = 4, 4, 8
GROUP = 5
WIDTH = GROUP * HEAD_DIM
ROWS = 32
HOPS = (0, 1, 7, 2, 6, 3, 5, 4)
CHUNKS = 12
ATTEND = (0, 1, 2, 3, 9, 10, 8, 4, 5, 11, 6, 7)
PLACE = tuple(ATTEND.index(i) for i in range(CHUNKS))
X_CHUNKS = 9
PARTS = ((0, 3), (3, 5))
KEYS = 8 * ROWS
LOG2E = 1.4426950408889634
HIDDEN = -1e30


def device(y, z, x, core):
    return {"chain": (y * 2 + z // 4) * NX + x, "head": (z % 4) * 2 + core}


def group_columns(z):
    group = (z % 4) * 2 + z // 4
    return pl.ds(pl.multiple_of(group * WIDTH, 128), WIDTH)


def part_columns(z, part):
    group = (z % 4) * 2 + z // 4
    lower, upper = PARTS[part]
    return pl.ds(pl.multiple_of(group * WIDTH + lower * HEAD_DIM, 128), (upper - lower) * HEAD_DIM)


def kernel(
    levels, timesteps, cache_mask, latent, query_in, key_in, value_in, cache_keys, cache_values, time_weight,
    out,
    query, kv, relay, attended, returned, shifted, weight, gate, peak, total, summed, bias,
    send_z, send_x, send_y, send_o, recv_q, recv_kv, recv_relay, recv_x, recv_y, recv_o, local,
):
    chain, head = lax.axis_index("chain"), lax.axis_index("head")
    y, x = chain // 8, chain % 4
    zh, zl, core = (chain // 4) % 2, head // 2, head % 2
    z = zh * 4 + zl
    up, down = (y + 1) % 4, (y + 3) % 4
    right, left = device(y, z, (x + 1) % 4, core), device(y, z, (x + 3) % 4, core)
    sibling = device(y, z, x, 1 - core)
    across = device(y, (z + 4) % 8, x, 1 - core)
    back_two = device(y, (z + 6) % 8, x, core)
    to_up, to_down = device(up, z, x, core), device(down, z, x, core)
    mine = group_columns(z)

    def remote(src, dst, send, recv, to):
        return pltpu.make_async_remote_copy(
            src_ref=src, dst_ref=dst, send_sem=send, recv_sem=recv, device_id=to, device_id_type=MESH
        )

    def chunk(i):
        return kv.at[PLACE[i]]

    own_query = pltpu.make_async_copy(query_in.at[:, mine], query.at[0], recv_q.at[0])
    own_query.start()
    for which, source in enumerate((key_in, value_in)):
        pltpu.make_async_copy(source.at[:, mine], chunk(0).at[which, 0], recv_kv.at[0, which]).start()
    weight_copy = pltpu.make_async_copy(time_weight, weight, local.at[0])
    weight_copy.start()

    @pl.when(core == zh)
    def _():
        for which, source in enumerate((cache_keys, cache_values)):
            pltpu.make_async_copy(source, chunk(1).at[which, 0], recv_kv.at[1, which]).start()

    barrier = pltpu.get_barrier_semaphore()
    partners = [sibling, across, right, left, to_up, to_down]
    for hop in HOPS[1:]:
        partners += [device(row, (z + hop) % 8, x, core) for row in (y, up, down)]
    for partner in partners:
        pl.semaphore_signal(barrier, inc=1, device_id=partner, device_id_type=MESH)
    pl.semaphore_wait(barrier, len(partners))

    def cache_across(which):
        source = (cache_keys, cache_values)[which]
        return remote(source, chunk(1).at[which, 0], send_z.at[0, which], recv_kv.at[1, which], across)

    def query_over_z(j):
        to = (z + HOPS[j]) % 8
        return remote(
            query_in.at[:, group_columns(to)], query.at[j], send_z.at[j, 2], recv_q.at[j], device(y, to, x, core)
        )

    def kv_over_z(j, which):
        to = (z + HOPS[j]) % 8
        source = (key_in, value_in)[which].at[:, group_columns(to)]
        if HOPS[j] == 4:
            return remote(source, relay.at[which], send_z.at[j, which], recv_relay.at[which], back_two)
        return remote(
            source, chunk(j + 1).at[which, 0], send_z.at[j, which], recv_kv.at[j + 1, which], device(y, to, x, core)
        )

    def relay_on(which):
        return remote(relay.at[which], chunk(8).at[which, 0], send_z.at[8, which], recv_kv.at[8, which], back_two)

    def x_copy(i, n):
        c = chunk(i)
        src, dst, to = (
            (c.at[:, 0], c.at[:, 1], right),
            (c.at[:, 0], c.at[:, 3], left),
            (c.at[0, 1], c.at[0, 2], right),
            (c.at[1, 3], c.at[1, 2], left),
            (c.at[:, 0], c.at[:, 4], sibling),
            (c.at[:, 1], c.at[:, 5], sibling),
            (c.at[:, 2], c.at[:, 6], sibling),
            (c.at[:, 3], c.at[:, 7], sibling),
        )[n]
        return remote(src, dst, send_x.at[i, n], recv_x.at[i, n], to)

    def y_copy(n):
        src, dst, to = (
            (chunk(1).at[:, 0:4], chunk(9).at[:, 0:4], to_up),
            (chunk(1).at[:, 0:4], chunk(10).at[:, 0:4], to_down),
            (chunk(9).at[0, 0:4], chunk(11).at[0, 0:4], to_up),
            (chunk(10).at[1, 0:4], chunk(11).at[1, 0:4], to_down),
            (chunk(9).at[:, 0:4], chunk(9).at[:, 4:8], sibling),
            (chunk(10).at[:, 0:4], chunk(10).at[:, 4:8], sibling),
            (chunk(11).at[:, 0:4], chunk(11).at[:, 4:8], sibling),
            (latent, shifted, to_down),
        )[n]
        return remote(src, dst, send_y.at[n], recv_y.at[n], to)

    def back(j, part):
        to = device(down, (z - HOPS[j] + 8) % 8, x, core)
        lower, upper = (PARTS[part][end] * HEAD_DIM for end in (0, 1))
        columns = part_columns(z, part)
        return remote(
            attended.at[j, :, lower:upper], returned.at[:, columns], send_o.at[j, part], recv_o.at[j, part], to
        )

    def start_z(*js):
        for j in js:
            for which in (0, 1):
                kv_over_z(j, which).start()

    def arrived(i):
        for which in (0, 1):
            place = chunk(i).at[which, 0]
            pltpu.make_async_copy(place, place, recv_kv.at[i, which]).wait()
        for n in (0, 1, 4):
            x_copy(i, n).start()

    def forward(i):
        x_copy(i, 0).wait_recv()
        x_copy(i, 2).start()
        x_copy(i, 1).wait_recv()
        x_copy(i, 3).start()
        x_copy(i, 5).start()
        x_copy(i, 7).start()

    def last_piece(i):
        x_copy(i, 2).wait_recv()
        x_copy(i, 3).wait_recv()
        x_copy(i, 6).start()

    def complete(i):
        if i >= X_CHUNKS:
            y_copy(i - 5).wait_recv()
        else:
            for n in (4, 5, 6, 7):
                x_copy(i, n).wait_recv()

    def start_y():
        y_copy(0).start()
        y_copy(1).start()

    def forward_y():
        for n in (0, 1):
            y_copy(n).wait_recv()
            y_copy(n + 2).start()
            y_copy(n + 4).start()

    def last_y():
        y_copy(2).wait_recv()
        y_copy(3).wait_recv()
        y_copy(6).start()

    def relay_all():
        for which in (0, 1):
            kv_over_z(7, which).wait_recv()
            relay_on(which).start()

    def queries(*js):
        for j in js:
            query_over_z(j).wait_recv()

    @pl.when(core != zh)
    def _():
        cache_across(0).start()
        cache_across(1).start()

    start_z(1, 2, 7)
    for j in range(1, 8):
        query_over_z(j).start()
    y_copy(7).start()

    for i in range(CHUNKS):
        for slot in range(8):
            shown = jnp.float32(0.0)
            if i == 1 or i >= 9:
                plane = {1: y, 9: down, 10: up, 11: (y + 2) % 4}[i]
                side = core if slot < 4 else 1 - core
                block = plane * 8 + side * 4 + (x + (0, 3, 2, 1)[slot % 4]) % 4
                shown = jnp.where(cache_mask[y, block] == 1, 0.0, HIDDEN).astype(jnp.float32)
            bias[PLACE[i] * 8 + slot] = shown

    peak[...] = jnp.full_like(peak, HIDDEN)
    total[...] = jnp.zeros_like(total)
    summed[...] = jnp.zeros_like(summed)

    arrived(0)

    stamp = timesteps[levels[up]].astype(jnp.float32)
    count = 128
    index = lax.broadcasted_iota(jnp.int32, (8, count), 1).astype(jnp.float32)
    phase = stamp * jnp.exp(-math.log(10000.0) * index / count)
    embed = jnp.concatenate([jnp.cos(phase), jnp.sin(phase)], axis=1).astype(jnp.bfloat16)
    weight_copy.wait()

    def gate_columns(c, carry):
        columns = pl.ds(pl.multiple_of(c * WIDTH, 128), WIDTH)
        gate[:, columns] = jnp.dot(embed, weight[:, columns], preferred_element_type=jnp.float32)
        return carry

    lax.fori_loop(0, 8, gate_columns, 0)

    def attend(c, finish=None):
        for h in range(GROUP):
            columns = slice(h * HEAD_DIM, (h + 1) * HEAD_DIM)
            keys = kv[c, 0, :, :, columns].reshape(KEYS, HEAD_DIM)
            values = kv[c, 1, :, :, columns].reshape(KEYS, HEAD_DIM)
            queries = query[:, :, columns].reshape(KEYS, HEAD_DIM)
            scores = lax.dot_general(keys, queries, (((1,), (1,)), ((), ())), preferred_element_type=jnp.float32)
            scores = scores * (LOG2E / math.sqrt(HEAD_DIM))
            scores = jnp.concatenate(
                [scores[slot * ROWS : (slot + 1) * ROWS] + bias[c * 8 + slot] for slot in range(8)], axis=0
            )
            old = peak[h]
            new = jnp.maximum(old, jnp.max(scores, axis=0, keepdims=True))
            weights = jnp.exp2(scores - new)
            factor = jnp.exp2(old - new)
            weight_sum = factor * total[h] + jnp.sum(weights, axis=0, keepdims=True)
            added = lax.dot_general(
                values, weights.astype(jnp.bfloat16), (((0,), (0,)), ((), ())), preferred_element_type=jnp.float32
            )
            value_sum = factor * summed[h] + added
            if finish is None:
                peak[h], total[h], summed[h] = new, weight_sum, value_sum
            else:
                finish(h, value_sum * (1.0 / weight_sum))

    def finish(h, result):
        columns = slice(h * HEAD_DIM, (h + 1) * HEAD_DIM)
        attended[:, :, columns] = result.T.astype(jnp.bfloat16).reshape(8, ROWS, HEAD_DIM)
        for part, (lower, upper) in enumerate(PARTS):
            if h == upper - 1:
                for j in range(8):
                    back(j, part).start()

    def before(c):
        if c == 0:
            arrived(1)
            forward(0)
            arrived(2)
            arrived(3)
            last_piece(0)
            forward(1)
            forward(2)
            last_piece(1)
            start_y()
            forward(3)
            last_piece(2)
            last_piece(3)
            relay_all()
            own_query.wait()
            queries(1, 2, 3, 4)
            start_z(3, 4)
            queries(5, 6, 7)
        if c == 3:
            arrived(8)
        if c == 4:
            arrived(4)
            start_z(5, 6)
            arrived(5)
            forward(8)
            forward_y()
        if c == 5:
            last_piece(8)
            forward(4)
            forward(5)
        if c == 6:
            last_piece(4)
            last_piece(5)
        if c == 8:
            arrived(6)
            arrived(7)
        if c == 9:
            forward(6)
            forward(7)
            last_y()
        if c == 10:
            last_piece(6)
            last_piece(7)
        complete(ATTEND[c])

    def turn(c, carry):
        for now in range(CHUNKS - 1):
            pl.when(c == now)(functools.partial(before, now))
        attend(c)
        return carry

    lax.fori_loop(0, CHUNKS - 1, turn, 0)
    before(CHUNKS - 1)
    attend(CHUNKS - 1, finish)

    y_copy(7).wait_recv()
    for part in range(len(PARTS)):
        for j in range(8):
            back(j, part).wait_recv()
            columns = part_columns((z + HOPS[j]) % 8, part)
            out[:, columns] = (
                shifted[:, columns].astype(jnp.float32) + gate[0:1, columns] * returned[:, columns].astype(jnp.float32)
            ).astype(jnp.bfloat16)

    @pl.when(core != zh)
    def _():
        cache_across(0).wait_send()
        cache_across(1).wait_send()

    for which in (0, 1):
        relay_on(which).wait_send()
    for j in range(1, 8):
        query_over_z(j).wait_send()
        for which in (0, 1):
            kv_over_z(j, which).wait_send()
    for i in range(X_CHUNKS):
        for n in range(8):
            x_copy(i, n).wait_send()
    for n in range(8):
        y_copy(n).wait_send()
    for part in range(len(PARTS)):
        for j in range(8):
            back(j, part).wait_send()


def shards(
    latent, query_in, key_in, value_in, cache_keys, cache_values, levels, timesteps, cache_mask, time_weight
):
    anywhere = pl.BlockSpec(memory_space=pl.ANY)
    scalars = pl.BlockSpec(memory_space=pltpu.SMEM)
    bf16, f32 = jnp.bfloat16, jnp.float32
    dma = pltpu.SemaphoreType.DMA
    return pl.pallas_call(
        kernel,
        out_shape=jax.ShapeDtypeStruct(latent.shape, latent.dtype),
        in_specs=[scalars] * 3 + [anywhere] * 7,
        out_specs=pl.BlockSpec(memory_space=pltpu.VMEM),
        scratch_shapes=[
            pltpu.VMEM((8, ROWS, WIDTH), bf16),
            pltpu.VMEM((CHUNKS, 2, 8, ROWS, WIDTH), bf16),
            pltpu.VMEM((2, ROWS, WIDTH), bf16),
            pltpu.VMEM((8, ROWS, WIDTH), bf16),
            pltpu.VMEM(latent.shape, bf16),
            pltpu.VMEM(latent.shape, bf16),
            pltpu.VMEM(time_weight.shape, bf16),
            pltpu.VMEM((8, latent.shape[1]), f32),
            pltpu.VMEM((GROUP, 1, KEYS), f32),
            pltpu.VMEM((GROUP, 1, KEYS), f32),
            pltpu.VMEM((GROUP, HEAD_DIM, KEYS), f32),
            pltpu.SMEM((CHUNKS * 8,), f32),
            dma((9, 3)),
            dma((X_CHUNKS, 8)),
            dma((8,)),
            dma((8, len(PARTS))),
            dma((8,)),
            dma((X_CHUNKS, 2)),
            dma((2,)),
            dma((X_CHUNKS, 8)),
            dma((8,)),
            dma((8, len(PARTS))),
            dma((1,)),
        ],
        compiler_params=pltpu.CompilerParams(
            collective_id=0, has_side_effects=True, vmem_limit_bytes=64 * 1024 * 1024
        ),
        cost_estimate=pl.CostEstimate(flops=2 * 10**9, bytes_accessed=5 * 10**6, transcendentals=4 * 10**6),
    )(
        levels, timesteps, cache_mask, latent, query_in, key_in, value_in, cache_keys, cache_values, time_weight
    )


def solution(mesh):
    return jax.shard_map(
        shards,
        mesh=mesh,
        in_specs=(
            P(("chain", "head"), None),
            P(("chain", "head"), None),
            P(("chain", "head"), None),
            P(("chain", "head"), None),
            P("chain", "head"),
            P("chain", "head"),
            P(),
            P(),
            P(),
            P(),
        ),
        out_specs=P(("chain", "head"), None),
        check_vma=False,
    )
```

```python
import functools
import math

import jax
import jax.numpy as jnp
from jax import lax
from jax.experimental import pallas as pl
from jax.experimental.pallas import tpu as pltpu
from jax.sharding import PartitionSpec as P

MESH = pl.DeviceIdType.MESH
HEAD_DIM = 128
SPANS = 4
NY, NX, NZ = 4, 4, 8
GROUP = 5
WIDTH = GROUP * HEAD_DIM
ROWS = 32
HOPS = (0, 1, 7, 2, 6, 3, 5, 4)
CHUNKS = 12
FIRST_Z = 2
X_CHUNKS = 9
KEYS = 8 * ROWS
LOG2E = 1.4426950408889634
HIDDEN = -1e30


def device(y, z, x, core):
    return {"chain": (y * 2 + z // 4) * NX + x, "head": (z % 4) * 2 + core}


def group_columns(z):
    group = (z % 4) * 2 + z // 4
    return pl.ds(pl.multiple_of(group * WIDTH, 128), WIDTH)


def kernel(
    levels, timesteps, cache_mask, latent, query_in, key_in, value_in, cache_keys, cache_values, time_weight,
    out,
    query, turned, kv, attended, returned, shifted, weight, gate, peak, total, summed, bias,
    send_z, send_x, send_y, send_o, recv_q, recv_k, recv_v, recv_x, recv_y, recv_o, local,
):
    chain, head = lax.axis_index("chain"), lax.axis_index("head")
    y, x = chain // 8, chain % 4
    zh, zl, core = (chain // 4) % 2, head // 2, head % 2
    z = zh * 4 + zl
    up, down = (y + 1) % 4, (y + 3) % 4
    right, left = (x + 1) % 4, (x + 3) % 4
    sibling = device(y, z, x, 1 - core)
    across = device(y, (z + 4) % 8, x, 1 - core)

    def remote(src, dst, send, recv, to):
        return pltpu.make_async_remote_copy(
            src_ref=src, dst_ref=dst, send_sem=send, recv_sem=recv, device_id=to, device_id_type=MESH
        )

    mine = group_columns(z)
    own = [
        pltpu.make_async_copy(key_in.at[:, mine], kv.at[0, 0, 0], recv_k.at[0]),
        pltpu.make_async_copy(value_in.at[:, mine], kv.at[0, 1, 0], recv_v.at[0]),
        pltpu.make_async_copy(query_in.at[:, mine], query.at[0], recv_q.at[0]),
    ]
    for copy in own:
        copy.start()
    weight_copy = pltpu.make_async_copy(time_weight, weight, local.at[0])
    weight_copy.start()

    @pl.when(core == zh)
    def _():
        pltpu.make_async_copy(cache_keys, kv.at[1, 0, 0], recv_k.at[1]).start()
        pltpu.make_async_copy(cache_values, kv.at[1, 1, 0], recv_v.at[1]).start()

    barrier = pltpu.get_barrier_semaphore()
    partners = [sibling, across, device(y, z, right, core), device(y, z, left, core)]
    partners += [device(up, z, x, core), device(down, z, x, core)]
    for hop in HOPS[1:]:
        partners += [device(row, (z + hop) % 8, x, core) for row in (y, up, down)]
    for partner in partners:
        pl.semaphore_signal(barrier, inc=1, device_id=partner, device_id_type=MESH)
    pl.semaphore_wait(barrier, len(partners))

    def cache_across(which, source, recv):
        return remote(source, kv.at[1, which, 0], send_z.at[0, which], recv.at[1], across)

    def query_over_z(j):
        to = (z + HOPS[j]) % 8
        return remote(
            query_in.at[:, group_columns(to)], query.at[j], send_z.at[j, 2], recv_q.at[j], device(y, to, x, core)
        )

    def kv_over_z(j, which, source, recv):
        to = (z + HOPS[j]) % 8
        return remote(
            source.at[:, group_columns(to)],
            kv.at[j + 1, which, 0],
            send_z.at[j, which],
            recv.at[j + 1],
            device(y, to, x, core),
        )

    def over_x(i):
        own_kv = kv.at[i, :, 0]
        return (
            remote(own_kv, kv.at[i, :, 1], send_x.at[i, 0], recv_x.at[i, 0], device(y, z, right, core)),
            remote(own_kv, kv.at[i, :, 3], send_x.at[i, 1], recv_x.at[i, 1], device(y, z, left, core)),
            remote(kv.at[i, 0, 1], kv.at[i, 0, 2], send_x.at[i, 2], recv_x.at[i, 2], device(y, z, right, core)),
            remote(kv.at[i, 1, 3], kv.at[i, 1, 2], send_x.at[i, 3], recv_x.at[i, 3], device(y, z, left, core)),
        )

    def to_sibling(i, send, recv):
        return remote(kv.at[i, :, 0:4], kv.at[i, :, 4:8], send, recv, sibling)

    def sibling_x(i):
        return to_sibling(i, send_x.at[i, 4], recv_x.at[i, 4])

    half = slice(0, 4)
    to_up, to_down = device(up, z, x, core), device(down, z, x, core)
    y_up = remote(kv.at[1, :, half], kv.at[9, :, half], send_y.at[0], recv_y.at[0], to_up)
    y_down = remote(kv.at[1, :, half], kv.at[10, :, half], send_y.at[1], recv_y.at[1], to_down)
    y_on_up = remote(kv.at[9, 0, half], kv.at[11, 0, half], send_y.at[2], recv_y.at[2], to_up)
    y_on_down = remote(kv.at[10, 1, half], kv.at[11, 1, half], send_y.at[3], recv_y.at[3], to_down)
    latent_down = remote(latent, shifted, send_y.at[7], recv_y.at[7], to_down)

    def sibling_y(i):
        return to_sibling(i, send_y.at[i - 5], recv_y.at[i - 5])

    def back(j):
        to = (z - HOPS[j] + 8) % 8
        return remote(attended.at[j], returned.at[:, mine], send_o.at[j], recv_o.at[j], device(down, to, x, core))

    @pl.when(core != zh)
    def _():
        cache_across(0, cache_keys, recv_k).start()
        cache_across(1, cache_values, recv_v).start()

    def start_kv(j):
        kv_over_z(j, 0, key_in, recv_k).start()
        kv_over_z(j, 1, value_in, recv_v).start()

    for j in range(1, 8):
        query_over_z(j).start()
    start_kv(1)
    start_kv(2)
    latent_down.start()

    for i in range(CHUNKS):
        for slot in range(8):
            if i == 1 or i >= 9:
                plane = {1: y, 9: down, 10: up, 11: (y + 2) % 4}[i]
                side = core if slot < 4 else 1 - core
                block = plane * 8 + side * 4 + (x + (0, 3, 2, 1)[slot % 4]) % 4
                bias[i * 8 + slot] = jnp.where(cache_mask[y, block] == 1, 0.0, HIDDEN).astype(jnp.float32)
            else:
                bias[i * 8 + slot] = jnp.float32(0.0)

    stamp = timesteps[levels[up]].astype(jnp.float32)
    count = 128
    index = lax.broadcasted_iota(jnp.int32, (8, count), 1).astype(jnp.float32)
    phase = stamp * jnp.exp(-math.log(10000.0) * index / count)
    embed = jnp.concatenate([jnp.cos(phase), jnp.sin(phase)], axis=1).astype(jnp.bfloat16)
    weight_copy.wait()

    def gate_columns(c, carry):
        columns = pl.ds(pl.multiple_of(c * WIDTH, 128), WIDTH)
        gate[:, columns] = jnp.dot(embed, weight[:, columns], preferred_element_type=jnp.float32)
        return carry

    lax.fori_loop(0, 8, gate_columns, 0)

    peak[...] = jnp.full_like(peak, HIDDEN)
    total[...] = jnp.zeros_like(total)
    summed[...] = jnp.zeros_like(summed)

    def attend(i, cached):
        def scores_of(h):
            keys = kv[i, 0, :, :, h * HEAD_DIM : (h + 1) * HEAD_DIM].reshape(KEYS, HEAD_DIM)
            return jnp.dot(keys, turned[h], preferred_element_type=jnp.float32)

        scale = LOG2E / math.sqrt(HEAD_DIM)
        following = scores_of(0)
        for h in range(GROUP):
            scores = following
            if h + 1 < GROUP:
                following = scores_of(h + 1)
            if cached:
                scores = jnp.concatenate(
                    [scores[slot * ROWS : (slot + 1) * ROWS] + bias[i * 8 + slot] for slot in range(8)], axis=0
                )
            old = peak[h]
            new = jnp.maximum(old, jnp.max(scores, axis=0, keepdims=True) * scale)
            weights = jnp.exp2(scores * scale - new)
            factor = jnp.exp2(old - new)
            values = kv[i, 1, :, :, h * HEAD_DIM : (h + 1) * HEAD_DIM].reshape(KEYS, HEAD_DIM)
            added = lax.dot_general(
                values, weights.astype(jnp.bfloat16), (((0,), (0,)), ((), ())), preferred_element_type=jnp.float32
            )
            peak[h] = new
            total[h] = factor * total[h] + jnp.sum(weights, axis=0, keepdims=True)
            summed[h] = factor * summed[h] + added

    def turn(t, carry):
        @pl.when(t < X_CHUNKS)
        def _():
            pltpu.make_async_copy(kv.at[t, 0, 0], kv.at[t, 0, 0], recv_k.at[t]).wait()
            pltpu.make_async_copy(kv.at[t, 1, 0], kv.at[t, 1, 0], recv_v.at[t]).wait()
            over_x(t)[0].start()
            over_x(t)[1].start()

        for turn_of, hops in ((1, (3, 4)), (3, (5, 6)), (5, (7,))):

            @pl.when(t == turn_of)
            def _(hops=hops):
                for j in hops:
                    start_kv(j)

        @pl.when((t >= 1) & (t < X_CHUNKS + 1))
        def _():
            copies = over_x(t - 1)
            copies[0].wait_recv()
            copies[2].start()
            copies[1].wait_recv()
            copies[3].start()

        @pl.when((t >= 2) & (t < X_CHUNKS + 2))
        def _():
            copies = over_x(t - 2)
            copies[2].wait_recv()
            copies[3].wait_recv()
            sibling_x(t - 2).start()

        @pl.when(t == 3)
        def _():
            y_up.start()
            y_down.start()
            own[2].wait()
            for j in range(1, 8):
                query_over_z(j).wait_recv()
            for h in range(GROUP):
                columns = slice(h * HEAD_DIM, (h + 1) * HEAD_DIM)
                turned[h] = query[:, :, columns].reshape(KEYS, HEAD_DIM).astype(jnp.float32).T.astype(jnp.bfloat16)

        @pl.when(t == 6)
        def _():
            y_up.wait_recv()
            y_on_up.start()
            y_down.wait_recv()
            y_on_down.start()
            sibling_y(9).start()
            sibling_y(10).start()

        @pl.when(t == 8)
        def _():
            y_on_up.wait_recv()
            y_on_down.wait_recv()
            sibling_y(11).start()

        @pl.when(t >= 3)
        def _():
            sibling_x(t - 3).wait_recv()

        @pl.when(t == 8)
        def _():
            sibling_y(9).wait_recv()

        @pl.when(t == 9)
        def _():
            sibling_y(10).wait_recv()

        @pl.when(t == 10)
        def _():
            sibling_y(11).wait_recv()

        @pl.when((t >= 3) & (t != 4))
        def _():
            attend(t - 3, False)

        @pl.when((t == 4) | ((t >= 8) & (t <= 10)))
        def _():
            attend(jnp.where(t == 4, 1, t + 1), True)

        return carry

    lax.fori_loop(0, X_CHUNKS + 3, turn, 0)

    for h in range(GROUP):
        result = summed[h] * (1.0 / total[h])
        attended[:, :, h * HEAD_DIM : (h + 1) * HEAD_DIM] = result.T.astype(jnp.bfloat16).reshape(8, ROWS, HEAD_DIM)
    for j in range(8):
        back(j).start()

    @pl.when(core != zh)
    def _():
        cache_across(0, cache_keys, recv_k).wait_send()
        cache_across(1, cache_values, recv_v).wait_send()

    for j in range(1, 8):
        query_over_z(j).wait_send()
        kv_over_z(j, 0, key_in, recv_k).wait_send()
        kv_over_z(j, 1, value_in, recv_v).wait_send()

    def sent(i, carry):
        for copy in over_x(i):
            copy.wait_send()
        sibling_x(i).wait_send()
        return carry

    lax.fori_loop(0, X_CHUNKS, sent, 0)
    for copy in (y_up, y_down, y_on_up, y_on_down, sibling_y(9), sibling_y(10), sibling_y(11), latent_down):
        copy.wait_send()

    latent_down.wait_recv()
    for j in range(8):
        back(j).wait_recv()
        columns = group_columns((z + HOPS[j]) % 8)
        out[:, columns] = (
            shifted[:, columns].astype(jnp.float32) + gate[0:1, columns] * returned[:, columns].astype(jnp.float32)
        ).astype(jnp.bfloat16)
    for j in range(8):
        back(j).wait_send()


def shards(
    latent, query_in, key_in, value_in, cache_keys, cache_values, levels, timesteps, cache_mask, time_weight
):
    anywhere = pl.BlockSpec(memory_space=pl.ANY)
    scalars = pl.BlockSpec(memory_space=pltpu.SMEM)
    bf16, f32 = jnp.bfloat16, jnp.float32
    dma = pltpu.SemaphoreType.DMA
    return pl.pallas_call(
        kernel,
        out_shape=jax.ShapeDtypeStruct(latent.shape, latent.dtype),
        in_specs=[scalars] * 3 + [anywhere] * 7,
        out_specs=pl.BlockSpec(memory_space=pltpu.VMEM),
        scratch_shapes=[
            pltpu.VMEM((8, ROWS, WIDTH), bf16),
            pltpu.VMEM((GROUP, HEAD_DIM, KEYS), bf16),
            pltpu.VMEM((CHUNKS, 2, 8, ROWS, WIDTH), bf16),
            pltpu.VMEM((8, ROWS, WIDTH), bf16),
            pltpu.VMEM(latent.shape, bf16),
            pltpu.VMEM(latent.shape, bf16),
            pltpu.VMEM(time_weight.shape, bf16),
            pltpu.VMEM((8, latent.shape[1]), f32),
            pltpu.VMEM((GROUP, 1, KEYS), f32),
            pltpu.VMEM((GROUP, 1, KEYS), f32),
            pltpu.VMEM((GROUP, HEAD_DIM, KEYS), f32),
            pltpu.SMEM((CHUNKS * 8,), f32),
            dma((8, 3)),
            dma((X_CHUNKS, 5)),
            dma((8,)),
            dma((8,)),
            dma((8,)),
            dma((X_CHUNKS,)),
            dma((X_CHUNKS,)),
            dma((X_CHUNKS, 5)),
            dma((8,)),
            dma((8,)),
            dma((1,)),
        ],
        compiler_params=pltpu.CompilerParams(
            collective_id=0, has_side_effects=True, vmem_limit_bytes=64 * 1024 * 1024
        ),
        cost_estimate=pl.CostEstimate(flops=2 * 10**9, bytes_accessed=5 * 10**6, transcendentals=4 * 10**6),
    )(
        levels, timesteps, cache_mask, latent, query_in, key_in, value_in, cache_keys, cache_values, time_weight
    )


def solution(mesh):
    return jax.shard_map(
        shards,
        mesh=mesh,
        in_specs=(
            P(("chain", "head"), None),
            P(("chain", "head"), None),
            P(("chain", "head"), None),
            P(("chain", "head"), None),
            P("chain", "head"),
            P("chain", "head"),
            P(),
            P(),
            P(),
            P(),
        ),
        out_specs=P(("chain", "head"), None),
        check_vma=False,
    )
```

```python
import functools
import math

import jax
import jax.numpy as jnp
from jax import lax
from jax.experimental import pallas as pl
from jax.experimental.pallas import tpu as pltpu
from jax.sharding import PartitionSpec as P

MESH = pl.DeviceIdType.MESH
HEAD_DIM = 128
SPANS = 4
NY, NX, NZ = 4, 4, 8
GROUP = 5
WIDTH = GROUP * HEAD_DIM
ROWS = 32
CHUNKS = 12
FIRST_Z = 2
X_CHUNKS = 9
KEYS = 8 * ROWS
LOG2E = 1.4426950408889634
HIDDEN = -1e30


def device(y, z, x, core):
    return {"chain": (y * 2 + z // 4) * NX + x, "head": (z % 4) * 2 + core}


def group_columns(z):
    group = (z % 4) * 2 + z // 4
    return pl.ds(pl.multiple_of(group * WIDTH, 128), WIDTH)


def hop_of(j):
    return jnp.where(j % 2 == 1, (j + 1) // 2, (8 - j // 2) % 8)


def kernel(
    levels, timesteps, cache_mask, latent, query_in, key_in, value_in, cache_keys, cache_values, time_weight,
    out,
    query, turned, kv, attended, returned, shifted, weight, gate, peak, total, summed, bias,
    send_z, send_x, send_y, send_o, recv_q, recv_kv, recv_x, recv_y, recv_o, local,
):
    chain, head = lax.axis_index("chain"), lax.axis_index("head")
    y, x = chain // 8, chain % 4
    zh, zl, core = (chain // 4) % 2, head // 2, head % 2
    z = zh * 4 + zl
    up, down = (y + 1) % 4, (y + 3) % 4
    right, left = device(y, z, (x + 1) % 4, core), device(y, z, (x + 3) % 4, core)
    sibling = device(y, z, x, 1 - core)
    across = device(y, (z + 4) % 8, x, 1 - core)
    to_up, to_down = device(up, z, x, core), device(down, z, x, core)
    mine = group_columns(z)

    def loop(lower, upper, body):
        def step(n, carry):
            body(n)
            return carry

        lax.fori_loop(lower, upper, step, 0)

    def remote(src, dst, send, recv, to):
        return pltpu.make_async_remote_copy(
            src_ref=src, dst_ref=dst, send_sem=send, recv_sem=recv, device_id=to, device_id_type=MESH
        )

    pltpu.make_async_copy(key_in.at[:, mine], kv.at[0, 0, 0], recv_kv.at[0, 0]).start()
    pltpu.make_async_copy(value_in.at[:, mine], kv.at[0, 1, 0], recv_kv.at[0, 1]).start()
    own_query = pltpu.make_async_copy(query_in.at[:, mine], query.at[0], recv_q.at[0])
    own_query.start()
    weight_copy = pltpu.make_async_copy(time_weight, weight, local.at[0])
    weight_copy.start()

    @pl.when(core == zh)
    def _():
        pltpu.make_async_copy(cache_keys, kv.at[1, 0, 0], recv_kv.at[1, 0]).start()
        pltpu.make_async_copy(cache_values, kv.at[1, 1, 0], recv_kv.at[1, 1]).start()

    barrier = pltpu.get_barrier_semaphore()

    def greet(partner):
        pl.semaphore_signal(barrier, inc=1, device_id=partner, device_id_type=MESH)

    for partner in (sibling, across, right, left, to_up, to_down):
        greet(partner)

    @functools.partial(loop, 1, 8)
    def _(hop):
        for row in (y, up, down):
            greet(device(row, (z + hop) % 8, x, core))

    pl.semaphore_wait(barrier, 6 + 21)

    def cache_across(which, source):
        return remote(source, kv.at[1, which, 0], send_z.at[0, which], recv_kv.at[1, which], across)

    def query_over_z(j):
        to = (z + hop_of(j)) % 8
        return remote(
            query_in.at[:, group_columns(to)], query.at[j], send_z.at[j, 2], recv_q.at[j], device(y, to, x, core)
        )

    def kv_over_z(j, which):
        to = (z + hop_of(j)) % 8
        return remote(
            (key_in, value_in)[which].at[:, group_columns(to)],
            kv.at[j + 1, which, 0],
            send_z.at[j, which],
            recv_kv.at[j + 1, which],
            device(y, to, x, core),
        )

    def x_copy(i, n):
        src, dst, to = (
            lambda: (kv.at[i, :, 0], kv.at[i, :, 1], right),
            lambda: (kv.at[i, :, 0], kv.at[i, :, 3], left),
            lambda: (kv.at[i, 0, 1], kv.at[i, 0, 2], right),
            lambda: (kv.at[i, 1, 3], kv.at[i, 1, 2], left),
            lambda: (kv.at[i, :, 0:4], kv.at[i, :, 4:8], sibling),
        )[n]()
        return remote(src, dst, send_x.at[i, n], recv_x.at[i, n], to)

    def y_copy(n):
        src, dst, to = (
            lambda: (kv.at[1, :, 0:4], kv.at[9, :, 0:4], to_up),
            lambda: (kv.at[1, :, 0:4], kv.at[10, :, 0:4], to_down),
            lambda: (kv.at[9, 0, 0:4], kv.at[11, 0, 0:4], to_up),
            lambda: (kv.at[10, 1, 0:4], kv.at[11, 1, 0:4], to_down),
            lambda: (kv.at[9, :, 0:4], kv.at[9, :, 4:8], sibling),
            lambda: (kv.at[10, :, 0:4], kv.at[10, :, 4:8], sibling),
            lambda: (kv.at[11, :, 0:4], kv.at[11, :, 4:8], sibling),
            lambda: (latent, shifted, to_down),
        )[n]()
        return remote(src, dst, send_y.at[n], recv_y.at[n], to)

    def back(j):
        to = device(down, (z - hop_of(j) + 8) % 8, x, core)
        return remote(attended.at[j], returned.at[:, mine], send_o.at[j], recv_o.at[j], to)

    def start_kv(j):
        kv_over_z(j, 0).start()
        kv_over_z(j, 1).start()

    @pl.when(core != zh)
    def _():
        cache_across(0, cache_keys).start()
        cache_across(1, cache_values).start()

    loop(1, 8, lambda j: query_over_z(j).start())
    loop(1, 3, start_kv)
    y_copy(7).start()

    def prepare():
        def show(n):
            i, slot = n // 8, n % 8
            plane = jnp.where(i == 1, y, jnp.where(i == 9, down, jnp.where(i == 10, up, (y + 2) % 4)))
            side = jnp.where(slot < 4, core, 1 - core)
            block = plane * 8 + side * 4 + (x + 4 - slot % 4) % 4
            hidden = ((i == 1) | (i >= 9)) & (cache_mask[y, block] == 0)
            bias[n] = jnp.where(hidden, HIDDEN, 0.0).astype(jnp.float32)

        loop(0, CHUNKS * 8, show)

        stamp = timesteps[levels[up]].astype(jnp.float32)
        count = 128
        index = lax.broadcasted_iota(jnp.int32, (8, count), 1).astype(jnp.float32)
        phase = stamp * jnp.exp(-math.log(10000.0) * index / count)
        embed = jnp.concatenate([jnp.cos(phase), jnp.sin(phase)], axis=1).astype(jnp.bfloat16)
        weight_copy.wait()

        def gate_columns(c):
            columns = pl.ds(pl.multiple_of(c * WIDTH, 128), WIDTH)
            gate[:, columns] = jnp.dot(embed, weight[:, columns], preferred_element_type=jnp.float32)

        loop(0, 8, gate_columns)

        def clear(h):
            peak[h] = jnp.full_like(peak[h], HIDDEN)
            total[h] = jnp.zeros_like(total[h])
            summed[h] = jnp.zeros_like(summed[h])

        loop(0, GROUP, clear)

    def of_head(h):
        return pl.ds(pl.multiple_of(h * HEAD_DIM, 128), HEAD_DIM)

    def turn_query(h):
        rows = query[:, :, of_head(h)].reshape(KEYS, HEAD_DIM)
        turned[h] = rows.astype(jnp.float32).T.astype(jnp.bfloat16)

    def attend(i):
        def scores_of(h):
            keys = kv[i, 0, :, :, of_head(h)].reshape(KEYS, HEAD_DIM)
            return jnp.dot(keys, turned[h], preferred_element_type=jnp.float32)

        scale = LOG2E / math.sqrt(HEAD_DIM)

        def one_head(h, scores):
            following = scores_of(jnp.minimum(h + 1, GROUP - 1))
            scores = jnp.concatenate(
                [scores[slot * ROWS : (slot + 1) * ROWS] + bias[i * 8 + slot] for slot in range(8)], axis=0
            )
            old = peak[h]
            new = jnp.maximum(old, jnp.max(scores, axis=0, keepdims=True) * scale)
            weights = jnp.exp2(scores * scale - new)
            factor = jnp.exp2(old - new)
            values = kv[i, 1, :, :, of_head(h)].reshape(KEYS, HEAD_DIM)
            added = lax.dot_general(
                values, weights.astype(jnp.bfloat16), (((0,), (0,)), ((), ())), preferred_element_type=jnp.float32
            )
            peak[h] = new
            total[h] = factor * total[h] + jnp.sum(weights, axis=0, keepdims=True)
            summed[h] = factor * summed[h] + added
            return following

        lax.fori_loop(0, GROUP, one_head, scores_of(0))

    def turn(t, carry):
        @pl.when(t < X_CHUNKS)
        def _():
            for which in (0, 1):
                place = kv.at[t, which, 0]
                pltpu.make_async_copy(place, place, recv_kv.at[t, which]).wait()
            x_copy(t, 0).start()
            x_copy(t, 1).start()

        @pl.when((t == 1) | (t == 3))
        def _():
            start_kv(t + 2)
            start_kv(t + 3)

        @pl.when(t == 5)
        def _():
            start_kv(7)

        @pl.when((t >= 1) & (t < X_CHUNKS + 1))
        def _():
            x_copy(t - 1, 0).wait_recv()
            x_copy(t - 1, 2).start()
            x_copy(t - 1, 1).wait_recv()
            x_copy(t - 1, 3).start()

        pl.when(t == 1)(prepare)

        @pl.when((t >= 2) & (t < X_CHUNKS + 2))
        def _():
            x_copy(t - 2, 2).wait_recv()
            x_copy(t - 2, 3).wait_recv()
            x_copy(t - 2, 4).start()

        @pl.when(t == 3)
        def _():
            y_copy(0).start()
            y_copy(1).start()
            own_query.wait()
            loop(1, 8, lambda j: query_over_z(j).wait_recv())
            loop(0, GROUP, turn_query)

        @pl.when(t == 6)
        def _():
            for n in (0, 1):
                y_copy(n).wait_recv()
                y_copy(n + 2).start()
                y_copy(n + 4).start()

        @pl.when(t == 8)
        def _():
            y_copy(2).wait_recv()
            y_copy(3).wait_recv()
            y_copy(6).start()

        @pl.when(t >= 3)
        def _():
            x_copy(t - 3, 4).wait_recv()

        for n in (4, 5, 6):

            @pl.when(t == n + 4)
            def _(n=n):
                y_copy(n).wait_recv()

        def ready(e):
            attend(jnp.where(e == 0, t - 3, t + 1))

        loop(0, jnp.where(t < 3, 0, jnp.where((t >= 8) & (t <= 10), 2, 1)), ready)
        return carry

    lax.fori_loop(0, X_CHUNKS + 3, turn, 0)

    def finish(h):
        result = summed[h] * (1.0 / total[h])
        attended[:, :, of_head(h)] = result.T.astype(jnp.bfloat16).reshape(8, ROWS, HEAD_DIM)

    loop(0, GROUP, finish)
    loop(0, 8, lambda j: back(j).start())

    @pl.when(core != zh)
    def _():
        cache_across(0, cache_keys).wait_send()
        cache_across(1, cache_values).wait_send()

    @functools.partial(loop, 1, 8)
    def _(j):
        query_over_z(j).wait_send()
        kv_over_z(j, 0).wait_send()
        kv_over_z(j, 1).wait_send()

    @functools.partial(loop, 0, X_CHUNKS)
    def _(i):
        for n in range(5):
            x_copy(i, n).wait_send()

    for n in range(8):
        y_copy(n).wait_send()

    y_copy(7).wait_recv()

    @functools.partial(loop, 0, 8)
    def _(j):
        back(j).wait_recv()
        columns = group_columns((z + hop_of(j)) % 8)
        out[:, columns] = (
            shifted[:, columns].astype(jnp.float32) + gate[0:1, columns] * returned[:, columns].astype(jnp.float32)
        ).astype(jnp.bfloat16)

    loop(0, 8, lambda j: back(j).wait_send())


def shards(
    latent, query_in, key_in, value_in, cache_keys, cache_values, levels, timesteps, cache_mask, time_weight
):
    anywhere = pl.BlockSpec(memory_space=pl.ANY)
    scalars = pl.BlockSpec(memory_space=pltpu.SMEM)
    bf16, f32 = jnp.bfloat16, jnp.float32
    dma = pltpu.SemaphoreType.DMA
    return pl.pallas_call(
        kernel,
        out_shape=jax.ShapeDtypeStruct(latent.shape, latent.dtype),
        in_specs=[scalars] * 3 + [anywhere] * 7,
        out_specs=pl.BlockSpec(memory_space=pltpu.VMEM),
        scratch_shapes=[
            pltpu.VMEM((8, ROWS, WIDTH), bf16),
            pltpu.VMEM((GROUP, HEAD_DIM, KEYS), bf16),
            pltpu.VMEM((CHUNKS, 2, 8, ROWS, WIDTH), bf16),
            pltpu.VMEM((8, ROWS, WIDTH), bf16),
            pltpu.VMEM(latent.shape, bf16),
            pltpu.VMEM(latent.shape, bf16),
            pltpu.VMEM(time_weight.shape, bf16),
            pltpu.VMEM((8, latent.shape[1]), f32),
            pltpu.VMEM((GROUP, 1, KEYS), f32),
            pltpu.VMEM((GROUP, 1, KEYS), f32),
            pltpu.VMEM((GROUP, HEAD_DIM, KEYS), f32),
            pltpu.SMEM((CHUNKS * 8,), f32),
            dma((8, 3)),
            dma((X_CHUNKS, 5)),
            dma((8,)),
            dma((8,)),
            dma((8,)),
            dma((X_CHUNKS, 2)),
            dma((X_CHUNKS, 5)),
            dma((8,)),
            dma((8,)),
            dma((1,)),
        ],
        compiler_params=pltpu.CompilerParams(
            collective_id=0, has_side_effects=True, vmem_limit_bytes=64 * 1024 * 1024
        ),
        cost_estimate=pl.CostEstimate(flops=2 * 10**9, bytes_accessed=5 * 10**6, transcendentals=4 * 10**6),
    )(
        levels, timesteps, cache_mask, latent, query_in, key_in, value_in, cache_keys, cache_values, time_weight
    )


def solution(mesh):
    return jax.shard_map(
        shards,
        mesh=mesh,
        in_specs=(
            P(("chain", "head"), None),
            P(("chain", "head"), None),
            P(("chain", "head"), None),
            P(("chain", "head"), None),
            P("chain", "head"),
            P("chain", "head"),
            P(),
            P(),
            P(),
            P(),
        ),
        out_specs=P(("chain", "head"), None),
        check_vma=False,
    )
```

```python
import functools
import math

import jax
import jax.numpy as jnp
from jax import lax
from jax.experimental import pallas as pl
from jax.experimental.pallas import tpu as pltpu
from jax.sharding import PartitionSpec as P

MESH = pl.DeviceIdType.MESH
HEAD_DIM = 128
SPANS = 4
NY, NX, NZ = 4, 4, 8
GROUP = 5
WIDTH = GROUP * HEAD_DIM
ROWS = 32
HOPS = (0, 1, 7, 2, 6, 3, 5, 4)
ITEMS = (0, 2, 3, 5, 6, 7, 8, 4)
CHUNKS = 12
FIRST_Z = 2
X_CHUNKS = 9
KEYS = 8 * ROWS
LOG2E = 1.4426950408889634
HIDDEN = -1e30


def device(y, z, x, core):
    return {"chain": (y * 2 + z // 4) * NX + x, "head": (z % 4) * 2 + core}


def first_column(z):
    return ((z % 4) * 2 + z // 4) * WIDTH


def group_columns(z):
    return pl.ds(pl.multiple_of(first_column(z), 128), WIDTH)


def kernel(
    levels, timesteps, cache_mask, latent, query_in, key_in, value_in, cache_keys, cache_values, time_weight,
    out,
    query, turned, kv, relay, relay_o, attended, returned, shifted, weight, gate, peak, total, summed, bias,
    send_z, send_x, send_y, send_o, recv_q, recv_k, recv_v, recv_relay, recv_x, recv_y, recv_o, local,
):
    chain, head = lax.axis_index("chain"), lax.axis_index("head")
    y, x = chain // 8, chain % 4
    zh, zl, core = (chain // 4) % 2, head // 2, head % 2
    z = zh * 4 + zl
    up, down = (y + 1) % 4, (y + 3) % 4
    right, left = (x + 1) % 4, (x + 3) % 4
    sibling = device(y, z, x, 1 - core)
    across = device(y, (z + 4) % 8, x, 1 - core)
    back_two = device(y, (z + 6) % 8, x, core)

    def remote(src, dst, send, recv, to):
        return pltpu.make_async_remote_copy(
            src_ref=src, dst_ref=dst, send_sem=send, recv_sem=recv, device_id=to, device_id_type=MESH
        )

    mine = group_columns(z)
    own = [
        pltpu.make_async_copy(key_in.at[:, mine], kv.at[0, 0, 0], recv_k.at[0]),
        pltpu.make_async_copy(value_in.at[:, mine], kv.at[0, 1, 0], recv_v.at[0]),
        pltpu.make_async_copy(query_in.at[:, mine], query.at[0], recv_q.at[0]),
    ]
    for copy in own:
        copy.start()
    weight_copy = pltpu.make_async_copy(time_weight, weight, local.at[0])
    weight_copy.start()

    @pl.when(core == zh)
    def _():
        pltpu.make_async_copy(cache_keys, kv.at[1, 0, 0], recv_k.at[1]).start()
        pltpu.make_async_copy(cache_values, kv.at[1, 1, 0], recv_v.at[1]).start()

    barrier = pltpu.get_barrier_semaphore()
    partners = [sibling, across, device(y, z, right, core), device(y, z, left, core)]
    partners += [device(up, z, x, core), device(down, z, x, core)]
    for hop in HOPS[1:]:
        partners += [device(row, (z + hop) % 8, x, core) for row in (y, up, down)]
    for partner in partners:
        pl.semaphore_signal(barrier, inc=1, device_id=partner, device_id_type=MESH)
    pl.semaphore_wait(barrier, len(partners))

    def cache_across(which, source, recv):
        return remote(source, kv.at[1, which, 0], send_z.at[0, which], recv.at[1], across)

    def query_over_z(j):
        to = (z + HOPS[j]) % 8
        return remote(
            query_in.at[:, group_columns(to)], query.at[j], send_z.at[j, 2], recv_q.at[j], device(y, to, x, core)
        )

    def kv_over_z(j, which, source, recv):
        to = (z + HOPS[j]) % 8
        source = source.at[:, group_columns(to)]
        if HOPS[j] == 4:
            return remote(source, relay.at[which], send_z.at[j, which], recv_relay.at[which], back_two)
        return remote(
            source, kv.at[ITEMS[j], which, 0], send_z.at[j, which], recv.at[ITEMS[j]], device(y, to, x, core)
        )

    def relay_on(which, recv):
        return remote(relay.at[which], kv.at[ITEMS[7], which, 0], send_z.at[8, which], recv.at[ITEMS[7]], back_two)

    def over_x(i):
        own_kv = kv.at[i, :, 0]
        return (
            remote(own_kv, kv.at[i, :, 1], send_x.at[i, 0], recv_x.at[i, 0], device(y, z, right, core)),
            remote(own_kv, kv.at[i, :, 3], send_x.at[i, 1], recv_x.at[i, 1], device(y, z, left, core)),
            remote(kv.at[i, 0, 1], kv.at[i, 0, 2], send_x.at[i, 2], recv_x.at[i, 2], device(y, z, right, core)),
            remote(kv.at[i, 1, 3], kv.at[i, 1, 2], send_x.at[i, 3], recv_x.at[i, 3], device(y, z, left, core)),
        )

    def to_sibling(i, send, recv):
        return remote(kv.at[i, :, 0:4], kv.at[i, :, 4:8], send, recv, sibling)

    def sibling_x(i):
        return to_sibling(i, send_x.at[i, 4], recv_x.at[i, 4])

    half = slice(0, 4)
    to_up, to_down = device(up, z, x, core), device(down, z, x, core)
    y_up = remote(kv.at[1, :, half], kv.at[9, :, half], send_y.at[0], recv_y.at[0], to_up)
    y_down = remote(kv.at[1, :, half], kv.at[10, :, half], send_y.at[1], recv_y.at[1], to_down)
    y_on_up = remote(kv.at[9, 0, half], kv.at[11, 0, half], send_y.at[2], recv_y.at[2], to_up)
    y_on_down = remote(kv.at[10, 1, half], kv.at[11, 1, half], send_y.at[3], recv_y.at[3], to_down)
    latent_down = remote(latent, shifted, send_y.at[7], recv_y.at[7], to_down)

    def sibling_y(i):
        return to_sibling(i, send_y.at[i - 5], recv_y.at[i - 5])

    cut = 3 * HEAD_DIM
    lower = pl.ds(pl.multiple_of(first_column(z), 128), cut)

    def upper(z):
        return pl.ds(pl.multiple_of(first_column(z) + cut, 128), WIDTH - cut)

    def back(j):
        to = device(down, (z - HOPS[j] + 8) % 8, x, core)
        if HOPS[j] == 4:
            return remote(attended.at[j, :, 0:cut], returned.at[:, lower], send_o.at[j], recv_o.at[j], to)
        return remote(attended.at[j], returned.at[:, mine], send_o.at[j], recv_o.at[j], to)

    back_relay = remote(
        attended.at[7, :, cut:WIDTH], relay_o, send_o.at[8], recv_o.at[8], device(down, (z + 6) % 8, x, core)
    )
    back_last = remote(relay_o, returned.at[:, upper((z + 2) % 8)], send_o.at[9], recv_o.at[9], back_two)

    @pl.when(core != zh)
    def _():
        cache_across(0, cache_keys, recv_k).start()
        cache_across(1, cache_values, recv_v).start()

    def start_kv(j):
        kv_over_z(j, 0, key_in, recv_k).start()
        kv_over_z(j, 1, value_in, recv_v).start()

    for j in range(1, 8):
        query_over_z(j).start()
    start_kv(1)
    start_kv(2)
    start_kv(7)
    latent_down.start()

    for i in range(CHUNKS):
        for slot in range(8):
            if i == 1 or i >= 9:
                plane = {1: y, 9: down, 10: up, 11: (y + 2) % 4}[i]
                side = core if slot < 4 else 1 - core
                block = plane * 8 + side * 4 + (x + (0, 3, 2, 1)[slot % 4]) % 4
                bias[i * 8 + slot] = jnp.where(cache_mask[y, block] == 1, 0.0, HIDDEN).astype(jnp.float32)
            else:
                bias[i * 8 + slot] = jnp.float32(0.0)

    stamp = timesteps[levels[up]].astype(jnp.float32)
    count = 128
    index = lax.broadcasted_iota(jnp.int32, (8, count), 1).astype(jnp.float32)
    phase = stamp * jnp.exp(-math.log(10000.0) * index / count)
    embed = jnp.concatenate([jnp.cos(phase), jnp.sin(phase)], axis=1).astype(jnp.bfloat16)
    weight_copy.wait()

    def gate_columns(c, carry):
        columns = pl.ds(pl.multiple_of(c * WIDTH, 128), WIDTH)
        gate[:, columns] = jnp.dot(embed, weight[:, columns], preferred_element_type=jnp.float32)
        return carry

    lax.fori_loop(0, 8, gate_columns, 0)

    peak[...] = jnp.full_like(peak, HIDDEN)
    total[...] = jnp.zeros_like(total)
    summed[...] = jnp.zeros_like(summed)

    def attend(i, cached):
        def scores_of(h):
            keys = kv[i, 0, :, :, h * HEAD_DIM : (h + 1) * HEAD_DIM].reshape(KEYS, HEAD_DIM)
            return jnp.dot(keys, turned[h], preferred_element_type=jnp.float32)

        scale = LOG2E / math.sqrt(HEAD_DIM)
        following = scores_of(0)
        for h in range(GROUP):
            scores = following
            if h + 1 < GROUP:
                following = scores_of(h + 1)
            if cached:
                scores = jnp.concatenate(
                    [scores[slot * ROWS : (slot + 1) * ROWS] + bias[i * 8 + slot] for slot in range(8)], axis=0
                )
            old = peak[h]
            new = jnp.maximum(old, jnp.max(scores, axis=0, keepdims=True) * scale)
            weights = jnp.exp2(scores * scale - new)
            factor = jnp.exp2(old - new)
            values = kv[i, 1, :, :, h * HEAD_DIM : (h + 1) * HEAD_DIM].reshape(KEYS, HEAD_DIM)
            added = lax.dot_general(
                values, weights.astype(jnp.bfloat16), (((0,), (0,)), ((), ())), preferred_element_type=jnp.float32
            )
            peak[h] = new
            total[h] = factor * total[h] + jnp.sum(weights, axis=0, keepdims=True)
            summed[h] = factor * summed[h] + added

    def turn(t, carry):
        @pl.when(t < X_CHUNKS)
        def _():
            pltpu.make_async_copy(kv.at[t, 0, 0], kv.at[t, 0, 0], recv_k.at[t]).wait()
            pltpu.make_async_copy(kv.at[t, 1, 0], kv.at[t, 1, 0], recv_v.at[t]).wait()
            over_x(t)[0].start()
            over_x(t)[1].start()

        for turn_of, hops in ((1, (3, 4)), (3, (5, 6))):

            @pl.when(t == turn_of)
            def _(hops=hops):
                for j in hops:
                    start_kv(j)

        @pl.when((t >= 1) & (t < X_CHUNKS + 1))
        def _():
            copies = over_x(t - 1)
            copies[0].wait_recv()
            copies[2].start()
            copies[1].wait_recv()
            copies[3].start()

        @pl.when((t >= 2) & (t < X_CHUNKS + 2))
        def _():
            copies = over_x(t - 2)
            copies[2].wait_recv()
            copies[3].wait_recv()
            sibling_x(t - 2).start()

        @pl.when(t == 3)
        def _():
            for which, source, recv in ((0, key_in, recv_k), (1, value_in, recv_v)):
                kv_over_z(7, which, source, recv).wait_recv()
                relay_on(which, recv).start()
            y_up.start()
            y_down.start()
            own[2].wait()
            for j in range(1, 8):
                query_over_z(j).wait_recv()
            for h in range(GROUP):
                columns = slice(h * HEAD_DIM, (h + 1) * HEAD_DIM)
                turned[h] = query[:, :, columns].reshape(KEYS, HEAD_DIM).astype(jnp.float32).T.astype(jnp.bfloat16)

        @pl.when(t == 6)
        def _():
            y_up.wait_recv()
            y_on_up.start()
            y_down.wait_recv()
            y_on_down.start()
            sibling_y(9).start()
            sibling_y(10).start()

        @pl.when(t == 8)
        def _():
            y_on_up.wait_recv()
            y_on_down.wait_recv()
            sibling_y(11).start()

        @pl.when(t >= 3)
        def _():
            sibling_x(t - 3).wait_recv()

        @pl.when(t == 8)
        def _():
            sibling_y(9).wait_recv()

        @pl.when(t == 9)
        def _():
            sibling_y(10).wait_recv()

        @pl.when(t == 10)
        def _():
            sibling_y(11).wait_recv()

        @pl.when((t >= 3) & (t != 4))
        def _():
            attend(t - 3, False)

        @pl.when((t == 4) | ((t >= 8) & (t <= 10)))
        def _():
            attend(jnp.where(t == 4, 1, t + 1), True)

        return carry

    lax.fori_loop(0, X_CHUNKS + 3, turn, 0)

    for h in range(GROUP):
        result = summed[h] * (1.0 / total[h])
        attended[:, :, h * HEAD_DIM : (h + 1) * HEAD_DIM] = result.T.astype(jnp.bfloat16).reshape(8, ROWS, HEAD_DIM)
    back_relay.start()
    for j in range(8):
        back(j).start()

    @pl.when(core != zh)
    def _():
        cache_across(0, cache_keys, recv_k).wait_send()
        cache_across(1, cache_values, recv_v).wait_send()

    relay_on(0, recv_k).wait_send()
    relay_on(1, recv_v).wait_send()
    for j in range(1, 8):
        query_over_z(j).wait_send()
        kv_over_z(j, 0, key_in, recv_k).wait_send()
        kv_over_z(j, 1, value_in, recv_v).wait_send()

    def sent(i, carry):
        for copy in over_x(i):
            copy.wait_send()
        sibling_x(i).wait_send()
        return carry

    lax.fori_loop(0, X_CHUNKS, sent, 0)
    for copy in (y_up, y_down, y_on_up, y_on_down, sibling_y(9), sibling_y(10), sibling_y(11), latent_down):
        copy.wait_send()

    latent_down.wait_recv()
    back_relay.wait_recv()
    back_last.start()
    for j in range(8):
        back(j).wait_recv()
        if j == 7:
            back_last.wait_recv()
        columns = group_columns((z + HOPS[j]) % 8)
        out[:, columns] = (
            shifted[:, columns].astype(jnp.float32) + gate[0:1, columns] * returned[:, columns].astype(jnp.float32)
        ).astype(jnp.bfloat16)
    for j in range(8):
        back(j).wait_send()
    back_relay.wait_send()
    back_last.wait_send()


def shards(
    latent, query_in, key_in, value_in, cache_keys, cache_values, levels, timesteps, cache_mask, time_weight
):
    anywhere = pl.BlockSpec(memory_space=pl.ANY)
    scalars = pl.BlockSpec(memory_space=pltpu.SMEM)
    bf16, f32 = jnp.bfloat16, jnp.float32
    dma = pltpu.SemaphoreType.DMA
    return pl.pallas_call(
        kernel,
        out_shape=jax.ShapeDtypeStruct(latent.shape, latent.dtype),
        in_specs=[scalars] * 3 + [anywhere] * 7,
        out_specs=pl.BlockSpec(memory_space=pltpu.VMEM),
        scratch_shapes=[
            pltpu.VMEM((8, ROWS, WIDTH), bf16),
            pltpu.VMEM((GROUP, HEAD_DIM, KEYS), bf16),
            pltpu.VMEM((CHUNKS, 2, 8, ROWS, WIDTH), bf16),
            pltpu.VMEM((2, ROWS, WIDTH), bf16),
            pltpu.VMEM((ROWS, 2 * HEAD_DIM), bf16),
            pltpu.VMEM((8, ROWS, WIDTH), bf16),
            pltpu.VMEM(latent.shape, bf16),
            pltpu.VMEM(latent.shape, bf16),
            pltpu.VMEM(time_weight.shape, bf16),
            pltpu.VMEM((8, latent.shape[1]), f32),
            pltpu.VMEM((GROUP, 1, KEYS), f32),
            pltpu.VMEM((GROUP, 1, KEYS), f32),
            pltpu.VMEM((GROUP, HEAD_DIM, KEYS), f32),
            pltpu.SMEM((CHUNKS * 8,), f32),
            dma((9, 3)),
            dma((X_CHUNKS, 5)),
            dma((8,)),
            dma((10,)),
            dma((8,)),
            dma((X_CHUNKS,)),
            dma((X_CHUNKS,)),
            dma((2,)),
            dma((X_CHUNKS, 5)),
            dma((8,)),
            dma((10,)),
            dma((1,)),
        ],
        compiler_params=pltpu.CompilerParams(
            collective_id=0, has_side_effects=True, vmem_limit_bytes=64 * 1024 * 1024
        ),
        cost_estimate=pl.CostEstimate(flops=2 * 10**9, bytes_accessed=5 * 10**6, transcendentals=4 * 10**6),
    )(
        levels, timesteps, cache_mask, latent, query_in, key_in, value_in, cache_keys, cache_values, time_weight
    )


def solution(mesh):
    return jax.shard_map(
        shards,
        mesh=mesh,
        in_specs=(
            P(("chain", "head"), None),
            P(("chain", "head"), None),
            P(("chain", "head"), None),
            P(("chain", "head"), None),
            P("chain", "head"),
            P("chain", "head"),
            P(),
            P(),
            P(),
            P(),
        ),
        out_specs=P(("chain", "head"), None),
        check_vma=False,
    )
```

```python
import functools
import math

import jax
import jax.numpy as jnp
from jax import lax
from jax.experimental import pallas as pl
from jax.experimental.pallas import tpu as pltpu
from jax.sharding import PartitionSpec as P

MESH = pl.DeviceIdType.MESH
HEAD_DIM = 128
SPANS = 4
NY, NX, NZ = 4, 4, 8
GROUP = 5
WIDTH = GROUP * HEAD_DIM
ROWS = 32
HOPS = (0, 1, 7, 2, 6, 3, 5, 4)
CHUNKS = 12
ATTEND = (0, 1, 2, 3, 9, 10, 4, 5, 11, 6, 7, 8)
PLACE = tuple(ATTEND.index(i) for i in range(CHUNKS))
X_CHUNKS = 9
PARTS = ((0, 3), (3, 5))
KEYS = 8 * ROWS
LOG2E = 1.4426950408889634
HIDDEN = -1e30


def device(y, z, x, core):
    return {"chain": (y * 2 + z // 4) * NX + x, "head": (z % 4) * 2 + core}


def group_columns(z):
    group = (z % 4) * 2 + z // 4
    return pl.ds(pl.multiple_of(group * WIDTH, 128), WIDTH)


def part_columns(z, part):
    group = (z % 4) * 2 + z // 4
    lower, upper = PARTS[part]
    return pl.ds(pl.multiple_of(group * WIDTH + lower * HEAD_DIM, 128), (upper - lower) * HEAD_DIM)


def kernel(
    levels, timesteps, cache_mask, latent, query_in, key_in, value_in, cache_keys, cache_values, time_weight,
    out,
    query, turned, kv, attended, returned, shifted, weight, gate, peak, total, summed, bias,
    send_z, send_x, send_y, send_o, recv_q, recv_kv, recv_x, recv_y, recv_o, local,
):
    chain, head = lax.axis_index("chain"), lax.axis_index("head")
    y, x = chain // 8, chain % 4
    zh, zl, core = (chain // 4) % 2, head // 2, head % 2
    z = zh * 4 + zl
    up, down = (y + 1) % 4, (y + 3) % 4
    right, left = device(y, z, (x + 1) % 4, core), device(y, z, (x + 3) % 4, core)
    sibling = device(y, z, x, 1 - core)
    across = device(y, (z + 4) % 8, x, 1 - core)
    to_up, to_down = device(up, z, x, core), device(down, z, x, core)
    mine = group_columns(z)

    def remote(src, dst, send, recv, to):
        return pltpu.make_async_remote_copy(
            src_ref=src, dst_ref=dst, send_sem=send, recv_sem=recv, device_id=to, device_id_type=MESH
        )

    def chunk(i):
        return kv.at[PLACE[i]]

    own_query = pltpu.make_async_copy(query_in.at[:, mine], query.at[0], recv_q.at[0])
    own_query.start()
    for which, source in enumerate((key_in, value_in)):
        pltpu.make_async_copy(source.at[:, mine], chunk(0).at[which, 0], recv_kv.at[0, which]).start()
    weight_copy = pltpu.make_async_copy(time_weight, weight, local.at[0])
    weight_copy.start()

    @pl.when(core == zh)
    def _():
        for which, source in enumerate((cache_keys, cache_values)):
            pltpu.make_async_copy(source, chunk(1).at[which, 0], recv_kv.at[1, which]).start()

    barrier = pltpu.get_barrier_semaphore()
    partners = [sibling, across, right, left, to_up, to_down]
    for hop in HOPS[1:]:
        partners += [device(row, (z + hop) % 8, x, core) for row in (y, up, down)]
    for partner in partners:
        pl.semaphore_signal(barrier, inc=1, device_id=partner, device_id_type=MESH)
    pl.semaphore_wait(barrier, len(partners))

    def cache_across(which):
        source = (cache_keys, cache_values)[which]
        return remote(source, chunk(1).at[which, 0], send_z.at[0, which], recv_kv.at[1, which], across)

    def query_over_z(j):
        to = (z + HOPS[j]) % 8
        return remote(
            query_in.at[:, group_columns(to)], query.at[j], send_z.at[j, 2], recv_q.at[j], device(y, to, x, core)
        )

    def kv_over_z(j, which):
        to = (z + HOPS[j]) % 8
        source = (key_in, value_in)[which].at[:, group_columns(to)]
        return remote(
            source, chunk(j + 1).at[which, 0], send_z.at[j, which], recv_kv.at[j + 1, which], device(y, to, x, core)
        )

    def x_copy(i, n):
        c = chunk(i)
        src, dst, to = (
            (c.at[:, 0], c.at[:, 1], right),
            (c.at[:, 0], c.at[:, 3], left),
            (c.at[0, 1], c.at[0, 2], right),
            (c.at[1, 3], c.at[1, 2], left),
            (c.at[:, 0:4], c.at[:, 4:8], sibling),
        )[n]
        return remote(src, dst, send_x.at[i, n], recv_x.at[i, n], to)

    def y_copy(n):
        src, dst, to = (
            (chunk(1).at[:, 0:4], chunk(9).at[:, 0:4], to_up),
            (chunk(1).at[:, 0:4], chunk(10).at[:, 0:4], to_down),
            (chunk(9).at[0, 0:4], chunk(11).at[0, 0:4], to_up),
            (chunk(10).at[1, 0:4], chunk(11).at[1, 0:4], to_down),
            (chunk(9).at[:, 0:4], chunk(9).at[:, 4:8], sibling),
            (chunk(10).at[:, 0:4], chunk(10).at[:, 4:8], sibling),
            (chunk(11).at[:, 0:4], chunk(11).at[:, 4:8], sibling),
            (latent, shifted, to_down),
        )[n]
        return remote(src, dst, send_y.at[n], recv_y.at[n], to)

    def back(j, part):
        to = device(down, (z - HOPS[j] + 8) % 8, x, core)
        lower, upper = (PARTS[part][end] * HEAD_DIM for end in (0, 1))
        columns = part_columns(z, part)
        return remote(
            attended.at[j, :, lower:upper], returned.at[:, columns], send_o.at[j, part], recv_o.at[j, part], to
        )

    def start_z(*js):
        for j in js:
            for which in (0, 1):
                kv_over_z(j, which).start()

    def arrived(i):
        for which in (0, 1):
            place = chunk(i).at[which, 0]
            pltpu.make_async_copy(place, place, recv_kv.at[i, which]).wait()
        for n in (0, 1):
            x_copy(i, n).start()

    def forward(i):
        x_copy(i, 0).wait_recv()
        x_copy(i, 2).start()
        x_copy(i, 1).wait_recv()
        x_copy(i, 3).start()

    def last_piece(i):
        x_copy(i, 2).wait_recv()
        x_copy(i, 3).wait_recv()
        x_copy(i, 4).start()

    def complete(i):
        if i >= X_CHUNKS:
            y_copy(i - 5).wait_recv()
        else:
            x_copy(i, 4).wait_recv()

    def start_y():
        y_copy(0).start()
        y_copy(1).start()

    def forward_y():
        for n in (0, 1):
            y_copy(n).wait_recv()
            y_copy(n + 2).start()
            y_copy(n + 4).start()

    def last_y():
        y_copy(2).wait_recv()
        y_copy(3).wait_recv()
        y_copy(6).start()

    def queries(*js):
        for j in js:
            query_over_z(j).wait_recv()

    @pl.when(core != zh)
    def _():
        cache_across(0).start()
        cache_across(1).start()

    start_z(1, 2)
    arrived(0)
    arrived(2)
    for j in range(1, 8):
        query_over_z(j).start()
    y_copy(7).start()

    for i in range(CHUNKS):
        for slot in range(8):
            shown = jnp.float32(0.0)
            if i == 1 or i >= 9:
                plane = {1: y, 9: down, 10: up, 11: (y + 2) % 4}[i]
                side = core if slot < 4 else 1 - core
                block = plane * 8 + side * 4 + (x + (0, 3, 2, 1)[slot % 4]) % 4
                shown = jnp.where(cache_mask[y, block] == 1, 0.0, HIDDEN).astype(jnp.float32)
            bias[PLACE[i] * 8 + slot] = shown

    peak[...] = jnp.full_like(peak, HIDDEN)
    total[...] = jnp.zeros_like(total)
    summed[...] = jnp.zeros_like(summed)

    arrived(1)
    arrived(3)

    stamp = timesteps[levels[up]].astype(jnp.float32)
    count = 128
    index = lax.broadcasted_iota(jnp.int32, (8, count), 1).astype(jnp.float32)
    phase = stamp * jnp.exp(-math.log(10000.0) * index / count)
    embed = jnp.concatenate([jnp.cos(phase), jnp.sin(phase)], axis=1).astype(jnp.bfloat16)
    weight_copy.wait()

    def gate_columns(c, carry):
        columns = pl.ds(pl.multiple_of(c * WIDTH, 128), WIDTH)
        gate[:, columns] = jnp.dot(embed, weight[:, columns], preferred_element_type=jnp.float32)
        return carry

    lax.fori_loop(0, 8, gate_columns, 0)

    def attend(c, cached, finish=None):
        def scores_of(h):
            keys = kv[c, 0, :, :, h * HEAD_DIM : (h + 1) * HEAD_DIM].reshape(KEYS, HEAD_DIM)
            return jnp.dot(keys, turned[h], preferred_element_type=jnp.float32)

        scale = LOG2E / math.sqrt(HEAD_DIM)
        following = scores_of(0)
        for h in range(GROUP):
            scores = following
            if h + 1 < GROUP:
                following = scores_of(h + 1)
            if cached:
                scores = jnp.concatenate(
                    [scores[slot * ROWS : (slot + 1) * ROWS] + bias[c * 8 + slot] for slot in range(8)], axis=0
                )
            old = peak[h]
            new = jnp.maximum(old, jnp.max(scores, axis=0, keepdims=True) * scale)
            weights = jnp.exp2(scores * scale - new)
            factor = jnp.exp2(old - new)
            values = kv[c, 1, :, :, h * HEAD_DIM : (h + 1) * HEAD_DIM].reshape(KEYS, HEAD_DIM)
            added = lax.dot_general(
                values, weights.astype(jnp.bfloat16), (((0,), (0,)), ((), ())), preferred_element_type=jnp.float32
            )
            weight_sum = factor * total[h] + jnp.sum(weights, axis=0, keepdims=True)
            value_sum = factor * summed[h] + added
            if finish is None:
                peak[h], total[h], summed[h] = new, weight_sum, value_sum
            else:
                finish(h, value_sum * (1.0 / weight_sum))

    def finish(h, result):
        columns = slice(h * HEAD_DIM, (h + 1) * HEAD_DIM)
        attended[:, :, columns] = result.T.astype(jnp.bfloat16).reshape(8, ROWS, HEAD_DIM)
        for part, (lower, upper) in enumerate(PARTS):
            if h == upper - 1:
                for j in range(8):
                    back(j, part).start()

    def before(c):
        if c == 0:
            forward(0)
            last_piece(0)
            forward(1)
            forward(2)
            last_piece(1)
            start_y()
            own_query.wait()
            queries(1, 2, 3, 4)
            start_z(3, 4)
            forward(3)
            last_piece(2)
            queries(5, 6, 7)
            for h in range(GROUP):
                columns = slice(h * HEAD_DIM, (h + 1) * HEAD_DIM)
                turned[h] = query[:, :, columns].reshape(KEYS, HEAD_DIM).astype(jnp.float32).T.astype(jnp.bfloat16)
        if c == 1:
            last_piece(3)
        if c == 3:
            arrived(4)
            start_z(5, 6)
            arrived(5)
        if c == 4:
            forward(4)
            forward_y()
        if c == 5:
            forward(5)
            last_piece(4)
            start_z(7)
        if c == 6:
            last_piece(5)
        if c == 7:
            arrived(6)
            arrived(7)
        if c == 8:
            forward(6)
            last_y()
        if c == 9:
            forward(7)
            last_piece(6)
            arrived(8)
        if c == 10:
            last_piece(7)
            forward(8)
        if c == 11:
            last_piece(8)
        complete(ATTEND[c])

    def turn(c, carry):
        cached = False
        for now in range(CHUNKS - 1):
            pl.when(c == now)(functools.partial(before, now))
            if ATTEND[now] == 1 or ATTEND[now] >= X_CHUNKS:
                cached = cached | (c == now)
        pl.when(cached)(functools.partial(attend, c, True))
        pl.when(jnp.logical_not(cached))(functools.partial(attend, c, False))
        return carry

    lax.fori_loop(0, CHUNKS - 1, turn, 0)
    before(CHUNKS - 1)
    attend(CHUNKS - 1, False, finish)

    @pl.when(core != zh)
    def _():
        cache_across(0).wait_send()
        cache_across(1).wait_send()

    for j in range(1, 8):
        query_over_z(j).wait_send()
        for which in (0, 1):
            kv_over_z(j, which).wait_send()
    for i in range(X_CHUNKS):
        for n in range(5):
            x_copy(i, n).wait_send()
    for n in range(8):
        y_copy(n).wait_send()

    y_copy(7).wait_recv()
    for part in range(len(PARTS)):
        for j in range(8):
            back(j, part).wait_recv()
            columns = part_columns((z + HOPS[j]) % 8, part)
            out[:, columns] = (
                shifted[:, columns].astype(jnp.float32) + gate[0:1, columns] * returned[:, columns].astype(jnp.float32)
            ).astype(jnp.bfloat16)
    for part in range(len(PARTS)):
        for j in range(8):
            back(j, part).wait_send()


def shards(
    latent, query_in, key_in, value_in, cache_keys, cache_values, levels, timesteps, cache_mask, time_weight
):
    anywhere = pl.BlockSpec(memory_space=pl.ANY)
    scalars = pl.BlockSpec(memory_space=pltpu.SMEM)
    bf16, f32 = jnp.bfloat16, jnp.float32
    dma = pltpu.SemaphoreType.DMA
    return pl.pallas_call(
        kernel,
        out_shape=jax.ShapeDtypeStruct(latent.shape, latent.dtype),
        in_specs=[scalars] * 3 + [anywhere] * 7,
        out_specs=pl.BlockSpec(memory_space=pltpu.VMEM),
        scratch_shapes=[
            pltpu.VMEM((8, ROWS, WIDTH), bf16),
            pltpu.VMEM((GROUP, HEAD_DIM, KEYS), bf16),
            pltpu.VMEM((CHUNKS, 2, 8, ROWS, WIDTH), bf16),
            pltpu.VMEM((8, ROWS, WIDTH), bf16),
            pltpu.VMEM(latent.shape, bf16),
            pltpu.VMEM(latent.shape, bf16),
            pltpu.VMEM(time_weight.shape, bf16),
            pltpu.VMEM((8, latent.shape[1]), f32),
            pltpu.VMEM((GROUP, 1, KEYS), f32),
            pltpu.VMEM((GROUP, 1, KEYS), f32),
            pltpu.VMEM((GROUP, HEAD_DIM, KEYS), f32),
            pltpu.SMEM((CHUNKS * 8,), f32),
            dma((8, 3)),
            dma((X_CHUNKS, 5)),
            dma((8,)),
            dma((8, len(PARTS))),
            dma((8,)),
            dma((X_CHUNKS, 2)),
            dma((X_CHUNKS, 5)),
            dma((8,)),
            dma((8, len(PARTS))),
            dma((1,)),
        ],
        compiler_params=pltpu.CompilerParams(
            collective_id=0, has_side_effects=True, vmem_limit_bytes=64 * 1024 * 1024
        ),
        cost_estimate=pl.CostEstimate(flops=2 * 10**9, bytes_accessed=5 * 10**6, transcendentals=4 * 10**6),
    )(
        levels, timesteps, cache_mask, latent, query_in, key_in, value_in, cache_keys, cache_values, time_weight
    )


def solution(mesh):
    return jax.shard_map(
        shards,
        mesh=mesh,
        in_specs=(
            P(("chain", "head"), None),
            P(("chain", "head"), None),
            P(("chain", "head"), None),
            P(("chain", "head"), None),
            P("chain", "head"),
            P("chain", "head"),
            P(),
            P(),
            P(),
            P(),
        ),
        out_specs=P(("chain", "head"), None),
        check_vma=False,
    )
```

```python
import functools
import math

import jax
import jax.numpy as jnp
from jax import lax
from jax.experimental import pallas as pl
from jax.experimental.pallas import tpu as pltpu
from jax.sharding import PartitionSpec as P

MESH = pl.DeviceIdType.MESH
HEAD_DIM = 128
SPANS = 4
NY, NX, NZ = 4, 4, 8
GROUP = 5
WIDTH = GROUP * HEAD_DIM
ROWS = 32
HOPS = (0, 1, 7, 2, 6, 3, 5, 4)
CHUNKS = 12
FIRST_Z = 2
X_CHUNKS = 9
KEYS = 8 * ROWS
HIDDEN = -1e30


def device(y, z, x, core):
    return {"chain": (y * 2 + z // 4) * NX + x, "head": (z % 4) * 2 + core}


def group_columns(z):
    group = (z % 4) * 2 + z // 4
    return pl.ds(pl.multiple_of(group * WIDTH, 128), WIDTH)


def kernel(
    levels, timesteps, cache_mask, latent, query_in, key_in, value_in, cache_keys, cache_values, time_weight,
    out,
    query, turned, kv, attended, returned, shifted, weight, gate, scored, weighed, factor, peak, total, summed, bias,
    send_z, send_x, send_y, send_o, recv_q, recv_k, recv_v, recv_x, recv_y, recv_o, local,
):
    chain, head = lax.axis_index("chain"), lax.axis_index("head")
    y, x = chain // 8, chain % 4
    zh, zl, core = (chain // 4) % 2, head // 2, head % 2
    z = zh * 4 + zl
    up, down = (y + 1) % 4, (y + 3) % 4
    right, left = (x + 1) % 4, (x + 3) % 4
    sibling = device(y, z, x, 1 - core)
    across = device(y, (z + 4) % 8, x, 1 - core)

    def remote(src, dst, send, recv, to):
        return pltpu.make_async_remote_copy(
            src_ref=src, dst_ref=dst, send_sem=send, recv_sem=recv, device_id=to, device_id_type=MESH
        )

    mine = group_columns(z)
    own = [
        pltpu.make_async_copy(key_in.at[:, mine], kv.at[0, 0, 0], recv_k.at[0]),
        pltpu.make_async_copy(value_in.at[:, mine], kv.at[0, 1, 0], recv_v.at[0]),
        pltpu.make_async_copy(query_in.at[:, mine], query.at[0], recv_q.at[0]),
    ]
    for copy in own:
        copy.start()
    weight_copy = pltpu.make_async_copy(time_weight, weight, local.at[0])
    weight_copy.start()

    @pl.when(core == zh)
    def _():
        pltpu.make_async_copy(cache_keys, kv.at[1, 0, 0], recv_k.at[1]).start()
        pltpu.make_async_copy(cache_values, kv.at[1, 1, 0], recv_v.at[1]).start()

    barrier = pltpu.get_barrier_semaphore()
    partners = [sibling, across, device(y, z, right, core), device(y, z, left, core)]
    partners += [device(up, z, x, core), device(down, z, x, core)]
    for hop in HOPS[1:]:
        partners += [device(row, (z + hop) % 8, x, core) for row in (y, up, down)]
    for partner in partners:
        pl.semaphore_signal(barrier, inc=1, device_id=partner, device_id_type=MESH)
    pl.semaphore_wait(barrier, len(partners))

    def cache_across(which, source, recv):
        return remote(source, kv.at[1, which, 0], send_z.at[0, which], recv.at[1], across)

    def query_over_z(j):
        to = (z + HOPS[j]) % 8
        return remote(
            query_in.at[:, group_columns(to)], query.at[j], send_z.at[j, 2], recv_q.at[j], device(y, to, x, core)
        )

    def kv_over_z(j, which, source, recv):
        to = (z + HOPS[j]) % 8
        return remote(
            source.at[:, group_columns(to)],
            kv.at[j + 1, which, 0],
            send_z.at[j, which],
            recv.at[j + 1],
            device(y, to, x, core),
        )

    def over_x(i):
        own_kv = kv.at[i, :, 0]
        return (
            remote(own_kv, kv.at[i, :, 1], send_x.at[i, 0], recv_x.at[i, 0], device(y, z, right, core)),
            remote(own_kv, kv.at[i, :, 3], send_x.at[i, 1], recv_x.at[i, 1], device(y, z, left, core)),
            remote(kv.at[i, 0, 1], kv.at[i, 0, 2], send_x.at[i, 2], recv_x.at[i, 2], device(y, z, right, core)),
            remote(kv.at[i, 1, 3], kv.at[i, 1, 2], send_x.at[i, 3], recv_x.at[i, 3], device(y, z, left, core)),
        )

    def to_sibling(i, send, recv):
        return remote(kv.at[i, :, 0:4], kv.at[i, :, 4:8], send, recv, sibling)

    def sibling_x(i):
        return to_sibling(i, send_x.at[i, 4], recv_x.at[i, 4])

    half = slice(0, 4)
    to_up, to_down = device(up, z, x, core), device(down, z, x, core)
    y_up = remote(kv.at[1, :, half], kv.at[9, :, half], send_y.at[0], recv_y.at[0], to_up)
    y_down = remote(kv.at[1, :, half], kv.at[10, :, half], send_y.at[1], recv_y.at[1], to_down)
    y_on_up = remote(kv.at[9, 0, half], kv.at[11, 0, half], send_y.at[2], recv_y.at[2], to_up)
    y_on_down = remote(kv.at[10, 1, half], kv.at[11, 1, half], send_y.at[3], recv_y.at[3], to_down)
    latent_down = remote(latent, shifted, send_y.at[7], recv_y.at[7], to_down)

    def sibling_y(i):
        return to_sibling(i, send_y.at[i - 5], recv_y.at[i - 5])

    def back(j):
        to = (z - HOPS[j] + 8) % 8
        return remote(attended.at[j], returned.at[:, mine], send_o.at[j], recv_o.at[j], device(down, to, x, core))

    @pl.when(core != zh)
    def _():
        cache_across(0, cache_keys, recv_k).start()
        cache_across(1, cache_values, recv_v).start()

    def start_kv(j):
        kv_over_z(j, 0, key_in, recv_k).start()
        kv_over_z(j, 1, value_in, recv_v).start()

    for j in range(1, 8):
        query_over_z(j).start()
    start_kv(1)
    start_kv(2)
    latent_down.start()

    for i in range(CHUNKS):
        for slot in range(8):
            if i == 1 or i >= 9:
                plane = {1: y, 9: down, 10: up, 11: (y + 2) % 4}[i]
                side = core if slot < 4 else 1 - core
                block = plane * 8 + side * 4 + (x + (0, 3, 2, 1)[slot % 4]) % 4
                bias[i * 8 + slot] = jnp.where(cache_mask[y, block] == 1, 0.0, HIDDEN).astype(jnp.float32)
            else:
                bias[i * 8 + slot] = jnp.float32(0.0)

    stamp = timesteps[levels[up]].astype(jnp.float32)
    count = 128
    index = lax.broadcasted_iota(jnp.int32, (8, count), 1).astype(jnp.float32)
    phase = stamp * jnp.exp(-math.log(10000.0) * index / count)
    embed = jnp.concatenate([jnp.cos(phase), jnp.sin(phase)], axis=1).astype(jnp.bfloat16)
    weight_copy.wait()

    def gate_columns(c, carry):
        columns = pl.ds(pl.multiple_of(c * WIDTH, 128), WIDTH)
        gate[:, columns] = jnp.dot(embed, weight[:, columns], preferred_element_type=jnp.float32)
        return carry

    lax.fori_loop(0, 8, gate_columns, 0)

    peak[...] = jnp.full_like(peak, HIDDEN)
    total[...] = jnp.zeros_like(total)
    summed[...] = jnp.zeros_like(summed)

    def attend(i, cached):
        def of_head(which, h):
            return kv[i, which, :, :, h * HEAD_DIM : (h + 1) * HEAD_DIM].reshape(KEYS, HEAD_DIM)

        scale = 1.0 / math.sqrt(HEAD_DIM)
        for h in range(GROUP):
            scored[h] = jnp.dot(of_head(0, h), turned[h], preferred_element_type=jnp.float32)
        for h in range(GROUP):
            for side in (slice(0, 128), slice(128, 256)):
                scores = scored[h, :, side]
                if cached:
                    scores = jnp.concatenate(
                        [scores[slot * ROWS : (slot + 1) * ROWS] + bias[i * 8 + slot] for slot in range(8)], axis=0
                    )
                old = peak[h, :, side]
                new = jnp.maximum(old, jnp.max(scores, axis=0, keepdims=True) * scale)
                weights = jnp.exp(scores * scale - new)
                shrink = jnp.exp(old - new)
                peak[h, :, side] = new
                factor[h, :, side] = shrink
                total[h, :, side] = shrink * total[h, :, side] + jnp.sum(weights, axis=0, keepdims=True)
                weighed[h, :, side] = weights.astype(jnp.bfloat16)
        for h in range(GROUP):
            added = lax.dot_general(
                of_head(1, h), weighed[h], (((0,), (0,)), ((), ())), preferred_element_type=jnp.float32
            )
            summed[h] = factor[h] * summed[h] + added

    def turn(t, carry):
        @pl.when(t < X_CHUNKS)
        def _():
            pltpu.make_async_copy(kv.at[t, 0, 0], kv.at[t, 0, 0], recv_k.at[t]).wait()
            pltpu.make_async_copy(kv.at[t, 1, 0], kv.at[t, 1, 0], recv_v.at[t]).wait()
            over_x(t)[0].start()
            over_x(t)[1].start()

        for turn_of, hops in ((1, (3, 4)), (3, (5, 6)), (5, (7,))):

            @pl.when(t == turn_of)
            def _(hops=hops):
                for j in hops:
                    start_kv(j)

        @pl.when((t >= 1) & (t < X_CHUNKS + 1))
        def _():
            copies = over_x(t - 1)
            copies[0].wait_recv()
            copies[2].start()
            copies[1].wait_recv()
            copies[3].start()

        @pl.when((t >= 2) & (t < X_CHUNKS + 2))
        def _():
            copies = over_x(t - 2)
            copies[2].wait_recv()
            copies[3].wait_recv()
            sibling_x(t - 2).start()

        @pl.when(t == 3)
        def _():
            y_up.start()
            y_down.start()
            own[2].wait()
            for j in range(1, 8):
                query_over_z(j).wait_recv()
            for h in range(GROUP):
                columns = slice(h * HEAD_DIM, (h + 1) * HEAD_DIM)
                turned[h] = query[:, :, columns].reshape(KEYS, HEAD_DIM).astype(jnp.float32).T.astype(jnp.bfloat16)

        @pl.when(t == 6)
        def _():
            y_up.wait_recv()
            y_on_up.start()
            y_down.wait_recv()
            y_on_down.start()
            sibling_y(9).start()
            sibling_y(10).start()

        @pl.when(t == 8)
        def _():
            y_on_up.wait_recv()
            y_on_down.wait_recv()
            sibling_y(11).start()

        @pl.when(t >= 3)
        def _():
            sibling_x(t - 3).wait_recv()

        @pl.when(t == 8)
        def _():
            sibling_y(9).wait_recv()

        @pl.when(t == 9)
        def _():
            sibling_y(10).wait_recv()

        @pl.when(t == 10)
        def _():
            sibling_y(11).wait_recv()

        @pl.when((t >= 3) & (t != 4))
        def _():
            attend(t - 3, False)

        @pl.when((t == 4) | ((t >= 8) & (t <= 10)))
        def _():
            attend(jnp.where(t == 4, 1, t + 1), True)

        return carry

    lax.fori_loop(0, X_CHUNKS + 3, turn, 0)

    for h in range(GROUP):
        result = summed[h] * (1.0 / total[h])
        attended[:, :, h * HEAD_DIM : (h + 1) * HEAD_DIM] = result.T.astype(jnp.bfloat16).reshape(8, ROWS, HEAD_DIM)
    for j in range(8):
        back(j).start()

    @pl.when(core != zh)
    def _():
        cache_across(0, cache_keys, recv_k).wait_send()
        cache_across(1, cache_values, recv_v).wait_send()

    for j in range(1, 8):
        query_over_z(j).wait_send()
        kv_over_z(j, 0, key_in, recv_k).wait_send()
        kv_over_z(j, 1, value_in, recv_v).wait_send()

    def sent(i, carry):
        for copy in over_x(i):
            copy.wait_send()
        sibling_x(i).wait_send()
        return carry

    lax.fori_loop(0, X_CHUNKS, sent, 0)
    for copy in (y_up, y_down, y_on_up, y_on_down, sibling_y(9), sibling_y(10), sibling_y(11), latent_down):
        copy.wait_send()

    latent_down.wait_recv()
    for j in range(8):
        back(j).wait_recv()
        columns = group_columns((z + HOPS[j]) % 8)
        out[:, columns] = (
            shifted[:, columns].astype(jnp.float32) + gate[0:1, columns] * returned[:, columns].astype(jnp.float32)
        ).astype(jnp.bfloat16)
    for j in range(8):
        back(j).wait_send()


def shards(
    latent, query_in, key_in, value_in, cache_keys, cache_values, levels, timesteps, cache_mask, time_weight
):
    anywhere = pl.BlockSpec(memory_space=pl.ANY)
    scalars = pl.BlockSpec(memory_space=pltpu.SMEM)
    bf16, f32 = jnp.bfloat16, jnp.float32
    dma = pltpu.SemaphoreType.DMA
    return pl.pallas_call(
        kernel,
        out_shape=jax.ShapeDtypeStruct(latent.shape, latent.dtype),
        in_specs=[scalars] * 3 + [anywhere] * 7,
        out_specs=pl.BlockSpec(memory_space=pltpu.VMEM),
        scratch_shapes=[
            pltpu.VMEM((8, ROWS, WIDTH), bf16),
            pltpu.VMEM((GROUP, HEAD_DIM, KEYS), bf16),
            pltpu.VMEM((CHUNKS, 2, 8, ROWS, WIDTH), bf16),
            pltpu.VMEM((8, ROWS, WIDTH), bf16),
            pltpu.VMEM(latent.shape, bf16),
            pltpu.VMEM(latent.shape, bf16),
            pltpu.VMEM(time_weight.shape, bf16),
            pltpu.VMEM((8, latent.shape[1]), f32),
            pltpu.VMEM((GROUP, KEYS, KEYS), f32),
            pltpu.VMEM((GROUP, KEYS, KEYS), bf16),
            pltpu.VMEM((GROUP, 1, KEYS), f32),
            pltpu.VMEM((GROUP, 1, KEYS), f32),
            pltpu.VMEM((GROUP, 1, KEYS), f32),
            pltpu.VMEM((GROUP, HEAD_DIM, KEYS), f32),
            pltpu.SMEM((CHUNKS * 8,), f32),
            dma((8, 3)),
            dma((X_CHUNKS, 5)),
            dma((8,)),
            dma((8,)),
            dma((8,)),
            dma((X_CHUNKS,)),
            dma((X_CHUNKS,)),
            dma((X_CHUNKS, 5)),
            dma((8,)),
            dma((8,)),
            dma((1,)),
        ],
        compiler_params=pltpu.CompilerParams(
            collective_id=0, has_side_effects=True, vmem_limit_bytes=64 * 1024 * 1024
        ),
        cost_estimate=pl.CostEstimate(flops=2 * 10**9, bytes_accessed=5 * 10**6, transcendentals=4 * 10**6),
    )(
        levels, timesteps, cache_mask, latent, query_in, key_in, value_in, cache_keys, cache_values, time_weight
    )


def solution(mesh):
    return jax.shard_map(
        shards,
        mesh=mesh,
        in_specs=(
            P(("chain", "head"), None),
            P(("chain", "head"), None),
            P(("chain", "head"), None),
            P(("chain", "head"), None),
            P("chain", "head"),
            P("chain", "head"),
            P(),
            P(),
            P(),
            P(),
        ),
        out_specs=P(("chain", "head"), None),
        check_vma=False,
    )
```

```python
import functools
import math

import jax
import jax.numpy as jnp
from jax import lax
from jax.experimental import pallas as pl
from jax.experimental.pallas import tpu as pltpu
from jax.sharding import PartitionSpec as P

MESH = pl.DeviceIdType.MESH
HEAD_DIM = 128
SPANS = 4
NY, NX, NZ = 4, 4, 8
GROUP = 5
WIDTH = GROUP * HEAD_DIM
ROWS = 32
HOPS = (0, 1, 7, 2, 6, 3, 5, 4)
CHUNKS = 12
FIRST_Z = 2
X_CHUNKS = 9
KEYS = 8 * ROWS
HIDDEN = -1e30


def device(y, z, x, core):
    return {"chain": (y * 2 + z // 4) * NX + x, "head": (z % 4) * 2 + core}


def group_columns(z):
    group = (z % 4) * 2 + z // 4
    return pl.ds(pl.multiple_of(group * WIDTH, 128), WIDTH)


def kernel(
    levels, timesteps, cache_mask, latent, query_in, key_in, value_in, cache_keys, cache_values, time_weight,
    out,
    query, turned, kv, attended, returned, shifted, weight, gate, scored, weighed, factor, peak, total, summed, bias,
    send_z, send_x, send_y, send_o, recv_q, recv_k, recv_v, recv_x, recv_y, recv_o, local,
):
    chain, head = lax.axis_index("chain"), lax.axis_index("head")
    y, x = chain // 8, chain % 4
    zh, zl, core = (chain // 4) % 2, head // 2, head % 2
    z = zh * 4 + zl
    up, down = (y + 1) % 4, (y + 3) % 4
    right, left = (x + 1) % 4, (x + 3) % 4
    sibling = device(y, z, x, 1 - core)
    across = device(y, (z + 4) % 8, x, 1 - core)

    def remote(src, dst, send, recv, to):
        return pltpu.make_async_remote_copy(
            src_ref=src, dst_ref=dst, send_sem=send, recv_sem=recv, device_id=to, device_id_type=MESH
        )

    mine = group_columns(z)
    own = [
        pltpu.make_async_copy(key_in.at[:, mine], kv.at[0, 0, 0], recv_k.at[0]),
        pltpu.make_async_copy(value_in.at[:, mine], kv.at[0, 1, 0], recv_v.at[0]),
        pltpu.make_async_copy(query_in.at[:, mine], query.at[0], recv_q.at[0]),
    ]
    for copy in own:
        copy.start()
    weight_copy = pltpu.make_async_copy(time_weight, weight, local.at[0])
    weight_copy.start()

    @pl.when(core == zh)
    def _():
        pltpu.make_async_copy(cache_keys, kv.at[1, 0, 0], recv_k.at[1]).start()
        pltpu.make_async_copy(cache_values, kv.at[1, 1, 0], recv_v.at[1]).start()

    barrier = pltpu.get_barrier_semaphore()
    partners = [sibling, across, device(y, z, right, core), device(y, z, left, core)]
    partners += [device(up, z, x, core), device(down, z, x, core)]
    for hop in HOPS[1:]:
        partners += [device(row, (z + hop) % 8, x, core) for row in (y, up, down)]
    for partner in partners:
        pl.semaphore_signal(barrier, inc=1, device_id=partner, device_id_type=MESH)
    pl.semaphore_wait(barrier, len(partners))

    def cache_across(which, source, recv):
        return remote(source, kv.at[1, which, 0], send_z.at[0, which], recv.at[1], across)

    def query_over_z(j):
        to = (z + HOPS[j]) % 8
        return remote(
            query_in.at[:, group_columns(to)], query.at[j], send_z.at[j, 2], recv_q.at[j], device(y, to, x, core)
        )

    def kv_over_z(j, which, source, recv):
        to = (z + HOPS[j]) % 8
        return remote(
            source.at[:, group_columns(to)],
            kv.at[j + 1, which, 0],
            send_z.at[j, which],
            recv.at[j + 1],
            device(y, to, x, core),
        )

    def over_x(i):
        own_kv = kv.at[i, :, 0]
        return (
            remote(own_kv, kv.at[i, :, 1], send_x.at[i, 0], recv_x.at[i, 0], device(y, z, right, core)),
            remote(own_kv, kv.at[i, :, 3], send_x.at[i, 1], recv_x.at[i, 1], device(y, z, left, core)),
            remote(kv.at[i, 0, 1], kv.at[i, 0, 2], send_x.at[i, 2], recv_x.at[i, 2], device(y, z, right, core)),
            remote(kv.at[i, 1, 3], kv.at[i, 1, 2], send_x.at[i, 3], recv_x.at[i, 3], device(y, z, left, core)),
        )

    def to_sibling(i, send, recv):
        return remote(kv.at[i, :, 0:4], kv.at[i, :, 4:8], send, recv, sibling)

    def sibling_x(i):
        return to_sibling(i, send_x.at[i, 4], recv_x.at[i, 4])

    half = slice(0, 4)
    to_up, to_down = device(up, z, x, core), device(down, z, x, core)
    y_up = remote(kv.at[1, :, half], kv.at[9, :, half], send_y.at[0], recv_y.at[0], to_up)
    y_down = remote(kv.at[1, :, half], kv.at[10, :, half], send_y.at[1], recv_y.at[1], to_down)
    y_on_up = remote(kv.at[9, 0, half], kv.at[11, 0, half], send_y.at[2], recv_y.at[2], to_up)
    y_on_down = remote(kv.at[10, 1, half], kv.at[11, 1, half], send_y.at[3], recv_y.at[3], to_down)
    latent_down = remote(latent, shifted, send_y.at[7], recv_y.at[7], to_down)

    def sibling_y(i):
        return to_sibling(i, send_y.at[i - 5], recv_y.at[i - 5])

    def back(j):
        to = (z - HOPS[j] + 8) % 8
        return remote(attended.at[j], returned.at[:, mine], send_o.at[j], recv_o.at[j], device(down, to, x, core))

    @pl.when(core != zh)
    def _():
        cache_across(0, cache_keys, recv_k).start()
        cache_across(1, cache_values, recv_v).start()

    def start_kv(j):
        kv_over_z(j, 0, key_in, recv_k).start()
        kv_over_z(j, 1, value_in, recv_v).start()

    for j in range(1, 8):
        query_over_z(j).start()
    for j in range(1, 5):
        start_kv(j)
    latent_down.start()

    def prepare():
        for i in range(CHUNKS):
            for slot in range(8):
                if i == 1 or i >= 9:
                    plane = {1: y, 9: down, 10: up, 11: (y + 2) % 4}[i]
                    side = core if slot < 4 else 1 - core
                    block = plane * 8 + side * 4 + (x + (0, 3, 2, 1)[slot % 4]) % 4
                    bias[i * 8 + slot] = jnp.where(cache_mask[y, block] == 1, 0.0, HIDDEN).astype(jnp.float32)
                else:
                    bias[i * 8 + slot] = jnp.float32(0.0)

        stamp = timesteps[levels[up]].astype(jnp.float32)
        count = 128
        index = lax.broadcasted_iota(jnp.int32, (8, count), 1).astype(jnp.float32)
        phase = stamp * jnp.exp(-math.log(10000.0) * index / count)
        embed = jnp.concatenate([jnp.cos(phase), jnp.sin(phase)], axis=1).astype(jnp.bfloat16)
        weight_copy.wait()

        def gate_columns(c, carry):
            columns = pl.ds(pl.multiple_of(c * WIDTH, 128), WIDTH)
            gate[:, columns] = jnp.dot(embed, weight[:, columns], preferred_element_type=jnp.float32)
            return carry

        lax.fori_loop(0, 8, gate_columns, 0)

        peak[...] = jnp.full_like(peak, HIDDEN)
        total[...] = jnp.zeros_like(total)
        summed[...] = jnp.zeros_like(summed)

    def attend(i, cached):
        def of_head(which, h):
            return kv[i, which, :, :, h * HEAD_DIM : (h + 1) * HEAD_DIM].reshape(KEYS, HEAD_DIM)

        scale = 1.0 / math.sqrt(HEAD_DIM)
        for h in range(GROUP):
            scored[h] = jnp.dot(of_head(0, h), turned[h], preferred_element_type=jnp.float32)
        for h in range(GROUP):
            for side in (slice(0, 128), slice(128, 256)):
                scores = scored[h, :, side]
                if cached:
                    scores = jnp.concatenate(
                        [scores[slot * ROWS : (slot + 1) * ROWS] + bias[i * 8 + slot] for slot in range(8)], axis=0
                    )
                old = peak[h, :, side]
                new = jnp.maximum(old, jnp.max(scores, axis=0, keepdims=True) * scale)
                weights = jnp.exp(scores * scale - new)
                shrink = jnp.exp(old - new)
                peak[h, :, side] = new
                factor[h, :, side] = shrink
                total[h, :, side] = shrink * total[h, :, side] + jnp.sum(weights, axis=0, keepdims=True)
                weighed[h, :, side] = weights.astype(jnp.bfloat16)
        for h in range(GROUP):
            added = lax.dot_general(
                of_head(1, h), weighed[h], (((0,), (0,)), ((), ())), preferred_element_type=jnp.float32
            )
            summed[h] = factor[h] * summed[h] + added

    def turn(t, carry):
        @pl.when((t >= 2) & (t < X_CHUNKS + 2))
        def _():
            copies = over_x(t - 2)
            copies[0].wait_recv()
            copies[2].start()
            copies[1].wait_recv()
            copies[3].start()

        @pl.when((t >= 3) & (t < X_CHUNKS + 3))
        def _():
            copies = over_x(t - 3)
            copies[2].wait_recv()
            copies[3].wait_recv()
            sibling_x(t - 3).start()

        @pl.when(t == 4)
        def _():
            y_up.start()
            y_down.start()
            own[2].wait()
            for j in range(1, 8):
                query_over_z(j).wait_recv()
            for h in range(GROUP):
                columns = slice(h * HEAD_DIM, (h + 1) * HEAD_DIM)
                turned[h] = query[:, :, columns].reshape(KEYS, HEAD_DIM).astype(jnp.float32).T.astype(jnp.bfloat16)

        @pl.when(t == 7)
        def _():
            y_up.wait_recv()
            y_on_up.start()
            y_down.wait_recv()
            y_on_down.start()
            sibling_y(9).start()
            sibling_y(10).start()

        @pl.when(t == 9)
        def _():
            y_on_up.wait_recv()
            y_on_down.wait_recv()
            sibling_y(11).start()

        @pl.when(t >= 4)
        def _():
            sibling_x(t - 4).wait_recv()

        @pl.when((t >= 4) & (t != 5))
        def _():
            attend(t - 4, False)

        for i in (9, 10, 11):

            @pl.when(t == i)
            def _(i=i):
                sibling_y(i).wait_recv()

        @pl.when((t == 5) | ((t >= 9) & (t <= 11)))
        def _():
            attend(jnp.where(t == 5, 1, t), True)

        @pl.when(t < X_CHUNKS)
        def _():
            pltpu.make_async_copy(kv.at[t, 0, 0], kv.at[t, 0, 0], recv_k.at[t]).wait()
            pltpu.make_async_copy(kv.at[t, 1, 0], kv.at[t, 1, 0], recv_v.at[t]).wait()
            over_x(t)[0].start()
            over_x(t)[1].start()

        for turn_of, hops in ((1, (5, 6)), (3, (7,))):

            @pl.when(t == turn_of)
            def _(hops=hops):
                for j in hops:
                    start_kv(j)

        pl.when(t == 1)(prepare)
        return carry

    lax.fori_loop(0, X_CHUNKS + 4, turn, 0)

    for h in range(GROUP):
        result = summed[h] * (1.0 / total[h])
        attended[:, :, h * HEAD_DIM : (h + 1) * HEAD_DIM] = result.T.astype(jnp.bfloat16).reshape(8, ROWS, HEAD_DIM)
    for j in range(8):
        back(j).start()

    @pl.when(core != zh)
    def _():
        cache_across(0, cache_keys, recv_k).wait_send()
        cache_across(1, cache_values, recv_v).wait_send()

    for j in range(1, 8):
        query_over_z(j).wait_send()
        kv_over_z(j, 0, key_in, recv_k).wait_send()
        kv_over_z(j, 1, value_in, recv_v).wait_send()

    def sent(i, carry):
        for copy in over_x(i):
            copy.wait_send()
        sibling_x(i).wait_send()
        return carry

    lax.fori_loop(0, X_CHUNKS, sent, 0)
    for copy in (y_up, y_down, y_on_up, y_on_down, sibling_y(9), sibling_y(10), sibling_y(11), latent_down):
        copy.wait_send()

    latent_down.wait_recv()
    for j in range(8):
        back(j).wait_recv()
        columns = group_columns((z + HOPS[j]) % 8)
        out[:, columns] = (
            shifted[:, columns].astype(jnp.float32) + gate[0:1, columns] * returned[:, columns].astype(jnp.float32)
        ).astype(jnp.bfloat16)
    for j in range(8):
        back(j).wait_send()


def shards(
    latent, query_in, key_in, value_in, cache_keys, cache_values, levels, timesteps, cache_mask, time_weight
):
    anywhere = pl.BlockSpec(memory_space=pl.ANY)
    scalars = pl.BlockSpec(memory_space=pltpu.SMEM)
    bf16, f32 = jnp.bfloat16, jnp.float32
    dma = pltpu.SemaphoreType.DMA
    return pl.pallas_call(
        kernel,
        out_shape=jax.ShapeDtypeStruct(latent.shape, latent.dtype),
        in_specs=[scalars] * 3 + [anywhere] * 7,
        out_specs=pl.BlockSpec(memory_space=pltpu.VMEM),
        scratch_shapes=[
            pltpu.VMEM((8, ROWS, WIDTH), bf16),
            pltpu.VMEM((GROUP, HEAD_DIM, KEYS), bf16),
            pltpu.VMEM((CHUNKS, 2, 8, ROWS, WIDTH), bf16),
            pltpu.VMEM((8, ROWS, WIDTH), bf16),
            pltpu.VMEM(latent.shape, bf16),
            pltpu.VMEM(latent.shape, bf16),
            pltpu.VMEM(time_weight.shape, bf16),
            pltpu.VMEM((8, latent.shape[1]), f32),
            pltpu.VMEM((GROUP, KEYS, KEYS), f32),
            pltpu.VMEM((GROUP, KEYS, KEYS), bf16),
            pltpu.VMEM((GROUP, 1, KEYS), f32),
            pltpu.VMEM((GROUP, 1, KEYS), f32),
            pltpu.VMEM((GROUP, 1, KEYS), f32),
            pltpu.VMEM((GROUP, HEAD_DIM, KEYS), f32),
            pltpu.SMEM((CHUNKS * 8,), f32),
            dma((8, 3)),
            dma((X_CHUNKS, 5)),
            dma((8,)),
            dma((8,)),
            dma((8,)),
            dma((X_CHUNKS,)),
            dma((X_CHUNKS,)),
            dma((X_CHUNKS, 5)),
            dma((8,)),
            dma((8,)),
            dma((1,)),
        ],
        compiler_params=pltpu.CompilerParams(
            collective_id=0, has_side_effects=True, vmem_limit_bytes=64 * 1024 * 1024
        ),
        cost_estimate=pl.CostEstimate(flops=2 * 10**9, bytes_accessed=5 * 10**6, transcendentals=4 * 10**6),
    )(
        levels, timesteps, cache_mask, latent, query_in, key_in, value_in, cache_keys, cache_values, time_weight
    )


def solution(mesh):
    return jax.shard_map(
        shards,
        mesh=mesh,
        in_specs=(
            P(("chain", "head"), None),
            P(("chain", "head"), None),
            P(("chain", "head"), None),
            P(("chain", "head"), None),
            P("chain", "head"),
            P("chain", "head"),
            P(),
            P(),
            P(),
            P(),
        ),
        out_specs=P(("chain", "head"), None),
        check_vma=False,
    )
```

```python
import functools
import math

import jax
import jax.numpy as jnp
from jax import lax
from jax.experimental import pallas as pl
from jax.experimental.pallas import tpu as pltpu
from jax.sharding import PartitionSpec as P

MESH = pl.DeviceIdType.MESH
HEAD_DIM = 128
SPANS = 4
NY, NX, NZ = 4, 4, 8
GROUP = 5
WIDTH = GROUP * HEAD_DIM
ROWS = 32
HOPS = (0, 1, 7, 2, 6, 3, 5, 4)
CHUNKS = 12
FIRST_Z = 2
X_CHUNKS = 9
KEYS = 8 * ROWS
HIDDEN = -1e30


def device(y, z, x, core):
    return {"chain": (y * 2 + z // 4) * NX + x, "head": (z % 4) * 2 + core}


def group_columns(z):
    group = (z % 4) * 2 + z // 4
    return pl.ds(pl.multiple_of(group * WIDTH, 128), WIDTH)


def kernel(
    levels, timesteps, cache_mask, latent, query_in, key_in, value_in, cache_keys, cache_values, time_weight,
    out,
    query, turned, kv, relay, attended, returned, shifted, weight, gate, scored, weighed, factor, peak, total, summed, bias,
    send_z, send_x, send_y, send_o, recv_q, recv_k, recv_v, recv_relay, recv_x, recv_y, recv_o, local,
):
    chain, head = lax.axis_index("chain"), lax.axis_index("head")
    y, x = chain // 8, chain % 4
    zh, zl, core = (chain // 4) % 2, head // 2, head % 2
    z = zh * 4 + zl
    up, down = (y + 1) % 4, (y + 3) % 4
    right, left = (x + 1) % 4, (x + 3) % 4
    sibling = device(y, z, x, 1 - core)
    across = device(y, (z + 4) % 8, x, 1 - core)
    back_two = device(y, (z + 6) % 8, x, core)

    def remote(src, dst, send, recv, to):
        return pltpu.make_async_remote_copy(
            src_ref=src, dst_ref=dst, send_sem=send, recv_sem=recv, device_id=to, device_id_type=MESH
        )

    mine = group_columns(z)
    own = [
        pltpu.make_async_copy(key_in.at[:, mine], kv.at[0, 0, 0], recv_k.at[0]),
        pltpu.make_async_copy(value_in.at[:, mine], kv.at[0, 1, 0], recv_v.at[0]),
        pltpu.make_async_copy(query_in.at[:, mine], query.at[0], recv_q.at[0]),
    ]
    for copy in own:
        copy.start()
    weight_copy = pltpu.make_async_copy(time_weight, weight, local.at[0])
    weight_copy.start()

    @pl.when(core == zh)
    def _():
        pltpu.make_async_copy(cache_keys, kv.at[1, 0, 0], recv_k.at[1]).start()
        pltpu.make_async_copy(cache_values, kv.at[1, 1, 0], recv_v.at[1]).start()

    barrier = pltpu.get_barrier_semaphore()
    partners = [sibling, across, device(y, z, right, core), device(y, z, left, core)]
    partners += [device(up, z, x, core), device(down, z, x, core)]
    for hop in HOPS[1:]:
        partners += [device(row, (z + hop) % 8, x, core) for row in (y, up, down)]
    for partner in partners:
        pl.semaphore_signal(barrier, inc=1, device_id=partner, device_id_type=MESH)
    pl.semaphore_wait(barrier, len(partners))

    def cache_across(which, source, recv):
        return remote(source, kv.at[1, which, 0], send_z.at[0, which], recv.at[1], across)

    def query_over_z(j):
        to = (z + HOPS[j]) % 8
        return remote(
            query_in.at[:, group_columns(to)], query.at[j], send_z.at[j, 2], recv_q.at[j], device(y, to, x, core)
        )

    def kv_over_z(j, which, source, recv):
        to = (z + HOPS[j]) % 8
        source = source.at[:, group_columns(to)]
        if HOPS[j] == 4:
            return remote(source, relay.at[which], send_z.at[j, which], recv_relay.at[which], back_two)
        return remote(source, kv.at[j + 1, which, 0], send_z.at[j, which], recv.at[j + 1], device(y, to, x, core))

    def relay_on(which, recv):
        return remote(relay.at[which], kv.at[8, which, 0], send_z.at[8, which], recv.at[8], back_two)

    def over_x(i):
        own_kv = kv.at[i, :, 0]
        return (
            remote(own_kv, kv.at[i, :, 1], send_x.at[i, 0], recv_x.at[i, 0], device(y, z, right, core)),
            remote(own_kv, kv.at[i, :, 3], send_x.at[i, 1], recv_x.at[i, 1], device(y, z, left, core)),
            remote(kv.at[i, 0, 1], kv.at[i, 0, 2], send_x.at[i, 2], recv_x.at[i, 2], device(y, z, right, core)),
            remote(kv.at[i, 1, 3], kv.at[i, 1, 2], send_x.at[i, 3], recv_x.at[i, 3], device(y, z, left, core)),
        )

    def to_sibling(i, send, recv):
        return remote(kv.at[i, :, 0:4], kv.at[i, :, 4:8], send, recv, sibling)

    def sibling_x(i):
        return to_sibling(i, send_x.at[i, 4], recv_x.at[i, 4])

    half = slice(0, 4)
    to_up, to_down = device(up, z, x, core), device(down, z, x, core)
    y_up = remote(kv.at[1, :, half], kv.at[9, :, half], send_y.at[0], recv_y.at[0], to_up)
    y_down = remote(kv.at[1, :, half], kv.at[10, :, half], send_y.at[1], recv_y.at[1], to_down)
    y_on_up = remote(kv.at[9, 0, half], kv.at[11, 0, half], send_y.at[2], recv_y.at[2], to_up)
    y_on_down = remote(kv.at[10, 1, half], kv.at[11, 1, half], send_y.at[3], recv_y.at[3], to_down)
    latent_down = remote(latent, shifted, send_y.at[7], recv_y.at[7], to_down)

    def sibling_y(i):
        return to_sibling(i, send_y.at[i - 5], recv_y.at[i - 5])

    def back(j):
        to = (z - HOPS[j] + 8) % 8
        return remote(attended.at[j], returned.at[:, mine], send_o.at[j], recv_o.at[j], device(down, to, x, core))

    @pl.when(core != zh)
    def _():
        cache_across(0, cache_keys, recv_k).start()
        cache_across(1, cache_values, recv_v).start()

    def start_kv(j):
        kv_over_z(j, 0, key_in, recv_k).start()
        kv_over_z(j, 1, value_in, recv_v).start()

    for j in range(1, 8):
        query_over_z(j).start()
    for j in (1, 2, 7, 3, 4):
        start_kv(j)
    latent_down.start()

    def prepare():
        for i in range(CHUNKS):
            for slot in range(8):
                if i == 1 or i >= 9:
                    plane = {1: y, 9: down, 10: up, 11: (y + 2) % 4}[i]
                    side = core if slot < 4 else 1 - core
                    block = plane * 8 + side * 4 + (x + (0, 3, 2, 1)[slot % 4]) % 4
                    bias[i * 8 + slot] = jnp.where(cache_mask[y, block] == 1, 0.0, HIDDEN).astype(jnp.float32)
                else:
                    bias[i * 8 + slot] = jnp.float32(0.0)

        stamp = timesteps[levels[up]].astype(jnp.float32)
        count = 128
        index = lax.broadcasted_iota(jnp.int32, (8, count), 1).astype(jnp.float32)
        phase = stamp * jnp.exp(-math.log(10000.0) * index / count)
        embed = jnp.concatenate([jnp.cos(phase), jnp.sin(phase)], axis=1).astype(jnp.bfloat16)
        weight_copy.wait()

        def gate_columns(c, carry):
            columns = pl.ds(pl.multiple_of(c * WIDTH, 128), WIDTH)
            gate[:, columns] = jnp.dot(embed, weight[:, columns], preferred_element_type=jnp.float32)
            return carry

        lax.fori_loop(0, 8, gate_columns, 0)

        peak[...] = jnp.full_like(peak, HIDDEN)
        total[...] = jnp.zeros_like(total)
        summed[...] = jnp.zeros_like(summed)

    def attend(i, cached):
        def of_head(which, h):
            return kv[i, which, :, :, h * HEAD_DIM : (h + 1) * HEAD_DIM].reshape(KEYS, HEAD_DIM)

        scale = 1.0 / math.sqrt(HEAD_DIM)
        for h in range(GROUP):
            scored[h] = jnp.dot(of_head(0, h), turned[h], preferred_element_type=jnp.float32)
        for h in range(GROUP):
            for side in (slice(0, 128), slice(128, 256)):
                scores = scored[h, :, side]
                if cached:
                    scores = jnp.concatenate(
                        [scores[slot * ROWS : (slot + 1) * ROWS] + bias[i * 8 + slot] for slot in range(8)], axis=0
                    )
                old = peak[h, :, side]
                new = jnp.maximum(old, jnp.max(scores, axis=0, keepdims=True) * scale)
                weights = jnp.exp(scores * scale - new)
                shrink = jnp.exp(old - new)
                peak[h, :, side] = new
                factor[h, :, side] = shrink
                total[h, :, side] = shrink * total[h, :, side] + jnp.sum(weights, axis=0, keepdims=True)
                weighed[h, :, side] = weights.astype(jnp.bfloat16)
        for h in range(GROUP):
            added = lax.dot_general(
                of_head(1, h), weighed[h], (((0,), (0,)), ((), ())), preferred_element_type=jnp.float32
            )
            summed[h] = factor[h] * summed[h] + added

    def turn(t, carry):
        @pl.when((t >= 2) & (t < X_CHUNKS + 2))
        def _():
            copies = over_x(t - 2)
            copies[0].wait_recv()
            copies[2].start()
            copies[1].wait_recv()
            copies[3].start()

        @pl.when((t >= 3) & (t < X_CHUNKS + 3))
        def _():
            copies = over_x(t - 3)
            copies[2].wait_recv()
            copies[3].wait_recv()
            sibling_x(t - 3).start()

        @pl.when(t == 4)
        def _():
            for which, source, recv in ((0, key_in, recv_k), (1, value_in, recv_v)):
                kv_over_z(7, which, source, recv).wait_recv()
                relay_on(which, recv).start()
            y_up.start()
            y_down.start()
            own[2].wait()
            for j in range(1, 8):
                query_over_z(j).wait_recv()
            for h in range(GROUP):
                columns = slice(h * HEAD_DIM, (h + 1) * HEAD_DIM)
                turned[h] = query[:, :, columns].reshape(KEYS, HEAD_DIM).astype(jnp.float32).T.astype(jnp.bfloat16)

        @pl.when(t == 7)
        def _():
            y_up.wait_recv()
            y_on_up.start()
            y_down.wait_recv()
            y_on_down.start()
            sibling_y(9).start()
            sibling_y(10).start()

        @pl.when(t == 9)
        def _():
            y_on_up.wait_recv()
            y_on_down.wait_recv()
            sibling_y(11).start()

        @pl.when(t >= 4)
        def _():
            sibling_x(t - 4).wait_recv()

        @pl.when((t >= 4) & (t != 5))
        def _():
            attend(t - 4, False)

        for i in (9, 10, 11):

            @pl.when(t == i)
            def _(i=i):
                sibling_y(i).wait_recv()

        @pl.when((t == 5) | ((t >= 9) & (t <= 11)))
        def _():
            attend(jnp.where(t == 5, 1, t), True)

        @pl.when(t < X_CHUNKS)
        def _():
            pltpu.make_async_copy(kv.at[t, 0, 0], kv.at[t, 0, 0], recv_k.at[t]).wait()
            pltpu.make_async_copy(kv.at[t, 1, 0], kv.at[t, 1, 0], recv_v.at[t]).wait()
            over_x(t)[0].start()
            over_x(t)[1].start()

        for turn_of, hops in ((1, (5, 6)),):

            @pl.when(t == turn_of)
            def _(hops=hops):
                for j in hops:
                    start_kv(j)

        pl.when(t == 1)(prepare)
        return carry

    lax.fori_loop(0, X_CHUNKS + 4, turn, 0)

    for h in range(GROUP):
        result = summed[h] * (1.0 / total[h])
        attended[:, :, h * HEAD_DIM : (h + 1) * HEAD_DIM] = result.T.astype(jnp.bfloat16).reshape(8, ROWS, HEAD_DIM)
    for j in range(8):
        back(j).start()

    @pl.when(core != zh)
    def _():
        cache_across(0, cache_keys, recv_k).wait_send()
        cache_across(1, cache_values, recv_v).wait_send()

    relay_on(0, recv_k).wait_send()
    relay_on(1, recv_v).wait_send()
    for j in range(1, 8):
        query_over_z(j).wait_send()
        kv_over_z(j, 0, key_in, recv_k).wait_send()
        kv_over_z(j, 1, value_in, recv_v).wait_send()

    def sent(i, carry):
        for copy in over_x(i):
            copy.wait_send()
        sibling_x(i).wait_send()
        return carry

    lax.fori_loop(0, X_CHUNKS, sent, 0)
    for copy in (y_up, y_down, y_on_up, y_on_down, sibling_y(9), sibling_y(10), sibling_y(11), latent_down):
        copy.wait_send()

    latent_down.wait_recv()
    for j in range(8):
        back(j).wait_recv()
        columns = group_columns((z + HOPS[j]) % 8)
        out[:, columns] = (
            shifted[:, columns].astype(jnp.float32) + gate[0:1, columns] * returned[:, columns].astype(jnp.float32)
        ).astype(jnp.bfloat16)
    for j in range(8):
        back(j).wait_send()


def shards(
    latent, query_in, key_in, value_in, cache_keys, cache_values, levels, timesteps, cache_mask, time_weight
):
    anywhere = pl.BlockSpec(memory_space=pl.ANY)
    scalars = pl.BlockSpec(memory_space=pltpu.SMEM)
    bf16, f32 = jnp.bfloat16, jnp.float32
    dma = pltpu.SemaphoreType.DMA
    return pl.pallas_call(
        kernel,
        out_shape=jax.ShapeDtypeStruct(latent.shape, latent.dtype),
        in_specs=[scalars] * 3 + [anywhere] * 7,
        out_specs=pl.BlockSpec(memory_space=pltpu.VMEM),
        scratch_shapes=[
            pltpu.VMEM((8, ROWS, WIDTH), bf16),
            pltpu.VMEM((GROUP, HEAD_DIM, KEYS), bf16),
            pltpu.VMEM((CHUNKS, 2, 8, ROWS, WIDTH), bf16),
            pltpu.VMEM((2, ROWS, WIDTH), bf16),
            pltpu.VMEM((8, ROWS, WIDTH), bf16),
            pltpu.VMEM(latent.shape, bf16),
            pltpu.VMEM(latent.shape, bf16),
            pltpu.VMEM(time_weight.shape, bf16),
            pltpu.VMEM((8, latent.shape[1]), f32),
            pltpu.VMEM((GROUP, KEYS, KEYS), f32),
            pltpu.VMEM((GROUP, KEYS, KEYS), bf16),
            pltpu.VMEM((GROUP, 1, KEYS), f32),
            pltpu.VMEM((GROUP, 1, KEYS), f32),
            pltpu.VMEM((GROUP, 1, KEYS), f32),
            pltpu.VMEM((GROUP, HEAD_DIM, KEYS), f32),
            pltpu.SMEM((CHUNKS * 8,), f32),
            dma((9, 3)),
            dma((X_CHUNKS, 5)),
            dma((8,)),
            dma((8,)),
            dma((8,)),
            dma((X_CHUNKS,)),
            dma((X_CHUNKS,)),
            dma((2,)),
            dma((X_CHUNKS, 5)),
            dma((8,)),
            dma((8,)),
            dma((1,)),
        ],
        compiler_params=pltpu.CompilerParams(
            collective_id=0, has_side_effects=True, vmem_limit_bytes=64 * 1024 * 1024
        ),
        cost_estimate=pl.CostEstimate(flops=2 * 10**9, bytes_accessed=5 * 10**6, transcendentals=4 * 10**6),
    )(
        levels, timesteps, cache_mask, latent, query_in, key_in, value_in, cache_keys, cache_values, time_weight
    )


def solution(mesh):
    return jax.shard_map(
        shards,
        mesh=mesh,
        in_specs=(
            P(("chain", "head"), None),
            P(("chain", "head"), None),
            P(("chain", "head"), None),
            P(("chain", "head"), None),
            P("chain", "head"),
            P("chain", "head"),
            P(),
            P(),
            P(),
            P(),
        ),
        out_specs=P(("chain", "head"), None),
        check_vma=False,
    )
```

```python
import functools
import math

import jax
import jax.numpy as jnp
from jax import lax
from jax.experimental import pallas as pl
from jax.experimental.pallas import tpu as pltpu
from jax.sharding import PartitionSpec as P

MESH = pl.DeviceIdType.MESH
HEAD_DIM = 128
SPANS = 4
NY, NX, NZ = 4, 4, 8
GROUP = 5
WIDTH = GROUP * HEAD_DIM
ROWS = 32
HOPS = (0, 1, 7, 2, 6, 3, 5, 4)
PAIRS = ((0, 1), (2, 3), (4, 5), (9, 10), (6, 7), (8, 11))
X_ITEMS = 9
KEYS = 8 * ROWS
HIDDEN = -1e30


def device(y, z, x, core):
    return {"chain": (y * 2 + z // 4) * NX + x, "head": (z % 4) * 2 + core}


def place(i):
    if isinstance(i, int):
        return next((n, pair.index(i)) for n, pair in enumerate(PAIRS) if i in pair)
    return jnp.where(i < 6, i // 2, jnp.where(i < 8, 4, 5)), i % 2


def group_columns(z):
    group = (z % 4) * 2 + z // 4
    return pl.ds(pl.multiple_of(group * WIDTH, 128), WIDTH)


def kernel(
    levels, timesteps, cache_mask, latent, query_in, key_in, value_in, cache_keys, cache_values, time_weight,
    out,
    query, turned, kv, attended, returned, shifted, weight, gate, scored, weighed, factor, peak, total, summed,
    other_query, partial, other_partial, other_peak, other_total, bias,
    send_z, send_x, send_y, send_o, send_c, recv_q, recv_k, recv_v, recv_x, recv_y, recv_o, recv_c, local,
):
    chain, head = lax.axis_index("chain"), lax.axis_index("head")
    y, x = chain // 8, chain % 4
    zh, zl, core = (chain // 4) % 2, head // 2, head % 2
    z = zh * 4 + zl
    up, down = (y + 1) % 4, (y + 3) % 4
    right, left = (x + 1) % 4, (x + 3) % 4
    sibling = device(y, z, x, 1 - core)
    across = device(y, (z + 4) % 8, x, 1 - core)

    def remote(src, dst, send, recv, to):
        return pltpu.make_async_remote_copy(
            src_ref=src, dst_ref=dst, send_sem=send, recv_sem=recv, device_id=to, device_id_type=MESH
        )

    def item(i):
        pair, member = place(i)
        return kv.at[pair, :, member]

    mine = group_columns(z)
    own = [
        pltpu.make_async_copy(key_in.at[:, mine], item(0).at[0, 0], recv_k.at[0]),
        pltpu.make_async_copy(value_in.at[:, mine], item(0).at[1, 0], recv_v.at[0]),
        pltpu.make_async_copy(query_in.at[:, mine], query.at[0], recv_q.at[0]),
    ]
    for copy in own:
        copy.start()
    weight_copy = pltpu.make_async_copy(time_weight, weight, local.at[0])
    weight_copy.start()

    @pl.when(core == zh)
    def _():
        pltpu.make_async_copy(cache_keys, item(1).at[0, 0], recv_k.at[1]).start()
        pltpu.make_async_copy(cache_values, item(1).at[1, 0], recv_v.at[1]).start()

    barrier = pltpu.get_barrier_semaphore()
    partners = [sibling, across, device(y, z, right, core), device(y, z, left, core)]
    partners += [device(up, z, x, core), device(down, z, x, core)]
    for hop in HOPS[1:]:
        partners += [device(row, (z + hop) % 8, x, core) for row in (y, up, down)]
    for partner in partners:
        pl.semaphore_signal(barrier, inc=1, device_id=partner, device_id_type=MESH)
    pl.semaphore_wait(barrier, len(partners))

    def cache_across(which, source, recv):
        return remote(source, item(1).at[which, 0], send_z.at[0, which], recv.at[1], across)

    def query_over_z(j):
        to = (z + HOPS[j]) % 8
        return remote(
            query_in.at[:, group_columns(to)], query.at[j], send_z.at[j, 2], recv_q.at[j], device(y, to, x, core)
        )

    def kv_over_z(j, which, source, recv):
        to = (z + HOPS[j]) % 8
        return remote(
            source.at[:, group_columns(to)],
            item(j + 1).at[which, 0],
            send_z.at[j, which],
            recv.at[j + 1],
            device(y, to, x, core),
        )

    def over_x(i):
        here = item(i)
        return (
            remote(here.at[:, 0], here.at[:, 1], send_x.at[i, 0], recv_x.at[i, 0], device(y, z, right, core)),
            remote(here.at[:, 0], here.at[:, 3], send_x.at[i, 1], recv_x.at[i, 1], device(y, z, left, core)),
            remote(here.at[0, 1], here.at[0, 2], send_x.at[i, 2], recv_x.at[i, 2], device(y, z, right, core)),
            remote(here.at[1, 3], here.at[1, 2], send_x.at[i, 3], recv_x.at[i, 3], device(y, z, left, core)),
        )

    to_up, to_down = device(up, z, x, core), device(down, z, x, core)
    y_up = remote(item(1), item(9), send_y.at[0], recv_y.at[0], to_up)
    y_down = remote(item(1), item(10), send_y.at[1], recv_y.at[1], to_down)
    y_on_up = remote(item(9).at[0], item(11).at[0], send_y.at[2], recv_y.at[2], to_up)
    y_on_down = remote(item(10).at[1], item(11).at[1], send_y.at[3], recv_y.at[3], to_down)
    latent_down = remote(latent, shifted, send_y.at[4], recv_y.at[4], to_down)

    query_across = remote(query, other_query, send_c.at[0], recv_c.at[0], sibling)
    theirs = slice(KEYS, 2 * KEYS)
    partial_across = remote(partial, other_partial, send_c.at[1], recv_c.at[1], sibling)
    peak_across = remote(peak.at[:, :, theirs], other_peak, send_c.at[2], recv_c.at[2], sibling)
    total_across = remote(total.at[:, :, theirs], other_total, send_c.at[3], recv_c.at[3], sibling)

    def back(j):
        to = (z - HOPS[j] + 8) % 8
        return remote(attended.at[j], returned.at[:, mine], send_o.at[j], recv_o.at[j], device(down, to, x, core))

    @pl.when(core != zh)
    def _():
        cache_across(0, cache_keys, recv_k).start()
        cache_across(1, cache_values, recv_v).start()

    def start_kv(j):
        kv_over_z(j, 0, key_in, recv_k).start()
        kv_over_z(j, 1, value_in, recv_v).start()

    for j in range(1, 8):
        query_over_z(j).start()
    for j in range(1, 5):
        start_kv(j)
    latent_down.start()

    def prepare():
        for pair, items in enumerate(PAIRS):
            for slot in range(8):
                i = items[slot // 4]
                shown = jnp.float32(0.0)
                if i == 1 or i >= 9:
                    plane = {1: y, 9: down, 10: up, 11: (y + 2) % 4}[i]
                    block = plane * 8 + core * 4 + (x + (0, 3, 2, 1)[slot % 4]) % 4
                    shown = jnp.where(cache_mask[y, block] == 1, 0.0, HIDDEN).astype(jnp.float32)
                bias[pair * 8 + slot] = shown

        stamp = timesteps[levels[up]].astype(jnp.float32)
        count = 128
        index = lax.broadcasted_iota(jnp.int32, (8, count), 1).astype(jnp.float32)
        phase = stamp * jnp.exp(-math.log(10000.0) * index / count)
        embed = jnp.concatenate([jnp.cos(phase), jnp.sin(phase)], axis=1).astype(jnp.bfloat16)
        weight_copy.wait()

        def gate_columns(c, carry):
            columns = pl.ds(pl.multiple_of(c * WIDTH, 128), WIDTH)
            gate[:, columns] = jnp.dot(embed, weight[:, columns], preferred_element_type=jnp.float32)
            return carry

        lax.fori_loop(0, 8, gate_columns, 0)

        peak[...] = jnp.full_like(peak, HIDDEN)
        total[...] = jnp.zeros_like(total)
        summed[...] = jnp.zeros_like(summed)

    def attend(pair, half):
        def of_head(which, h):
            return kv[pair, which, :, :, :, h * HEAD_DIM : (h + 1) * HEAD_DIM].reshape(KEYS, HEAD_DIM)

        scale = 1.0 / math.sqrt(HEAD_DIM)
        for h in range(GROUP):
            scored[h] = jnp.dot(of_head(0, h), turned[half, h], preferred_element_type=jnp.float32)
        for h in range(GROUP):
            for side in (0, 128):
                scores = scored[h, :, side : side + 128]
                scores = jnp.concatenate(
                    [scores[slot * ROWS : (slot + 1) * ROWS] + bias[pair * 8 + slot] for slot in range(8)], axis=0
                )
                columns = pl.ds(pl.multiple_of(half * KEYS + side, 128), 128)
                old = peak[h, :, columns]
                new = jnp.maximum(old, jnp.max(scores, axis=0, keepdims=True) * scale)
                weights = jnp.exp(scores * scale - new)
                shrink = jnp.exp(old - new)
                peak[h, :, columns] = new
                factor[h, :, side : side + 128] = shrink
                total[h, :, columns] = shrink * total[h, :, columns] + jnp.sum(weights, axis=0, keepdims=True)
                weighed[h, :, side : side + 128] = weights.astype(jnp.bfloat16)
        for h in range(GROUP):
            added = lax.dot_general(
                of_head(1, h), weighed[h], (((0,), (0,)), ((), ())), preferred_element_type=jnp.float32
            )
            summed[half, h] = factor[h] * summed[half, h] + added

    def attend_both(pair):
        def half(n, carry):
            attend(pair, n)
            return carry

        lax.fori_loop(0, 2, half, 0)

    def turn_query(source, half):
        for h in range(GROUP):
            columns = slice(h * HEAD_DIM, (h + 1) * HEAD_DIM)
            turned[half, h] = source[:, :, columns].reshape(KEYS, HEAD_DIM).astype(jnp.float32).T.astype(jnp.bfloat16)

    def turn(t, carry):
        @pl.when((t >= 2) & (t < X_ITEMS + 2))
        def _():
            copies = over_x(t - 2)
            copies[0].wait_recv()
            copies[2].start()
            copies[1].wait_recv()
            copies[3].start()

        @pl.when(t >= 3)
        def _():
            copies = over_x(t - 3)
            copies[2].wait_recv()
            copies[3].wait_recv()

        @pl.when(t == 3)
        def _():
            own[2].wait()
            for j in range(1, 8):
                query_over_z(j).wait_recv()
            query_across.start()
            turn_query(query, 0)

        @pl.when(t == 4)
        def _():
            y_up.start()
            y_down.start()
            query_across.wait_recv()
            turn_query(other_query, 1)

        @pl.when(t == 7)
        def _():
            y_up.wait_recv()
            y_on_up.start()
            y_down.wait_recv()
            y_on_down.start()

        @pl.when((t == 4) | (t == 6) | ((t >= 8) & (t <= 10)))
        def _():
            attend_both(jnp.where(t < 8, (t - 4) // 2, t - 6))

        @pl.when(t < X_ITEMS)
        def _():
            here = item(t)
            pltpu.make_async_copy(here.at[0, 0], here.at[0, 0], recv_k.at[t]).wait()
            pltpu.make_async_copy(here.at[1, 0], here.at[1, 0], recv_v.at[t]).wait()
            over_x(t)[0].start()
            over_x(t)[1].start()

        for turn_of, hops in ((1, (5, 6)), (3, (7,))):

            @pl.when(t == turn_of)
            def _(hops=hops):
                for j in hops:
                    start_kv(j)

        pl.when(t == 1)(prepare)
        return carry

    lax.fori_loop(0, X_ITEMS + 3, turn, 0)
    y_on_up.wait_recv()
    y_on_down.wait_recv()
    attend(len(PAIRS) - 1, 1)
    for h in range(GROUP):
        partial[h] = (summed[1, h] * (1.0 / total[h, :, theirs])).astype(jnp.bfloat16)
    across_copies = (partial_across, peak_across, total_across)
    for copy in across_copies:
        copy.start()
    attend(len(PAIRS) - 1, 0)
    for copy in across_copies:
        copy.wait_recv()

    ours = slice(0, KEYS)
    for h in range(GROUP):
        new = jnp.maximum(peak[h, :, ours], other_peak[h])
        shrink = jnp.exp(peak[h, :, ours] - new)
        other_weight = other_total[h] * jnp.exp(other_peak[h] - new)
        whole = 1.0 / (shrink * total[h, :, ours] + other_weight)
        result = (shrink * whole) * summed[0, h] + (other_weight * whole) * other_partial[h].astype(jnp.float32)
        attended[:, :, h * HEAD_DIM : (h + 1) * HEAD_DIM] = result.T.astype(jnp.bfloat16).reshape(8, ROWS, HEAD_DIM)
    for j in range(8):
        back(j).start()

    @pl.when(core != zh)
    def _():
        cache_across(0, cache_keys, recv_k).wait_send()
        cache_across(1, cache_values, recv_v).wait_send()

    for j in range(1, 8):
        query_over_z(j).wait_send()
        kv_over_z(j, 0, key_in, recv_k).wait_send()
        kv_over_z(j, 1, value_in, recv_v).wait_send()

    def sent(i, carry):
        for copy in over_x(i):
            copy.wait_send()
        return carry

    lax.fori_loop(0, X_ITEMS, sent, 0)
    for copy in (y_up, y_down, y_on_up, y_on_down, latent_down, query_across) + across_copies:
        copy.wait_send()

    latent_down.wait_recv()
    for j in range(8):
        back(j).wait_recv()
        columns = group_columns((z + HOPS[j]) % 8)
        out[:, columns] = (
            shifted[:, columns].astype(jnp.float32) + gate[0:1, columns] * returned[:, columns].astype(jnp.float32)
        ).astype(jnp.bfloat16)
    for j in range(8):
        back(j).wait_send()


def shards(
    latent, query_in, key_in, value_in, cache_keys, cache_values, levels, timesteps, cache_mask, time_weight
):
    anywhere = pl.BlockSpec(memory_space=pl.ANY)
    scalars = pl.BlockSpec(memory_space=pltpu.SMEM)
    bf16, f32 = jnp.bfloat16, jnp.float32
    dma = pltpu.SemaphoreType.DMA
    return pl.pallas_call(
        kernel,
        out_shape=jax.ShapeDtypeStruct(latent.shape, latent.dtype),
        in_specs=[scalars] * 3 + [anywhere] * 7,
        out_specs=pl.BlockSpec(memory_space=pltpu.VMEM),
        scratch_shapes=[
            pltpu.VMEM((8, ROWS, WIDTH), bf16),
            pltpu.VMEM((2, GROUP, HEAD_DIM, KEYS), bf16),
            pltpu.VMEM((len(PAIRS), 2, 2, 4, ROWS, WIDTH), bf16),
            pltpu.VMEM((8, ROWS, WIDTH), bf16),
            pltpu.VMEM(latent.shape, bf16),
            pltpu.VMEM(latent.shape, bf16),
            pltpu.VMEM(time_weight.shape, bf16),
            pltpu.VMEM((8, latent.shape[1]), f32),
            pltpu.VMEM((GROUP, KEYS, KEYS), f32),
            pltpu.VMEM((GROUP, KEYS, KEYS), bf16),
            pltpu.VMEM((GROUP, 1, KEYS), f32),
            pltpu.VMEM((GROUP, 1, 2 * KEYS), f32),
            pltpu.VMEM((GROUP, 1, 2 * KEYS), f32),
            pltpu.VMEM((2, GROUP, HEAD_DIM, KEYS), f32),
            pltpu.VMEM((8, ROWS, WIDTH), bf16),
            pltpu.VMEM((GROUP, HEAD_DIM, KEYS), bf16),
            pltpu.VMEM((GROUP, HEAD_DIM, KEYS), bf16),
            pltpu.VMEM((GROUP, 1, KEYS), f32),
            pltpu.VMEM((GROUP, 1, KEYS), f32),
            pltpu.SMEM((len(PAIRS) * 8,), f32),
            dma((8, 3)),
            dma((X_ITEMS, 4)),
            dma((5,)),
            dma((8,)),
            dma((4,)),
            dma((8,)),
            dma((X_ITEMS,)),
            dma((X_ITEMS,)),
            dma((X_ITEMS, 4)),
            dma((5,)),
            dma((8,)),
            dma((4,)),
            dma((1,)),
        ],
        compiler_params=pltpu.CompilerParams(
            collective_id=0, has_side_effects=True, vmem_limit_bytes=64 * 1024 * 1024
        ),
        cost_estimate=pl.CostEstimate(flops=2 * 10**9, bytes_accessed=5 * 10**6, transcendentals=4 * 10**6),
    )(
        levels, timesteps, cache_mask, latent, query_in, key_in, value_in, cache_keys, cache_values, time_weight
    )


def solution(mesh):
    return jax.shard_map(
        shards,
        mesh=mesh,
        in_specs=(
            P(("chain", "head"), None),
            P(("chain", "head"), None),
            P(("chain", "head"), None),
            P(("chain", "head"), None),
            P("chain", "head"),
            P("chain", "head"),
            P(),
            P(),
            P(),
            P(),
        ),
        out_specs=P(("chain", "head"), None),
        check_vma=False,
    )
```

```python
import functools
import math

import jax
import jax.numpy as jnp
from jax import lax
from jax.experimental import pallas as pl
from jax.experimental.pallas import tpu as pltpu
from jax.sharding import PartitionSpec as P

MESH = pl.DeviceIdType.MESH
HEAD_DIM = 128
SPANS = 4
NY, NX, NZ = 4, 4, 8
GROUP = 5
WIDTH = GROUP * HEAD_DIM
ROWS = 32
HOPS = (0, 1, 7, 2, 6, 3, 5, 4)
CHUNKS = 12
FIRST_Z = 2
X_CHUNKS = 9
KEYS = 8 * ROWS
HIDDEN = -1e30


def device(y, z, x, core):
    return {"chain": (y * 2 + z // 4) * NX + x, "head": (z % 4) * 2 + core}


def group_columns(z):
    group = (z % 4) * 2 + z // 4
    return pl.ds(pl.multiple_of(group * WIDTH, 128), WIDTH)


def kernel(
    levels, timesteps, cache_mask, latent, query_in, key_in, value_in, cache_keys, cache_values, time_weight,
    out,
    query, turned, kv, attended, returned, shifted, weight, gate, scored, weighed, factor, peak, total, summed, bias,
    send_z, send_x, send_y, send_o, recv_q, recv_k, recv_v, recv_x, recv_y, recv_o, local,
):
    chain, head = lax.axis_index("chain"), lax.axis_index("head")
    y, x = chain // 8, chain % 4
    zh, zl, core = (chain // 4) % 2, head // 2, head % 2
    z = zh * 4 + zl
    up, down = (y + 1) % 4, (y + 3) % 4
    right, left = (x + 1) % 4, (x + 3) % 4
    sibling = device(y, z, x, 1 - core)
    across = device(y, (z + 4) % 8, x, 1 - core)

    def remote(src, dst, send, recv, to):
        return pltpu.make_async_remote_copy(
            src_ref=src, dst_ref=dst, send_sem=send, recv_sem=recv, device_id=to, device_id_type=MESH
        )

    mine = group_columns(z)
    own = [
        pltpu.make_async_copy(key_in.at[:, mine], kv.at[0, 0, 0], recv_k.at[0]),
        pltpu.make_async_copy(value_in.at[:, mine], kv.at[0, 1, 0], recv_v.at[0]),
        pltpu.make_async_copy(query_in.at[:, mine], query.at[0], recv_q.at[0]),
    ]
    for copy in own:
        copy.start()
    weight_copy = pltpu.make_async_copy(time_weight, weight, local.at[0])
    weight_copy.start()

    @pl.when(core == zh)
    def _():
        pltpu.make_async_copy(cache_keys, kv.at[1, 0, 0], recv_k.at[1]).start()
        pltpu.make_async_copy(cache_values, kv.at[1, 1, 0], recv_v.at[1]).start()

    barrier = pltpu.get_barrier_semaphore()
    partners = [sibling, across, device(y, z, right, core), device(y, z, left, core)]
    partners += [device(up, z, x, core), device(down, z, x, core)]
    for hop in HOPS[1:]:
        partners += [device(row, (z + hop) % 8, x, core) for row in (y, up, down)]
    for partner in partners:
        pl.semaphore_signal(barrier, inc=1, device_id=partner, device_id_type=MESH)
    pl.semaphore_wait(barrier, len(partners))

    def cache_across(which, source, recv):
        return remote(source, kv.at[1, which, 0], send_z.at[0, which], recv.at[1], across)

    def query_over_z(j):
        to = (z + HOPS[j]) % 8
        return remote(
            query_in.at[:, group_columns(to)], query.at[j], send_z.at[j, 2], recv_q.at[j], device(y, to, x, core)
        )

    def kv_over_z(j, which, source, recv):
        to = (z + HOPS[j]) % 8
        return remote(
            source.at[:, group_columns(to)],
            kv.at[j + 1, which, 0],
            send_z.at[j, which],
            recv.at[j + 1],
            device(y, to, x, core),
        )

    def over_x(i):
        own_kv = kv.at[i, :, 0]
        return (
            remote(own_kv, kv.at[i, :, 1], send_x.at[i, 0], recv_x.at[i, 0], device(y, z, right, core)),
            remote(own_kv, kv.at[i, :, 3], send_x.at[i, 1], recv_x.at[i, 1], device(y, z, left, core)),
            remote(kv.at[i, 0, 1], kv.at[i, 0, 2], send_x.at[i, 2], recv_x.at[i, 2], device(y, z, right, core)),
            remote(kv.at[i, 1, 3], kv.at[i, 1, 2], send_x.at[i, 3], recv_x.at[i, 3], device(y, z, left, core)),
        )

    def to_sibling(i, send, recv):
        return remote(kv.at[i, :, 0:4], kv.at[i, :, 4:8], send, recv, sibling)

    def sibling_x(i):
        return to_sibling(i, send_x.at[i, 4], recv_x.at[i, 4])

    half = slice(0, 4)
    to_up, to_down = device(up, z, x, core), device(down, z, x, core)
    y_up = remote(kv.at[1, :, half], kv.at[9, :, half], send_y.at[0], recv_y.at[0], to_up)
    y_down = remote(kv.at[1, :, half], kv.at[10, :, half], send_y.at[1], recv_y.at[1], to_down)
    y_on_up = remote(kv.at[9, 0, half], kv.at[11, 0, half], send_y.at[2], recv_y.at[2], to_up)
    y_on_down = remote(kv.at[10, 1, half], kv.at[11, 1, half], send_y.at[3], recv_y.at[3], to_down)
    latent_down = remote(latent, shifted, send_y.at[7], recv_y.at[7], to_down)

    def sibling_y(i):
        return to_sibling(i, send_y.at[i - 5], recv_y.at[i - 5])

    def back(j):
        to = (z - HOPS[j] + 8) % 8
        return remote(attended.at[j], returned.at[:, mine], send_o.at[j], recv_o.at[j], device(down, to, x, core))

    @pl.when(core != zh)
    def _():
        cache_across(0, cache_keys, recv_k).start()
        cache_across(1, cache_values, recv_v).start()

    def start_kv(j):
        kv_over_z(j, 0, key_in, recv_k).start()
        kv_over_z(j, 1, value_in, recv_v).start()

    for j in range(1, 8):
        query_over_z(j).start()
    start_kv(1)
    start_kv(2)
    latent_down.start()

    for i in range(CHUNKS):
        for slot in range(8):
            if i == 1 or i >= 9:
                plane = {1: y, 9: down, 10: up, 11: (y + 2) % 4}[i]
                side = core if slot < 4 else 1 - core
                block = plane * 8 + side * 4 + (x + (0, 3, 2, 1)[slot % 4]) % 4
                bias[i * 8 + slot] = jnp.where(cache_mask[y, block] == 1, 0.0, HIDDEN).astype(jnp.float32)
            else:
                bias[i * 8 + slot] = jnp.float32(0.0)

    stamp = timesteps[levels[up]].astype(jnp.float32)
    count = 128
    index = lax.broadcasted_iota(jnp.int32, (8, count), 1).astype(jnp.float32)
    phase = stamp * jnp.exp(-math.log(10000.0) * index / count)
    embed = jnp.concatenate([jnp.cos(phase), jnp.sin(phase)], axis=1).astype(jnp.bfloat16)
    weight_copy.wait()

    def gate_columns(c, carry):
        columns = pl.ds(pl.multiple_of(c * WIDTH, 128), WIDTH)
        gate[:, columns] = jnp.dot(embed, weight[:, columns], preferred_element_type=jnp.float32)
        return carry

    lax.fori_loop(0, 8, gate_columns, 0)

    peak[...] = jnp.full_like(peak, HIDDEN)
    total[...] = jnp.zeros_like(total)
    summed[...] = jnp.zeros_like(summed)

    def attend(i, cached):
        def of_head(which, h):
            return kv[i, which, :, :, h * HEAD_DIM : (h + 1) * HEAD_DIM].reshape(KEYS, HEAD_DIM)

        scale = 1.0 / math.sqrt(HEAD_DIM)
        for h in range(GROUP):
            scored[h] = jnp.dot(of_head(0, h), turned[h], preferred_element_type=jnp.float32)
        for h in range(GROUP):
            for side in (slice(0, 128), slice(128, 256)):
                scores = scored[h, :, side]
                if cached:
                    scores = jnp.concatenate(
                        [scores[slot * ROWS : (slot + 1) * ROWS] + bias[i * 8 + slot] for slot in range(8)], axis=0
                    )
                old = peak[h, :, side]
                new = jnp.maximum(old, jnp.max(scores, axis=0, keepdims=True) * scale)
                weights = jnp.exp(scores * scale - new)
                shrink = jnp.exp(old - new)
                peak[h, :, side] = new
                factor[h, :, side] = shrink
                total[h, :, side] = shrink * total[h, :, side] + jnp.sum(weights, axis=0, keepdims=True)
                weighed[h, :, side] = weights.astype(jnp.bfloat16)
        for h in range(GROUP):
            added = lax.dot_general(
                of_head(1, h), weighed[h], (((0,), (0,)), ((), ())), preferred_element_type=jnp.float32
            )
            summed[h] = factor[h] * summed[h] + added

    def turn(t, carry):
        @pl.when(t < X_CHUNKS)
        def _():
            pltpu.make_async_copy(kv.at[t, 0, 0], kv.at[t, 0, 0], recv_k.at[t]).wait()
            pltpu.make_async_copy(kv.at[t, 1, 0], kv.at[t, 1, 0], recv_v.at[t]).wait()
            over_x(t)[0].start()
            over_x(t)[1].start()

        for turn_of, hops in ((1, (3, 4)), (3, (5, 6)), (5, (7,))):

            @pl.when(t == turn_of)
            def _(hops=hops):
                for j in hops:
                    start_kv(j)

        @pl.when((t >= 1) & (t < X_CHUNKS + 1))
        def _():
            copies = over_x(t - 1)
            copies[0].wait_recv()
            copies[2].start()
            copies[1].wait_recv()
            copies[3].start()

        @pl.when((t >= 2) & (t < X_CHUNKS + 2))
        def _():
            copies = over_x(t - 2)
            copies[2].wait_recv()
            copies[3].wait_recv()
            sibling_x(t - 2).start()

        @pl.when(t == 3)
        def _():
            y_up.start()
            y_down.start()
            own[2].wait()
            for j in range(1, 8):
                query_over_z(j).wait_recv()
            for h in range(GROUP):
                columns = slice(h * HEAD_DIM, (h + 1) * HEAD_DIM)
                turned[h] = query[:, :, columns].reshape(KEYS, HEAD_DIM).astype(jnp.float32).T.astype(jnp.bfloat16)

        @pl.when(t == 6)
        def _():
            y_up.wait_recv()
            y_on_up.start()
            y_down.wait_recv()
            y_on_down.start()
            sibling_y(9).start()
            sibling_y(10).start()

        @pl.when(t == 8)
        def _():
            y_on_up.wait_recv()
            y_on_down.wait_recv()
            sibling_y(11).start()

        @pl.when(t >= 3)
        def _():
            sibling_x(t - 3).wait_recv()

        @pl.when(t == 8)
        def _():
            sibling_y(9).wait_recv()

        @pl.when(t == 9)
        def _():
            sibling_y(10).wait_recv()

        @pl.when(t == 10)
        def _():
            sibling_y(11).wait_recv()

        @pl.when((t >= 3) & (t != 4))
        def _():
            attend(t - 3, False)

        @pl.when((t == 4) | ((t >= 8) & (t <= 10)))
        def _():
            attend(jnp.where(t == 4, 1, t + 1), True)

        return carry

    lax.fori_loop(0, X_CHUNKS + 3, turn, 0)

    for h in range(GROUP):
        result = summed[h] * (1.0 / total[h])
        attended[:, :, h * HEAD_DIM : (h + 1) * HEAD_DIM] = result.T.astype(jnp.bfloat16).reshape(8, ROWS, HEAD_DIM)
    for j in range(8):
        back(j).start()

    @pl.when(core != zh)
    def _():
        cache_across(0, cache_keys, recv_k).wait_send()
        cache_across(1, cache_values, recv_v).wait_send()

    for j in range(1, 8):
        query_over_z(j).wait_send()
        kv_over_z(j, 0, key_in, recv_k).wait_send()
        kv_over_z(j, 1, value_in, recv_v).wait_send()

    def sent(i, carry):
        for copy in over_x(i):
            copy.wait_send()
        sibling_x(i).wait_send()
        return carry

    lax.fori_loop(0, X_CHUNKS, sent, 0)
    for copy in (y_up, y_down, y_on_up, y_on_down, sibling_y(9), sibling_y(10), sibling_y(11), latent_down):
        copy.wait_send()

    latent_down.wait_recv()
    for j in range(8):
        back(j).wait_recv()
        columns = group_columns((z + HOPS[j]) % 8)
        out[:, columns] = (
            shifted[:, columns].astype(jnp.float32) + gate[0:1, columns] * returned[:, columns].astype(jnp.float32)
        ).astype(jnp.bfloat16)
    for j in range(8):
        back(j).wait_send()


def shards(
    latent, query_in, key_in, value_in, cache_keys, cache_values, levels, timesteps, cache_mask, time_weight
):
    anywhere = pl.BlockSpec(memory_space=pl.ANY)
    scalars = pl.BlockSpec(memory_space=pltpu.SMEM)
    bf16, f32 = jnp.bfloat16, jnp.float32
    dma = pltpu.SemaphoreType.DMA
    return pl.pallas_call(
        kernel,
        out_shape=jax.ShapeDtypeStruct(latent.shape, latent.dtype),
        in_specs=[scalars] * 3 + [anywhere] * 7,
        out_specs=pl.BlockSpec(memory_space=pltpu.VMEM),
        scratch_shapes=[
            pltpu.VMEM((8, ROWS, WIDTH), bf16),
            pltpu.VMEM((GROUP, HEAD_DIM, KEYS), bf16),
            pltpu.VMEM((CHUNKS, 2, 8, ROWS, WIDTH), bf16),
            pltpu.VMEM((8, ROWS, WIDTH), bf16),
            pltpu.VMEM(latent.shape, bf16),
            pltpu.VMEM(latent.shape, bf16),
            pltpu.VMEM(time_weight.shape, bf16),
            pltpu.VMEM((8, latent.shape[1]), f32),
            pltpu.VMEM((GROUP, KEYS, KEYS), f32),
            pltpu.VMEM((GROUP, KEYS, KEYS), bf16),
            pltpu.VMEM((GROUP, 1, KEYS), f32),
            pltpu.VMEM((GROUP, 1, KEYS), f32),
            pltpu.VMEM((GROUP, 1, KEYS), f32),
            pltpu.VMEM((GROUP, HEAD_DIM, KEYS), f32),
            pltpu.SMEM((CHUNKS * 8,), f32),
            dma((8, 3)),
            dma((X_CHUNKS, 5)),
            dma((8,)),
            dma((8,)),
            dma((8,)),
            dma((X_CHUNKS,)),
            dma((X_CHUNKS,)),
            dma((X_CHUNKS, 5)),
            dma((8,)),
            dma((8,)),
            dma((1,)),
        ],
        compiler_params=pltpu.CompilerParams(
            collective_id=0,
            has_side_effects=True,
            vmem_limit_bytes=64 * 1024 * 1024,
            fuse_transposed_lhs_in_matmul=True,
        ),
        cost_estimate=pl.CostEstimate(flops=2 * 10**9, bytes_accessed=5 * 10**6, transcendentals=4 * 10**6),
    )(
        levels, timesteps, cache_mask, latent, query_in, key_in, value_in, cache_keys, cache_values, time_weight
    )


def solution(mesh):
    return jax.shard_map(
        shards,
        mesh=mesh,
        in_specs=(
            P(("chain", "head"), None),
            P(("chain", "head"), None),
            P(("chain", "head"), None),
            P(("chain", "head"), None),
            P("chain", "head"),
            P("chain", "head"),
            P(),
            P(),
            P(),
            P(),
        ),
        out_specs=P(("chain", "head"), None),
        check_vma=False,
    )
```

```python
import functools
import math

import jax
import jax.numpy as jnp
from jax import lax
from jax.experimental import pallas as pl
from jax.experimental.pallas import tpu as pltpu
from jax.sharding import PartitionSpec as P

MESH = pl.DeviceIdType.MESH
HEAD_DIM = 128
SPANS = 4
NY, NX, NZ = 4, 4, 8
GROUP = 5
WIDTH = GROUP * HEAD_DIM
ROWS = 32
HOPS = (0, 1, 7, 2, 6, 3, 5, 4)
CHUNKS = 12
FIRST_Z = 2
X_CHUNKS = 9
KEYS = 8 * ROWS
HIDDEN = -1e30


def device(y, z, x, core):
    return {"chain": (y * 2 + z // 4) * NX + x, "head": (z % 4) * 2 + core}


def group_of(z):
    return (z % 4) * 2 + z // 4


def group_columns(z):
    return pl.ds(pl.multiple_of(group_of(z) * WIDTH, 128), WIDTH)


def kernel(
    levels, timesteps, cache_mask, latent, query_in, key_in, value_in, cache_keys, cache_values, time_weight,
    out,
    staged, query, turned, kv, attended, returned, shifted, weight, gate, scored, weighed, factor, peak, total, summed, bias,
    send_z, send_x, send_y, send_o, recv_q, recv_k, recv_v, recv_x, recv_y, recv_o, local,
):
    chain, head = lax.axis_index("chain"), lax.axis_index("head")
    y, x = chain // 8, chain % 4
    zh, zl, core = (chain // 4) % 2, head // 2, head % 2
    z = zh * 4 + zl
    up, down = (y + 1) % 4, (y + 3) % 4
    right, left = (x + 1) % 4, (x + 3) % 4
    sibling = device(y, z, x, 1 - core)
    across = device(y, (z + 4) % 8, x, 1 - core)

    def remote(src, dst, send, recv, to):
        return pltpu.make_async_remote_copy(
            src_ref=src, dst_ref=dst, send_sem=send, recv_sem=recv, device_id=to, device_id_type=MESH
        )

    for n, source in enumerate((query_in, key_in, value_in)):
        for group in range(8):
            columns = slice(group * WIDTH, (group + 1) * WIDTH)
            pltpu.make_async_copy(source.at[:, columns], staged.at[n, group], local.at[n + 1]).start()
    mine = group_columns(z)
    own = [
        pltpu.make_async_copy(key_in.at[:, mine], kv.at[0, 0, 0], recv_k.at[0]),
        pltpu.make_async_copy(value_in.at[:, mine], kv.at[0, 1, 0], recv_v.at[0]),
        pltpu.make_async_copy(query_in.at[:, mine], query.at[0], recv_q.at[0]),
    ]
    for copy in own:
        copy.start()
    weight_copy = pltpu.make_async_copy(time_weight, weight, local.at[0])
    weight_copy.start()

    @pl.when(core == zh)
    def _():
        pltpu.make_async_copy(cache_keys, kv.at[1, 0, 0], recv_k.at[1]).start()
        pltpu.make_async_copy(cache_values, kv.at[1, 1, 0], recv_v.at[1]).start()

    barrier = pltpu.get_barrier_semaphore()
    partners = [sibling, across, device(y, z, right, core), device(y, z, left, core)]
    partners += [device(up, z, x, core), device(down, z, x, core)]
    for hop in HOPS[1:]:
        partners += [device(row, (z + hop) % 8, x, core) for row in (y, up, down)]
    for partner in partners:
        pl.semaphore_signal(barrier, inc=1, device_id=partner, device_id_type=MESH)
    pl.semaphore_wait(barrier, len(partners))

    for n in range(3):
        pltpu.make_async_copy(staged.at[n], staged.at[n], local.at[n + 1]).wait()

    def cache_across(which, source, recv):
        return remote(source, kv.at[1, which, 0], send_z.at[0, which], recv.at[1], across)

    def query_over_z(j):
        to = (z + HOPS[j]) % 8
        return remote(
            staged.at[0, group_of(to)], query.at[j], send_z.at[j, 2], recv_q.at[j], device(y, to, x, core)
        )

    def kv_over_z(j, which, source, recv):
        to = (z + HOPS[j]) % 8
        return remote(
            staged.at[1 + which, group_of(to)],
            kv.at[j + 1, which, 0],
            send_z.at[j, which],
            recv.at[j + 1],
            device(y, to, x, core),
        )

    def over_x(i):
        own_kv = kv.at[i, :, 0]
        return (
            remote(own_kv, kv.at[i, :, 1], send_x.at[i, 0], recv_x.at[i, 0], device(y, z, right, core)),
            remote(own_kv, kv.at[i, :, 3], send_x.at[i, 1], recv_x.at[i, 1], device(y, z, left, core)),
            remote(kv.at[i, 0, 1], kv.at[i, 0, 2], send_x.at[i, 2], recv_x.at[i, 2], device(y, z, right, core)),
            remote(kv.at[i, 1, 3], kv.at[i, 1, 2], send_x.at[i, 3], recv_x.at[i, 3], device(y, z, left, core)),
        )

    def to_sibling(i, send, recv):
        return remote(kv.at[i, :, 0:4], kv.at[i, :, 4:8], send, recv, sibling)

    def sibling_x(i):
        return to_sibling(i, send_x.at[i, 4], recv_x.at[i, 4])

    half = slice(0, 4)
    to_up, to_down = device(up, z, x, core), device(down, z, x, core)
    y_up = remote(kv.at[1, :, half], kv.at[9, :, half], send_y.at[0], recv_y.at[0], to_up)
    y_down = remote(kv.at[1, :, half], kv.at[10, :, half], send_y.at[1], recv_y.at[1], to_down)
    y_on_up = remote(kv.at[9, 0, half], kv.at[11, 0, half], send_y.at[2], recv_y.at[2], to_up)
    y_on_down = remote(kv.at[10, 1, half], kv.at[11, 1, half], send_y.at[3], recv_y.at[3], to_down)
    latent_down = remote(latent, shifted, send_y.at[7], recv_y.at[7], to_down)

    def sibling_y(i):
        return to_sibling(i, send_y.at[i - 5], recv_y.at[i - 5])

    def back(j):
        to = (z - HOPS[j] + 8) % 8
        return remote(attended.at[j], returned.at[j], send_o.at[j], recv_o.at[j], device(down, to, x, core))

    @pl.when(core != zh)
    def _():
        cache_across(0, cache_keys, recv_k).start()
        cache_across(1, cache_values, recv_v).start()

    def start_kv(j):
        kv_over_z(j, 0, key_in, recv_k).start()
        kv_over_z(j, 1, value_in, recv_v).start()

    for j in range(1, 8):
        query_over_z(j).start()
    for j in range(1, 5):
        start_kv(j)
    latent_down.start()

    def prepare():
        for i in range(CHUNKS):
            for slot in range(8):
                if i == 1 or i >= 9:
                    plane = {1: y, 9: down, 10: up, 11: (y + 2) % 4}[i]
                    side = core if slot < 4 else 1 - core
                    block = plane * 8 + side * 4 + (x + (0, 3, 2, 1)[slot % 4]) % 4
                    bias[i * 8 + slot] = jnp.where(cache_mask[y, block] == 1, 0.0, HIDDEN).astype(jnp.float32)
                else:
                    bias[i * 8 + slot] = jnp.float32(0.0)

        stamp = timesteps[levels[up]].astype(jnp.float32)
        count = 128
        index = lax.broadcasted_iota(jnp.int32, (8, count), 1).astype(jnp.float32)
        phase = stamp * jnp.exp(-math.log(10000.0) * index / count)
        embed = jnp.concatenate([jnp.cos(phase), jnp.sin(phase)], axis=1).astype(jnp.bfloat16)
        weight_copy.wait()

        def gate_columns(c, carry):
            columns = pl.ds(pl.multiple_of(c * WIDTH, 128), WIDTH)
            gate[:, columns] = jnp.dot(embed, weight[:, columns], preferred_element_type=jnp.float32)
            return carry

        lax.fori_loop(0, 8, gate_columns, 0)

        peak[...] = jnp.full_like(peak, HIDDEN)
        total[...] = jnp.zeros_like(total)
        summed[...] = jnp.zeros_like(summed)

    def attend(i, cached):
        def of_head(which, h):
            return kv[i, which, :, :, h * HEAD_DIM : (h + 1) * HEAD_DIM].reshape(KEYS, HEAD_DIM)

        scale = 1.0 / math.sqrt(HEAD_DIM)
        for h in range(GROUP):
            scored[h] = jnp.dot(of_head(0, h), turned[h], preferred_element_type=jnp.float32)
        for h in range(GROUP):
            for side in (slice(0, 128), slice(128, 256)):
                scores = scored[h, :, side]
                if cached:
                    scores = jnp.concatenate(
                        [scores[slot * ROWS : (slot + 1) * ROWS] + bias[i * 8 + slot] for slot in range(8)], axis=0
                    )
                old = peak[h, :, side]
                new = jnp.maximum(old, jnp.max(scores, axis=0, keepdims=True) * scale)
                weights = jnp.exp(scores * scale - new)
                shrink = jnp.exp(old - new)
                peak[h, :, side] = new
                factor[h, :, side] = shrink
                total[h, :, side] = shrink * total[h, :, side] + jnp.sum(weights, axis=0, keepdims=True)
                weighed[h, :, side] = weights.astype(jnp.bfloat16)
        for h in range(GROUP):
            added = lax.dot_general(
                of_head(1, h), weighed[h], (((0,), (0,)), ((), ())), preferred_element_type=jnp.float32
            )
            summed[h] = factor[h] * summed[h] + added

    def turn(t, carry):
        @pl.when((t >= 2) & (t < X_CHUNKS + 2))
        def _():
            copies = over_x(t - 2)
            copies[0].wait_recv()
            copies[2].start()
            copies[1].wait_recv()
            copies[3].start()

        @pl.when((t >= 3) & (t < X_CHUNKS + 3))
        def _():
            copies = over_x(t - 3)
            copies[2].wait_recv()
            copies[3].wait_recv()
            sibling_x(t - 3).start()

        @pl.when(t == 4)
        def _():
            y_up.start()
            y_down.start()
            own[2].wait()
            for j in range(1, 8):
                query_over_z(j).wait_recv()
            for h in range(GROUP):
                columns = slice(h * HEAD_DIM, (h + 1) * HEAD_DIM)
                turned[h] = query[:, :, columns].reshape(KEYS, HEAD_DIM).astype(jnp.float32).T.astype(jnp.bfloat16)

        @pl.when(t == 7)
        def _():
            y_up.wait_recv()
            y_on_up.start()
            y_down.wait_recv()
            y_on_down.start()
            sibling_y(9).start()
            sibling_y(10).start()

        @pl.when(t == 9)
        def _():
            y_on_up.wait_recv()
            y_on_down.wait_recv()
            sibling_y(11).start()

        @pl.when(t >= 4)
        def _():
            sibling_x(t - 4).wait_recv()

        @pl.when((t >= 4) & (t != 5))
        def _():
            attend(t - 4, False)

        for i in (9, 10, 11):

            @pl.when(t == i)
            def _(i=i):
                sibling_y(i).wait_recv()

        @pl.when((t == 5) | ((t >= 9) & (t <= 11)))
        def _():
            attend(jnp.where(t == 5, 1, t), True)

        @pl.when(t < X_CHUNKS)
        def _():
            pltpu.make_async_copy(kv.at[t, 0, 0], kv.at[t, 0, 0], recv_k.at[t]).wait()
            pltpu.make_async_copy(kv.at[t, 1, 0], kv.at[t, 1, 0], recv_v.at[t]).wait()
            over_x(t)[0].start()
            over_x(t)[1].start()

        for turn_of, hops in ((1, (5, 6)), (3, (7,))):

            @pl.when(t == turn_of)
            def _(hops=hops):
                for j in hops:
                    start_kv(j)

        pl.when(t == 1)(prepare)
        return carry

    lax.fori_loop(0, X_CHUNKS + 4, turn, 0)

    for h in range(GROUP):
        result = summed[h] * (1.0 / total[h])
        attended[:, :, h * HEAD_DIM : (h + 1) * HEAD_DIM] = result.T.astype(jnp.bfloat16).reshape(8, ROWS, HEAD_DIM)
    for j in range(8):
        back(j).start()

    @pl.when(core != zh)
    def _():
        cache_across(0, cache_keys, recv_k).wait_send()
        cache_across(1, cache_values, recv_v).wait_send()

    for j in range(1, 8):
        query_over_z(j).wait_send()
        kv_over_z(j, 0, key_in, recv_k).wait_send()
        kv_over_z(j, 1, value_in, recv_v).wait_send()

    def sent(i, carry):
        for copy in over_x(i):
            copy.wait_send()
        sibling_x(i).wait_send()
        return carry

    lax.fori_loop(0, X_CHUNKS, sent, 0)
    for copy in (y_up, y_down, y_on_up, y_on_down, sibling_y(9), sibling_y(10), sibling_y(11), latent_down):
        copy.wait_send()

    latent_down.wait_recv()
    for j in range(8):
        back(j).wait_recv()
        columns = group_columns((z + HOPS[j]) % 8)
        out[:, columns] = (
            shifted[:, columns].astype(jnp.float32) + gate[0:1, columns] * returned[j].astype(jnp.float32)
        ).astype(jnp.bfloat16)
    for j in range(8):
        back(j).wait_send()


def shards(
    latent, query_in, key_in, value_in, cache_keys, cache_values, levels, timesteps, cache_mask, time_weight
):
    anywhere = pl.BlockSpec(memory_space=pl.ANY)
    scalars = pl.BlockSpec(memory_space=pltpu.SMEM)
    bf16, f32 = jnp.bfloat16, jnp.float32
    dma = pltpu.SemaphoreType.DMA
    return pl.pallas_call(
        kernel,
        out_shape=jax.ShapeDtypeStruct(latent.shape, latent.dtype),
        in_specs=[scalars] * 3 + [anywhere] * 7,
        out_specs=pl.BlockSpec(memory_space=pltpu.VMEM),
        scratch_shapes=[
            pltpu.VMEM((3, 8, ROWS, WIDTH), bf16),
            pltpu.VMEM((8, ROWS, WIDTH), bf16),
            pltpu.VMEM((GROUP, HEAD_DIM, KEYS), bf16),
            pltpu.VMEM((CHUNKS, 2, 8, ROWS, WIDTH), bf16),
            pltpu.VMEM((8, ROWS, WIDTH), bf16),
            pltpu.VMEM((8, ROWS, WIDTH), bf16),
            pltpu.VMEM(latent.shape, bf16),
            pltpu.VMEM(time_weight.shape, bf16),
            pltpu.VMEM((8, latent.shape[1]), f32),
            pltpu.VMEM((GROUP, KEYS, KEYS), f32),
            pltpu.VMEM((GROUP, KEYS, KEYS), bf16),
            pltpu.VMEM((GROUP, 1, KEYS), f32),
            pltpu.VMEM((GROUP, 1, KEYS), f32),
            pltpu.VMEM((GROUP, 1, KEYS), f32),
            pltpu.VMEM((GROUP, HEAD_DIM, KEYS), f32),
            pltpu.SMEM((CHUNKS * 8,), f32),
            dma((8, 3)),
            dma((X_CHUNKS, 5)),
            dma((8,)),
            dma((8,)),
            dma((8,)),
            dma((X_CHUNKS,)),
            dma((X_CHUNKS,)),
            dma((X_CHUNKS, 5)),
            dma((8,)),
            dma((8,)),
            dma((4,)),
        ],
        compiler_params=pltpu.CompilerParams(
            collective_id=0, has_side_effects=True, vmem_limit_bytes=64 * 1024 * 1024
        ),
        cost_estimate=pl.CostEstimate(flops=2 * 10**9, bytes_accessed=5 * 10**6, transcendentals=4 * 10**6),
    )(
        levels, timesteps, cache_mask, latent, query_in, key_in, value_in, cache_keys, cache_values, time_weight
    )


def solution(mesh):
    return jax.shard_map(
        shards,
        mesh=mesh,
        in_specs=(
            P(("chain", "head"), None),
            P(("chain", "head"), None),
            P(("chain", "head"), None),
            P(("chain", "head"), None),
            P("chain", "head"),
            P("chain", "head"),
            P(),
            P(),
            P(),
            P(),
        ),
        out_specs=P(("chain", "head"), None),
        check_vma=False,
    )
```

```python
import functools
import math

import jax
import jax.numpy as jnp
from jax import lax
from jax.experimental import pallas as pl
from jax.experimental.pallas import tpu as pltpu
from jax.sharding import PartitionSpec as P

MESH = pl.DeviceIdType.MESH
HEAD_DIM = 128
SPANS = 4
NY, NX, NZ = 4, 4, 8
GROUP = 5
WIDTH = GROUP * HEAD_DIM
ROWS = 32
HOPS = (0, 1, 7, 2, 6, 3, 5, 4)
CHUNKS = 12
FIRST_Z = 2
X_CHUNKS = 9
KEYS = 8 * ROWS
HIDDEN = -1e30


def device(y, z, x, core):
    return {"chain": (y * 2 + z // 4) * NX + x, "head": (z % 4) * 2 + core}


def group_of(z):
    return (z % 4) * 2 + z // 4


def group_columns(z):
    return pl.ds(pl.multiple_of(group_of(z) * WIDTH, 128), WIDTH)


def kernel(
    levels, timesteps, cache_mask, latent, query_in, key_in, value_in, cache_keys, cache_values, time_weight,
    out,
    query, row_query, turned, landed, kv, attended, returned, shifted, weight, gate,
    scored, weighed, factor, peak, total, summed, bias,
    send_z, send_x, send_y, send_q, send_o, recv_q, recv_kv, recv_x, recv_y, recv_rq, recv_o, local, own_x,
):
    chain, head = lax.axis_index("chain"), lax.axis_index("head")
    y, x = chain // 8, chain % 4
    zh, zl, core = (chain // 4) % 2, head // 2, head % 2
    z = zh * 4 + zl
    up, down = (y + 1) % 4, (y + 3) % 4
    x_right, x_left, x_far = (x + 1) % 4, (x + 3) % 4, (x + 2) % 4
    right, left, far = (device(y, z, to, core) for to in (x_right, x_left, x_far))
    sibling = device(y, z, x, 1 - core)
    across = device(y, (z + 4) % 8, x, 1 - core)
    to_up, to_down = device(up, z, x, core), device(down, z, x, core)
    mine = group_columns(z)

    def remote(src, dst, send, recv, to):
        return pltpu.make_async_remote_copy(
            src_ref=src, dst_ref=dst, send_sem=send, recv_sem=recv, device_id=to, device_id_type=MESH
        )

    def of_head(h):
        return pl.ds(pl.multiple_of(h * HEAD_DIM, 128), HEAD_DIM)

    own_query = pltpu.make_async_copy(query_in.at[:, mine], query.at[0], recv_q.at[0])
    own_query.start()
    pltpu.make_async_copy(key_in.at[:, mine], landed.at[0, 0], recv_kv.at[0, 0]).start()
    pltpu.make_async_copy(value_in.at[:, mine], landed.at[0, 1], recv_kv.at[0, 1]).start()
    weight_copy = pltpu.make_async_copy(time_weight, weight, local.at[0])
    weight_copy.start()

    @pl.when(core == zh)
    def _():
        pltpu.make_async_copy(cache_keys, landed.at[1, 0], recv_kv.at[1, 0]).start()
        pltpu.make_async_copy(cache_values, landed.at[1, 1], recv_kv.at[1, 1]).start()

    barrier = pltpu.get_barrier_semaphore()
    partners = [sibling, across, right, left, far, to_up, to_down]
    partners += [device(y, (z + hop) % 8, x, core) for hop in HOPS[1:]]
    for partner in partners:
        pl.semaphore_signal(barrier, inc=1, device_id=partner, device_id_type=MESH)
    pl.semaphore_wait(barrier, len(partners))

    def cache_across(which):
        source = (cache_keys, cache_values)[which]
        return remote(source, landed.at[1, which], send_z.at[0, which], recv_kv.at[1, which], across)

    def query_over_z(j):
        to = (z + HOPS[j]) % 8
        return remote(
            query_in.at[:, group_columns(to)], query.at[j], send_z.at[j, 2], recv_q.at[j], device(y, to, x, core)
        )

    def kv_over_z(j, which):
        to = (z + HOPS[j]) % 8
        source = (key_in, value_in)[which].at[:, group_columns(to)]
        return remote(
            source, landed.at[j + 1, which], send_z.at[j, which], recv_kv.at[j + 1, which], device(y, to, x, core)
        )

    shared = slice((GROUP - 1) * HEAD_DIM, GROUP * HEAD_DIM)

    def own_copies(i):
        return (
            pltpu.make_async_copy(landed.at[i, :, :, of_head(x)], kv.at[i, :, 0, 0], own_x.at[i, 0]),
            pltpu.make_async_copy(landed.at[i, :, :, shared], kv.at[i, :, 1, 0], own_x.at[i, 1]),
        )

    def x_copy(i, n):
        src, dst, to = (
            lambda: (landed.at[i, :, :, of_head(x_right)], kv.at[i, :, 0, 1], right),
            lambda: (landed.at[i, :, :, shared], kv.at[i, :, 1, 1], right),
            lambda: (landed.at[i, :, :, of_head(x_left)], kv.at[i, :, 0, 3], left),
            lambda: (landed.at[i, :, :, shared], kv.at[i, :, 1, 3], left),
            lambda: (landed.at[i, :, :, of_head(x_far)], kv.at[i, :, 0, 2], far),
            lambda: (kv.at[i, 0, 1, 1], kv.at[i, 0, 1, 2], right),
            lambda: (kv.at[i, 1, 1, 3], kv.at[i, 1, 1, 2], left),
            lambda: (kv.at[i, :, :, 0:4], kv.at[i, :, :, 4:8], sibling),
        )[n]()
        return remote(src, dst, send_x.at[i, n], recv_x.at[i, n], to)

    def y_copy(n):
        src, dst, to = (
            lambda: (kv.at[1, :, :, 0:4], kv.at[9, :, :, 0:4], to_up),
            lambda: (kv.at[1, :, :, 0:4], kv.at[10, :, :, 0:4], to_down),
            lambda: (kv.at[9, 0, :, 0:4], kv.at[11, 0, :, 0:4], to_up),
            lambda: (kv.at[10, 1, :, 0:4], kv.at[11, 1, :, 0:4], to_down),
            lambda: (kv.at[9, :, :, 0:4], kv.at[9, :, :, 4:8], sibling),
            lambda: (kv.at[10, :, :, 0:4], kv.at[10, :, :, 4:8], sibling),
            lambda: (kv.at[11, :, :, 0:4], kv.at[11, :, :, 4:8], sibling),
            lambda: (latent, shifted, to_down),
        )[n]()
        return remote(src, dst, send_y.at[n], recv_y.at[n], to)

    def query_over_x(n):
        to, slot = ((x_right, 0), (x_far, 1), (x_left, 2))[n]
        return remote(
            query.at[:, :, of_head(to)], row_query.at[slot], send_q.at[n], recv_rq.at[n], device(y, z, to, core)
        )

    def back(tile, j):
        to_x = x if tile == GROUP - 1 else (x + (0, 3, 2, 1)[tile]) % 4
        to = device(down, (z - HOPS[j] + 8) % 8, to_x, core)
        return remote(attended.at[tile, j], returned.at[tile, j], send_o.at[tile, j], recv_o.at[tile, j], to)

    def start_kv(j):
        kv_over_z(j, 0).start()
        kv_over_z(j, 1).start()

    @pl.when(core != zh)
    def _():
        cache_across(0).start()
        cache_across(1).start()

    for j in range(1, 8):
        query_over_z(j).start()
    for j in range(1, 5):
        start_kv(j)
    y_copy(7).start()

    def prepare():
        for i in range(CHUNKS):
            for slot in range(8):
                if i == 1 or i >= 9:
                    plane = {1: y, 9: down, 10: up, 11: (y + 2) % 4}[i]
                    side = core if slot < 4 else 1 - core
                    block = plane * 8 + side * 4 + (x + (0, 3, 2, 1)[slot % 4]) % 4
                    bias[i * 8 + slot] = jnp.where(cache_mask[y, block] == 1, 0.0, HIDDEN).astype(jnp.float32)
                else:
                    bias[i * 8 + slot] = jnp.float32(0.0)

        stamp = timesteps[levels[up]].astype(jnp.float32)
        count = 128
        index = lax.broadcasted_iota(jnp.int32, (8, count), 1).astype(jnp.float32)
        phase = stamp * jnp.exp(-math.log(10000.0) * index / count)
        embed = jnp.concatenate([jnp.cos(phase), jnp.sin(phase)], axis=1).astype(jnp.bfloat16)
        weight_copy.wait()

        def gate_columns(c, carry):
            columns = pl.ds(pl.multiple_of(c * WIDTH, 128), WIDTH)
            gate[:, columns] = jnp.dot(embed, weight[:, columns], preferred_element_type=jnp.float32)
            return carry

        lax.fori_loop(0, 8, gate_columns, 0)

        peak[...] = jnp.full_like(peak, HIDDEN)
        total[...] = jnp.zeros_like(total)
        summed[...] = jnp.zeros_like(summed)

    def attend(i, cached, finish=None):
        def rows(which, tile):
            return kv[i, which, tile // (GROUP - 1)].reshape(KEYS, HEAD_DIM)

        scale = 1.0 / math.sqrt(HEAD_DIM)
        for h in range(GROUP):
            scored[h] = jnp.dot(rows(0, h), turned[h], preferred_element_type=jnp.float32)
        for h in range(GROUP):
            for side in (slice(0, 128), slice(128, 256)):
                scores = scored[h, :, side]
                if cached:
                    scores = jnp.concatenate(
                        [scores[slot * ROWS : (slot + 1) * ROWS] + bias[i * 8 + slot] for slot in range(8)], axis=0
                    )
                old = peak[h, :, side]
                new = jnp.maximum(old, jnp.max(scores, axis=0, keepdims=True) * scale)
                weights = jnp.exp(scores * scale - new)
                shrink = jnp.exp(old - new)
                peak[h, :, side] = new
                factor[h, :, side] = shrink
                total[h, :, side] = shrink * total[h, :, side] + jnp.sum(weights, axis=0, keepdims=True)
                weighed[h, :, side] = weights.astype(jnp.bfloat16)
        for h in range(GROUP):
            added = lax.dot_general(
                rows(1, h), weighed[h], (((0,), (0,)), ((), ())), preferred_element_type=jnp.float32
            )
            value_sum = factor[h] * summed[h] + added
            if finish is None:
                summed[h] = value_sum
            else:
                finish(h, value_sum)

    def finish(h, value_sum):
        result = value_sum * (1.0 / total[h])
        attended[h] = result.T.astype(jnp.bfloat16).reshape(8, ROWS, HEAD_DIM)
        for j in range(8):
            back(h, j).start()

    def turn_query(h, rows):
        turned[h] = rows.reshape(KEYS, HEAD_DIM).astype(jnp.float32).T.astype(jnp.bfloat16)

    def turn(t, carry):
        @pl.when((t >= 2) & (t < X_CHUNKS + 2))
        def _():
            i = t - 2
            x_copy(i, 0).wait_recv()
            x_copy(i, 1).wait_recv()
            x_copy(i, 5).start()
            x_copy(i, 2).wait_recv()
            x_copy(i, 3).wait_recv()
            x_copy(i, 6).start()

        @pl.when(t >= 3)
        def _():
            i = t - 3
            for copy in own_copies(i):
                copy.wait()
            for n in (4, 5, 6):
                x_copy(i, n).wait_recv()
            x_copy(i, 7).start()

        @pl.when(t == 3)
        def _():
            own_query.wait()
            for j in range(1, 8):
                query_over_z(j).wait_recv()
            for n in range(3):
                query_over_x(n).start()

        @pl.when(t == 4)
        def _():
            y_copy(0).start()
            y_copy(1).start()
            turn_query(0, query[:, :, of_head(x)])
            turn_query(4, query[:, :, shared])
            for n in range(3):
                query_over_x(n).wait_recv()
            turn_query(1, row_query[0])
            turn_query(2, row_query[1])
            turn_query(3, row_query[2])

        @pl.when(t == 7)
        def _():
            for n in (0, 1):
                y_copy(n).wait_recv()
                y_copy(n + 2).start()
                y_copy(n + 4).start()

        @pl.when(t == 9)
        def _():
            y_copy(2).wait_recv()
            y_copy(3).wait_recv()
            y_copy(6).start()

        @pl.when(t >= 4)
        def _():
            x_copy(t - 4, 7).wait_recv()

        @pl.when((t >= 4) & (t != 5))
        def _():
            attend(t - 4, False)

        for i in (9, 10, 11):

            @pl.when(t == i)
            def _(i=i):
                y_copy(i - 5).wait_recv()

        @pl.when((t == 5) | (t >= 9))
        def _():
            attend(jnp.where(t == 5, 1, t), True)

        @pl.when(t < X_CHUNKS)
        def _():
            for which in (0, 1):
                place = landed.at[t, which]
                pltpu.make_async_copy(place, place, recv_kv.at[t, which]).wait()
            for n in range(5):
                x_copy(t, n).start()
            for copy in own_copies(t):
                copy.start()

        for turn_of, hops in ((1, (5, 6)), (3, (7,))):

            @pl.when(t == turn_of)
            def _(hops=hops):
                for j in hops:
                    start_kv(j)

        pl.when(t == 1)(prepare)
        return carry

    lax.fori_loop(0, X_CHUNKS + 3, turn, 0)
    x_copy(X_CHUNKS - 1, 7).wait_recv()
    attend(X_CHUNKS - 1, False, finish)

    @pl.when(core != zh)
    def _():
        cache_across(0).wait_send()
        cache_across(1).wait_send()

    for j in range(1, 8):
        query_over_z(j).wait_send()
        kv_over_z(j, 0).wait_send()
        kv_over_z(j, 1).wait_send()

    def sent(i, carry):
        for n in range(8):
            x_copy(i, n).wait_send()
        return carry

    lax.fori_loop(0, X_CHUNKS, sent, 0)
    for n in range(8):
        y_copy(n).wait_send()
    for n in range(3):
        query_over_x(n).wait_send()

    y_copy(7).wait_recv()
    for tile in range(GROUP):
        for j in range(8):
            back(tile, j).wait_recv()
            of = GROUP - 1 if tile == GROUP - 1 else (x + tile) % 4
            first = group_of((z + HOPS[j]) % 8) * WIDTH + of * HEAD_DIM
            columns = pl.ds(pl.multiple_of(first, 128), HEAD_DIM)
            out[:, columns] = (
                shifted[:, columns].astype(jnp.float32)
                + gate[0:1, columns] * returned[tile, j].astype(jnp.float32)
            ).astype(jnp.bfloat16)
    for tile in range(GROUP):
        for j in range(8):
            back(tile, j).wait_send()


def shards(
    latent, query_in, key_in, value_in, cache_keys, cache_values, levels, timesteps, cache_mask, time_weight
):
    anywhere = pl.BlockSpec(memory_space=pl.ANY)
    scalars = pl.BlockSpec(memory_space=pltpu.SMEM)
    bf16, f32 = jnp.bfloat16, jnp.float32
    dma = pltpu.SemaphoreType.DMA
    return pl.pallas_call(
        kernel,
        out_shape=jax.ShapeDtypeStruct(latent.shape, latent.dtype),
        in_specs=[scalars] * 3 + [anywhere] * 7,
        out_specs=pl.BlockSpec(memory_space=pltpu.VMEM),
        scratch_shapes=[
            pltpu.VMEM((8, ROWS, WIDTH), bf16),
            pltpu.VMEM((3, 8, ROWS, HEAD_DIM), bf16),
            pltpu.VMEM((GROUP, HEAD_DIM, KEYS), bf16),
            pltpu.VMEM((X_CHUNKS, 2, ROWS, WIDTH), bf16),
            pltpu.VMEM((CHUNKS, 2, 2, 8, ROWS, HEAD_DIM), bf16),
            pltpu.VMEM((GROUP, 8, ROWS, HEAD_DIM), bf16),
            pltpu.VMEM((GROUP, 8, ROWS, HEAD_DIM), bf16),
            pltpu.VMEM(latent.shape, bf16),
            pltpu.VMEM(time_weight.shape, bf16),
            pltpu.VMEM((8, latent.shape[1]), f32),
            pltpu.VMEM((GROUP, KEYS, KEYS), f32),
            pltpu.VMEM((GROUP, KEYS, KEYS), bf16),
            pltpu.VMEM((GROUP, 1, KEYS), f32),
            pltpu.VMEM((GROUP, 1, KEYS), f32),
            pltpu.VMEM((GROUP, 1, KEYS), f32),
            pltpu.VMEM((GROUP, HEAD_DIM, KEYS), f32),
            pltpu.SMEM((CHUNKS * 8,), f32),
            dma((8, 3)),
            dma((X_CHUNKS, 8)),
            dma((8,)),
            dma((3,)),
            dma((GROUP, 8)),
            dma((8,)),
            dma((X_CHUNKS, 2)),
            dma((X_CHUNKS, 8)),
            dma((8,)),
            dma((3,)),
            dma((GROUP, 8)),
            dma((1,)),
            dma((X_CHUNKS, 2)),
        ],
        compiler_params=pltpu.CompilerParams(
            collective_id=0, has_side_effects=True, vmem_limit_bytes=64 * 1024 * 1024
        ),
        cost_estimate=pl.CostEstimate(flops=2 * 10**9, bytes_accessed=5 * 10**6, transcendentals=4 * 10**6),
    )(
        levels, timesteps, cache_mask, latent, query_in, key_in, value_in, cache_keys, cache_values, time_weight
    )


def solution(mesh):
    return jax.shard_map(
        shards,
        mesh=mesh,
        in_specs=(
            P(("chain", "head"), None),
            P(("chain", "head"), None),
            P(("chain", "head"), None),
            P(("chain", "head"), None),
            P("chain", "head"),
            P("chain", "head"),
            P(),
            P(),
            P(),
            P(),
        ),
        out_specs=P(("chain", "head"), None),
        check_vma=False,
    )
```

```python
import functools
import math

import jax
import jax.numpy as jnp
from jax import lax
from jax.experimental import pallas as pl
from jax.experimental.pallas import tpu as pltpu
from jax.sharding import PartitionSpec as P

MESH = pl.DeviceIdType.MESH
HEAD_DIM = 128
SPANS = 4
NY, NX, NZ = 4, 4, 8
GROUP = 5
WIDTH = GROUP * HEAD_DIM
ROWS = 32
HOPS = (0, 1, 7, 2, 6, 3, 5, 4)
CHUNKS = 12
FIRST_Z = 2
X_CHUNKS = 9
KEYS = 8 * ROWS
HIDDEN = -1e30


def device(y, z, x, core):
    return {"chain": (y * 2 + z // 4) * NX + x, "head": (z % 4) * 2 + core}


def group_of(z):
    return (z % 4) * 2 + z // 4


def group_columns(z):
    return pl.ds(pl.multiple_of(group_of(z) * WIDTH, 128), WIDTH)


def kernel(
    levels, timesteps, cache_mask, latent, query_in, key_in, value_in, cache_keys, cache_values, time_weight,
    out,
    query, row_query, turned, landed, kv, attended, returned, shifted, weight, gate,
    scored, weighed, factor, peak, total, summed, bias,
    send_z, send_x, send_y, send_q, send_o, recv_q, recv_kv, recv_x, recv_y, recv_rq, recv_o, local, own_x,
):
    chain, head = lax.axis_index("chain"), lax.axis_index("head")
    y, x = chain // 8, chain % 4
    zh, zl, core = (chain // 4) % 2, head // 2, head % 2
    z = zh * 4 + zl
    up, down = (y + 1) % 4, (y + 3) % 4
    x_right, x_left, x_far = (x + 1) % 4, (x + 3) % 4, (x + 2) % 4
    right, left, far = (device(y, z, to, core) for to in (x_right, x_left, x_far))
    sibling = device(y, z, x, 1 - core)
    across = device(y, (z + 4) % 8, x, 1 - core)
    to_up, to_down = device(up, z, x, core), device(down, z, x, core)
    mine = group_columns(z)

    def remote(src, dst, send, recv, to):
        return pltpu.make_async_remote_copy(
            src_ref=src, dst_ref=dst, send_sem=send, recv_sem=recv, device_id=to, device_id_type=MESH
        )

    def of_head(h):
        return pl.ds(pl.multiple_of(h * HEAD_DIM, 128), HEAD_DIM)

    own_query = pltpu.make_async_copy(query_in.at[:, mine], query.at[0], recv_q.at[0])
    own_query.start()
    pltpu.make_async_copy(key_in.at[:, mine], landed.at[0, 0], recv_kv.at[0, 0]).start()
    pltpu.make_async_copy(value_in.at[:, mine], landed.at[0, 1], recv_kv.at[0, 1]).start()
    weight_copy = pltpu.make_async_copy(time_weight, weight, local.at[0])
    weight_copy.start()

    @pl.when(core == zh)
    def _():
        pltpu.make_async_copy(cache_keys, landed.at[1, 0], recv_kv.at[1, 0]).start()
        pltpu.make_async_copy(cache_values, landed.at[1, 1], recv_kv.at[1, 1]).start()

    barrier = pltpu.get_barrier_semaphore()
    partners = [sibling, across, right, left, far, to_up, to_down]
    partners += [device(y, (z + hop) % 8, x, core) for hop in HOPS[1:]]
    for partner in partners:
        pl.semaphore_signal(barrier, inc=1, device_id=partner, device_id_type=MESH)
    pl.semaphore_wait(barrier, len(partners))

    def cache_across(which):
        source = (cache_keys, cache_values)[which]
        return remote(source, landed.at[1, which], send_z.at[0, which], recv_kv.at[1, which], across)

    def query_over_z(j):
        to = (z + HOPS[j]) % 8
        return remote(
            query_in.at[:, group_columns(to)], query.at[j], send_z.at[j, 2], recv_q.at[j], device(y, to, x, core)
        )

    def kv_over_z(j, which):
        to = (z + HOPS[j]) % 8
        source = (key_in, value_in)[which].at[:, group_columns(to)]
        return remote(
            source, landed.at[j + 1, which], send_z.at[j, which], recv_kv.at[j + 1, which], device(y, to, x, core)
        )

    shared = slice((GROUP - 1) * HEAD_DIM, GROUP * HEAD_DIM)

    def own_copies(i):
        return (
            pltpu.make_async_copy(landed.at[i, :, :, of_head(x)], kv.at[i, :, 0, 0], own_x.at[i, 0]),
            pltpu.make_async_copy(landed.at[i, :, :, shared], kv.at[i, :, 1, 0], own_x.at[i, 1]),
        )

    def x_copy(i, n):
        src, dst, to = (
            lambda: (landed.at[i, :, :, of_head(x_right)], kv.at[i, :, 0, 1], right),
            lambda: (landed.at[i, :, :, shared], kv.at[i, :, 1, 1], right),
            lambda: (landed.at[i, :, :, of_head(x_left)], kv.at[i, :, 0, 3], left),
            lambda: (landed.at[i, :, :, shared], kv.at[i, :, 1, 3], left),
            lambda: (landed.at[i, :, :, of_head(x_far)], kv.at[i, :, 0, 2], far),
            lambda: (kv.at[i, 0, 1, 1], kv.at[i, 0, 1, 2], right),
            lambda: (kv.at[i, 1, 1, 3], kv.at[i, 1, 1, 2], left),
            lambda: (kv.at[i, :, :, 0:4], kv.at[i, :, :, 4:8], sibling),
        )[n]()
        return remote(src, dst, send_x.at[i, n], recv_x.at[i, n], to)

    def y_copy(n):
        src, dst, to = (
            lambda: (kv.at[1, :, :, 0:4], kv.at[9, :, :, 0:4], to_up),
            lambda: (kv.at[1, :, :, 0:4], kv.at[10, :, :, 0:4], to_down),
            lambda: (kv.at[9, 0, :, 0:4], kv.at[11, 0, :, 0:4], to_up),
            lambda: (kv.at[10, 1, :, 0:4], kv.at[11, 1, :, 0:4], to_down),
            lambda: (kv.at[9, :, :, 0:4], kv.at[9, :, :, 4:8], sibling),
            lambda: (kv.at[10, :, :, 0:4], kv.at[10, :, :, 4:8], sibling),
            lambda: (kv.at[11, :, :, 0:4], kv.at[11, :, :, 4:8], sibling),
            lambda: (latent, shifted, to_down),
        )[n]()
        return remote(src, dst, send_y.at[n], recv_y.at[n], to)

    def query_over_x(n):
        to, slot = ((x_right, 0), (x_far, 1), (x_left, 2))[n]
        return remote(
            query.at[:, :, of_head(to)], row_query.at[slot], send_q.at[n], recv_rq.at[n], device(y, z, to, core)
        )

    def back(tile, j):
        to_x = x if tile == GROUP - 1 else (x + (0, 3, 2, 1)[tile]) % 4
        to = device(down, (z - HOPS[j] + 8) % 8, to_x, core)
        return remote(attended.at[tile, j], returned.at[tile, j], send_o.at[tile, j], recv_o.at[tile, j], to)

    def start_kv(j):
        kv_over_z(j, 0).start()
        kv_over_z(j, 1).start()

    @pl.when(core != zh)
    def _():
        cache_across(0).start()
        cache_across(1).start()

    for j in range(1, 8):
        query_over_z(j).start()
    for j in range(1, 5):
        start_kv(j)
    y_copy(7).start()

    def prepare():
        for i in range(CHUNKS):
            for slot in range(8):
                if i == 1 or i >= 9:
                    plane = {1: y, 9: down, 10: up, 11: (y + 2) % 4}[i]
                    side = core if slot < 4 else 1 - core
                    block = plane * 8 + side * 4 + (x + (0, 3, 2, 1)[slot % 4]) % 4
                    bias[i * 8 + slot] = jnp.where(cache_mask[y, block] == 1, 0.0, HIDDEN).astype(jnp.float32)
                else:
                    bias[i * 8 + slot] = jnp.float32(0.0)

        stamp = timesteps[levels[up]].astype(jnp.float32)
        count = 128
        index = lax.broadcasted_iota(jnp.int32, (8, count), 1).astype(jnp.float32)
        phase = stamp * jnp.exp(-math.log(10000.0) * index / count)
        embed = jnp.concatenate([jnp.cos(phase), jnp.sin(phase)], axis=1).astype(jnp.bfloat16)
        weight_copy.wait()

        def gate_columns(c, carry):
            columns = pl.ds(pl.multiple_of(c * WIDTH, 128), WIDTH)
            gate[:, columns] = jnp.dot(embed, weight[:, columns], preferred_element_type=jnp.float32)
            return carry

        lax.fori_loop(0, 8, gate_columns, 0)

        peak[...] = jnp.full_like(peak, HIDDEN)
        total[...] = jnp.zeros_like(total)
        summed[...] = jnp.zeros_like(summed)

    def attend(i, cached):
        scale = 1.0 / math.sqrt(HEAD_DIM)
        spans = (slice(0, 4 * KEYS), slice(4 * KEYS, 5 * KEYS))
        keys = [kv[i, 0, n].reshape(KEYS, HEAD_DIM) for n in (0, 1)]
        scores = [jnp.dot(keys[n], turned[:, spans[n]], preferred_element_type=jnp.float32) for n in (0, 1)]
        for n in (0, 1):
            scored[:, spans[n]] = scores[n]
        for first in range(0, GROUP * KEYS, 128):
            side = slice(first, first + 128)
            scores = scored[:, side]
            if cached:
                scores = jnp.concatenate(
                    [scores[slot * ROWS : (slot + 1) * ROWS] + bias[i * 8 + slot] for slot in range(8)], axis=0
                )
            old = peak[:, side]
            new = jnp.maximum(old, jnp.max(scores, axis=0, keepdims=True) * scale)
            weights = jnp.exp(scores * scale - new)
            shrink = jnp.exp(old - new)
            peak[:, side] = new
            factor[:, side] = shrink
            total[:, side] = shrink * total[:, side] + jnp.sum(weights, axis=0, keepdims=True)
            weighed[:, side] = weights.astype(jnp.bfloat16)
        values = [kv[i, 1, n].reshape(KEYS, HEAD_DIM) for n in (0, 1)]
        added = [
            lax.dot_general(
                values[n], weighed[:, spans[n]], (((0,), (0,)), ((), ())), preferred_element_type=jnp.float32
            )
            for n in (0, 1)
        ]
        for n in (0, 1):
            summed[:, spans[n]] = factor[:, spans[n]] * summed[:, spans[n]] + added[n]

    def finish(h):
        tile = slice(h * KEYS, (h + 1) * KEYS)
        result = summed[:, tile] * (1.0 / total[:, tile])
        attended[h] = result.T.astype(jnp.bfloat16).reshape(8, ROWS, HEAD_DIM)
        for j in range(8):
            back(h, j).start()

    def turn_query(h, rows):
        tile = slice(h * KEYS, (h + 1) * KEYS)
        turned[:, tile] = rows.reshape(KEYS, HEAD_DIM).astype(jnp.float32).T.astype(jnp.bfloat16)

    def turn(t, carry):
        @pl.when((t >= 2) & (t < X_CHUNKS + 2))
        def _():
            i = t - 2
            x_copy(i, 0).wait_recv()
            x_copy(i, 1).wait_recv()
            x_copy(i, 5).start()
            x_copy(i, 2).wait_recv()
            x_copy(i, 3).wait_recv()
            x_copy(i, 6).start()

        @pl.when(t >= 3)
        def _():
            i = t - 3
            for copy in own_copies(i):
                copy.wait()
            for n in (4, 5, 6):
                x_copy(i, n).wait_recv()
            x_copy(i, 7).start()

        @pl.when(t == 3)
        def _():
            own_query.wait()
            for j in range(1, 8):
                query_over_z(j).wait_recv()
            for n in range(3):
                query_over_x(n).start()

        @pl.when(t == 4)
        def _():
            y_copy(0).start()
            y_copy(1).start()
            turn_query(0, query[:, :, of_head(x)])
            turn_query(4, query[:, :, shared])
            for n in range(3):
                query_over_x(n).wait_recv()
            turn_query(1, row_query[0])
            turn_query(2, row_query[1])
            turn_query(3, row_query[2])

        @pl.when(t == 7)
        def _():
            for n in (0, 1):
                y_copy(n).wait_recv()
                y_copy(n + 2).start()
                y_copy(n + 4).start()

        @pl.when(t == 9)
        def _():
            y_copy(2).wait_recv()
            y_copy(3).wait_recv()
            y_copy(6).start()

        @pl.when(t >= 4)
        def _():
            x_copy(t - 4, 7).wait_recv()

        @pl.when((t >= 4) & (t != 5))
        def _():
            attend(t - 4, False)

        for i in (9, 10, 11):

            @pl.when(t == i)
            def _(i=i):
                y_copy(i - 5).wait_recv()

        @pl.when((t == 5) | (t >= 9))
        def _():
            attend(jnp.where(t == 5, 1, t), True)

        @pl.when(t < X_CHUNKS)
        def _():
            for which in (0, 1):
                place = landed.at[t, which]
                pltpu.make_async_copy(place, place, recv_kv.at[t, which]).wait()
            for n in range(5):
                x_copy(t, n).start()
            for copy in own_copies(t):
                copy.start()

        for turn_of, hops in ((1, (5, 6)), (3, (7,))):

            @pl.when(t == turn_of)
            def _(hops=hops):
                for j in hops:
                    start_kv(j)

        pl.when(t == 1)(prepare)
        return carry

    lax.fori_loop(0, X_CHUNKS + 3, turn, 0)
    x_copy(X_CHUNKS - 1, 7).wait_recv()
    attend(X_CHUNKS - 1, False)
    for h in range(GROUP):
        finish(h)

    @pl.when(core != zh)
    def _():
        cache_across(0).wait_send()
        cache_across(1).wait_send()

    for j in range(1, 8):
        query_over_z(j).wait_send()
        kv_over_z(j, 0).wait_send()
        kv_over_z(j, 1).wait_send()

    def sent(i, carry):
        for n in range(8):
            x_copy(i, n).wait_send()
        return carry

    lax.fori_loop(0, X_CHUNKS, sent, 0)
    for n in range(8):
        y_copy(n).wait_send()
    for n in range(3):
        query_over_x(n).wait_send()

    y_copy(7).wait_recv()
    for tile in range(GROUP):
        for j in range(8):
            back(tile, j).wait_recv()
            of = GROUP - 1 if tile == GROUP - 1 else (x + tile) % 4
            first = group_of((z + HOPS[j]) % 8) * WIDTH + of * HEAD_DIM
            columns = pl.ds(pl.multiple_of(first, 128), HEAD_DIM)
            out[:, columns] = (
                shifted[:, columns].astype(jnp.float32)
                + gate[0:1, columns] * returned[tile, j].astype(jnp.float32)
            ).astype(jnp.bfloat16)
    for tile in range(GROUP):
        for j in range(8):
            back(tile, j).wait_send()


def shards(
    latent, query_in, key_in, value_in, cache_keys, cache_values, levels, timesteps, cache_mask, time_weight
):
    anywhere = pl.BlockSpec(memory_space=pl.ANY)
    scalars = pl.BlockSpec(memory_space=pltpu.SMEM)
    bf16, f32 = jnp.bfloat16, jnp.float32
    dma = pltpu.SemaphoreType.DMA
    return pl.pallas_call(
        kernel,
        out_shape=jax.ShapeDtypeStruct(latent.shape, latent.dtype),
        in_specs=[scalars] * 3 + [anywhere] * 7,
        out_specs=pl.BlockSpec(memory_space=pltpu.VMEM),
        scratch_shapes=[
            pltpu.VMEM((8, ROWS, WIDTH), bf16),
            pltpu.VMEM((3, 8, ROWS, HEAD_DIM), bf16),
            pltpu.VMEM((HEAD_DIM, GROUP * KEYS), bf16),
            pltpu.VMEM((X_CHUNKS, 2, ROWS, WIDTH), bf16),
            pltpu.VMEM((CHUNKS, 2, 2, 8, ROWS, HEAD_DIM), bf16),
            pltpu.VMEM((GROUP, 8, ROWS, HEAD_DIM), bf16),
            pltpu.VMEM((GROUP, 8, ROWS, HEAD_DIM), bf16),
            pltpu.VMEM(latent.shape, bf16),
            pltpu.VMEM(time_weight.shape, bf16),
            pltpu.VMEM((8, latent.shape[1]), f32),
            pltpu.VMEM((KEYS, GROUP * KEYS), f32),
            pltpu.VMEM((KEYS, GROUP * KEYS), bf16),
            pltpu.VMEM((1, GROUP * KEYS), f32),
            pltpu.VMEM((1, GROUP * KEYS), f32),
            pltpu.VMEM((1, GROUP * KEYS), f32),
            pltpu.VMEM((HEAD_DIM, GROUP * KEYS), f32),
            pltpu.SMEM((CHUNKS * 8,), f32),
            dma((8, 3)),
            dma((X_CHUNKS, 8)),
            dma((8,)),
            dma((3,)),
            dma((GROUP, 8)),
            dma((8,)),
            dma((X_CHUNKS, 2)),
            dma((X_CHUNKS, 8)),
            dma((8,)),
            dma((3,)),
            dma((GROUP, 8)),
            dma((1,)),
            dma((X_CHUNKS, 2)),
        ],
        compiler_params=pltpu.CompilerParams(
            collective_id=0, has_side_effects=True, vmem_limit_bytes=64 * 1024 * 1024
        ),
        cost_estimate=pl.CostEstimate(flops=2 * 10**9, bytes_accessed=5 * 10**6, transcendentals=4 * 10**6),
    )(
        levels, timesteps, cache_mask, latent, query_in, key_in, value_in, cache_keys, cache_values, time_weight
    )


def solution(mesh):
    return jax.shard_map(
        shards,
        mesh=mesh,
        in_specs=(
            P(("chain", "head"), None),
            P(("chain", "head"), None),
            P(("chain", "head"), None),
            P(("chain", "head"), None),
            P("chain", "head"),
            P("chain", "head"),
            P(),
            P(),
            P(),
            P(),
        ),
        out_specs=P(("chain", "head"), None),
        check_vma=False,
    )
```

```python
import functools
import math

import jax
import jax.numpy as jnp
from jax import lax
from jax.experimental import pallas as pl
from jax.experimental.pallas import tpu as pltpu
from jax.sharding import PartitionSpec as P

MESH = pl.DeviceIdType.MESH
HEAD_DIM = 128
SPANS = 4
NY, NX, NZ = 4, 4, 8
GROUP = 5
WIDTH = GROUP * HEAD_DIM
ROWS = 32
HOPS = (0, 1, 7, 2, 6, 3, 5, 4)
CHUNKS = 12
FIRST_Z = 2
X_CHUNKS = 9
KEYS = 8 * ROWS
HIDDEN = -1e30


def device(y, z, x, core):
    return {"chain": (y * 2 + z // 4) * NX + x, "head": (z % 4) * 2 + core}


def group_of(z):
    return (z % 4) * 2 + z // 4


def group_columns(z):
    return pl.ds(pl.multiple_of(group_of(z) * WIDTH, 128), WIDTH)


def kernel(
    levels_in, timesteps_in, mask_in, latent, query_in, key_in, value_in, cache_keys, cache_values, time_weight,
    returned, shifted, gate,
    levels, timesteps, cache_mask, query, row_query, turned, landed, kv, attended, weight,
    scored, weighed, factor, peak, total, summed, bias,
    send_z, send_x, send_y, send_q, send_o, recv_q, recv_kv, recv_x, recv_y, recv_rq, recv_o, local, own_x,
):
    chain, head = lax.axis_index("chain"), lax.axis_index("head")
    y, x = chain // 8, chain % 4
    zh, zl, core = (chain // 4) % 2, head // 2, head % 2
    z = zh * 4 + zl
    up, down = (y + 1) % 4, (y + 3) % 4
    x_right, x_left, x_far = (x + 1) % 4, (x + 3) % 4, (x + 2) % 4
    right, left, far = (device(y, z, to, core) for to in (x_right, x_left, x_far))
    sibling = device(y, z, x, 1 - core)
    across = device(y, (z + 4) % 8, x, 1 - core)
    to_up, to_down = device(up, z, x, core), device(down, z, x, core)
    mine = group_columns(z)

    def remote(src, dst, send, recv, to):
        return pltpu.make_async_remote_copy(
            src_ref=src, dst_ref=dst, send_sem=send, recv_sem=recv, device_id=to, device_id_type=MESH
        )

    def of_head(h):
        return pl.ds(pl.multiple_of(h * HEAD_DIM, 128), HEAD_DIM)

    own_query = pltpu.make_async_copy(query_in.at[:, mine], query.at[0], recv_q.at[0])
    own_query.start()
    pltpu.make_async_copy(key_in.at[:, mine], landed.at[0, 0], recv_kv.at[0, 0]).start()
    pltpu.make_async_copy(value_in.at[:, mine], landed.at[0, 1], recv_kv.at[0, 1]).start()
    weight_copy = pltpu.make_async_copy(time_weight, weight, local.at[0])
    weight_copy.start()
    scalar_copies = [
        pltpu.make_async_copy(source, place, local.at[n])
        for n, (source, place) in enumerate(
            ((levels_in, levels), (timesteps_in, timesteps), (mask_in, cache_mask)), start=1
        )
    ]
    for copy in scalar_copies:
        copy.start()

    @pl.when(core == zh)
    def _():
        pltpu.make_async_copy(cache_keys, landed.at[1, 0], recv_kv.at[1, 0]).start()
        pltpu.make_async_copy(cache_values, landed.at[1, 1], recv_kv.at[1, 1]).start()

    barrier = pltpu.get_barrier_semaphore()
    partners = [sibling, across, right, left, far, to_up, to_down]
    partners += [device(y, (z + hop) % 8, x, core) for hop in HOPS[1:]]
    for partner in partners:
        pl.semaphore_signal(barrier, inc=1, device_id=partner, device_id_type=MESH)
    pl.semaphore_wait(barrier, len(partners))

    def cache_across(which):
        source = (cache_keys, cache_values)[which]
        return remote(source, landed.at[1, which], send_z.at[0, which], recv_kv.at[1, which], across)

    def query_over_z(j):
        to = (z + HOPS[j]) % 8
        return remote(
            query_in.at[:, group_columns(to)], query.at[j], send_z.at[j, 2], recv_q.at[j], device(y, to, x, core)
        )

    def kv_over_z(j, which):
        to = (z + HOPS[j]) % 8
        source = (key_in, value_in)[which].at[:, group_columns(to)]
        return remote(
            source, landed.at[j + 1, which], send_z.at[j, which], recv_kv.at[j + 1, which], device(y, to, x, core)
        )

    shared = slice((GROUP - 1) * HEAD_DIM, GROUP * HEAD_DIM)

    def own_copies(i):
        return (
            pltpu.make_async_copy(landed.at[i, :, :, of_head(x)], kv.at[i, :, 0, 0], own_x.at[i, 0]),
            pltpu.make_async_copy(landed.at[i, :, :, shared], kv.at[i, :, 1, 0], own_x.at[i, 1]),
        )

    def x_copy(i, n):
        src, dst, to = (
            lambda: (landed.at[i, :, :, of_head(x_right)], kv.at[i, :, 0, 1], right),
            lambda: (landed.at[i, :, :, shared], kv.at[i, :, 1, 1], right),
            lambda: (landed.at[i, :, :, of_head(x_left)], kv.at[i, :, 0, 3], left),
            lambda: (landed.at[i, :, :, shared], kv.at[i, :, 1, 3], left),
            lambda: (landed.at[i, :, :, of_head(x_far)], kv.at[i, :, 0, 2], far),
            lambda: (landed.at[i, :, :, shared], kv.at[i, :, 1, 2], far),
            lambda: (kv.at[i, :, :, 0:4], kv.at[i, :, :, 4:8], sibling),
        )[n]()
        return remote(src, dst, send_x.at[i, n], recv_x.at[i, n], to)

    def y_copy(n):
        src, dst, to = (
            lambda: (kv.at[1, :, :, 0:4], kv.at[9, :, :, 0:4], to_up),
            lambda: (kv.at[1, :, :, 0:4], kv.at[10, :, :, 0:4], to_down),
            lambda: (kv.at[9, 0, :, 0:4], kv.at[11, 0, :, 0:4], to_up),
            lambda: (kv.at[10, 1, :, 0:4], kv.at[11, 1, :, 0:4], to_down),
            lambda: (kv.at[9, :, :, 0:4], kv.at[9, :, :, 4:8], sibling),
            lambda: (kv.at[10, :, :, 0:4], kv.at[10, :, :, 4:8], sibling),
            lambda: (kv.at[11, :, :, 0:4], kv.at[11, :, :, 4:8], sibling),
            lambda: (latent, shifted, to_down),
        )[n]()
        return remote(src, dst, send_y.at[n], recv_y.at[n], to)

    def query_over_x(n):
        to, slot = ((x_right, 0), (x_far, 1), (x_left, 2))[n]
        return remote(
            query.at[:, :, of_head(to)], row_query.at[slot], send_q.at[n], recv_rq.at[n], device(y, z, to, core)
        )

    def back(tile, j):
        to_x, of = (x, GROUP - 1) if tile == GROUP - 1 else ((x + (0, 3, 2, 1)[tile]) % 4, x)
        to = device(down, (z - HOPS[j] + 8) % 8, to_x, core)
        columns = pl.ds(pl.multiple_of(group_of(z) * WIDTH + of * HEAD_DIM, 128), HEAD_DIM)
        return remote(attended.at[tile, j], returned.at[:, columns], send_o.at[tile, j], recv_o.at[tile, j], to)

    def start_kv(j):
        kv_over_z(j, 0).start()
        kv_over_z(j, 1).start()

    @pl.when(core != zh)
    def _():
        cache_across(0).start()
        cache_across(1).start()

    start_kv(1)
    start_kv(2)
    for j in range(1, 8):
        query_over_z(j).start()
    y_copy(7).start()

    def prepare():
        for copy in scalar_copies:
            copy.wait()
        for i in range(CHUNKS):
            for slot in range(8):
                if i == 1 or i >= 9:
                    plane = {1: y, 9: down, 10: up, 11: (y + 2) % 4}[i]
                    side = core if slot < 4 else 1 - core
                    block = plane * 8 + side * 4 + (x + (0, 3, 2, 1)[slot % 4]) % 4
                    bias[i * 8 + slot] = jnp.where(cache_mask[y, block] == 1, 0.0, HIDDEN).astype(jnp.float32)
                else:
                    bias[i * 8 + slot] = jnp.float32(0.0)

        stamp = timesteps[levels[up]].astype(jnp.float32)
        count = 128
        index = lax.broadcasted_iota(jnp.int32, (8, count), 1).astype(jnp.float32)
        phase = stamp * jnp.exp(-math.log(10000.0) * index / count)
        embed = jnp.concatenate([jnp.cos(phase), jnp.sin(phase)], axis=1).astype(jnp.bfloat16)
        weight_copy.wait()

        def gate_columns(c, carry):
            columns = pl.ds(pl.multiple_of(c * WIDTH, 128), WIDTH)
            gate[:, columns] = jnp.dot(embed, weight[:, columns], preferred_element_type=jnp.float32)[0:1]
            return carry

        lax.fori_loop(0, 8, gate_columns, 0)

        peak[...] = jnp.full_like(peak, HIDDEN)
        total[...] = jnp.zeros_like(total)
        summed[...] = jnp.zeros_like(summed)

    def attend(i, cached):
        scale = 1.0 / math.sqrt(HEAD_DIM)
        spans = (slice(0, 4 * KEYS), slice(4 * KEYS, 5 * KEYS))
        keys = [kv[i, 0, n].reshape(KEYS, HEAD_DIM) for n in (0, 1)]
        scores = [jnp.dot(keys[n], turned[:, spans[n]], preferred_element_type=jnp.float32) for n in (0, 1)]
        for n in (0, 1):
            scored[:, spans[n]] = scores[n]
        for first in range(0, GROUP * KEYS, 128):
            side = slice(first, first + 128)
            scores = scored[:, side]
            if cached:
                scores = jnp.concatenate(
                    [scores[slot * ROWS : (slot + 1) * ROWS] + bias[i * 8 + slot] for slot in range(8)], axis=0
                )
            old = peak[:, side]
            new = jnp.maximum(old, jnp.max(scores, axis=0, keepdims=True) * scale)
            weights = jnp.exp(scores * scale - new)
            shrink = jnp.exp(old - new)
            peak[:, side] = new
            factor[:, side] = shrink
            total[:, side] = shrink * total[:, side] + jnp.sum(weights, axis=0, keepdims=True)
            weighed[:, side] = weights.astype(jnp.bfloat16)
        values = [kv[i, 1, n].reshape(KEYS, HEAD_DIM) for n in (0, 1)]
        added = [
            lax.dot_general(
                values[n], weighed[:, spans[n]], (((0,), (0,)), ((), ())), preferred_element_type=jnp.float32
            )
            for n in (0, 1)
        ]
        for n in (0, 1):
            summed[:, spans[n]] = factor[:, spans[n]] * summed[:, spans[n]] + added[n]

    def finish(h):
        tile = slice(h * KEYS, (h + 1) * KEYS)
        result = summed[:, tile] * (1.0 / total[:, tile])
        attended[h] = result.T.astype(jnp.bfloat16).reshape(8, ROWS, HEAD_DIM)
        for j in range(8):
            back(h, j).start()

    def turn_query(h, rows):
        tile = slice(h * KEYS, (h + 1) * KEYS)
        turned[:, tile] = rows.reshape(KEYS, HEAD_DIM).astype(jnp.float32).T.astype(jnp.bfloat16)

    def turn(t, carry):
        @pl.when(t >= 2)
        def _():
            i = t - 2
            for copy in own_copies(i):
                copy.wait()
            for n in range(6):
                x_copy(i, n).wait_recv()
            x_copy(i, 6).start()

        @pl.when(t == 3)
        def _():
            y_copy(0).start()
            y_copy(1).start()

        @pl.when(t == 4)
        def _():
            own_query.wait()
            for j in range(1, 8):
                query_over_z(j).wait_recv()
            for n in range(3):
                query_over_x(n).start()
            for n in (0, 1):
                y_copy(n).wait_recv()
                y_copy(n + 2).start()
                y_copy(n + 4).start()
            turn_query(0, query[:, :, of_head(x)])
            turn_query(4, query[:, :, shared])
            for n in range(3):
                query_over_x(n).wait_recv()
            for n in range(3):
                turn_query(n + 1, row_query[n])
            x_copy(0, 6).wait_recv()

        @pl.when(t >= 4)
        def _():
            x_copy(t - 3, 6).wait_recv()

        for i in (9, 10, 11):

            @pl.when(t == i - 4)
            def _(i=i):
                if i == 9:
                    y_copy(2).wait_recv()
                    y_copy(3).wait_recv()
                    y_copy(6).start()
                y_copy(i - 5).wait_recv()

        @pl.when(t >= 4)
        def _():
            attend(jnp.where(t == 4, 0, t - 3), False)

        @pl.when((t >= 4) & (t <= 7))
        def _():
            attend(jnp.where(t == 4, 1, t + 4), True)

        @pl.when(t < X_CHUNKS)
        def _():
            for which in (0, 1):
                place = landed.at[t, which]
                pltpu.make_async_copy(place, place, recv_kv.at[t, which]).wait()
            for n in range(6):
                x_copy(t, n).start()
            for copy in own_copies(t):
                copy.start()

        for turn_of, hops in ((1, (3, 4)), (2, (5, 6)), (3, (7,))):

            @pl.when(t == turn_of)
            def _(hops=hops):
                for j in hops:
                    start_kv(j)

        pl.when(t == 3)(prepare)
        return carry

    lax.fori_loop(0, X_CHUNKS + 2, turn, 0)
    x_copy(X_CHUNKS - 1, 6).wait_recv()
    attend(X_CHUNKS - 1, False)
    for h in range(GROUP):
        finish(h)

    @pl.when(core != zh)
    def _():
        cache_across(0).wait_send()
        cache_across(1).wait_send()

    for j in range(1, 8):
        query_over_z(j).wait_send()
        kv_over_z(j, 0).wait_send()
        kv_over_z(j, 1).wait_send()

    def sent(i, carry):
        for n in range(7):
            x_copy(i, n).wait_send()
        return carry

    lax.fori_loop(0, X_CHUNKS, sent, 0)
    for n in range(8):
        y_copy(n).wait_send()
    for n in range(3):
        query_over_x(n).wait_send()

    y_copy(7).wait_recv()
    for tile in range(GROUP):
        for j in range(8):
            back(tile, j).wait_recv()
    for tile in range(GROUP):
        for j in range(8):
            back(tile, j).wait_send()


def shards(
    latent, query_in, key_in, value_in, cache_keys, cache_values, levels, timesteps, cache_mask, time_weight
):
    anywhere = pl.BlockSpec(memory_space=pl.ANY)
    bf16, f32, i32 = jnp.bfloat16, jnp.float32, jnp.int32
    dma = pltpu.SemaphoreType.DMA
    returned, shifted, gate = pl.pallas_call(
        kernel,
        out_shape=(
            jax.ShapeDtypeStruct(latent.shape, bf16),
            jax.ShapeDtypeStruct(latent.shape, bf16),
            jax.ShapeDtypeStruct((1, latent.shape[1]), f32),
        ),
        in_specs=[anywhere] * 10,
        out_specs=(anywhere, anywhere, pl.BlockSpec(memory_space=pltpu.VMEM)),
        scratch_shapes=[
            pltpu.SMEM(levels.shape, i32),
            pltpu.SMEM(timesteps.shape, i32),
            pltpu.SMEM(cache_mask.shape, i32),
            pltpu.VMEM((8, ROWS, WIDTH), bf16),
            pltpu.VMEM((3, 8, ROWS, HEAD_DIM), bf16),
            pltpu.VMEM((HEAD_DIM, GROUP * KEYS), bf16),
            pltpu.VMEM((X_CHUNKS, 2, ROWS, WIDTH), bf16),
            pltpu.VMEM((CHUNKS, 2, 2, 8, ROWS, HEAD_DIM), bf16),
            pltpu.VMEM((GROUP, 8, ROWS, HEAD_DIM), bf16),
            pltpu.VMEM(time_weight.shape, bf16),
            pltpu.VMEM((KEYS, GROUP * KEYS), f32),
            pltpu.VMEM((KEYS, GROUP * KEYS), bf16),
            pltpu.VMEM((1, GROUP * KEYS), f32),
            pltpu.VMEM((1, GROUP * KEYS), f32),
            pltpu.VMEM((1, GROUP * KEYS), f32),
            pltpu.VMEM((HEAD_DIM, GROUP * KEYS), f32),
            pltpu.SMEM((CHUNKS * 8,), f32),
            dma((8, 3)),
            dma((X_CHUNKS, 7)),
            dma((8,)),
            dma((3,)),
            dma((GROUP, 8)),
            dma((8,)),
            dma((X_CHUNKS, 2)),
            dma((X_CHUNKS, 7)),
            dma((8,)),
            dma((3,)),
            dma((GROUP, 8)),
            dma((4,)),
            dma((X_CHUNKS, 2)),
        ],
        compiler_params=pltpu.CompilerParams(
            collective_id=0, has_side_effects=True, vmem_limit_bytes=64 * 1024 * 1024
        ),
        cost_estimate=pl.CostEstimate(flops=2 * 10**9, bytes_accessed=5 * 10**6, transcendentals=4 * 10**6),
    )(
        levels, timesteps, cache_mask, latent, query_in, key_in, value_in, cache_keys, cache_values, time_weight
    )
    return (shifted.astype(f32) + gate * returned.astype(f32)).astype(bf16)


def solution(mesh):
    return jax.shard_map(
        shards,
        mesh=mesh,
        in_specs=(
            P(("chain", "head"), None),
            P(("chain", "head"), None),
            P(("chain", "head"), None),
            P(("chain", "head"), None),
            P("chain", "head"),
            P("chain", "head"),
            P(),
            P(),
            P(),
            P(),
        ),
        out_specs=P(("chain", "head"), None),
        check_vma=False,
    )
```

```python
import functools
import math

import jax
import jax.numpy as jnp
from jax import lax
from jax.experimental import pallas as pl
from jax.experimental.pallas import tpu as pltpu
from jax.sharding import PartitionSpec as P

MESH = pl.DeviceIdType.MESH
HEAD_DIM = 128
SPANS = 4
NY, NX, NZ = 4, 4, 8
GROUP = 5
WIDTH = GROUP * HEAD_DIM
ROWS = 32
CHUNKS = 12
FIRST_Z = 2
X_CHUNKS = 9
KEYS = 8 * ROWS
HIDDEN = -1e30


def device(y, z, x, core):
    return {"chain": (y * 2 + z // 4) * NX + x, "head": (z % 4) * 2 + core}


def hop_of(j):
    return jnp.where(j % 2 == 1, (j + 1) // 2, (8 - j // 2) % 8)


def group_of(z):
    return (z % 4) * 2 + z // 4


def group_columns(z):
    return pl.ds(pl.multiple_of(group_of(z) * WIDTH, 128), WIDTH)


def kernel(
    levels, timesteps, cache_mask, latent, query_in, key_in, value_in, cache_keys, cache_values, time_weight,
    out,
    query, row_query, turned, landed, kv, attended, returned, shifted, weight, gate,
    scored, weighed, factor, peak, total, summed, bias,
    send_z, send_x, send_y, send_q, send_o, recv_q, recv_kv, recv_x, recv_y, recv_rq, recv_o, local, own_x,
):
    chain, head = lax.axis_index("chain"), lax.axis_index("head")
    y, x = chain // 8, chain % 4
    zh, zl, core = (chain // 4) % 2, head // 2, head % 2
    z = zh * 4 + zl
    up, down = (y + 1) % 4, (y + 3) % 4
    x_right, x_left, x_far = (x + 1) % 4, (x + 3) % 4, (x + 2) % 4
    right, left, far = (device(y, z, to, core) for to in (x_right, x_left, x_far))
    sibling = device(y, z, x, 1 - core)
    across = device(y, (z + 4) % 8, x, 1 - core)
    to_up, to_down = device(up, z, x, core), device(down, z, x, core)
    mine = group_columns(z)

    def loop(lower, upper, body):
        def step(n, carry):
            body(n)
            return carry

        lax.fori_loop(lower, upper, step, 0)

    def remote(src, dst, send, recv, to):
        return pltpu.make_async_remote_copy(
            src_ref=src, dst_ref=dst, send_sem=send, recv_sem=recv, device_id=to, device_id_type=MESH
        )

    def of_head(h):
        return pl.ds(pl.multiple_of(h * HEAD_DIM, 128), HEAD_DIM)

    own_query = pltpu.make_async_copy(query_in.at[:, mine], query.at[0], recv_q.at[0])
    own_query.start()
    pltpu.make_async_copy(key_in.at[:, mine], landed.at[0, 0], recv_kv.at[0, 0]).start()
    pltpu.make_async_copy(value_in.at[:, mine], landed.at[0, 1], recv_kv.at[0, 1]).start()
    weight_copy = pltpu.make_async_copy(time_weight, weight, local.at[0])
    weight_copy.start()

    @pl.when(core == zh)
    def _():
        pltpu.make_async_copy(cache_keys, landed.at[1, 0], recv_kv.at[1, 0]).start()
        pltpu.make_async_copy(cache_values, landed.at[1, 1], recv_kv.at[1, 1]).start()

    barrier = pltpu.get_barrier_semaphore()
    partners = [sibling, across, right, left, far, to_up, to_down]

    def greet(partner):
        pl.semaphore_signal(barrier, inc=1, device_id=partner, device_id_type=MESH)

    loop(1, 8, lambda hop: greet(device(y, (z + hop) % 8, x, core)))
    for partner in partners:
        greet(partner)
    pl.semaphore_wait(barrier, 7 + len(partners))

    def cache_across(which):
        source = (cache_keys, cache_values)[which]
        return remote(source, landed.at[1, which], send_z.at[0, which], recv_kv.at[1, which], across)

    def query_over_z(j):
        to = (z + hop_of(j)) % 8
        return remote(
            query_in.at[:, group_columns(to)], query.at[j], send_z.at[j, 2], recv_q.at[j], device(y, to, x, core)
        )

    def kv_over_z(j, which):
        to = (z + hop_of(j)) % 8
        source = (key_in, value_in)[which].at[:, group_columns(to)]
        return remote(
            source, landed.at[j + 1, which], send_z.at[j, which], recv_kv.at[j + 1, which], device(y, to, x, core)
        )

    shared = slice((GROUP - 1) * HEAD_DIM, GROUP * HEAD_DIM)

    def own_copies(i):
        return (
            pltpu.make_async_copy(landed.at[i, :, :, of_head(x)], kv.at[i, :, 0, 0], own_x.at[i, 0]),
            pltpu.make_async_copy(landed.at[i, :, :, shared], kv.at[i, :, 1, 0], own_x.at[i, 1]),
        )

    def x_copy(i, n):
        src, dst, to = (
            lambda: (landed.at[i, :, :, of_head(x_right)], kv.at[i, :, 0, 1], right),
            lambda: (landed.at[i, :, :, shared], kv.at[i, :, 1, 1], right),
            lambda: (landed.at[i, :, :, of_head(x_left)], kv.at[i, :, 0, 3], left),
            lambda: (landed.at[i, :, :, shared], kv.at[i, :, 1, 3], left),
            lambda: (landed.at[i, :, :, of_head(x_far)], kv.at[i, :, 0, 2], far),
            lambda: (kv.at[i, 0, 1, 1], kv.at[i, 0, 1, 2], right),
            lambda: (kv.at[i, 1, 1, 3], kv.at[i, 1, 1, 2], left),
            lambda: (kv.at[i, :, :, 0:4], kv.at[i, :, :, 4:8], sibling),
        )[n]()
        return remote(src, dst, send_x.at[i, n], recv_x.at[i, n], to)

    def y_copy(n):
        src, dst, to = (
            lambda: (kv.at[1, :, :, 0:4], kv.at[9, :, :, 0:4], to_up),
            lambda: (kv.at[1, :, :, 0:4], kv.at[10, :, :, 0:4], to_down),
            lambda: (kv.at[9, 0, :, 0:4], kv.at[11, 0, :, 0:4], to_up),
            lambda: (kv.at[10, 1, :, 0:4], kv.at[11, 1, :, 0:4], to_down),
            lambda: (kv.at[9, :, :, 0:4], kv.at[9, :, :, 4:8], sibling),
            lambda: (kv.at[10, :, :, 0:4], kv.at[10, :, :, 4:8], sibling),
            lambda: (kv.at[11, :, :, 0:4], kv.at[11, :, :, 4:8], sibling),
            lambda: (latent, shifted, to_down),
        )[n]()
        return remote(src, dst, send_y.at[n], recv_y.at[n], to)

    def query_over_x(n):
        to = (x + n) % 4
        return remote(
            query.at[:, :, of_head(to)], row_query.at[n], send_q.at[n], recv_rq.at[n], device(y, z, to, core)
        )

    def own_query_copies():
        return (
            pltpu.make_async_copy(query.at[:, :, of_head(x)], row_query.at[0], recv_rq.at[0]),
            pltpu.make_async_copy(query.at[:, :, shared], row_query.at[4], recv_rq.at[4]),
        )

    def back(tile, j):
        to = device(down, (z - hop_of(j) + 8) % 8, (x + 4 - tile) % 4, core)
        return remote(attended.at[tile, j], returned.at[tile, j], send_o.at[tile, j], recv_o.at[tile, j], to)

    def start_kv(j):
        kv_over_z(j, 0).start()
        kv_over_z(j, 1).start()

    @pl.when(core != zh)
    def _():
        cache_across(0).start()
        cache_across(1).start()

    loop(1, 8, lambda j: query_over_z(j).start())
    loop(1, 5, start_kv)
    y_copy(7).start()

    def prepare():
        def show(n):
            i, slot = n // 8, n % 8
            plane = jnp.where(i == 1, y, jnp.where(i == 9, down, jnp.where(i == 10, up, (y + 2) % 4)))
            side = jnp.where(slot < 4, core, 1 - core)
            block = plane * 8 + side * 4 + (x + 4 - slot % 4) % 4
            hidden = ((i == 1) | (i >= 9)) & (cache_mask[y, block] == 0)
            bias[n] = jnp.where(hidden, HIDDEN, 0.0).astype(jnp.float32)

        loop(0, CHUNKS * 8, show)

        stamp = timesteps[levels[up]].astype(jnp.float32)
        count = 128
        index = lax.broadcasted_iota(jnp.int32, (8, count), 1).astype(jnp.float32)
        phase = stamp * jnp.exp(-math.log(10000.0) * index / count)
        embed = jnp.concatenate([jnp.cos(phase), jnp.sin(phase)], axis=1).astype(jnp.bfloat16)
        weight_copy.wait()

        def gate_columns(c, carry):
            columns = pl.ds(pl.multiple_of(c * WIDTH, 128), WIDTH)
            gate[:, columns] = jnp.dot(embed, weight[:, columns], preferred_element_type=jnp.float32)
            return carry

        lax.fori_loop(0, 8, gate_columns, 0)

        peak[...] = jnp.full_like(peak, HIDDEN)
        total[...] = jnp.zeros_like(total)
        summed[...] = jnp.zeros_like(summed)

    def attend(i):
        scale = 1.0 / math.sqrt(HEAD_DIM)
        spans = (slice(0, 4 * KEYS), slice(4 * KEYS, 5 * KEYS))
        keys = [kv[i, 0, n].reshape(KEYS, HEAD_DIM) for n in (0, 1)]
        scores = [jnp.dot(keys[n], turned[:, spans[n]], preferred_element_type=jnp.float32) for n in (0, 1)]
        for n in (0, 1):
            scored[:, spans[n]] = scores[n]
        shown = [bias[i * 8 + slot] for slot in range(8)]

        def softmax(tile):
            for half in (0, 128):
                side = pl.ds(pl.multiple_of(tile * KEYS + half, 128), 128)
                scores = scored[:, side]
                scores = jnp.concatenate(
                    [scores[slot * ROWS : (slot + 1) * ROWS] + shown[slot] for slot in range(8)], axis=0
                )
                old = peak[:, side]
                new = jnp.maximum(old, jnp.max(scores, axis=0, keepdims=True) * scale)
                weights = jnp.exp(scores * scale - new)
                shrink = jnp.exp(old - new)
                peak[:, side] = new
                factor[:, side] = shrink
                total[:, side] = shrink * total[:, side] + jnp.sum(weights, axis=0, keepdims=True)
                weighed[:, side] = weights.astype(jnp.bfloat16)

        loop(0, GROUP, softmax)
        values = [kv[i, 1, n].reshape(KEYS, HEAD_DIM) for n in (0, 1)]
        added = [
            lax.dot_general(
                values[n], weighed[:, spans[n]], (((0,), (0,)), ((), ())), preferred_element_type=jnp.float32
            )
            for n in (0, 1)
        ]
        for n in (0, 1):
            summed[:, spans[n]] = factor[:, spans[n]] * summed[:, spans[n]] + added[n]

    def tile_columns(h):
        return pl.ds(pl.multiple_of(h * KEYS, 128), KEYS)

    def finish(h):
        result = summed[:, tile_columns(h)] * (1.0 / total[:, tile_columns(h)])
        attended[h] = result.T.astype(jnp.bfloat16).reshape(8, ROWS, HEAD_DIM)
        loop(0, 8, lambda j: back(h, j).start())

    def turn_query(h):
        rows = row_query[h].reshape(KEYS, HEAD_DIM)
        turned[:, tile_columns(h)] = rows.astype(jnp.float32).T.astype(jnp.bfloat16)

    def turn(t):
        @pl.when((t >= 2) & (t < X_CHUNKS + 2))
        def _():
            i = t - 2
            x_copy(i, 0).wait_recv()
            x_copy(i, 1).wait_recv()
            x_copy(i, 5).start()
            x_copy(i, 2).wait_recv()
            x_copy(i, 3).wait_recv()
            x_copy(i, 6).start()

        @pl.when((t >= 3) & (t < X_CHUNKS + 3))
        def _():
            i = t - 3
            for copy in own_copies(i):
                copy.wait()
            for n in (4, 5, 6):
                x_copy(i, n).wait_recv()
            x_copy(i, 7).start()

        @pl.when(t == 3)
        def _():
            own_query.wait()
            loop(1, 8, lambda j: query_over_z(j).wait_recv())
            loop(1, 4, lambda n: query_over_x(n).start())
            for copy in own_query_copies():
                copy.start()

        @pl.when(t == 4)
        def _():
            y_copy(0).start()
            y_copy(1).start()
            for copy in own_query_copies():
                copy.wait()
            loop(1, 4, lambda n: query_over_x(n).wait_recv())
            loop(0, GROUP, turn_query)

        @pl.when(t == 7)
        def _():
            for n in (0, 1):
                y_copy(n).wait_recv()
                y_copy(n + 2).start()
                y_copy(n + 4).start()

        @pl.when(t == 9)
        def _():
            y_copy(2).wait_recv()
            y_copy(3).wait_recv()
            y_copy(6).start()

        @pl.when(t >= 4)
        def _():
            x_copy(t - 4, 7).wait_recv()

        for i in (9, 10, 11):

            @pl.when(t == i)
            def _(i=i):
                y_copy(i - 5).wait_recv()

        ready = jnp.where(t < 4, 0, jnp.where((t >= 9) & (t <= 11), 2, 1))
        loop(0, ready, lambda n: attend(jnp.where(n == 0, t - 4, t)))

        @pl.when(t < X_CHUNKS)
        def _():
            for which in (0, 1):
                place = landed.at[t, which]
                pltpu.make_async_copy(place, place, recv_kv.at[t, which]).wait()
            for n in range(5):
                x_copy(t, n).start()
            for copy in own_copies(t):
                copy.start()

        pl.when(t == 1)(lambda: loop(5, 7, start_kv))
        pl.when(t == 3)(lambda: start_kv(7))
        pl.when(t == 1)(prepare)

    loop(0, X_CHUNKS + 4, turn)
    loop(0, GROUP, finish)

    @pl.when(core != zh)
    def _():
        cache_across(0).wait_send()
        cache_across(1).wait_send()

    @functools.partial(loop, 1, 8)
    def _(j):
        query_over_z(j).wait_send()
        kv_over_z(j, 0).wait_send()
        kv_over_z(j, 1).wait_send()

    @functools.partial(loop, 0, X_CHUNKS)
    def _(i):
        for n in range(8):
            x_copy(i, n).wait_send()

    for n in range(8):
        y_copy(n).wait_send()
    loop(1, 4, lambda n: query_over_x(n).wait_send())

    y_copy(7).wait_recv()

    @functools.partial(loop, 0, GROUP * 8)
    def _(n):
        tile, j = n // 8, n % 8
        back(tile, j).wait_recv()
        of = jnp.where(tile == GROUP - 1, GROUP - 1, (x + tile) % 4)
        first = group_of((z + hop_of(j)) % 8) * WIDTH + of * HEAD_DIM
        columns = pl.ds(pl.multiple_of(first, 128), HEAD_DIM)
        out[:, columns] = (
            shifted[:, columns].astype(jnp.float32) + gate[0:1, columns] * returned[tile, j].astype(jnp.float32)
        ).astype(jnp.bfloat16)

    loop(0, GROUP * 8, lambda n: back(n // 8, n % 8).wait_send())


def shards(
    latent, query_in, key_in, value_in, cache_keys, cache_values, levels, timesteps, cache_mask, time_weight
):
    anywhere = pl.BlockSpec(memory_space=pl.ANY)
    scalars = pl.BlockSpec(memory_space=pltpu.SMEM)
    bf16, f32 = jnp.bfloat16, jnp.float32
    dma = pltpu.SemaphoreType.DMA
    return pl.pallas_call(
        kernel,
        out_shape=jax.ShapeDtypeStruct(latent.shape, latent.dtype),
        in_specs=[scalars] * 3 + [anywhere] * 7,
        out_specs=pl.BlockSpec(memory_space=pltpu.VMEM),
        scratch_shapes=[
            pltpu.VMEM((8, ROWS, WIDTH), bf16),
            pltpu.VMEM((5, 8, ROWS, HEAD_DIM), bf16),
            pltpu.VMEM((HEAD_DIM, GROUP * KEYS), bf16),
            pltpu.VMEM((X_CHUNKS, 2, ROWS, WIDTH), bf16),
            pltpu.VMEM((CHUNKS, 2, 2, 8, ROWS, HEAD_DIM), bf16),
            pltpu.VMEM((GROUP, 8, ROWS, HEAD_DIM), bf16),
            pltpu.VMEM((GROUP, 8, ROWS, HEAD_DIM), bf16),
            pltpu.VMEM(latent.shape, bf16),
            pltpu.VMEM(time_weight.shape, bf16),
            pltpu.VMEM((8, latent.shape[1]), f32),
            pltpu.VMEM((KEYS, GROUP * KEYS), f32),
            pltpu.VMEM((KEYS, GROUP * KEYS), bf16),
            pltpu.VMEM((1, GROUP * KEYS), f32),
            pltpu.VMEM((1, GROUP * KEYS), f32),
            pltpu.VMEM((1, GROUP * KEYS), f32),
            pltpu.VMEM((HEAD_DIM, GROUP * KEYS), f32),
            pltpu.SMEM((CHUNKS * 8,), f32),
            dma((8, 3)),
            dma((X_CHUNKS, 8)),
            dma((8,)),
            dma((5,)),
            dma((GROUP, 8)),
            dma((8,)),
            dma((X_CHUNKS, 2)),
            dma((X_CHUNKS, 8)),
            dma((8,)),
            dma((5,)),
            dma((GROUP, 8)),
            dma((1,)),
            dma((X_CHUNKS, 2)),
        ],
        compiler_params=pltpu.CompilerParams(
            collective_id=0, has_side_effects=True, vmem_limit_bytes=64 * 1024 * 1024
        ),
        cost_estimate=pl.CostEstimate(flops=2 * 10**9, bytes_accessed=5 * 10**6, transcendentals=4 * 10**6),
    )(
        levels, timesteps, cache_mask, latent, query_in, key_in, value_in, cache_keys, cache_values, time_weight
    )


def solution(mesh):
    return jax.shard_map(
        shards,
        mesh=mesh,
        in_specs=(
            P(("chain", "head"), None),
            P(("chain", "head"), None),
            P(("chain", "head"), None),
            P(("chain", "head"), None),
            P("chain", "head"),
            P("chain", "head"),
            P(),
            P(),
            P(),
            P(),
        ),
        out_specs=P(("chain", "head"), None),
        check_vma=False,
    )
```

```python
import functools
import math

import jax
import jax.numpy as jnp
from jax import lax
from jax.experimental import pallas as pl
from jax.experimental.pallas import tpu as pltpu
from jax.sharding import PartitionSpec as P

MESH = pl.DeviceIdType.MESH
HEAD_DIM = 128
SPANS = 4
NY, NX, NZ = 4, 4, 8
GROUP = 5
WIDTH = GROUP * HEAD_DIM
ROWS = 32
HOPS = (0, 1, 7, 2, 6, 3, 5, 4)
CHUNKS = 12
FIRST_Z = 2
X_CHUNKS = 9
KEYS = 8 * ROWS
LOG2E = 1.4426950408889634
ATTEND = (0, 1, 9, 10, 2, 3, 11, 4, 5, 6, 7, 8)
PLACE = tuple(ATTEND.index(i) for i in range(CHUNKS))
HIDDEN = -1e30


def device(y, z, x, core):
    return {"chain": (y * 2 + z // 4) * NX + x, "head": (z % 4) * 2 + core}


def group_of(z):
    return (z % 4) * 2 + z // 4


def group_columns(z):
    return pl.ds(pl.multiple_of(group_of(z) * WIDTH, 128), WIDTH)


def kernel(
    levels_in, timesteps_in, mask_in, latent, query_in, key_in, value_in, cache_keys, cache_values, time_weight,
    returned, shifted, gate,
    levels, timesteps, cache_mask, query, row_query, turned, landed, kv, attended, weight,
    scored, weighed, factor, peak, total, summed, bias,
    send_z, send_x, send_y, send_q, send_o, recv_q, recv_kv, recv_x, recv_y, recv_rq, recv_o, local, own_x,
):
    chain, head = lax.axis_index("chain"), lax.axis_index("head")
    y, x = chain // 8, chain % 4
    zh, zl, core = (chain // 4) % 2, head // 2, head % 2
    z = zh * 4 + zl
    up, down = (y + 1) % 4, (y + 3) % 4
    x_right, x_left, x_far = (x + 1) % 4, (x + 3) % 4, (x + 2) % 4
    right, left, far = (device(y, z, to, core) for to in (x_right, x_left, x_far))
    sibling = device(y, z, x, 1 - core)
    across = device(y, (z + 4) % 8, x, 1 - core)
    to_up, to_down = device(up, z, x, core), device(down, z, x, core)
    mine = group_columns(z)

    def remote(src, dst, send, recv, to):
        return pltpu.make_async_remote_copy(
            src_ref=src, dst_ref=dst, send_sem=send, recv_sem=recv, device_id=to, device_id_type=MESH
        )

    def of_head(h):
        return pl.ds(pl.multiple_of(h * HEAD_DIM, 128), HEAD_DIM)

    own_query = pltpu.make_async_copy(query_in.at[:, mine], query.at[0], recv_q.at[0])
    own_query.start()
    pltpu.make_async_copy(key_in.at[:, mine], landed.at[0, 0], recv_kv.at[0, 0]).start()
    pltpu.make_async_copy(value_in.at[:, mine], landed.at[0, 1], recv_kv.at[0, 1]).start()
    weight_copy = pltpu.make_async_copy(time_weight, weight, local.at[0])
    weight_copy.start()
    scalar_copies = [
        pltpu.make_async_copy(source, place, local.at[n])
        for n, (source, place) in enumerate(
            ((levels_in, levels), (timesteps_in, timesteps), (mask_in, cache_mask)), start=1
        )
    ]
    for copy in scalar_copies:
        copy.start()

    @pl.when(core == zh)
    def _():
        pltpu.make_async_copy(cache_keys, landed.at[1, 0], recv_kv.at[1, 0]).start()
        pltpu.make_async_copy(cache_values, landed.at[1, 1], recv_kv.at[1, 1]).start()

    barrier = pltpu.get_barrier_semaphore()
    partners = [sibling, across, right, left, far, to_up, to_down]
    partners += [device(y, (z + hop) % 8, x, core) for hop in HOPS[1:]]
    for partner in partners:
        pl.semaphore_signal(barrier, inc=1, device_id=partner, device_id_type=MESH)
    pl.semaphore_wait(barrier, len(partners))

    def cache_across(which):
        source = (cache_keys, cache_values)[which]
        return remote(source, landed.at[1, which], send_z.at[0, which], recv_kv.at[1, which], across)

    def query_over_z(j):
        to = (z + HOPS[j]) % 8
        return remote(
            query_in.at[:, group_columns(to)], query.at[j], send_z.at[j, 2], recv_q.at[j], device(y, to, x, core)
        )

    def kv_over_z(j, which):
        to = (z + HOPS[j]) % 8
        source = (key_in, value_in)[which].at[:, group_columns(to)]
        return remote(
            source, landed.at[j + 1, which], send_z.at[j, which], recv_kv.at[j + 1, which], device(y, to, x, core)
        )

    shared = slice((GROUP - 1) * HEAD_DIM, GROUP * HEAD_DIM)

    def chunk(i):
        return kv.at[PLACE[i]]

    def own_copies(i):
        return (
            pltpu.make_async_copy(landed.at[i, :, :, of_head(x)], chunk(i).at[:, 0, 0], own_x.at[i, 0]),
            pltpu.make_async_copy(landed.at[i, :, :, shared], chunk(i).at[:, 1, 0], own_x.at[i, 1]),
        )

    def x_copy(i, n):
        src, dst, to = (
            lambda: (landed.at[i, :, :, of_head(x_right)], chunk(i).at[:, 0, 1], right),
            lambda: (landed.at[i, :, :, shared], chunk(i).at[:, 1, 1], right),
            lambda: (landed.at[i, :, :, of_head(x_left)], chunk(i).at[:, 0, 3], left),
            lambda: (landed.at[i, :, :, shared], chunk(i).at[:, 1, 3], left),
            lambda: (landed.at[i, :, :, of_head(x_far)], chunk(i).at[:, 0, 2], far),
            lambda: (landed.at[i, :, :, shared], chunk(i).at[:, 1, 2], far),
            lambda: (chunk(i).at[:, :, 0:4], chunk(i).at[:, :, 4:8], sibling),
        )[n]()
        return remote(src, dst, send_x.at[i, n], recv_x.at[i, n], to)

    def y_copy(n):
        src, dst, to = (
            lambda: (chunk(1).at[:, :, 0:4], chunk(9).at[:, :, 0:4], to_up),
            lambda: (chunk(1).at[:, :, 0:4], chunk(10).at[:, :, 0:4], to_down),
            lambda: (chunk(9).at[0, :, 0:4], chunk(11).at[0, :, 0:4], to_up),
            lambda: (chunk(10).at[1, :, 0:4], chunk(11).at[1, :, 0:4], to_down),
            lambda: (chunk(9).at[:, :, 0:4], chunk(9).at[:, :, 4:8], sibling),
            lambda: (chunk(10).at[:, :, 0:4], chunk(10).at[:, :, 4:8], sibling),
            lambda: (chunk(11).at[:, :, 0:4], chunk(11).at[:, :, 4:8], sibling),
            lambda: (latent, shifted, to_down),
        )[n]()
        return remote(src, dst, send_y.at[n], recv_y.at[n], to)

    def query_over_x(n):
        to, slot = ((x_right, 0), (x_far, 1), (x_left, 2))[n]
        return remote(
            query.at[:, :, of_head(to)], row_query.at[slot], send_q.at[n], recv_rq.at[n], device(y, z, to, core)
        )

    def back(tile, j):
        to_x, of = (x, GROUP - 1) if tile == GROUP - 1 else ((x + (0, 3, 2, 1)[tile]) % 4, x)
        to = device(down, (z - HOPS[j] + 8) % 8, to_x, core)
        columns = pl.ds(pl.multiple_of(group_of(z) * WIDTH + of * HEAD_DIM, 128), HEAD_DIM)
        return remote(attended.at[tile, j], returned.at[:, columns], send_o.at[tile, j], recv_o.at[tile, j], to)

    def start_kv(j):
        kv_over_z(j, 0).start()
        kv_over_z(j, 1).start()

    @pl.when(core != zh)
    def _():
        cache_across(0).start()
        cache_across(1).start()

    for j in reversed(range(1, 8)):
        query_over_z(j).start()
    y_copy(7).start()

    def prepare():
        for copy in scalar_copies:
            copy.wait()
        for i in range(CHUNKS):
            for slot in range(8):
                if i == 1 or i >= 9:
                    plane = {1: y, 9: down, 10: up, 11: (y + 2) % 4}[i]
                    side = core if slot < 4 else 1 - core
                    block = plane * 8 + side * 4 + (x + (0, 3, 2, 1)[slot % 4]) % 4
                    bias[PLACE[i] * 8 + slot] = jnp.where(cache_mask[y, block] == 1, 0.0, HIDDEN).astype(jnp.float32)
                else:
                    bias[PLACE[i] * 8 + slot] = jnp.float32(0.0)

        stamp = timesteps[levels[up]].astype(jnp.float32)
        count = 128
        index = lax.broadcasted_iota(jnp.int32, (8, count), 1).astype(jnp.float32)
        phase = stamp * jnp.exp(-math.log(10000.0) * index / count)
        embed = jnp.concatenate([jnp.cos(phase), jnp.sin(phase)], axis=1).astype(jnp.bfloat16)
        weight_copy.wait()

        def gate_columns(c, carry):
            columns = pl.ds(pl.multiple_of(c * WIDTH, 128), WIDTH)
            gate[:, columns] = jnp.dot(embed, weight[:, columns], preferred_element_type=jnp.float32)[0:1]
            return carry

        lax.fori_loop(0, 8, gate_columns, 0)

        peak[...] = jnp.full_like(peak, HIDDEN)
        total[...] = jnp.zeros_like(total)
        summed[...] = jnp.zeros_like(summed)

    scale = LOG2E / math.sqrt(HEAD_DIM)
    spans = (slice(0, 4 * KEYS), slice(4 * KEYS, 5 * KEYS))

    def score(c):
        keys = [kv[c, 0, n].reshape(KEYS, HEAD_DIM) for n in (0, 1)]
        scores = [jnp.dot(keys[n], turned[:, spans[n]], preferred_element_type=jnp.float32) for n in (0, 1)]
        for n in (0, 1):
            scored[:, spans[n]] = scores[n]

    def softmax(c, lower, upper, cached):
        for first in range(lower, upper, 128):
            side = slice(first, first + 128)
            scores = scored[:, side]
            if cached:
                scores = jnp.concatenate(
                    [scores[slot * ROWS : (slot + 1) * ROWS] + bias[c * 8 + slot] for slot in range(8)], axis=0
                )
            old = peak[:, side]
            new = jnp.maximum(old, jnp.max(scores, axis=0, keepdims=True) * scale)
            weights = jnp.exp2(scores * scale - new)
            shrink = jnp.exp2(old - new)
            peak[:, side] = new
            factor[:, side] = shrink
            total[:, side] = shrink * total[:, side] + jnp.sum(weights, axis=0, keepdims=True)
            weighed[:, side] = weights.astype(jnp.bfloat16)

    def add_values(values, columns):
        added = lax.dot_general(
            values, weighed[:, columns], (((0,), (0,)), ((), ())), preferred_element_type=jnp.float32
        )
        return factor[:, columns] * summed[:, columns] + added

    def attend(c, cached):
        score(c)
        softmax(c, 0, GROUP * KEYS, cached)
        values = [kv[c, 1, n].reshape(KEYS, HEAD_DIM) for n in (0, 1)]
        sums = [add_values(values[n], spans[n]) for n in (0, 1)]
        for n in (0, 1):
            summed[:, spans[n]] = sums[n]

    def attend_last(c):
        score(c)
        values = [kv[c, 1, n].reshape(KEYS, HEAD_DIM) for n in (0, 1)]
        for h in range(GROUP):
            tile = slice(h * KEYS, (h + 1) * KEYS)
            softmax(c, h * KEYS, (h + 1) * KEYS, False)
            result = add_values(values[h // (GROUP - 1)], tile) * (1.0 / total[:, tile])
            attended[h] = result.T.astype(jnp.bfloat16).reshape(8, ROWS, HEAD_DIM)
            for j in reversed(range(8)):
                back(h, j).start()

    def turn_query(h, rows):
        tile = slice(h * KEYS, (h + 1) * KEYS)
        turned[:, tile] = rows.reshape(KEYS, HEAD_DIM).astype(jnp.float32).T.astype(jnp.bfloat16)

    def arrived(*items):
        for i in items:
            for which in (0, 1):
                place = landed.at[i, which]
                pltpu.make_async_copy(place, place, recv_kv.at[i, which]).wait()
            for n in range(6):
                x_copy(i, n).start()
            for copy in own_copies(i):
                copy.start()

    def gathered(*items):
        for i in items:
            for copy in own_copies(i):
                copy.wait()
            for n in range(6):
                x_copy(i, n).wait_recv()
            x_copy(i, 6).start()

    def complete(i):
        if i >= X_CHUNKS:
            y_copy(i - 5).wait_recv()
        else:
            x_copy(i, 6).wait_recv()

    def before(c):
        if c == 0:
            arrived(0)
            prepare()
            arrived(1)
            gathered(0, 1)
            y_copy(0).start()
            y_copy(1).start()
            for j in (1, 2, 3, 4):
                query_over_z(j).wait_recv()
            start_kv(1)
            start_kv(2)
            own_query.wait()
            for j in (5, 6, 7):
                query_over_z(j).wait_recv()
            for n in range(3):
                query_over_x(n).start()
            for j in (3, 4, 5, 6):
                start_kv(j)
            turn_query(0, query[:, :, of_head(x)])
            turn_query(4, query[:, :, shared])
            for n in (0, 1):
                y_copy(n).wait_recv()
                y_copy(n + 2).start()
                y_copy(n + 4).start()
            for n in range(3):
                query_over_x(n).wait_recv()
            for n in range(3):
                turn_query(n + 1, row_query[n])
        if c == 1:
            arrived(2, 3)
        if c == 2:
            start_kv(7)
            y_copy(2).wait_recv()
            y_copy(3).wait_recv()
            y_copy(6).start()
        if c == 3:
            gathered(2, 3)
        if c == 5:
            arrived(4, 5)
        if c == 6:
            gathered(4)
        if c == 7:
            gathered(5)
            arrived(6)
        if c == 8:
            arrived(7)
        if c == 9:
            gathered(6, 7)
            arrived(8)
        if c == 11:
            gathered(8)
        complete(ATTEND[c])

    def turn(c, carry):
        cached = False
        for now in range(CHUNKS - 1):
            pl.when(c == now)(functools.partial(before, now))
            if ATTEND[now] == 1 or ATTEND[now] >= X_CHUNKS:
                cached = cached | (c == now)
        pl.when(cached)(functools.partial(attend, c, True))
        pl.when(jnp.logical_not(cached))(functools.partial(attend, c, False))
        return carry

    lax.fori_loop(0, CHUNKS - 1, turn, 0)
    before(CHUNKS - 1)
    attend_last(CHUNKS - 1)

    @pl.when(core != zh)
    def _():
        cache_across(0).wait_send()
        cache_across(1).wait_send()

    for j in range(1, 8):
        query_over_z(j).wait_send()
        kv_over_z(j, 0).wait_send()
        kv_over_z(j, 1).wait_send()

    for i in range(X_CHUNKS):
        for n in range(7):
            x_copy(i, n).wait_send()
    for n in range(8):
        y_copy(n).wait_send()
    for n in range(3):
        query_over_x(n).wait_send()

    y_copy(7).wait_recv()
    for tile in range(GROUP):
        for j in range(8):
            back(tile, j).wait_recv()
    for tile in range(GROUP):
        for j in range(8):
            back(tile, j).wait_send()


def shards(
    latent, query_in, key_in, value_in, cache_keys, cache_values, levels, timesteps, cache_mask, time_weight
):
    anywhere = pl.BlockSpec(memory_space=pl.ANY)
    bf16, f32, i32 = jnp.bfloat16, jnp.float32, jnp.int32
    dma = pltpu.SemaphoreType.DMA
    returned, shifted, gate = pl.pallas_call(
        kernel,
        out_shape=(
            jax.ShapeDtypeStruct(latent.shape, bf16),
            jax.ShapeDtypeStruct(latent.shape, bf16),
            jax.ShapeDtypeStruct((1, latent.shape[1]), f32),
        ),
        in_specs=[anywhere] * 10,
        out_specs=(anywhere, anywhere, pl.BlockSpec(memory_space=pltpu.VMEM)),
        scratch_shapes=[
            pltpu.SMEM(levels.shape, i32),
            pltpu.SMEM(timesteps.shape, i32),
            pltpu.SMEM(cache_mask.shape, i32),
            pltpu.VMEM((8, ROWS, WIDTH), bf16),
            pltpu.VMEM((3, 8, ROWS, HEAD_DIM), bf16),
            pltpu.VMEM((HEAD_DIM, GROUP * KEYS), bf16),
            pltpu.VMEM((X_CHUNKS, 2, ROWS, WIDTH), bf16),
            pltpu.VMEM((CHUNKS, 2, 2, 8, ROWS, HEAD_DIM), bf16),
            pltpu.VMEM((GROUP, 8, ROWS, HEAD_DIM), bf16),
            pltpu.VMEM(time_weight.shape, bf16),
            pltpu.VMEM((KEYS, GROUP * KEYS), f32),
            pltpu.VMEM((KEYS, GROUP * KEYS), bf16),
            pltpu.VMEM((1, GROUP * KEYS), f32),
            pltpu.VMEM((1, GROUP * KEYS), f32),
            pltpu.VMEM((1, GROUP * KEYS), f32),
            pltpu.VMEM((HEAD_DIM, GROUP * KEYS), f32),
            pltpu.SMEM((CHUNKS * 8,), f32),
            dma((8, 3)),
            dma((X_CHUNKS, 7)),
            dma((8,)),
            dma((3,)),
            dma((GROUP, 8)),
            dma((8,)),
            dma((X_CHUNKS, 2)),
            dma((X_CHUNKS, 7)),
            dma((8,)),
            dma((3,)),
            dma((GROUP, 8)),
            dma((4,)),
            dma((X_CHUNKS, 2)),
        ],
        compiler_params=pltpu.CompilerParams(
            collective_id=0, has_side_effects=True, vmem_limit_bytes=64 * 1024 * 1024
        ),
        cost_estimate=pl.CostEstimate(flops=2 * 10**9, bytes_accessed=5 * 10**6, transcendentals=4 * 10**6),
    )(
        levels, timesteps, cache_mask, latent, query_in, key_in, value_in, cache_keys, cache_values, time_weight
    )
    return (shifted.astype(f32) + gate * returned.astype(f32)).astype(bf16)


def solution(mesh):
    return jax.shard_map(
        shards,
        mesh=mesh,
        in_specs=(
            P(("chain", "head"), None),
            P(("chain", "head"), None),
            P(("chain", "head"), None),
            P(("chain", "head"), None),
            P("chain", "head"),
            P("chain", "head"),
            P(),
            P(),
            P(),
            P(),
        ),
        out_specs=P(("chain", "head"), None),
        check_vma=False,
    )
```

```python
import functools
import math

import jax
import jax.numpy as jnp
from jax import lax
from jax.experimental import pallas as pl
from jax.experimental.pallas import tpu as pltpu
from jax.sharding import PartitionSpec as P

MESH = pl.DeviceIdType.MESH
HEAD_DIM = 128
SPANS = 4
NY, NX, NZ = 4, 4, 8
GROUP = 5
WIDTH = GROUP * HEAD_DIM
ROWS = 32
HOPS = (0, 1, 7, 2, 6, 3, 5, 4)
CHUNKS = 12
FIRST_Z = 2
X_CHUNKS = 9
KEYS = 8 * ROWS
LOG2E = 1.4426950408889634
ATTEND = (0, 1, 9, 10, 2, 3, 11, 4, 5, 6, 7, 8)
PLACE = tuple(ATTEND.index(i) for i in range(CHUNKS))
HIDDEN = -1e30


def device(y, z, x, core):
    return {"chain": (y * 2 + z // 4) * NX + x, "head": (z % 4) * 2 + core}


def group_of(z):
    return (z % 4) * 2 + z // 4


def group_columns(z):
    return pl.ds(pl.multiple_of(group_of(z) * WIDTH, 128), WIDTH)


def kernel(
    levels_in, timesteps_in, mask_in, latent, query_in, key_in, value_in, cache_keys, cache_values, time_weight,
    returned, shifted, gate,
    levels, timesteps, cache_mask, query, row_query, turned, landed, kv, attended, weight,
    scored, weighed, factor, peak, total, summed, bias,
    send_z, send_x, send_y, send_q, send_o, recv_q, recv_kv, recv_x, recv_y, recv_rq, recv_o, local, own_x,
):
    chain, head = lax.axis_index("chain"), lax.axis_index("head")
    y, x = chain // 8, chain % 4
    zh, zl, core = (chain // 4) % 2, head // 2, head % 2
    z = zh * 4 + zl
    up, down = (y + 1) % 4, (y + 3) % 4
    x_right, x_left, x_far = (x + 1) % 4, (x + 3) % 4, (x + 2) % 4
    right, left, far = (device(y, z, to, core) for to in (x_right, x_left, x_far))
    sibling = device(y, z, x, 1 - core)
    across = device(y, (z + 4) % 8, x, 1 - core)
    to_up, to_down = device(up, z, x, core), device(down, z, x, core)
    mine = group_columns(z)

    def remote(src, dst, send, recv, to):
        return pltpu.make_async_remote_copy(
            src_ref=src, dst_ref=dst, send_sem=send, recv_sem=recv, device_id=to, device_id_type=MESH
        )

    def of_head(h):
        return pl.ds(pl.multiple_of(h * HEAD_DIM, 128), HEAD_DIM)

    own_query = pltpu.make_async_copy(query_in.at[:, mine], query.at[0], recv_q.at[0])
    own_query.start()
    pltpu.make_async_copy(key_in.at[:, mine], landed.at[0, 0], recv_kv.at[0, 0]).start()
    pltpu.make_async_copy(value_in.at[:, mine], landed.at[0, 1], recv_kv.at[0, 1]).start()
    weight_copy = pltpu.make_async_copy(time_weight, weight, local.at[0])
    weight_copy.start()
    scalar_copies = [
        pltpu.make_async_copy(source, place, local.at[n])
        for n, (source, place) in enumerate(
            ((levels_in, levels), (timesteps_in, timesteps), (mask_in, cache_mask)), start=1
        )
    ]
    for copy in scalar_copies:
        copy.start()

    @pl.when(core == zh)
    def _():
        pltpu.make_async_copy(cache_keys, landed.at[1, 0], recv_kv.at[1, 0]).start()
        pltpu.make_async_copy(cache_values, landed.at[1, 1], recv_kv.at[1, 1]).start()

    barrier = pltpu.get_barrier_semaphore()
    partners = [sibling, across, right, left, far, to_up, to_down]
    partners += [device(y, (z + hop) % 8, x, core) for hop in HOPS[1:]]
    for partner in partners:
        pl.semaphore_signal(barrier, inc=1, device_id=partner, device_id_type=MESH)
    pl.semaphore_wait(barrier, len(partners))

    def cache_across(which):
        source = (cache_keys, cache_values)[which]
        return remote(source, landed.at[1, which], send_z.at[0, which], recv_kv.at[1, which], across)

    def query_over_z(j):
        to = (z + HOPS[j]) % 8
        return remote(
            query_in.at[:, group_columns(to)], query.at[j], send_z.at[j, 2], recv_q.at[j], device(y, to, x, core)
        )

    def kv_over_z(j, which):
        to = (z + HOPS[j]) % 8
        source = (key_in, value_in)[which].at[:, group_columns(to)]
        return remote(
            source, landed.at[j + 1, which], send_z.at[j, which], recv_kv.at[j + 1, which], device(y, to, x, core)
        )

    shared = slice((GROUP - 1) * HEAD_DIM, GROUP * HEAD_DIM)

    def chunk(i):
        return kv.at[PLACE[i]]

    def own_copies(i):
        return (
            pltpu.make_async_copy(landed.at[i, :, :, of_head(x)], chunk(i).at[:, 0, 0], own_x.at[i, 0]),
            pltpu.make_async_copy(landed.at[i, :, :, shared], chunk(i).at[:, 1, 0], own_x.at[i, 1]),
        )

    def x_copy(i, n):
        src, dst, to = (
            lambda: (landed.at[i, :, :, of_head(x_right)], chunk(i).at[:, 0, 1], right),
            lambda: (landed.at[i, :, :, shared], chunk(i).at[:, 1, 1], right),
            lambda: (landed.at[i, :, :, of_head(x_left)], chunk(i).at[:, 0, 3], left),
            lambda: (landed.at[i, :, :, shared], chunk(i).at[:, 1, 3], left),
            lambda: (landed.at[i, :, :, of_head(x_far)], chunk(i).at[:, 0, 2], far),
            lambda: (landed.at[i, :, :, shared], chunk(i).at[:, 1, 2], far),
            lambda: (chunk(i).at[:, :, 0:4], chunk(i).at[:, :, 4:8], sibling),
        )[n]()
        return remote(src, dst, send_x.at[i, n], recv_x.at[i, n], to)

    def y_copy(n):
        src, dst, to = (
            lambda: (chunk(1).at[:, :, 0:4], chunk(9).at[:, :, 0:4], to_up),
            lambda: (chunk(1).at[:, :, 0:4], chunk(10).at[:, :, 0:4], to_down),
            lambda: (chunk(9).at[0, :, 0:4], chunk(11).at[0, :, 0:4], to_up),
            lambda: (chunk(10).at[1, :, 0:4], chunk(11).at[1, :, 0:4], to_down),
            lambda: (chunk(9).at[:, :, 0:4], chunk(9).at[:, :, 4:8], sibling),
            lambda: (chunk(10).at[:, :, 0:4], chunk(10).at[:, :, 4:8], sibling),
            lambda: (chunk(11).at[:, :, 0:4], chunk(11).at[:, :, 4:8], sibling),
            lambda: (latent, shifted, to_down),
        )[n]()
        return remote(src, dst, send_y.at[n], recv_y.at[n], to)

    def query_over_x(n):
        to, slot = ((x_right, 0), (x_far, 1), (x_left, 2))[n]
        return remote(
            query.at[:, :, of_head(to)], row_query.at[slot], send_q.at[n], recv_rq.at[n], device(y, z, to, core)
        )

    def back(tile, j):
        to_x, of = (x, GROUP - 1) if tile == GROUP - 1 else ((x + (0, 3, 2, 1)[tile]) % 4, x)
        to = device(down, (z - HOPS[j] + 8) % 8, to_x, core)
        columns = pl.ds(pl.multiple_of(group_of(z) * WIDTH + of * HEAD_DIM, 128), HEAD_DIM)
        return remote(attended.at[tile, j], returned.at[:, columns], send_o.at[tile, j], recv_o.at[tile, j], to)

    def start_kv(j):
        kv_over_z(j, 0).start()
        kv_over_z(j, 1).start()

    @pl.when(core != zh)
    def _():
        cache_across(0).start()
        cache_across(1).start()

    for j in reversed(range(1, 8)):
        query_over_z(j).start()
    y_copy(7).start()

    def prepare():
        for copy in scalar_copies:
            copy.wait()
        for i in range(CHUNKS):
            for slot in range(8):
                if i == 1 or i >= 9:
                    plane = {1: y, 9: down, 10: up, 11: (y + 2) % 4}[i]
                    side = core if slot < 4 else 1 - core
                    block = plane * 8 + side * 4 + (x + (0, 3, 2, 1)[slot % 4]) % 4
                    bias[PLACE[i] * 8 + slot] = jnp.where(cache_mask[y, block] == 1, 0.0, HIDDEN).astype(jnp.float32)
                else:
                    bias[PLACE[i] * 8 + slot] = jnp.float32(0.0)

        stamp = timesteps[levels[up]].astype(jnp.float32)
        count = 128
        index = lax.broadcasted_iota(jnp.int32, (8, count), 1).astype(jnp.float32)
        phase = stamp * jnp.exp(-math.log(10000.0) * index / count)
        embed = jnp.concatenate([jnp.cos(phase), jnp.sin(phase)], axis=1).astype(jnp.bfloat16)
        weight_copy.wait()

        def gate_columns(c, carry):
            columns = pl.ds(pl.multiple_of(c * WIDTH, 128), WIDTH)
            gate[:, columns] = jnp.dot(embed, weight[:, columns], preferred_element_type=jnp.float32)[0:1]
            return carry

        lax.fori_loop(0, 8, gate_columns, 0)

        peak[...] = jnp.full_like(peak, HIDDEN)
        total[...] = jnp.zeros_like(total)
        summed[...] = jnp.zeros_like(summed)

    scale = LOG2E / math.sqrt(HEAD_DIM)

    def attend(c, cached, last=False):
        def tile_of(h):
            return slice(h * KEYS, (h + 1) * KEYS)

        keys = [kv[c, 0, n].reshape(KEYS, HEAD_DIM) for n in (0, 1)]
        values = [kv[c, 1, n].reshape(KEYS, HEAD_DIM) for n in (0, 1)]

        def score(h):
            if h < GROUP:
                scored[:, tile_of(h)] = jnp.dot(
                    keys[h // (GROUP - 1)], turned[:, tile_of(h)], preferred_element_type=jnp.float32
                )

        def softmax(h):
            for first in (h * KEYS, h * KEYS + 128):
                side = slice(first, first + 128)
                scores = scored[:, side]
                if cached:
                    scores = jnp.concatenate(
                        [scores[slot * ROWS : (slot + 1) * ROWS] + bias[c * 8 + slot] for slot in range(8)], axis=0
                    )
                old = peak[:, side]
                new = jnp.maximum(old, jnp.max(scores, axis=0, keepdims=True) * scale)
                weights = jnp.exp2(scores * scale - new)
                shrink = jnp.exp2(old - new)
                peak[:, side] = new
                factor[:, side] = shrink
                total[:, side] = shrink * total[:, side] + jnp.sum(weights, axis=0, keepdims=True)
                weighed[:, side] = weights.astype(jnp.bfloat16)

        def add_values(h):
            tile = tile_of(h)
            added = lax.dot_general(
                values[h // (GROUP - 1)],
                weighed[:, tile],
                (((0,), (0,)), ((), ())),
                preferred_element_type=jnp.float32,
            )
            sums = factor[:, tile] * summed[:, tile] + added
            if not last:
                summed[:, tile] = sums
                return
            result = sums * (1.0 / total[:, tile])
            attended[h] = result.T.astype(jnp.bfloat16).reshape(8, ROWS, HEAD_DIM)
            for j in reversed(range(8)):
                back(h, j).start()

        score(0)
        score(1)
        for h in range(GROUP):
            softmax(h)
            score(h + 2)
            if h:
                add_values(h - 1)
        add_values(GROUP - 1)

    def turn_query(h, rows):
        tile = slice(h * KEYS, (h + 1) * KEYS)
        turned[:, tile] = rows.reshape(KEYS, HEAD_DIM).astype(jnp.float32).T.astype(jnp.bfloat16)

    def arrived(*items):
        for i in items:
            for which in (0, 1):
                place = landed.at[i, which]
                pltpu.make_async_copy(place, place, recv_kv.at[i, which]).wait()
            for n in range(6):
                x_copy(i, n).start()
            for copy in own_copies(i):
                copy.start()

    def gathered(*items):
        for i in items:
            for copy in own_copies(i):
                copy.wait()
            for n in range(6):
                x_copy(i, n).wait_recv()
            x_copy(i, 6).start()

    def complete(i):
        if i >= X_CHUNKS:
            y_copy(i - 5).wait_recv()
        else:
            x_copy(i, 6).wait_recv()

    def before(c):
        if c == 0:
            arrived(0)
            prepare()
            arrived(1)
            gathered(0, 1)
            y_copy(0).start()
            y_copy(1).start()
            for j in (1, 2, 3, 4):
                query_over_z(j).wait_recv()
            start_kv(1)
            start_kv(2)
            own_query.wait()
            for j in (5, 6, 7):
                query_over_z(j).wait_recv()
            for n in range(3):
                query_over_x(n).start()
            for j in (3, 4, 5, 6, 7):
                start_kv(j)
            turn_query(0, query[:, :, of_head(x)])
            turn_query(4, query[:, :, shared])
            for n in range(3):
                query_over_x(n).wait_recv()
            for n in range(3):
                turn_query(n + 1, row_query[n])
        if c == 1:
            for n in (0, 1):
                y_copy(n).wait_recv()
                y_copy(n + 2).start()
                y_copy(n + 4).start()
            arrived(2, 3)
        if c == 3:
            y_copy(2).wait_recv()
            y_copy(3).wait_recv()
            y_copy(6).start()
        if c == 3:
            gathered(2, 3)
        if c == 5:
            arrived(4, 5)
        if c == 6:
            gathered(4)
        if c == 7:
            gathered(5)
            arrived(6)
        if c == 8:
            arrived(7)
        if c == 9:
            gathered(6, 7)
            arrived(8)
        if c == 11:
            gathered(8)
        complete(ATTEND[c])

    def turn(c, carry):
        cached = False
        for now in range(CHUNKS - 1):
            pl.when(c == now)(functools.partial(before, now))
            if ATTEND[now] == 1 or ATTEND[now] >= X_CHUNKS:
                cached = cached | (c == now)
        pl.when(cached)(functools.partial(attend, c, True))
        pl.when(jnp.logical_not(cached))(functools.partial(attend, c, False))
        return carry

    lax.fori_loop(0, CHUNKS - 1, turn, 0)
    before(CHUNKS - 1)
    attend(CHUNKS - 1, False, True)

    @pl.when(core != zh)
    def _():
        cache_across(0).wait_send()
        cache_across(1).wait_send()

    for j in range(1, 8):
        query_over_z(j).wait_send()
        kv_over_z(j, 0).wait_send()
        kv_over_z(j, 1).wait_send()

    for i in range(X_CHUNKS):
        for n in range(7):
            x_copy(i, n).wait_send()
    for n in range(8):
        y_copy(n).wait_send()
    for n in range(3):
        query_over_x(n).wait_send()

    y_copy(7).wait_recv()
    for tile in range(GROUP):
        for j in range(8):
            back(tile, j).wait_recv()
    for tile in range(GROUP):
        for j in range(8):
            back(tile, j).wait_send()


def shards(
    latent, query_in, key_in, value_in, cache_keys, cache_values, levels, timesteps, cache_mask, time_weight
):
    anywhere = pl.BlockSpec(memory_space=pl.ANY)
    bf16, f32, i32 = jnp.bfloat16, jnp.float32, jnp.int32
    dma = pltpu.SemaphoreType.DMA
    returned, shifted, gate = pl.pallas_call(
        kernel,
        out_shape=(
            jax.ShapeDtypeStruct(latent.shape, bf16),
            jax.ShapeDtypeStruct(latent.shape, bf16),
            jax.ShapeDtypeStruct((1, latent.shape[1]), f32),
        ),
        in_specs=[anywhere] * 10,
        out_specs=(anywhere, anywhere, pl.BlockSpec(memory_space=pltpu.VMEM)),
        scratch_shapes=[
            pltpu.SMEM(levels.shape, i32),
            pltpu.SMEM(timesteps.shape, i32),
            pltpu.SMEM(cache_mask.shape, i32),
            pltpu.VMEM((8, ROWS, WIDTH), bf16),
            pltpu.VMEM((3, 8, ROWS, HEAD_DIM), bf16),
            pltpu.VMEM((HEAD_DIM, GROUP * KEYS), bf16),
            pltpu.VMEM((X_CHUNKS, 2, ROWS, WIDTH), bf16),
            pltpu.VMEM((CHUNKS, 2, 2, 8, ROWS, HEAD_DIM), bf16),
            pltpu.VMEM((GROUP, 8, ROWS, HEAD_DIM), bf16),
            pltpu.VMEM(time_weight.shape, bf16),
            pltpu.VMEM((KEYS, GROUP * KEYS), f32),
            pltpu.VMEM((KEYS, GROUP * KEYS), bf16),
            pltpu.VMEM((1, GROUP * KEYS), f32),
            pltpu.VMEM((1, GROUP * KEYS), f32),
            pltpu.VMEM((1, GROUP * KEYS), f32),
            pltpu.VMEM((HEAD_DIM, GROUP * KEYS), f32),
            pltpu.SMEM((CHUNKS * 8,), f32),
            dma((8, 3)),
            dma((X_CHUNKS, 7)),
            dma((8,)),
            dma((3,)),
            dma((GROUP, 8)),
            dma((8,)),
            dma((X_CHUNKS, 2)),
            dma((X_CHUNKS, 7)),
            dma((8,)),
            dma((3,)),
            dma((GROUP, 8)),
            dma((4,)),
            dma((X_CHUNKS, 2)),
        ],
        compiler_params=pltpu.CompilerParams(
            collective_id=0, has_side_effects=True, vmem_limit_bytes=64 * 1024 * 1024
        ),
        cost_estimate=pl.CostEstimate(flops=2 * 10**9, bytes_accessed=5 * 10**6, transcendentals=4 * 10**6),
    )(
        levels, timesteps, cache_mask, latent, query_in, key_in, value_in, cache_keys, cache_values, time_weight
    )
    return (shifted.astype(f32) + gate * returned.astype(f32)).astype(bf16)


def solution(mesh):
    return jax.shard_map(
        shards,
        mesh=mesh,
        in_specs=(
            P(("chain", "head"), None),
            P(("chain", "head"), None),
            P(("chain", "head"), None),
            P(("chain", "head"), None),
            P("chain", "head"),
            P("chain", "head"),
            P(),
            P(),
            P(),
            P(),
        ),
        out_specs=P(("chain", "head"), None),
        check_vma=False,
    )
```

```python
import functools
import math

import jax
import jax.numpy as jnp
from jax import lax
from jax.experimental import pallas as pl
from jax.experimental.pallas import tpu as pltpu
from jax.sharding import PartitionSpec as P

MESH = pl.DeviceIdType.MESH
HEAD_DIM = 128
SPANS = 4
NY, NX, NZ = 4, 4, 8
GROUP = 5
WIDTH = GROUP * HEAD_DIM
ROWS = 32
HOPS = (0, 1, 7, 2, 6, 3, 5, 4)
CHUNKS = 12
FIRST_Z = 2
X_CHUNKS = 9
KEYS = 8 * ROWS
RELAYED = 2
LOG2E = 1.4426950408889634
ATTEND = (0, 1, 9, 10, 2, 3, 11, 4, 5, 6, 7, 8)
PLACE = tuple(ATTEND.index(i) for i in range(CHUNKS))
HIDDEN = -1e30


def device(y, z, x, core):
    return {"chain": (y * 2 + z // 4) * NX + x, "head": (z % 4) * 2 + core}


def group_of(z):
    return (z % 4) * 2 + z // 4


def group_columns(z):
    return pl.ds(pl.multiple_of(group_of(z) * WIDTH, 128), WIDTH)


def kernel(
    levels_in, timesteps_in, mask_in, latent, query_in, key_in, value_in, cache_keys, cache_values, time_weight,
    returned, shifted, gate,
    levels, timesteps, cache_mask, query, row_query, turned, landed, relay, relay_o, kv, attended, weight,
    scored, weighed, factor, peak, total, summed, bias,
    send_z, send_x, send_y, send_q, send_o, recv_q, recv_kv, recv_relay, recv_x, recv_y, recv_rq, recv_o, local, own_x,
):
    chain, head = lax.axis_index("chain"), lax.axis_index("head")
    y, x = chain // 8, chain % 4
    zh, zl, core = (chain // 4) % 2, head // 2, head % 2
    z = zh * 4 + zl
    up, down = (y + 1) % 4, (y + 3) % 4
    x_right, x_left, x_far = (x + 1) % 4, (x + 3) % 4, (x + 2) % 4
    right, left, far = (device(y, z, to, core) for to in (x_right, x_left, x_far))
    sibling = device(y, z, x, 1 - core)
    across = device(y, (z + 4) % 8, x, 1 - core)
    to_up, to_down = device(up, z, x, core), device(down, z, x, core)
    on_two = device(y, (z + 2) % 8, x, core)
    mine = group_columns(z)

    def remote(src, dst, send, recv, to):
        return pltpu.make_async_remote_copy(
            src_ref=src, dst_ref=dst, send_sem=send, recv_sem=recv, device_id=to, device_id_type=MESH
        )

    def of_head(h):
        return pl.ds(pl.multiple_of(h * HEAD_DIM, 128), HEAD_DIM)

    own_query = pltpu.make_async_copy(query_in.at[:, mine], query.at[0], recv_q.at[0])
    own_query.start()
    pltpu.make_async_copy(key_in.at[:, mine], landed.at[0, 0], recv_kv.at[0, 0]).start()
    pltpu.make_async_copy(value_in.at[:, mine], landed.at[0, 1], recv_kv.at[0, 1]).start()
    weight_copy = pltpu.make_async_copy(time_weight, weight, local.at[0])
    weight_copy.start()
    scalar_copies = [
        pltpu.make_async_copy(source, place, local.at[n])
        for n, (source, place) in enumerate(
            ((levels_in, levels), (timesteps_in, timesteps), (mask_in, cache_mask)), start=1
        )
    ]
    for copy in scalar_copies:
        copy.start()

    @pl.when(core == zh)
    def _():
        pltpu.make_async_copy(cache_keys, landed.at[1, 0], recv_kv.at[1, 0]).start()
        pltpu.make_async_copy(cache_values, landed.at[1, 1], recv_kv.at[1, 1]).start()

    barrier = pltpu.get_barrier_semaphore()
    partners = [sibling, across, right, left, far, to_up, to_down]
    partners += [device(y, (z + hop) % 8, x, core) for hop in HOPS[1:]]
    for partner in partners:
        pl.semaphore_signal(barrier, inc=1, device_id=partner, device_id_type=MESH)
    pl.semaphore_wait(barrier, len(partners))

    def cache_across(which):
        source = (cache_keys, cache_values)[which]
        return remote(source, landed.at[1, which], send_z.at[0, which], recv_kv.at[1, which], across)

    def query_over_z(j):
        to = (z + HOPS[j]) % 8
        return remote(
            query_in.at[:, group_columns(to)], query.at[j], send_z.at[j, 2], recv_q.at[j], device(y, to, x, core)
        )

    def kv_over_z(j, which):
        to = (z + HOPS[j]) % 8
        source = (key_in, value_in)[which].at[:, group_columns(to)]
        if HOPS[j] == 4:
            return remote(source, relay.at[which], send_z.at[j, which], recv_relay.at[which], on_two)
        return remote(
            source, landed.at[j + 1, which], send_z.at[j, which], recv_kv.at[j + 1, which], device(y, to, x, core)
        )

    def relay_on(which):
        return remote(relay.at[which], landed.at[8, which], send_z.at[8, which], recv_kv.at[8, which], on_two)

    shared = slice((GROUP - 1) * HEAD_DIM, GROUP * HEAD_DIM)

    def chunk(i):
        return kv.at[PLACE[i]]

    def own_copies(i):
        return (
            pltpu.make_async_copy(landed.at[i, :, :, of_head(x)], chunk(i).at[:, 0, 0], own_x.at[i, 0]),
            pltpu.make_async_copy(landed.at[i, :, :, shared], chunk(i).at[:, 1, 0], own_x.at[i, 1]),
        )

    def x_copy(i, n):
        src, dst, to = (
            lambda: (landed.at[i, :, :, of_head(x_right)], chunk(i).at[:, 0, 1], right),
            lambda: (landed.at[i, :, :, shared], chunk(i).at[:, 1, 1], right),
            lambda: (landed.at[i, :, :, of_head(x_left)], chunk(i).at[:, 0, 3], left),
            lambda: (landed.at[i, :, :, shared], chunk(i).at[:, 1, 3], left),
            lambda: (landed.at[i, :, :, of_head(x_far)], chunk(i).at[:, 0, 2], far),
            lambda: (landed.at[i, :, :, shared], chunk(i).at[:, 1, 2], far),
            lambda: (chunk(i).at[:, :, 0:4], chunk(i).at[:, :, 4:8], sibling),
        )[n]()
        return remote(src, dst, send_x.at[i, n], recv_x.at[i, n], to)

    def y_copy(n):
        src, dst, to = (
            lambda: (chunk(1).at[:, :, 0:4], chunk(9).at[:, :, 0:4], to_up),
            lambda: (chunk(1).at[:, :, 0:4], chunk(10).at[:, :, 0:4], to_down),
            lambda: (chunk(9).at[0, :, 0:4], chunk(11).at[0, :, 0:4], to_up),
            lambda: (chunk(10).at[1, :, 0:4], chunk(11).at[1, :, 0:4], to_down),
            lambda: (chunk(9).at[:, :, 0:4], chunk(9).at[:, :, 4:8], sibling),
            lambda: (chunk(10).at[:, :, 0:4], chunk(10).at[:, :, 4:8], sibling),
            lambda: (chunk(11).at[:, :, 0:4], chunk(11).at[:, :, 4:8], sibling),
            lambda: (latent, shifted, to_down),
        )[n]()
        return remote(src, dst, send_y.at[n], recv_y.at[n], to)

    def query_over_x(n):
        to, slot = ((x_right, 0), (x_far, 1), (x_left, 2))[n]
        return remote(
            query.at[:, :, of_head(to)], row_query.at[slot], send_q.at[n], recv_rq.at[n], device(y, z, to, core)
        )

    def back(tile, j):
        to_x, of = (x, GROUP - 1) if tile == GROUP - 1 else ((x + (0, 3, 2, 1)[tile]) % 4, x)
        if HOPS[j] == 4 and tile < RELAYED:
            to = device(down, (z + 2) % 8, to_x, core)
            return remote(attended.at[tile, j], relay_o.at[tile], send_o.at[tile, j], recv_relay.at[2 + tile], to)
        to = device(down, (z - HOPS[j] + 8) % 8, to_x, core)
        columns = pl.ds(pl.multiple_of(group_of(z) * WIDTH + of * HEAD_DIM, 128), HEAD_DIM)
        return remote(attended.at[tile, j], returned.at[:, columns], send_o.at[tile, j], recv_o.at[tile, j], to)

    def back_on(tile):
        first = group_of((z + 6) % 8) * WIDTH + (x + tile) % 4 * HEAD_DIM
        columns = pl.ds(pl.multiple_of(first, 128), HEAD_DIM)
        return remote(relay_o.at[tile], returned.at[:, columns], send_o.at[tile, 8], recv_o.at[tile, 7], on_two)

    def start_kv(j):
        kv_over_z(j, 0).start()
        kv_over_z(j, 1).start()

    @pl.when(core != zh)
    def _():
        cache_across(0).start()
        cache_across(1).start()

    for j in reversed(range(1, 8)):
        query_over_z(j).start()
    start_kv(7)
    y_copy(7).start()

    def prepare():
        for copy in scalar_copies:
            copy.wait()
        for i in range(CHUNKS):
            for slot in range(8):
                if i == 1 or i >= 9:
                    plane = {1: y, 9: down, 10: up, 11: (y + 2) % 4}[i]
                    side = core if slot < 4 else 1 - core
                    block = plane * 8 + side * 4 + (x + (0, 3, 2, 1)[slot % 4]) % 4
                    bias[PLACE[i] * 8 + slot] = jnp.where(cache_mask[y, block] == 1, 0.0, HIDDEN).astype(jnp.float32)
                else:
                    bias[PLACE[i] * 8 + slot] = jnp.float32(0.0)

        stamp = timesteps[levels[up]].astype(jnp.float32)
        count = 128
        index = lax.broadcasted_iota(jnp.int32, (8, count), 1).astype(jnp.float32)
        phase = stamp * jnp.exp(-math.log(10000.0) * index / count)
        embed = jnp.concatenate([jnp.cos(phase), jnp.sin(phase)], axis=1).astype(jnp.bfloat16)
        weight_copy.wait()

        def gate_columns(c, carry):
            columns = pl.ds(pl.multiple_of(c * WIDTH, 128), WIDTH)
            gate[:, columns] = jnp.dot(embed, weight[:, columns], preferred_element_type=jnp.float32)[0:1]
            return carry

        lax.fori_loop(0, 8, gate_columns, 0)

        peak[...] = jnp.full_like(peak, HIDDEN)
        total[...] = jnp.zeros_like(total)
        summed[...] = jnp.zeros_like(summed)

    scale = LOG2E / math.sqrt(HEAD_DIM)

    def attend(c, cached, last=False):
        def tile_of(h):
            return slice(h * KEYS, (h + 1) * KEYS)

        keys = [kv[c, 0, n].reshape(KEYS, HEAD_DIM) for n in (0, 1)]
        values = [kv[c, 1, n].reshape(KEYS, HEAD_DIM) for n in (0, 1)]

        def score(h):
            if h < GROUP:
                scored[:, tile_of(h)] = jnp.dot(
                    keys[h // (GROUP - 1)], turned[:, tile_of(h)], preferred_element_type=jnp.float32
                )

        def softmax(h):
            for first in (h * KEYS, h * KEYS + 128):
                side = slice(first, first + 128)
                scores = scored[:, side]
                if cached:
                    scores = jnp.concatenate(
                        [scores[slot * ROWS : (slot + 1) * ROWS] + bias[c * 8 + slot] for slot in range(8)], axis=0
                    )
                old = peak[:, side]
                new = jnp.maximum(old, jnp.max(scores, axis=0, keepdims=True) * scale)
                weights = jnp.exp2(scores * scale - new)
                shrink = jnp.exp2(old - new)
                peak[:, side] = new
                factor[:, side] = shrink
                total[:, side] = shrink * total[:, side] + jnp.sum(weights, axis=0, keepdims=True)
                weighed[:, side] = weights.astype(jnp.bfloat16)

        def add_values(h):
            tile = tile_of(h)
            added = lax.dot_general(
                values[h // (GROUP - 1)],
                weighed[:, tile],
                (((0,), (0,)), ((), ())),
                preferred_element_type=jnp.float32,
            )
            sums = factor[:, tile] * summed[:, tile] + added
            if not last:
                summed[:, tile] = sums
                return
            result = sums * (1.0 / total[:, tile])
            attended[h] = result.T.astype(jnp.bfloat16).reshape(8, ROWS, HEAD_DIM)
            for j in reversed(range(8)):
                back(h, j).start()

        score(0)
        score(1)
        for h in range(GROUP):
            softmax(h)
            score(h + 2)
            if h:
                add_values(h - 1)
        add_values(GROUP - 1)

    def turn_query(h, rows):
        tile = slice(h * KEYS, (h + 1) * KEYS)
        turned[:, tile] = rows.reshape(KEYS, HEAD_DIM).astype(jnp.float32).T.astype(jnp.bfloat16)

    def arrived(*items):
        for i in items:
            for which in (0, 1):
                place = landed.at[i, which]
                pltpu.make_async_copy(place, place, recv_kv.at[i, which]).wait()
            for n in range(6):
                x_copy(i, n).start()
            for copy in own_copies(i):
                copy.start()

    def gathered(*items):
        for i in items:
            for copy in own_copies(i):
                copy.wait()
            for n in range(6):
                x_copy(i, n).wait_recv()
            x_copy(i, 6).start()

    def complete(i):
        if i >= X_CHUNKS:
            y_copy(i - 5).wait_recv()
        else:
            x_copy(i, 6).wait_recv()

    def before(c):
        if c == 0:
            arrived(0)
            prepare()
            arrived(1)
            gathered(0, 1)
            y_copy(0).start()
            y_copy(1).start()
            for j in (1, 2, 3, 4):
                query_over_z(j).wait_recv()
            start_kv(1)
            start_kv(2)
            own_query.wait()
            for j in (5, 6, 7):
                query_over_z(j).wait_recv()
            for n in range(3):
                query_over_x(n).start()
            for j in (3, 4, 5, 6):
                start_kv(j)
            for which in (0, 1):
                kv_over_z(7, which).wait_recv()
                relay_on(which).start()
            turn_query(0, query[:, :, of_head(x)])
            turn_query(4, query[:, :, shared])
            for n in range(3):
                query_over_x(n).wait_recv()
            for n in range(3):
                turn_query(n + 1, row_query[n])
        if c == 1:
            for n in (0, 1):
                y_copy(n).wait_recv()
                y_copy(n + 2).start()
                y_copy(n + 4).start()
            arrived(2, 3)
        if c == 3:
            y_copy(2).wait_recv()
            y_copy(3).wait_recv()
            y_copy(6).start()
        if c == 3:
            gathered(2, 3)
        if c == 5:
            arrived(4, 5)
        if c == 6:
            gathered(4)
        if c == 7:
            gathered(5)
            arrived(6)
        if c == 8:
            arrived(7)
        if c == 9:
            gathered(6, 7)
            arrived(8)
        if c == 11:
            gathered(8)
        complete(ATTEND[c])

    def turn(c, carry):
        cached = False
        for now in range(CHUNKS - 1):
            pl.when(c == now)(functools.partial(before, now))
            if ATTEND[now] == 1 or ATTEND[now] >= X_CHUNKS:
                cached = cached | (c == now)
        pl.when(cached)(functools.partial(attend, c, True))
        pl.when(jnp.logical_not(cached))(functools.partial(attend, c, False))
        return carry

    lax.fori_loop(0, CHUNKS - 1, turn, 0)
    before(CHUNKS - 1)
    attend(CHUNKS - 1, False, True)

    for tile in range(RELAYED):
        back(tile, 7).wait_recv()
        back_on(tile).start()

    @pl.when(core != zh)
    def _():
        cache_across(0).wait_send()
        cache_across(1).wait_send()

    relay_on(0).wait_send()
    relay_on(1).wait_send()
    for j in range(1, 8):
        query_over_z(j).wait_send()
        kv_over_z(j, 0).wait_send()
        kv_over_z(j, 1).wait_send()

    for i in range(X_CHUNKS):
        for n in range(7):
            x_copy(i, n).wait_send()
    for n in range(8):
        y_copy(n).wait_send()
    for n in range(3):
        query_over_x(n).wait_send()

    y_copy(7).wait_recv()
    for tile in range(GROUP):
        for j in range(8):
            if j == 7 and tile < RELAYED:
                back_on(tile).wait_recv()
            else:
                back(tile, j).wait_recv()
    for tile in range(RELAYED):
        back_on(tile).wait_send()
    for tile in range(GROUP):
        for j in range(8):
            back(tile, j).wait_send()


def shards(
    latent, query_in, key_in, value_in, cache_keys, cache_values, levels, timesteps, cache_mask, time_weight
):
    anywhere = pl.BlockSpec(memory_space=pl.ANY)
    bf16, f32, i32 = jnp.bfloat16, jnp.float32, jnp.int32
    dma = pltpu.SemaphoreType.DMA
    returned, shifted, gate = pl.pallas_call(
        kernel,
        out_shape=(
            jax.ShapeDtypeStruct(latent.shape, bf16),
            jax.ShapeDtypeStruct(latent.shape, bf16),
            jax.ShapeDtypeStruct((1, latent.shape[1]), f32),
        ),
        in_specs=[anywhere] * 10,
        out_specs=(anywhere, anywhere, pl.BlockSpec(memory_space=pltpu.VMEM)),
        scratch_shapes=[
            pltpu.SMEM(levels.shape, i32),
            pltpu.SMEM(timesteps.shape, i32),
            pltpu.SMEM(cache_mask.shape, i32),
            pltpu.VMEM((8, ROWS, WIDTH), bf16),
            pltpu.VMEM((3, 8, ROWS, HEAD_DIM), bf16),
            pltpu.VMEM((HEAD_DIM, GROUP * KEYS), bf16),
            pltpu.VMEM((X_CHUNKS, 2, ROWS, WIDTH), bf16),
            pltpu.VMEM((2, ROWS, WIDTH), bf16),
            pltpu.VMEM((RELAYED, ROWS, HEAD_DIM), bf16),
            pltpu.VMEM((CHUNKS, 2, 2, 8, ROWS, HEAD_DIM), bf16),
            pltpu.VMEM((GROUP, 8, ROWS, HEAD_DIM), bf16),
            pltpu.VMEM(time_weight.shape, bf16),
            pltpu.VMEM((KEYS, GROUP * KEYS), f32),
            pltpu.VMEM((KEYS, GROUP * KEYS), bf16),
            pltpu.VMEM((1, GROUP * KEYS), f32),
            pltpu.VMEM((1, GROUP * KEYS), f32),
            pltpu.VMEM((1, GROUP * KEYS), f32),
            pltpu.VMEM((HEAD_DIM, GROUP * KEYS), f32),
            pltpu.SMEM((CHUNKS * 8,), f32),
            dma((9, 3)),
            dma((X_CHUNKS, 7)),
            dma((8,)),
            dma((3,)),
            dma((GROUP, 9)),
            dma((8,)),
            dma((X_CHUNKS, 2)),
            dma((2 + RELAYED,)),
            dma((X_CHUNKS, 7)),
            dma((8,)),
            dma((3,)),
            dma((GROUP, 8)),
            dma((4,)),
            dma((X_CHUNKS, 2)),
        ],
        compiler_params=pltpu.CompilerParams(
            collective_id=0, has_side_effects=True, vmem_limit_bytes=64 * 1024 * 1024
        ),
        cost_estimate=pl.CostEstimate(flops=2 * 10**9, bytes_accessed=5 * 10**6, transcendentals=4 * 10**6),
    )(
        levels, timesteps, cache_mask, latent, query_in, key_in, value_in, cache_keys, cache_values, time_weight
    )
    return (shifted.astype(f32) + gate * returned.astype(f32)).astype(bf16)


def solution(mesh):
    return jax.shard_map(
        shards,
        mesh=mesh,
        in_specs=(
            P(("chain", "head"), None),
            P(("chain", "head"), None),
            P(("chain", "head"), None),
            P(("chain", "head"), None),
            P("chain", "head"),
            P("chain", "head"),
            P(),
            P(),
            P(),
            P(),
        ),
        out_specs=P(("chain", "head"), None),
        check_vma=False,
    )
```

```python
import functools
import math

import jax
import jax.numpy as jnp
from jax import lax
from jax.experimental import pallas as pl
from jax.experimental.pallas import tpu as pltpu
from jax.sharding import PartitionSpec as P

MESH = pl.DeviceIdType.MESH
HEAD_DIM = 128
SPANS = 4
NY, NX, NZ = 4, 4, 8
GROUP = 5
WIDTH = GROUP * HEAD_DIM
ROWS = 32
HOPS = (0, 1, 7, 2, 6, 3, 5, 4)
CHUNKS = 12
FIRST_Z = 2
X_CHUNKS = 9
KEYS = 8 * ROWS
LOG2E = 1.4426950408889634
ATTEND = (0, 1, 9, 10, 2, 3, 11, 4, 5, 6, 7, 8)
PLACE = tuple(ATTEND.index(i) for i in range(CHUNKS))
HIDDEN = -1e30


def device(y, z, x, core):
    return {"chain": (y * 2 + z // 4) * NX + x, "head": (z % 4) * 2 + core}


def group_of(z):
    return (z % 4) * 2 + z // 4


def group_columns(z):
    return pl.ds(pl.multiple_of(group_of(z) * WIDTH, 128), WIDTH)


def kernel(
    levels_in, timesteps_in, mask_in, latent, query_in, key_in, value_in, cache_keys, cache_values, time_weight,
    returned, shifted, gate,
    levels, timesteps, cache_mask, query, row_query, turned, landed, kv, attended, weight,
    scored, weighed, factor, peak, total, summed, bias,
    send_z, send_x, send_y, send_q, send_o, recv_q, recv_kv, recv_x, recv_y, recv_rq, recv_o, local, own_x,
):
    chain, head = lax.axis_index("chain"), lax.axis_index("head")
    y, x = chain // 8, chain % 4
    zh, zl, core = (chain // 4) % 2, head // 2, head % 2
    z = zh * 4 + zl
    up, down = (y + 1) % 4, (y + 3) % 4
    x_right, x_left, x_far = (x + 1) % 4, (x + 3) % 4, (x + 2) % 4
    right, left, far = (device(y, z, to, core) for to in (x_right, x_left, x_far))
    sibling = device(y, z, x, 1 - core)
    across = device(y, (z + 4) % 8, x, 1 - core)
    to_up, to_down = device(up, z, x, core), device(down, z, x, core)
    mine = group_columns(z)

    def remote(src, dst, send, recv, to):
        return pltpu.make_async_remote_copy(
            src_ref=src, dst_ref=dst, send_sem=send, recv_sem=recv, device_id=to, device_id_type=MESH
        )

    def of_head(h):
        return pl.ds(pl.multiple_of(h * HEAD_DIM, 128), HEAD_DIM)

    own_query = pltpu.make_async_copy(query_in.at[:, mine], query.at[0], recv_q.at[0])
    own_query.start()
    pltpu.make_async_copy(key_in.at[:, mine], landed.at[0, 0], recv_kv.at[0, 0]).start()
    pltpu.make_async_copy(value_in.at[:, mine], landed.at[0, 1], recv_kv.at[0, 1]).start()
    weight_copy = pltpu.make_async_copy(time_weight, weight, local.at[0])
    weight_copy.start()
    scalar_copies = [
        pltpu.make_async_copy(source, place, local.at[n])
        for n, (source, place) in enumerate(
            ((levels_in, levels), (timesteps_in, timesteps), (mask_in, cache_mask)), start=1
        )
    ]
    for copy in scalar_copies:
        copy.start()

    @pl.when(core == zh)
    def _():
        pltpu.make_async_copy(cache_keys, landed.at[1, 0], recv_kv.at[1, 0]).start()
        pltpu.make_async_copy(cache_values, landed.at[1, 1], recv_kv.at[1, 1]).start()

    barrier = pltpu.get_barrier_semaphore()
    partners = [sibling, across, right, left, far, to_up, to_down]
    partners += [device(y, (z + hop) % 8, x, core) for hop in HOPS[1:]]
    for partner in partners:
        pl.semaphore_signal(barrier, inc=1, device_id=partner, device_id_type=MESH)
    pl.semaphore_wait(barrier, len(partners))

    def cache_across(which):
        source = (cache_keys, cache_values)[which]
        return remote(source, landed.at[1, which], send_z.at[0, which], recv_kv.at[1, which], across)

    def query_over_z(j):
        to = (z + HOPS[j]) % 8
        return remote(
            query_in.at[:, group_columns(to)], query.at[j], send_z.at[j, 2], recv_q.at[j], device(y, to, x, core)
        )

    def kv_over_z(j, which):
        to = (z + HOPS[j]) % 8
        source = (key_in, value_in)[which].at[:, group_columns(to)]
        return remote(
            source, landed.at[j + 1, which], send_z.at[j, which], recv_kv.at[j + 1, which], device(y, to, x, core)
        )

    shared = slice((GROUP - 1) * HEAD_DIM, GROUP * HEAD_DIM)

    def chunk(i):
        return kv.at[PLACE[i]]

    def own_copies(i):
        return (
            pltpu.make_async_copy(landed.at[i, :, :, of_head(x)], chunk(i).at[:, 0, 0], own_x.at[i, 0]),
            pltpu.make_async_copy(landed.at[i, :, :, shared], chunk(i).at[:, 1, 0], own_x.at[i, 1]),
        )

    def x_copy(i, n):
        src, dst, to = (
            lambda: (landed.at[i, :, :, of_head(x_right)], chunk(i).at[:, 0, 1], right),
            lambda: (landed.at[i, :, :, shared], chunk(i).at[:, 1, 1], right),
            lambda: (landed.at[i, :, :, of_head(x_left)], chunk(i).at[:, 0, 3], left),
            lambda: (landed.at[i, :, :, shared], chunk(i).at[:, 1, 3], left),
            lambda: (landed.at[i, :, :, of_head(x_far)], chunk(i).at[:, 0, 2], far),
            lambda: (landed.at[i, :, :, shared], chunk(i).at[:, 1, 2], far),
            lambda: (chunk(i).at[:, :, 0:4], chunk(i).at[:, :, 4:8], sibling),
        )[n]()
        return remote(src, dst, send_x.at[i, n], recv_x.at[i, n], to)

    def y_copy(n):
        src, dst, to = (
            lambda: (chunk(1).at[:, :, 0:4], chunk(9).at[:, :, 0:4], to_up),
            lambda: (chunk(1).at[:, :, 0:4], chunk(10).at[:, :, 0:4], to_down),
            lambda: (chunk(9).at[0, :, 0:4], chunk(11).at[0, :, 0:4], to_up),
            lambda: (chunk(10).at[1, :, 0:4], chunk(11).at[1, :, 0:4], to_down),
            lambda: (chunk(9).at[:, :, 0:4], chunk(9).at[:, :, 4:8], sibling),
            lambda: (chunk(10).at[:, :, 0:4], chunk(10).at[:, :, 4:8], sibling),
            lambda: (chunk(11).at[:, :, 0:4], chunk(11).at[:, :, 4:8], sibling),
            lambda: (latent, shifted, to_down),
        )[n]()
        return remote(src, dst, send_y.at[n], recv_y.at[n], to)

    def query_over_x(n):
        to, slot = ((x_right, 0), (x_far, 1), (x_left, 2))[n]
        return remote(
            query.at[:, :, of_head(to)], row_query.at[slot], send_q.at[n], recv_rq.at[n], device(y, z, to, core)
        )

    def back(tile, j):
        to_x, of = (x, GROUP - 1) if tile == GROUP - 1 else ((x + (0, 3, 2, 1)[tile]) % 4, x)
        to = device(down, (z - HOPS[j] + 8) % 8, to_x, core)
        columns = pl.ds(pl.multiple_of(group_of(z) * WIDTH + of * HEAD_DIM, 128), HEAD_DIM)
        return remote(attended.at[tile, j], returned.at[:, columns], send_o.at[tile, j], recv_o.at[tile, j], to)

    def start_kv(j):
        kv_over_z(j, 0).start()
        kv_over_z(j, 1).start()

    @pl.when(core != zh)
    def _():
        cache_across(0).start()
        cache_across(1).start()

    for j in reversed(range(1, 8)):
        query_over_z(j).start()
    y_copy(7).start()

    def prepare():
        for copy in scalar_copies:
            copy.wait()
        for i in range(CHUNKS):
            for slot in range(8):
                if i == 1 or i >= 9:
                    plane = {1: y, 9: down, 10: up, 11: (y + 2) % 4}[i]
                    side = core if slot < 4 else 1 - core
                    block = plane * 8 + side * 4 + (x + (0, 3, 2, 1)[slot % 4]) % 4
                    bias[PLACE[i] * 8 + slot] = jnp.where(cache_mask[y, block] == 1, 0.0, HIDDEN).astype(jnp.float32)
                else:
                    bias[PLACE[i] * 8 + slot] = jnp.float32(0.0)

        peak[...] = jnp.full_like(peak, HIDDEN)
        total[...] = jnp.zeros_like(total)
        summed[...] = jnp.zeros_like(summed)

    scale = LOG2E / math.sqrt(HEAD_DIM)

    def attend(c, cached, last=False):
        def tile_of(h):
            return slice(h * KEYS, (h + 1) * KEYS)

        keys = [kv[c, 0, n].reshape(KEYS, HEAD_DIM) for n in (0, 1)]
        values = [kv[c, 1, n].reshape(KEYS, HEAD_DIM) for n in (0, 1)]

        def score(h):
            if h < GROUP:
                scored[:, tile_of(h)] = jnp.dot(
                    keys[h // (GROUP - 1)], turned[:, tile_of(h)], preferred_element_type=jnp.float32
                )

        def softmax(h):
            for first in (h * KEYS, h * KEYS + 128):
                side = slice(first, first + 128)
                scores = scored[:, side]
                if cached:
                    scores = jnp.concatenate(
                        [scores[slot * ROWS : (slot + 1) * ROWS] + bias[c * 8 + slot] for slot in range(8)], axis=0
                    )
                old = peak[:, side]
                new = jnp.maximum(old, jnp.max(scores, axis=0, keepdims=True) * scale)
                weights = jnp.exp2(scores * scale - new)
                shrink = jnp.exp2(old - new)
                peak[:, side] = new
                factor[:, side] = shrink
                total[:, side] = shrink * total[:, side] + jnp.sum(weights, axis=0, keepdims=True)
                weighed[:, side] = weights.astype(jnp.bfloat16)

        def add_values(h):
            tile = tile_of(h)
            added = lax.dot_general(
                values[h // (GROUP - 1)],
                weighed[:, tile],
                (((0,), (0,)), ((), ())),
                preferred_element_type=jnp.float32,
            )
            sums = factor[:, tile] * summed[:, tile] + added
            if not last:
                summed[:, tile] = sums
                return
            result = sums * (1.0 / total[:, tile])
            attended[h] = result.T.astype(jnp.bfloat16).reshape(8, ROWS, HEAD_DIM)
            for j in reversed(range(8)):
                back(h, j).start()

        score(0)
        score(1)
        for h in range(GROUP):
            softmax(h)
            score(h + 2)
            if h:
                add_values(h - 1)
        add_values(GROUP - 1)

    def turn_query(h, rows):
        tile = slice(h * KEYS, (h + 1) * KEYS)
        turned[:, tile] = rows.reshape(KEYS, HEAD_DIM).astype(jnp.float32).T.astype(jnp.bfloat16)

    def arrived(*items):
        for i in items:
            for which in (0, 1):
                place = landed.at[i, which]
                pltpu.make_async_copy(place, place, recv_kv.at[i, which]).wait()
            for n in range(6):
                x_copy(i, n).start()
            for copy in own_copies(i):
                copy.start()

    def gathered(*items):
        for i in items:
            for copy in own_copies(i):
                copy.wait()
            for n in range(6):
                x_copy(i, n).wait_recv()
            x_copy(i, 6).start()

    def complete(i):
        if i >= X_CHUNKS:
            y_copy(i - 5).wait_recv()
        else:
            x_copy(i, 6).wait_recv()

    def before(c):
        if c == 0:
            arrived(0)
            prepare()
            arrived(1)
            gathered(0, 1)
            y_copy(0).start()
            y_copy(1).start()
            for j in (1, 2, 3, 4):
                query_over_z(j).wait_recv()
            start_kv(1)
            start_kv(2)
            own_query.wait()
            for j in (5, 6, 7):
                query_over_z(j).wait_recv()
            for n in range(3):
                query_over_x(n).start()
            for j in (3, 4, 5, 6, 7):
                start_kv(j)
            turn_query(0, query[:, :, of_head(x)])
            turn_query(4, query[:, :, shared])
            for n in range(3):
                query_over_x(n).wait_recv()
            for n in range(3):
                turn_query(n + 1, row_query[n])
        if c == 1:
            for n in (0, 1):
                y_copy(n).wait_recv()
                y_copy(n + 2).start()
                y_copy(n + 4).start()
            arrived(2, 3)
        if c == 3:
            y_copy(2).wait_recv()
            y_copy(3).wait_recv()
            y_copy(6).start()
        if c == 3:
            gathered(2, 3)
        if c == 5:
            arrived(4, 5)
        if c == 6:
            gathered(4)
        if c == 7:
            gathered(5)
            arrived(6)
        if c == 8:
            arrived(7)
        if c == 9:
            gathered(6, 7)
            arrived(8)
        if c == 11:
            gathered(8)
        complete(ATTEND[c])

    def turn(c, carry):
        cached = False
        for now in range(CHUNKS - 1):
            pl.when(c == now)(functools.partial(before, now))
            if ATTEND[now] == 1 or ATTEND[now] >= X_CHUNKS:
                cached = cached | (c == now)
        pl.when(cached)(functools.partial(attend, c, True))
        pl.when(jnp.logical_not(cached))(functools.partial(attend, c, False))
        return carry

    lax.fori_loop(0, CHUNKS - 1, turn, 0)
    before(CHUNKS - 1)
    attend(CHUNKS - 1, False, True)

    stamp = timesteps[levels[up]].astype(jnp.float32)
    count = 128
    index = lax.broadcasted_iota(jnp.int32, (8, count), 1).astype(jnp.float32)
    phase = stamp * jnp.exp(-math.log(10000.0) * index / count)
    embed = jnp.concatenate([jnp.cos(phase), jnp.sin(phase)], axis=1).astype(jnp.bfloat16)
    weight_copy.wait()

    def gate_columns(c, carry):
        columns = pl.ds(pl.multiple_of(c * WIDTH, 128), WIDTH)
        gate[:, columns] = jnp.dot(embed, weight[:, columns], preferred_element_type=jnp.float32)[0:1]
        return carry

    lax.fori_loop(0, 8, gate_columns, 0)

    @pl.when(core != zh)
    def _():
        cache_across(0).wait_send()
        cache_across(1).wait_send()

    for j in range(1, 8):
        query_over_z(j).wait_send()
        kv_over_z(j, 0).wait_send()
        kv_over_z(j, 1).wait_send()

    for i in range(X_CHUNKS):
        for n in range(7):
            x_copy(i, n).wait_send()
    for n in range(8):
        y_copy(n).wait_send()
    for n in range(3):
        query_over_x(n).wait_send()

    y_copy(7).wait_recv()
    for tile in range(GROUP):
        for j in range(8):
            back(tile, j).wait_recv()
    for tile in range(GROUP):
        for j in range(8):
            back(tile, j).wait_send()


def shards(
    latent, query_in, key_in, value_in, cache_keys, cache_values, levels, timesteps, cache_mask, time_weight
):
    anywhere = pl.BlockSpec(memory_space=pl.ANY)
    bf16, f32, i32 = jnp.bfloat16, jnp.float32, jnp.int32
    dma = pltpu.SemaphoreType.DMA
    returned, shifted, gate = pl.pallas_call(
        kernel,
        out_shape=(
            jax.ShapeDtypeStruct(latent.shape, bf16),
            jax.ShapeDtypeStruct(latent.shape, bf16),
            jax.ShapeDtypeStruct((1, latent.shape[1]), f32),
        ),
        in_specs=[anywhere] * 10,
        out_specs=(anywhere, anywhere, pl.BlockSpec(memory_space=pltpu.VMEM)),
        scratch_shapes=[
            pltpu.SMEM(levels.shape, i32),
            pltpu.SMEM(timesteps.shape, i32),
            pltpu.SMEM(cache_mask.shape, i32),
            pltpu.VMEM((8, ROWS, WIDTH), bf16),
            pltpu.VMEM((3, 8, ROWS, HEAD_DIM), bf16),
            pltpu.VMEM((HEAD_DIM, GROUP * KEYS), bf16),
            pltpu.VMEM((X_CHUNKS, 2, ROWS, WIDTH), bf16),
            pltpu.VMEM((CHUNKS, 2, 2, 8, ROWS, HEAD_DIM), bf16),
            pltpu.VMEM((GROUP, 8, ROWS, HEAD_DIM), bf16),
            pltpu.VMEM(time_weight.shape, bf16),
            pltpu.VMEM((KEYS, GROUP * KEYS), f32),
            pltpu.VMEM((KEYS, GROUP * KEYS), bf16),
            pltpu.VMEM((1, GROUP * KEYS), f32),
            pltpu.VMEM((1, GROUP * KEYS), f32),
            pltpu.VMEM((1, GROUP * KEYS), f32),
            pltpu.VMEM((HEAD_DIM, GROUP * KEYS), f32),
            pltpu.SMEM((CHUNKS * 8,), f32),
            dma((8, 3)),
            dma((X_CHUNKS, 7)),
            dma((8,)),
            dma((3,)),
            dma((GROUP, 8)),
            dma((8,)),
            dma((X_CHUNKS, 2)),
            dma((X_CHUNKS, 7)),
            dma((8,)),
            dma((3,)),
            dma((GROUP, 8)),
            dma((4,)),
            dma((X_CHUNKS, 2)),
        ],
        compiler_params=pltpu.CompilerParams(
            collective_id=0, has_side_effects=True, vmem_limit_bytes=64 * 1024 * 1024
        ),
        cost_estimate=pl.CostEstimate(flops=2 * 10**9, bytes_accessed=5 * 10**6, transcendentals=4 * 10**6),
    )(
        levels, timesteps, cache_mask, latent, query_in, key_in, value_in, cache_keys, cache_values, time_weight
    )
    return (shifted.astype(f32) + gate * returned.astype(f32)).astype(bf16)


def solution(mesh):
    return jax.shard_map(
        shards,
        mesh=mesh,
        in_specs=(
            P(("chain", "head"), None),
            P(("chain", "head"), None),
            P(("chain", "head"), None),
            P(("chain", "head"), None),
            P("chain", "head"),
            P("chain", "head"),
            P(),
            P(),
            P(),
            P(),
        ),
        out_specs=P(("chain", "head"), None),
        check_vma=False,
    )
```

```python
import functools
import math

import jax
import jax.numpy as jnp
from jax import lax
from jax.experimental import pallas as pl
from jax.experimental.pallas import tpu as pltpu
from jax.sharding import PartitionSpec as P

MESH = pl.DeviceIdType.MESH
HEAD_DIM = 128
SPANS = 4
NY, NX, NZ = 4, 4, 8
GROUP = 5
WIDTH = GROUP * HEAD_DIM
ROWS = 32
HOPS = (0, 1, 7, 2, 6, 3, 5, 4)
CHUNKS = 12
FIRST_Z = 2
X_CHUNKS = 9
KEYS = 8 * ROWS
LOG2E = 1.4426950408889634
ATTEND = (0, 1, 9, 10, 2, 3, 11, 4, 5, 6, 7, 8)
PLACE = tuple(ATTEND.index(i) for i in range(CHUNKS))
HIDDEN = -1e30


def device(y, z, x, core):
    return {"chain": (y * 2 + z // 4) * NX + x, "head": (z % 4) * 2 + core}


def group_of(z):
    return (z % 4) * 2 + z // 4


def group_columns(z):
    return pl.ds(pl.multiple_of(group_of(z) * WIDTH, 128), WIDTH)


def kernel(
    levels_in, timesteps_in, mask_in, latent, query_in, key_in, value_in, cache_keys, cache_values, time_weight,
    returned, shifted, gate,
    levels, timesteps, cache_mask, query, row_query, landed, kv, attended, weight,
    scored, weighed, factor, peak, total, summed, bias,
    send_z, send_x, send_y, send_q, send_o, recv_q, recv_kv, recv_x, recv_y, recv_rq, recv_o, local, own_x,
):
    chain, head = lax.axis_index("chain"), lax.axis_index("head")
    y, x = chain // 8, chain % 4
    zh, zl, core = (chain // 4) % 2, head // 2, head % 2
    z = zh * 4 + zl
    up, down = (y + 1) % 4, (y + 3) % 4
    x_right, x_left, x_far = (x + 1) % 4, (x + 3) % 4, (x + 2) % 4
    right, left, far = (device(y, z, to, core) for to in (x_right, x_left, x_far))
    sibling = device(y, z, x, 1 - core)
    across = device(y, (z + 4) % 8, x, 1 - core)
    to_up, to_down = device(up, z, x, core), device(down, z, x, core)
    mine = group_columns(z)

    def remote(src, dst, send, recv, to):
        return pltpu.make_async_remote_copy(
            src_ref=src, dst_ref=dst, send_sem=send, recv_sem=recv, device_id=to, device_id_type=MESH
        )

    def of_head(h):
        return pl.ds(pl.multiple_of(h * HEAD_DIM, 128), HEAD_DIM)

    own_query = pltpu.make_async_copy(query_in.at[:, mine], query.at[0], recv_q.at[0])
    own_query.start()
    pltpu.make_async_copy(key_in.at[:, mine], landed.at[0, 0], recv_kv.at[0, 0]).start()
    pltpu.make_async_copy(value_in.at[:, mine], landed.at[0, 1], recv_kv.at[0, 1]).start()
    weight_copy = pltpu.make_async_copy(time_weight, weight, local.at[0])
    weight_copy.start()
    scalar_copies = [
        pltpu.make_async_copy(source, place, local.at[n])
        for n, (source, place) in enumerate(
            ((levels_in, levels), (timesteps_in, timesteps), (mask_in, cache_mask)), start=1
        )
    ]
    for copy in scalar_copies:
        copy.start()

    @pl.when(core == zh)
    def _():
        pltpu.make_async_copy(cache_keys, landed.at[1, 0], recv_kv.at[1, 0]).start()
        pltpu.make_async_copy(cache_values, landed.at[1, 1], recv_kv.at[1, 1]).start()

    barrier = pltpu.get_barrier_semaphore()
    partners = [sibling, across, right, left, far, to_up, to_down]
    partners += [device(y, (z + hop) % 8, x, core) for hop in HOPS[1:]]
    for partner in partners:
        pl.semaphore_signal(barrier, inc=1, device_id=partner, device_id_type=MESH)
    pl.semaphore_wait(barrier, len(partners))

    def cache_across(which):
        source = (cache_keys, cache_values)[which]
        return remote(source, landed.at[1, which], send_z.at[0, which], recv_kv.at[1, which], across)

    def query_over_z(j):
        to = (z + HOPS[j]) % 8
        return remote(
            query_in.at[:, group_columns(to)], query.at[j], send_z.at[j, 2], recv_q.at[j], device(y, to, x, core)
        )

    def kv_over_z(j, which):
        to = (z + HOPS[j]) % 8
        source = (key_in, value_in)[which].at[:, group_columns(to)]
        return remote(
            source, landed.at[j + 1, which], send_z.at[j, which], recv_kv.at[j + 1, which], device(y, to, x, core)
        )

    shared = slice((GROUP - 1) * HEAD_DIM, GROUP * HEAD_DIM)

    def chunk(i):
        return kv.at[PLACE[i]]

    def own_copies(i):
        return (
            pltpu.make_async_copy(landed.at[i, :, :, of_head(x)], chunk(i).at[:, 0, 0], own_x.at[i, 0]),
            pltpu.make_async_copy(landed.at[i, :, :, shared], chunk(i).at[:, 1, 0], own_x.at[i, 1]),
        )

    def x_copy(i, n):
        src, dst, to = (
            lambda: (landed.at[i, :, :, of_head(x_right)], chunk(i).at[:, 0, 1], right),
            lambda: (landed.at[i, :, :, shared], chunk(i).at[:, 1, 1], right),
            lambda: (landed.at[i, :, :, of_head(x_left)], chunk(i).at[:, 0, 3], left),
            lambda: (landed.at[i, :, :, shared], chunk(i).at[:, 1, 3], left),
            lambda: (landed.at[i, :, :, of_head(x_far)], chunk(i).at[:, 0, 2], far),
            lambda: (landed.at[i, :, :, shared], chunk(i).at[:, 1, 2], far),
            lambda: (chunk(i).at[:, :, 0:4], chunk(i).at[:, :, 4:8], sibling),
        )[n]()
        return remote(src, dst, send_x.at[i, n], recv_x.at[i, n], to)

    def y_copy(n):
        src, dst, to = (
            lambda: (chunk(1).at[:, :, 0:4], chunk(9).at[:, :, 0:4], to_up),
            lambda: (chunk(1).at[:, :, 0:4], chunk(10).at[:, :, 0:4], to_down),
            lambda: (chunk(9).at[0, :, 0:4], chunk(11).at[0, :, 0:4], to_up),
            lambda: (chunk(10).at[1, :, 0:4], chunk(11).at[1, :, 0:4], to_down),
            lambda: (chunk(9).at[:, :, 0:4], chunk(9).at[:, :, 4:8], sibling),
            lambda: (chunk(10).at[:, :, 0:4], chunk(10).at[:, :, 4:8], sibling),
            lambda: (chunk(11).at[:, :, 0:4], chunk(11).at[:, :, 4:8], sibling),
            lambda: (latent, shifted, to_down),
        )[n]()
        return remote(src, dst, send_y.at[n], recv_y.at[n], to)

    def query_over_x(n):
        to, slot = ((x_right, 1), (x_far, 2), (x_left, 3))[n]
        return remote(
            query.at[:, :, of_head(to)], row_query.at[slot], send_q.at[n], recv_rq.at[n], device(y, z, to, core)
        )

    def back(tile, j):
        to_x, of = (x, GROUP - 1) if tile == GROUP - 1 else ((x + (0, 3, 2, 1)[tile]) % 4, x)
        to = device(down, (z - HOPS[j] + 8) % 8, to_x, core)
        columns = pl.ds(pl.multiple_of(group_of(z) * WIDTH + of * HEAD_DIM, 128), HEAD_DIM)
        return remote(attended.at[tile, j], returned.at[:, columns], send_o.at[tile, j], recv_o.at[tile, j], to)

    def start_kv(j):
        kv_over_z(j, 0).start()
        kv_over_z(j, 1).start()

    @pl.when(core != zh)
    def _():
        cache_across(0).start()
        cache_across(1).start()

    for j in reversed(range(1, 8)):
        query_over_z(j).start()
    y_copy(7).start()

    def prepare():
        for copy in scalar_copies:
            copy.wait()
        slots = lax.broadcasted_iota(jnp.int32, (1, KEYS), 1) // ROWS
        for i in (1, 9, 10, 11):
            plane = {1: y, 9: down, 10: up, 11: (y + 2) % 4}[i]
            shown = jnp.zeros((1, KEYS), jnp.float32)
            for slot in range(8):
                side = core if slot < 4 else 1 - core
                block = plane * 8 + side * 4 + (x + (0, 3, 2, 1)[slot % 4]) % 4
                hidden = jnp.where(cache_mask[y, block] == 1, 0.0, HIDDEN).astype(jnp.float32)
                shown = jnp.where(slots == slot, hidden, shown)
            bias[PLACE[i]] = shown

        peak[...] = jnp.full_like(peak, HIDDEN)
        total[...] = jnp.zeros_like(total)
        summed[...] = jnp.zeros_like(summed)

    scale = LOG2E / math.sqrt(HEAD_DIM)

    def attend(c, cached, last=False):
        def tile_of(h):
            return slice(h * KEYS, (h + 1) * KEYS)

        keys = [kv[c, 0, n].reshape(KEYS, HEAD_DIM) for n in (0, 1)]
        values = [kv[c, 1, n].reshape(KEYS, HEAD_DIM) for n in (0, 1)]

        def score(h):
            if h < GROUP:
                scored[tile_of(h)] = lax.dot_general(
                    row_query[h].reshape(KEYS, HEAD_DIM),
                    keys[h // (GROUP - 1)],
                    (((1,), (1,)), ((), ())),
                    preferred_element_type=jnp.float32,
                )

        def softmax(h):
            for first in (h * KEYS, h * KEYS + 128):
                rows = slice(first, first + 128)
                sides = [scored[rows, 0:128], scored[rows, 128:256]]
                if cached:
                    sides = [sides[n] + bias[c, :, n * 128 : (n + 1) * 128] for n in (0, 1)]
                old = peak[rows]
                new = jnp.maximum(old, jnp.max(jnp.maximum(*sides), axis=1, keepdims=True) * scale)
                weights = [jnp.exp2(side * scale - new) for side in sides]
                shrink = jnp.exp2(old - new)
                peak[rows] = new
                factor[rows] = shrink
                total[rows] = shrink * total[rows] + (weights[0] + weights[1])
                weighed[rows, 0:128] = weights[0].astype(jnp.bfloat16)
                weighed[rows, 128:256] = weights[1].astype(jnp.bfloat16)

        def add_values(h):
            tile = tile_of(h)
            added = jnp.dot(weighed[tile], values[h // (GROUP - 1)], preferred_element_type=jnp.float32)
            sums = factor[tile] * summed[tile] + added
            if not last:
                summed[tile] = sums
                return
            result = sums * (1.0 / jnp.sum(total[tile], axis=1, keepdims=True))
            attended[h] = result.astype(jnp.bfloat16).reshape(8, ROWS, HEAD_DIM)
            for j in reversed(range(8)):
                back(h, j).start()

        score(0)
        score(1)
        for h in range(GROUP):
            softmax(h)
            score(h + 2)
            if h:
                add_values(h - 1)
        add_values(GROUP - 1)

    def arrived(*items):
        for i in items:
            for which in (0, 1):
                place = landed.at[i, which]
                pltpu.make_async_copy(place, place, recv_kv.at[i, which]).wait()
            for n in range(6):
                x_copy(i, n).start()
            for copy in own_copies(i):
                copy.start()

    def gathered(*items):
        for i in items:
            for copy in own_copies(i):
                copy.wait()
            for n in range(6):
                x_copy(i, n).wait_recv()
            x_copy(i, 6).start()

    def complete(i):
        if i >= X_CHUNKS:
            y_copy(i - 5).wait_recv()
        else:
            x_copy(i, 6).wait_recv()

    def before(c):
        if c == 0:
            arrived(0)
            prepare()
            arrived(1)
            gathered(0, 1)
            y_copy(0).start()
            y_copy(1).start()
            for j in (1, 2, 3, 4):
                query_over_z(j).wait_recv()
            start_kv(1)
            start_kv(2)
            own_query.wait()
            for j in (5, 6, 7):
                query_over_z(j).wait_recv()
            for n in range(3):
                query_over_x(n).start()
            for j in (3, 4, 5, 6, 7):
                start_kv(j)
            row_query[0] = query[:, :, of_head(x)]
            row_query[4] = query[:, :, shared]
            for n in range(3):
                query_over_x(n).wait_recv()
        if c == 1:
            for n in (0, 1):
                y_copy(n).wait_recv()
                y_copy(n + 2).start()
                y_copy(n + 4).start()
            arrived(2, 3)
        if c == 3:
            y_copy(2).wait_recv()
            y_copy(3).wait_recv()
            y_copy(6).start()
        if c == 3:
            gathered(2, 3)
        if c == 5:
            arrived(4, 5)
        if c == 6:
            gathered(4)
        if c == 7:
            gathered(5)
            arrived(6)
        if c == 8:
            arrived(7)
        if c == 9:
            gathered(6, 7)
            arrived(8)
        if c == 11:
            gathered(8)
        complete(ATTEND[c])

    def turn(c, carry):
        cached = False
        for now in range(CHUNKS - 1):
            pl.when(c == now)(functools.partial(before, now))
            if ATTEND[now] == 1 or ATTEND[now] >= X_CHUNKS:
                cached = cached | (c == now)
        pl.when(cached)(functools.partial(attend, c, True))
        pl.when(jnp.logical_not(cached))(functools.partial(attend, c, False))
        return carry

    lax.fori_loop(0, CHUNKS - 1, turn, 0)
    before(CHUNKS - 1)
    attend(CHUNKS - 1, False, True)

    stamp = timesteps[levels[up]].astype(jnp.float32)
    count = 128
    index = lax.broadcasted_iota(jnp.int32, (8, count), 1).astype(jnp.float32)
    phase = stamp * jnp.exp(-math.log(10000.0) * index / count)
    embed = jnp.concatenate([jnp.cos(phase), jnp.sin(phase)], axis=1).astype(jnp.bfloat16)
    weight_copy.wait()

    def gate_columns(c, carry):
        columns = pl.ds(pl.multiple_of(c * WIDTH, 128), WIDTH)
        gate[:, columns] = jnp.dot(embed, weight[:, columns], preferred_element_type=jnp.float32)[0:1]
        return carry

    lax.fori_loop(0, 8, gate_columns, 0)

    @pl.when(core != zh)
    def _():
        cache_across(0).wait_send()
        cache_across(1).wait_send()

    for j in range(1, 8):
        query_over_z(j).wait_send()
        kv_over_z(j, 0).wait_send()
        kv_over_z(j, 1).wait_send()

    for i in range(X_CHUNKS):
        for n in range(7):
            x_copy(i, n).wait_send()
    for n in range(8):
        y_copy(n).wait_send()
    for n in range(3):
        query_over_x(n).wait_send()

    y_copy(7).wait_recv()
    for tile in range(GROUP):
        for j in range(8):
            back(tile, j).wait_recv()
    for tile in range(GROUP):
        for j in range(8):
            back(tile, j).wait_send()


def shards(
    latent, query_in, key_in, value_in, cache_keys, cache_values, levels, timesteps, cache_mask, time_weight
):
    anywhere = pl.BlockSpec(memory_space=pl.ANY)
    bf16, f32, i32 = jnp.bfloat16, jnp.float32, jnp.int32
    dma = pltpu.SemaphoreType.DMA
    returned, shifted, gate = pl.pallas_call(
        kernel,
        out_shape=(
            jax.ShapeDtypeStruct(latent.shape, bf16),
            jax.ShapeDtypeStruct(latent.shape, bf16),
            jax.ShapeDtypeStruct((1, latent.shape[1]), f32),
        ),
        in_specs=[anywhere] * 10,
        out_specs=(anywhere, anywhere, pl.BlockSpec(memory_space=pltpu.VMEM)),
        scratch_shapes=[
            pltpu.SMEM(levels.shape, i32),
            pltpu.SMEM(timesteps.shape, i32),
            pltpu.SMEM(cache_mask.shape, i32),
            pltpu.VMEM((8, ROWS, WIDTH), bf16),
            pltpu.VMEM((GROUP, 8, ROWS, HEAD_DIM), bf16),
            pltpu.VMEM((X_CHUNKS, 2, ROWS, WIDTH), bf16),
            pltpu.VMEM((CHUNKS, 2, 2, 8, ROWS, HEAD_DIM), bf16),
            pltpu.VMEM((GROUP, 8, ROWS, HEAD_DIM), bf16),
            pltpu.VMEM(time_weight.shape, bf16),
            pltpu.VMEM((GROUP * KEYS, KEYS), f32),
            pltpu.VMEM((GROUP * KEYS, KEYS), bf16),
            pltpu.VMEM((GROUP * KEYS, HEAD_DIM), f32),
            pltpu.VMEM((GROUP * KEYS, HEAD_DIM), f32),
            pltpu.VMEM((GROUP * KEYS, HEAD_DIM), f32),
            pltpu.VMEM((GROUP * KEYS, HEAD_DIM), f32),
            pltpu.VMEM((CHUNKS, 1, KEYS), f32),
            dma((8, 3)),
            dma((X_CHUNKS, 7)),
            dma((8,)),
            dma((3,)),
            dma((GROUP, 8)),
            dma((8,)),
            dma((X_CHUNKS, 2)),
            dma((X_CHUNKS, 7)),
            dma((8,)),
            dma((3,)),
            dma((GROUP, 8)),
            dma((4,)),
            dma((X_CHUNKS, 2)),
        ],
        compiler_params=pltpu.CompilerParams(
            collective_id=0, has_side_effects=True, vmem_limit_bytes=64 * 1024 * 1024
        ),
        cost_estimate=pl.CostEstimate(flops=2 * 10**9, bytes_accessed=5 * 10**6, transcendentals=4 * 10**6),
    )(
        levels, timesteps, cache_mask, latent, query_in, key_in, value_in, cache_keys, cache_values, time_weight
    )
    return (shifted.astype(f32) + gate * returned.astype(f32)).astype(bf16)


def solution(mesh):
    return jax.shard_map(
        shards,
        mesh=mesh,
        in_specs=(
            P(("chain", "head"), None),
            P(("chain", "head"), None),
            P(("chain", "head"), None),
            P(("chain", "head"), None),
            P("chain", "head"),
            P("chain", "head"),
            P(),
            P(),
            P(),
            P(),
        ),
        out_specs=P(("chain", "head"), None),
        check_vma=False,
    )
```

```python
import functools
import math

import jax
import jax.numpy as jnp
from jax import lax
from jax.experimental import pallas as pl
from jax.experimental.pallas import tpu as pltpu
from jax.sharding import PartitionSpec as P

MESH = pl.DeviceIdType.MESH
HEAD_DIM = 128
SPANS = 4
NY, NX, NZ = 4, 4, 8
GROUP = 5
WIDTH = GROUP * HEAD_DIM
ROWS = 32
HOPS = (0, 1, 7, 2, 6, 3, 5, 4)
CHUNKS = 12
FIRST_Z = 2
X_CHUNKS = 9
KEYS = 8 * ROWS
LOG2E = 1.4426950408889634
ATTEND = (0, 1, 9, 10, 2, 3, 11, 4, 5, 6, 7, 8)
PLACE = tuple(ATTEND.index(i) for i in range(CHUNKS))
HIDDEN = -1e30


def device(y, z, x, core):
    return {"chain": (y * 2 + z // 4) * NX + x, "head": (z % 4) * 2 + core}


def group_of(z):
    return (z % 4) * 2 + z // 4


def group_columns(z):
    return pl.ds(pl.multiple_of(group_of(z) * WIDTH, 128), WIDTH)


def kernel(
    levels_in, timesteps_in, mask_in, latent, query_in, key_in, value_in, cache_keys, cache_values, time_weight,
    returned, shifted, gate,
    levels, timesteps, cache_mask, query, row_query, landed, kv, attended, weight,
    scored, weighed, factor, peak, total, summed, bias,
    send_z, send_x, send_y, send_q, send_o, recv_q, recv_kv, recv_x, recv_y, recv_rq, recv_o, local, own_x,
):
    chain, head = lax.axis_index("chain"), lax.axis_index("head")
    y, x = chain // 8, chain % 4
    zh, zl, core = (chain // 4) % 2, head // 2, head % 2
    z = zh * 4 + zl
    up, down = (y + 1) % 4, (y + 3) % 4
    x_right, x_left, x_far = (x + 1) % 4, (x + 3) % 4, (x + 2) % 4
    right, left, far = (device(y, z, to, core) for to in (x_right, x_left, x_far))
    sibling = device(y, z, x, 1 - core)
    across = device(y, (z + 4) % 8, x, 1 - core)
    to_up, to_down = device(up, z, x, core), device(down, z, x, core)
    mine = group_columns(z)

    def remote(src, dst, send, recv, to):
        return pltpu.make_async_remote_copy(
            src_ref=src, dst_ref=dst, send_sem=send, recv_sem=recv, device_id=to, device_id_type=MESH
        )

    def of_head(h):
        return pl.ds(pl.multiple_of(h * HEAD_DIM, 128), HEAD_DIM)

    own_query = pltpu.make_async_copy(query_in.at[:, mine], query.at[0], recv_q.at[0])
    own_query.start()
    pltpu.make_async_copy(key_in.at[:, mine], landed.at[0, 0], recv_kv.at[0, 0]).start()
    pltpu.make_async_copy(value_in.at[:, mine], landed.at[0, 1], recv_kv.at[0, 1]).start()
    weight_copy = pltpu.make_async_copy(time_weight, weight, local.at[0])
    weight_copy.start()
    scalar_copies = [
        pltpu.make_async_copy(source, place, local.at[n])
        for n, (source, place) in enumerate(
            ((levels_in, levels), (timesteps_in, timesteps), (mask_in, cache_mask)), start=1
        )
    ]
    for copy in scalar_copies:
        copy.start()

    @pl.when(core == zh)
    def _():
        pltpu.make_async_copy(cache_keys, landed.at[1, 0], recv_kv.at[1, 0]).start()
        pltpu.make_async_copy(cache_values, landed.at[1, 1], recv_kv.at[1, 1]).start()

    barrier = pltpu.get_barrier_semaphore()
    partners = [sibling, across, right, left, far, to_up, to_down]
    partners += [device(y, (z + hop) % 8, x, core) for hop in HOPS[1:]]
    for partner in partners:
        pl.semaphore_signal(barrier, inc=1, device_id=partner, device_id_type=MESH)
    pl.semaphore_wait(barrier, len(partners))

    def cache_across(which):
        source = (cache_keys, cache_values)[which]
        return remote(source, landed.at[1, which], send_z.at[0, which], recv_kv.at[1, which], across)

    def query_over_z(j):
        to = (z + HOPS[j]) % 8
        return remote(
            query_in.at[:, group_columns(to)], query.at[j], send_z.at[j, 2], recv_q.at[j], device(y, to, x, core)
        )

    def kv_over_z(j, which):
        to = (z + HOPS[j]) % 8
        source = (key_in, value_in)[which].at[:, group_columns(to)]
        return remote(
            source, landed.at[j + 1, which], send_z.at[j, which], recv_kv.at[j + 1, which], device(y, to, x, core)
        )

    shared = slice((GROUP - 1) * HEAD_DIM, GROUP * HEAD_DIM)

    def chunk(i):
        return kv.at[PLACE[i]]

    def own_copies(i):
        return (
            pltpu.make_async_copy(landed.at[i, :, :, of_head(x)], chunk(i).at[:, 0, 0], own_x.at[i, 0]),
            pltpu.make_async_copy(landed.at[i, :, :, shared], chunk(i).at[:, 1, 0], own_x.at[i, 1]),
        )

    def x_copy(i, n):
        src, dst, to = (
            lambda: (landed.at[i, :, :, of_head(x_right)], chunk(i).at[:, 0, 1], right),
            lambda: (landed.at[i, :, :, shared], chunk(i).at[:, 1, 1], right),
            lambda: (landed.at[i, :, :, of_head(x_left)], chunk(i).at[:, 0, 3], left),
            lambda: (landed.at[i, :, :, shared], chunk(i).at[:, 1, 3], left),
            lambda: (landed.at[i, :, :, of_head(x_far)], chunk(i).at[:, 0, 2], far),
            lambda: (landed.at[i, :, :, shared], chunk(i).at[:, 1, 2], far),
            lambda: (chunk(i).at[:, :, 0:4], chunk(i).at[:, :, 4:8], sibling),
        )[n]()
        return remote(src, dst, send_x.at[i, n], recv_x.at[i, n], to)

    def y_copy(n):
        src, dst, to = (
            lambda: (chunk(1).at[:, :, 0:4], chunk(9).at[:, :, 0:4], to_up),
            lambda: (chunk(1).at[:, :, 0:4], chunk(10).at[:, :, 0:4], to_down),
            lambda: (chunk(9).at[0, :, 0:4], chunk(11).at[0, :, 0:4], to_up),
            lambda: (chunk(10).at[1, :, 0:4], chunk(11).at[1, :, 0:4], to_down),
            lambda: (chunk(9).at[:, :, 0:4], chunk(9).at[:, :, 4:8], sibling),
            lambda: (chunk(10).at[:, :, 0:4], chunk(10).at[:, :, 4:8], sibling),
            lambda: (chunk(11).at[:, :, 0:4], chunk(11).at[:, :, 4:8], sibling),
            lambda: (latent, shifted, to_down),
        )[n]()
        return remote(src, dst, send_y.at[n], recv_y.at[n], to)

    def query_over_x(n):
        to, slot = ((x_right, 1), (x_far, 2), (x_left, 3))[n]
        return remote(
            query.at[:, :, of_head(to)], row_query.at[slot], send_q.at[n], recv_rq.at[n], device(y, z, to, core)
        )

    def back(tile, j):
        to_x, of = (x, GROUP - 1) if tile == GROUP - 1 else ((x + (0, 3, 2, 1)[tile]) % 4, x)
        to = device(down, (z - HOPS[j] + 8) % 8, to_x, core)
        columns = pl.ds(pl.multiple_of(group_of(z) * WIDTH + of * HEAD_DIM, 128), HEAD_DIM)
        return remote(attended.at[tile, j], returned.at[:, columns], send_o.at[tile, j], recv_o.at[tile, j], to)

    def start_kv(j):
        kv_over_z(j, 0).start()
        kv_over_z(j, 1).start()

    @pl.when(core != zh)
    def _():
        cache_across(0).start()
        cache_across(1).start()

    for j in reversed(range(1, 8)):
        query_over_z(j).start()
    y_copy(7).start()

    def prepare():
        for copy in scalar_copies:
            copy.wait()
        slots = lax.broadcasted_iota(jnp.int32, (1, KEYS), 1) // ROWS
        for i in (1, 9, 10, 11):
            plane = {1: y, 9: down, 10: up, 11: (y + 2) % 4}[i]
            shown = jnp.zeros((1, KEYS), jnp.float32)
            for slot in range(8):
                side = core if slot < 4 else 1 - core
                block = plane * 8 + side * 4 + (x + (0, 3, 2, 1)[slot % 4]) % 4
                hidden = jnp.where(cache_mask[y, block] == 1, 0.0, HIDDEN).astype(jnp.float32)
                shown = jnp.where(slots == slot, hidden, shown)
            bias[PLACE[i]] = shown

        peak[...] = jnp.full_like(peak, HIDDEN)
        total[...] = jnp.zeros_like(total)
        summed[...] = jnp.zeros_like(summed)

    scale = LOG2E / math.sqrt(HEAD_DIM)

    def attend(c, cached, last=False):
        def tile_of(h):
            return slice(h * KEYS, (h + 1) * KEYS)

        keys = [kv[c, 0, n].reshape(KEYS, HEAD_DIM) for n in (0, 1)]
        values = [kv[c, 1, n].reshape(KEYS, HEAD_DIM) for n in (0, 1)]

        def score(h):
            if h < GROUP:
                scored[tile_of(h)] = lax.dot_general(
                    row_query[h].reshape(KEYS, HEAD_DIM),
                    keys[h // (GROUP - 1)],
                    (((1,), (1,)), ((), ())),
                    preferred_element_type=jnp.float32,
                )

        def softmax(h):
            for first in (h * KEYS, h * KEYS + 128):
                rows = slice(first, first + 128)
                sides = [scored[rows, 0:128], scored[rows, 128:256]]
                if cached:
                    sides = [sides[n] + bias[c, :, n * 128 : (n + 1) * 128] for n in (0, 1)]
                old = peak[rows]
                new = jnp.maximum(old, jnp.max(jnp.maximum(*sides), axis=1, keepdims=True) * scale)
                weights = [jnp.exp2(side * scale - new) for side in sides]
                shrink = jnp.exp2(old - new)
                peak[rows] = new
                factor[rows] = shrink
                total[rows] = shrink * total[rows] + (weights[0] + weights[1])
                weighed[rows, 0:128] = weights[0].astype(jnp.bfloat16)
                weighed[rows, 128:256] = weights[1].astype(jnp.bfloat16)

        def add_values(h):
            tile = tile_of(h)
            added = jnp.dot(weighed[tile], values[h // (GROUP - 1)], preferred_element_type=jnp.float32)
            sums = factor[tile] * summed[tile] + added
            if not last:
                summed[tile] = sums
                return
            result = sums * (1.0 / jnp.sum(total[tile], axis=1, keepdims=True))
            attended[h] = result.astype(jnp.bfloat16).reshape(8, ROWS, HEAD_DIM)
            for j in reversed(range(8)):
                back(h, j).start()

        score(0)
        score(1)
        for h in range(GROUP):
            softmax(h)
            score(h + 2)
            if h:
                add_values(h - 1)
        add_values(GROUP - 1)

    def arrived(*items):
        for i in items:
            for which in (0, 1):
                place = landed.at[i, which]
                pltpu.make_async_copy(place, place, recv_kv.at[i, which]).wait()
            for n in range(6):
                x_copy(i, n).start()
            for copy in own_copies(i):
                copy.start()

    def gathered(*items):
        for i in items:
            for copy in own_copies(i):
                copy.wait()
            for n in range(6):
                x_copy(i, n).wait_recv()
            x_copy(i, 6).start()

    def complete(i):
        if i >= X_CHUNKS:
            y_copy(i - 5).wait_recv()
        else:
            x_copy(i, 6).wait_recv()

    def before(c):
        if c == 0:
            arrived(0)
            prepare()
            arrived(1)
            gathered(0, 1)
            y_copy(0).start()
            y_copy(1).start()
            for j in (1, 2, 3, 4):
                query_over_z(j).wait_recv()
            start_kv(1)
            start_kv(2)
            own_query.wait()
            for j in (5, 6, 7):
                query_over_z(j).wait_recv()
            for n in range(3):
                query_over_x(n).start()
            start_kv(3)
            start_kv(4)
            row_query[0] = query[:, :, of_head(x)]
            row_query[4] = query[:, :, shared]
            for n in range(3):
                query_over_x(n).wait_recv()
        if c == 1:
            arrived(2)
            start_kv(5)
            start_kv(6)
            arrived(3)
            for n in (0, 1):
                y_copy(n).wait_recv()
                y_copy(n + 2).start()
                y_copy(n + 4).start()
        if c == 3:
            gathered(2, 3)
            y_copy(2).wait_recv()
            y_copy(3).wait_recv()
            y_copy(6).start()
        if c == 4:
            arrived(4)
            start_kv(7)
            arrived(5)
        if c == 6:
            gathered(4, 5)
        if c == 7:
            arrived(6)
        if c == 8:
            arrived(7)
        if c == 9:
            gathered(6, 7)
            arrived(8)
        if c == 11:
            gathered(8)
        complete(ATTEND[c])

    def turn(c, carry):
        cached = False
        for now in range(CHUNKS - 1):
            pl.when(c == now)(functools.partial(before, now))
            if ATTEND[now] == 1 or ATTEND[now] >= X_CHUNKS:
                cached = cached | (c == now)
        pl.when(cached)(functools.partial(attend, c, True))
        pl.when(jnp.logical_not(cached))(functools.partial(attend, c, False))
        return carry

    lax.fori_loop(0, CHUNKS - 1, turn, 0)
    before(CHUNKS - 1)
    attend(CHUNKS - 1, False, True)

    stamp = timesteps[levels[up]].astype(jnp.float32)
    count = 128
    index = lax.broadcasted_iota(jnp.int32, (8, count), 1).astype(jnp.float32)
    phase = stamp * jnp.exp(-math.log(10000.0) * index / count)
    embed = jnp.concatenate([jnp.cos(phase), jnp.sin(phase)], axis=1).astype(jnp.bfloat16)
    weight_copy.wait()

    def gate_columns(c, carry):
        columns = pl.ds(pl.multiple_of(c * WIDTH, 128), WIDTH)
        gate[:, columns] = jnp.dot(embed, weight[:, columns], preferred_element_type=jnp.float32)[0:1]
        return carry

    lax.fori_loop(0, 8, gate_columns, 0)

    @pl.when(core != zh)
    def _():
        cache_across(0).wait_send()
        cache_across(1).wait_send()

    for j in range(1, 8):
        query_over_z(j).wait_send()
        kv_over_z(j, 0).wait_send()
        kv_over_z(j, 1).wait_send()

    for i in range(X_CHUNKS):
        for n in range(7):
            x_copy(i, n).wait_send()
    for n in range(8):
        y_copy(n).wait_send()
    for n in range(3):
        query_over_x(n).wait_send()

    y_copy(7).wait_recv()
    for tile in range(GROUP):
        for j in range(8):
            back(tile, j).wait_recv()
    for tile in range(GROUP):
        for j in range(8):
            back(tile, j).wait_send()


def shards(
    latent, query_in, key_in, value_in, cache_keys, cache_values, levels, timesteps, cache_mask, time_weight
):
    anywhere = pl.BlockSpec(memory_space=pl.ANY)
    bf16, f32, i32 = jnp.bfloat16, jnp.float32, jnp.int32
    dma = pltpu.SemaphoreType.DMA
    returned, shifted, gate = pl.pallas_call(
        kernel,
        out_shape=(
            jax.ShapeDtypeStruct(latent.shape, bf16),
            jax.ShapeDtypeStruct(latent.shape, bf16),
            jax.ShapeDtypeStruct((1, latent.shape[1]), f32),
        ),
        in_specs=[anywhere] * 10,
        out_specs=(anywhere, anywhere, pl.BlockSpec(memory_space=pltpu.VMEM)),
        scratch_shapes=[
            pltpu.SMEM(levels.shape, i32),
            pltpu.SMEM(timesteps.shape, i32),
            pltpu.SMEM(cache_mask.shape, i32),
            pltpu.VMEM((8, ROWS, WIDTH), bf16),
            pltpu.VMEM((GROUP, 8, ROWS, HEAD_DIM), bf16),
            pltpu.VMEM((X_CHUNKS, 2, ROWS, WIDTH), bf16),
            pltpu.VMEM((CHUNKS, 2, 2, 8, ROWS, HEAD_DIM), bf16),
            pltpu.VMEM((GROUP, 8, ROWS, HEAD_DIM), bf16),
            pltpu.VMEM(time_weight.shape, bf16),
            pltpu.VMEM((GROUP * KEYS, KEYS), f32),
            pltpu.VMEM((GROUP * KEYS, KEYS), bf16),
            pltpu.VMEM((GROUP * KEYS, HEAD_DIM), f32),
            pltpu.VMEM((GROUP * KEYS, HEAD_DIM), f32),
            pltpu.VMEM((GROUP * KEYS, HEAD_DIM), f32),
            pltpu.VMEM((GROUP * KEYS, HEAD_DIM), f32),
            pltpu.VMEM((CHUNKS, 1, KEYS), f32),
            dma((8, 3)),
            dma((X_CHUNKS, 7)),
            dma((8,)),
            dma((3,)),
            dma((GROUP, 8)),
            dma((8,)),
            dma((X_CHUNKS, 2)),
            dma((X_CHUNKS, 7)),
            dma((8,)),
            dma((3,)),
            dma((GROUP, 8)),
            dma((4,)),
            dma((X_CHUNKS, 2)),
        ],
        compiler_params=pltpu.CompilerParams(
            collective_id=0, has_side_effects=True, vmem_limit_bytes=64 * 1024 * 1024
        ),
        cost_estimate=pl.CostEstimate(flops=2 * 10**9, bytes_accessed=5 * 10**6, transcendentals=4 * 10**6),
    )(
        levels, timesteps, cache_mask, latent, query_in, key_in, value_in, cache_keys, cache_values, time_weight
    )
    return (shifted.astype(f32) + gate * returned.astype(f32)).astype(bf16)


def solution(mesh):
    return jax.shard_map(
        shards,
        mesh=mesh,
        in_specs=(
            P(("chain", "head"), None),
            P(("chain", "head"), None),
            P(("chain", "head"), None),
            P(("chain", "head"), None),
            P("chain", "head"),
            P("chain", "head"),
            P(),
            P(),
            P(),
            P(),
        ),
        out_specs=P(("chain", "head"), None),
        check_vma=False,
    )
```

```python
import functools
import math

import jax
import jax.numpy as jnp
from jax import lax
from jax.experimental import pallas as pl
from jax.experimental.pallas import tpu as pltpu
from jax.sharding import PartitionSpec as P

MESH = pl.DeviceIdType.MESH
HEAD_DIM = 128
SPANS = 4
NY, NX, NZ = 4, 4, 8
GROUP = 5
WIDTH = GROUP * HEAD_DIM
ROWS = 32
HOPS = (0, 1, 7, 2, 6, 3, 5, 4)
CHUNKS = 12
FIRST_Z = 2
X_CHUNKS = 9
KEYS = 8 * ROWS
LOG2E = 1.4426950408889634
ATTEND = (0, 1, 9, 10, 2, 3, 11, 4, 5, 6, 7, 8)
PLACE = tuple(ATTEND.index(i) for i in range(CHUNKS))
HIDDEN = -1e30


def device(y, z, x, core):
    return {"chain": (y * 2 + z // 4) * NX + x, "head": (z % 4) * 2 + core}


def group_of(z):
    return (z % 4) * 2 + z // 4


def group_columns(z):
    return pl.ds(pl.multiple_of(group_of(z) * WIDTH, 128), WIDTH)


def kernel(
    levels_in, timesteps_in, mask_in, latent, query_in, key_in, value_in, cache_keys, cache_values, time_weight,
    returned, shifted, gate,
    levels, timesteps, cache_mask, query, row_query, landed, kv, attended, weight,
    scored, weighed, factor, peak, total, summed, bias,
    send_z, send_x, send_y, send_q, send_o, recv_q, recv_kv, recv_x, recv_y, recv_rq, recv_o, local, own_x,
):
    chain, head = lax.axis_index("chain"), lax.axis_index("head")
    y, x = chain // 8, chain % 4
    zh, zl, core = (chain // 4) % 2, head // 2, head % 2
    z = zh * 4 + zl
    up, down = (y + 1) % 4, (y + 3) % 4
    x_right, x_left, x_far = (x + 1) % 4, (x + 3) % 4, (x + 2) % 4
    right, left, far = (device(y, z, to, core) for to in (x_right, x_left, x_far))
    sibling = device(y, z, x, 1 - core)
    across = device(y, (z + 4) % 8, x, 1 - core)
    to_up, to_down = device(up, z, x, core), device(down, z, x, core)
    mine = group_columns(z)

    def remote(src, dst, send, recv, to):
        return pltpu.make_async_remote_copy(
            src_ref=src, dst_ref=dst, send_sem=send, recv_sem=recv, device_id=to, device_id_type=MESH
        )

    def of_head(h):
        return pl.ds(pl.multiple_of(h * HEAD_DIM, 128), HEAD_DIM)

    own_query = pltpu.make_async_copy(query_in.at[:, mine], query.at[0], recv_q.at[0])
    own_query.start()
    pltpu.make_async_copy(key_in.at[:, mine], landed.at[0, 0], recv_kv.at[0, 0]).start()
    pltpu.make_async_copy(value_in.at[:, mine], landed.at[0, 1], recv_kv.at[0, 1]).start()
    weight_copy = pltpu.make_async_copy(time_weight, weight, local.at[0])
    weight_copy.start()
    scalar_copies = [
        pltpu.make_async_copy(source, place, local.at[n])
        for n, (source, place) in enumerate(
            ((levels_in, levels), (timesteps_in, timesteps), (mask_in, cache_mask)), start=1
        )
    ]
    for copy in scalar_copies:
        copy.start()

    @pl.when(core == zh)
    def _():
        pltpu.make_async_copy(cache_keys, landed.at[1, 0], recv_kv.at[1, 0]).start()
        pltpu.make_async_copy(cache_values, landed.at[1, 1], recv_kv.at[1, 1]).start()

    barrier = pltpu.get_barrier_semaphore()
    partners = [sibling, across, right, left, far, to_up, to_down]
    partners += [device(y, (z + hop) % 8, x, core) for hop in HOPS[1:]]
    for partner in partners:
        pl.semaphore_signal(barrier, inc=1, device_id=partner, device_id_type=MESH)
    pl.semaphore_wait(barrier, len(partners))

    def cache_across(which):
        source = (cache_keys, cache_values)[which]
        return remote(source, landed.at[1, which], send_z.at[0, which], recv_kv.at[1, which], across)

    def query_over_z(j):
        to = (z + HOPS[j]) % 8
        return remote(
            query_in.at[:, group_columns(to)], query.at[j], send_z.at[j, 2], recv_q.at[j], device(y, to, x, core)
        )

    def kv_over_z(j, which):
        to = (z + HOPS[j]) % 8
        source = (key_in, value_in)[which].at[:, group_columns(to)]
        return remote(
            source, landed.at[j + 1, which], send_z.at[j, which], recv_kv.at[j + 1, which], device(y, to, x, core)
        )

    shared = slice((GROUP - 1) * HEAD_DIM, GROUP * HEAD_DIM)

    def chunk(i):
        return kv.at[PLACE[i]]

    def own_copies(i):
        return (
            pltpu.make_async_copy(landed.at[i, :, :, of_head(x)], chunk(i).at[:, 0, 0], own_x.at[i, 0]),
            pltpu.make_async_copy(landed.at[i, :, :, shared], chunk(i).at[:, 1, 0], own_x.at[i, 1]),
        )

    def x_copy(i, n):
        src, dst, to = (
            lambda: (landed.at[i, :, :, of_head(x_right)], chunk(i).at[:, 0, 1], right),
            lambda: (landed.at[i, :, :, shared], chunk(i).at[:, 1, 1], right),
            lambda: (landed.at[i, :, :, of_head(x_left)], chunk(i).at[:, 0, 3], left),
            lambda: (landed.at[i, :, :, shared], chunk(i).at[:, 1, 3], left),
            lambda: (landed.at[i, :, :, of_head(x_far)], chunk(i).at[:, 0, 2], far),
            lambda: (landed.at[i, :, :, shared], chunk(i).at[:, 1, 2], far),
            lambda: (chunk(i).at[:, :, 0:4], chunk(i).at[:, :, 4:8], sibling),
        )[n]()
        return remote(src, dst, send_x.at[i, n], recv_x.at[i, n], to)

    def y_copy(n):
        src, dst, to = (
            lambda: (chunk(1).at[:, :, 0:4], chunk(9).at[:, :, 0:4], to_up),
            lambda: (chunk(1).at[:, :, 0:4], chunk(10).at[:, :, 0:4], to_down),
            lambda: (chunk(9).at[0, :, 0:4], chunk(11).at[0, :, 0:4], to_up),
            lambda: (chunk(10).at[1, :, 0:4], chunk(11).at[1, :, 0:4], to_down),
            lambda: (chunk(9).at[:, :, 0:4], chunk(9).at[:, :, 4:8], sibling),
            lambda: (chunk(10).at[:, :, 0:4], chunk(10).at[:, :, 4:8], sibling),
            lambda: (chunk(11).at[:, :, 0:4], chunk(11).at[:, :, 4:8], sibling),
            lambda: (latent, shifted, to_down),
        )[n]()
        return remote(src, dst, send_y.at[n], recv_y.at[n], to)

    def query_over_x(n):
        to, slot = ((x_right, 1), (x_far, 2), (x_left, 3))[n]
        return remote(
            query.at[:, :, of_head(to)], row_query.at[slot], send_q.at[n], recv_rq.at[n], device(y, z, to, core)
        )

    def back(tile, j):
        to_x, of = (x, GROUP - 1) if tile == GROUP - 1 else ((x + (0, 3, 2, 1)[tile]) % 4, x)
        to = device(down, (z - HOPS[j] + 8) % 8, to_x, core)
        columns = pl.ds(pl.multiple_of(group_of(z) * WIDTH + of * HEAD_DIM, 128), HEAD_DIM)
        return remote(attended.at[tile, j], returned.at[:, columns], send_o.at[tile, j], recv_o.at[tile, j], to)

    def start_kv(j):
        kv_over_z(j, 0).start()
        kv_over_z(j, 1).start()

    @pl.when(core != zh)
    def _():
        cache_across(0).start()
        cache_across(1).start()

    for j in reversed(range(1, 8)):
        query_over_z(j).start()
    start_kv(1)
    start_kv(2)
    y_copy(7).start()

    def prepare():
        for copy in scalar_copies:
            copy.wait()
        slots = lax.broadcasted_iota(jnp.int32, (1, KEYS), 1) // ROWS
        for i in (1, 9, 10, 11):
            plane = {1: y, 9: down, 10: up, 11: (y + 2) % 4}[i]
            shown = jnp.zeros((1, KEYS), jnp.float32)
            for slot in range(8):
                side = core if slot < 4 else 1 - core
                block = plane * 8 + side * 4 + (x + (0, 3, 2, 1)[slot % 4]) % 4
                hidden = jnp.where(cache_mask[y, block] == 1, 0.0, HIDDEN).astype(jnp.float32)
                shown = jnp.where(slots == slot, hidden, shown)
            bias[PLACE[i]] = shown

        peak[...] = jnp.full_like(peak, HIDDEN)
        total[...] = jnp.zeros_like(total)
        summed[...] = jnp.zeros_like(summed)

    scale = LOG2E / math.sqrt(HEAD_DIM)

    def attend(c, cached, last=False):
        def tile_of(h):
            return slice(h * KEYS, (h + 1) * KEYS)

        keys = [kv[c, 0, n].reshape(KEYS, HEAD_DIM) for n in (0, 1)]
        values = [kv[c, 1, n].reshape(KEYS, HEAD_DIM) for n in (0, 1)]

        def score(h):
            if h < GROUP:
                scored[tile_of(h)] = lax.dot_general(
                    row_query[h].reshape(KEYS, HEAD_DIM),
                    keys[h // (GROUP - 1)],
                    (((1,), (1,)), ((), ())),
                    preferred_element_type=jnp.float32,
                )

        def softmax(h):
            for first in (h * KEYS, h * KEYS + 128):
                rows = slice(first, first + 128)
                sides = [scored[rows, 0:128], scored[rows, 128:256]]
                if cached:
                    sides = [sides[n] + bias[c, :, n * 128 : (n + 1) * 128] for n in (0, 1)]
                old = peak[rows]
                new = jnp.maximum(old, jnp.max(jnp.maximum(*sides), axis=1, keepdims=True) * scale)
                weights = [jnp.exp2(side * scale - new) for side in sides]
                shrink = jnp.exp2(old - new)
                peak[rows] = new
                factor[rows] = shrink
                total[rows] = shrink * total[rows] + (weights[0] + weights[1])
                weighed[rows, 0:128] = weights[0].astype(jnp.bfloat16)
                weighed[rows, 128:256] = weights[1].astype(jnp.bfloat16)

        def add_values(h):
            tile = tile_of(h)
            added = jnp.dot(weighed[tile], values[h // (GROUP - 1)], preferred_element_type=jnp.float32)
            sums = factor[tile] * summed[tile] + added
            if not last:
                summed[tile] = sums
                return
            result = sums * (1.0 / jnp.sum(total[tile], axis=1, keepdims=True))
            attended[h] = result.astype(jnp.bfloat16).reshape(8, ROWS, HEAD_DIM)
            for j in reversed(range(8)):
                back(h, j).start()

        score(0)
        score(1)
        for h in range(GROUP):
            softmax(h)
            score(h + 2)
            if h:
                add_values(h - 1)
        add_values(GROUP - 1)

    def arrived(*items):
        for i in items:
            for which in (0, 1):
                place = landed.at[i, which]
                pltpu.make_async_copy(place, place, recv_kv.at[i, which]).wait()
            for n in range(6):
                x_copy(i, n).start()
            for copy in own_copies(i):
                copy.start()

    def gathered(*items):
        for i in items:
            for copy in own_copies(i):
                copy.wait()
            for n in range(6):
                x_copy(i, n).wait_recv()
            x_copy(i, 6).start()

    def complete(i):
        if i >= X_CHUNKS:
            y_copy(i - 5).wait_recv()
        else:
            x_copy(i, 6).wait_recv()

    def before(c):
        if c == 0:
            arrived(0)
            prepare()
            arrived(1)
            gathered(0, 1)
            y_copy(0).start()
            y_copy(1).start()
            for j in (1, 2, 3, 4):
                query_over_z(j).wait_recv()
            start_kv(3)
            start_kv(4)
            own_query.wait()
            for j in (5, 6, 7):
                query_over_z(j).wait_recv()
            for n in range(3):
                query_over_x(n).start()
            start_kv(5)
            start_kv(6)
            arrived(2, 3)
            row_query[0] = query[:, :, of_head(x)]
            row_query[4] = query[:, :, shared]
            for n in range(3):
                query_over_x(n).wait_recv()
        if c == 1:
            for n in (0, 1):
                y_copy(n).wait_recv()
                y_copy(n + 2).start()
                y_copy(n + 4).start()
        if c == 3:
            gathered(2, 3)
            arrived(4)
            start_kv(7)
            arrived(5)
            y_copy(2).wait_recv()
            y_copy(3).wait_recv()
            y_copy(6).start()
        if c == 6:
            gathered(4, 5)
        if c == 7:
            arrived(6)
        if c == 8:
            arrived(7)
        if c == 9:
            gathered(6, 7)
            arrived(8)
        if c == 11:
            gathered(8)
        complete(ATTEND[c])

    def turn(c, carry):
        cached = False
        for now in range(CHUNKS - 1):
            pl.when(c == now)(functools.partial(before, now))
            if ATTEND[now] == 1 or ATTEND[now] >= X_CHUNKS:
                cached = cached | (c == now)
        pl.when(cached)(functools.partial(attend, c, True))
        pl.when(jnp.logical_not(cached))(functools.partial(attend, c, False))
        return carry

    lax.fori_loop(0, CHUNKS - 1, turn, 0)
    before(CHUNKS - 1)
    attend(CHUNKS - 1, False, True)

    stamp = timesteps[levels[up]].astype(jnp.float32)
    count = 128
    index = lax.broadcasted_iota(jnp.int32, (8, count), 1).astype(jnp.float32)
    phase = stamp * jnp.exp(-math.log(10000.0) * index / count)
    embed = jnp.concatenate([jnp.cos(phase), jnp.sin(phase)], axis=1).astype(jnp.bfloat16)
    weight_copy.wait()

    def gate_columns(c, carry):
        columns = pl.ds(pl.multiple_of(c * WIDTH, 128), WIDTH)
        gate[:, columns] = jnp.dot(embed, weight[:, columns], preferred_element_type=jnp.float32)[0:1]
        return carry

    lax.fori_loop(0, 8, gate_columns, 0)

    @pl.when(core != zh)
    def _():
        cache_across(0).wait_send()
        cache_across(1).wait_send()

    for j in range(1, 8):
        query_over_z(j).wait_send()
        kv_over_z(j, 0).wait_send()
        kv_over_z(j, 1).wait_send()

    for i in range(X_CHUNKS):
        for n in range(7):
            x_copy(i, n).wait_send()
    for n in range(8):
        y_copy(n).wait_send()
    for n in range(3):
        query_over_x(n).wait_send()

    y_copy(7).wait_recv()
    for tile in range(GROUP):
        for j in range(8):
            back(tile, j).wait_recv()
    for tile in range(GROUP):
        for j in range(8):
            back(tile, j).wait_send()


def shards(
    latent, query_in, key_in, value_in, cache_keys, cache_values, levels, timesteps, cache_mask, time_weight
):
    anywhere = pl.BlockSpec(memory_space=pl.ANY)
    bf16, f32, i32 = jnp.bfloat16, jnp.float32, jnp.int32
    dma = pltpu.SemaphoreType.DMA
    returned, shifted, gate = pl.pallas_call(
        kernel,
        out_shape=(
            jax.ShapeDtypeStruct(latent.shape, bf16),
            jax.ShapeDtypeStruct(latent.shape, bf16),
            jax.ShapeDtypeStruct((1, latent.shape[1]), f32),
        ),
        in_specs=[anywhere] * 10,
        out_specs=(anywhere, anywhere, pl.BlockSpec(memory_space=pltpu.VMEM)),
        scratch_shapes=[
            pltpu.SMEM(levels.shape, i32),
            pltpu.SMEM(timesteps.shape, i32),
            pltpu.SMEM(cache_mask.shape, i32),
            pltpu.VMEM((8, ROWS, WIDTH), bf16),
            pltpu.VMEM((GROUP, 8, ROWS, HEAD_DIM), bf16),
            pltpu.VMEM((X_CHUNKS, 2, ROWS, WIDTH), bf16),
            pltpu.VMEM((CHUNKS, 2, 2, 8, ROWS, HEAD_DIM), bf16),
            pltpu.VMEM((GROUP, 8, ROWS, HEAD_DIM), bf16),
            pltpu.VMEM(time_weight.shape, bf16),
            pltpu.VMEM((GROUP * KEYS, KEYS), f32),
            pltpu.VMEM((GROUP * KEYS, KEYS), bf16),
            pltpu.VMEM((GROUP * KEYS, HEAD_DIM), f32),
            pltpu.VMEM((GROUP * KEYS, HEAD_DIM), f32),
            pltpu.VMEM((GROUP * KEYS, HEAD_DIM), f32),
            pltpu.VMEM((GROUP * KEYS, HEAD_DIM), f32),
            pltpu.VMEM((CHUNKS, 1, KEYS), f32),
            dma((8, 3)),
            dma((X_CHUNKS, 7)),
            dma((8,)),
            dma((3,)),
            dma((GROUP, 8)),
            dma((8,)),
            dma((X_CHUNKS, 2)),
            dma((X_CHUNKS, 7)),
            dma((8,)),
            dma((3,)),
            dma((GROUP, 8)),
            dma((4,)),
            dma((X_CHUNKS, 2)),
        ],
        compiler_params=pltpu.CompilerParams(
            collective_id=0, has_side_effects=True, vmem_limit_bytes=64 * 1024 * 1024
        ),
        cost_estimate=pl.CostEstimate(flops=2 * 10**9, bytes_accessed=5 * 10**6, transcendentals=4 * 10**6),
    )(
        levels, timesteps, cache_mask, latent, query_in, key_in, value_in, cache_keys, cache_values, time_weight
    )
    return (shifted.astype(f32) + gate * returned.astype(f32)).astype(bf16)


def solution(mesh):
    return jax.shard_map(
        shards,
        mesh=mesh,
        in_specs=(
            P(("chain", "head"), None),
            P(("chain", "head"), None),
            P(("chain", "head"), None),
            P(("chain", "head"), None),
            P("chain", "head"),
            P("chain", "head"),
            P(),
            P(),
            P(),
            P(),
        ),
        out_specs=P(("chain", "head"), None),
        check_vma=False,
    )
```

```python
import functools
import math

import jax
import jax.numpy as jnp
from jax import lax
from jax.experimental import pallas as pl
from jax.experimental.pallas import tpu as pltpu
from jax.sharding import PartitionSpec as P

MESH = pl.DeviceIdType.MESH
HEAD_DIM = 128
SPANS = 4
NY, NX, NZ = 4, 4, 8
GROUP = 5
WIDTH = GROUP * HEAD_DIM
ROWS = 32
HOPS = (0, 1, 7, 2, 6, 3, 5, 4)
CHUNKS = 12
FIRST_Z = 2
X_CHUNKS = 9
KEYS = 8 * ROWS
LOG2E = 1.4426950408889634
ATTEND = (0, 1, 9, 10, 2, 3, 11, 4, 5, 6, 7, 8)
PLACE = tuple(ATTEND.index(i) for i in range(CHUNKS))
HIDDEN = -1e30


def device(y, z, x, core):
    return {"chain": (y * 2 + z // 4) * NX + x, "head": (z % 4) * 2 + core}


def group_of(z):
    return (z % 4) * 2 + z // 4


def group_columns(z):
    return pl.ds(pl.multiple_of(group_of(z) * WIDTH, 128), WIDTH)


def kernel(
    levels_in, timesteps_in, mask_in, latent, query_in, key_in, value_in, cache_keys, cache_values, time_weight,
    returned, shifted, gate,
    levels, timesteps, cache_mask, query, row_query, landed, kv, attended, weight,
    scored, weighed, factor, peak, total, summed, bias,
    send_z, send_x, send_y, send_q, send_o, recv_q, recv_kv, recv_x, recv_y, recv_rq, recv_o, local, own_x,
):
    chain, head = lax.axis_index("chain"), lax.axis_index("head")
    y, x = chain // 8, chain % 4
    zh, zl, core = (chain // 4) % 2, head // 2, head % 2
    z = zh * 4 + zl
    up, down = (y + 1) % 4, (y + 3) % 4
    x_right, x_left, x_far = (x + 1) % 4, (x + 3) % 4, (x + 2) % 4
    right, left, far = (device(y, z, to, core) for to in (x_right, x_left, x_far))
    sibling = device(y, z, x, 1 - core)
    across = device(y, (z + 4) % 8, x, 1 - core)
    to_up, to_down = device(up, z, x, core), device(down, z, x, core)
    mine = group_columns(z)

    def remote(src, dst, send, recv, to):
        return pltpu.make_async_remote_copy(
            src_ref=src, dst_ref=dst, send_sem=send, recv_sem=recv, device_id=to, device_id_type=MESH
        )

    def of_head(h):
        return pl.ds(pl.multiple_of(h * HEAD_DIM, 128), HEAD_DIM)

    own_query = pltpu.make_async_copy(query_in.at[:, mine], query.at[0], recv_q.at[0])
    own_query.start()
    pltpu.make_async_copy(key_in.at[:, mine], landed.at[0, 0], recv_kv.at[0, 0]).start()
    pltpu.make_async_copy(value_in.at[:, mine], landed.at[0, 1], recv_kv.at[0, 1]).start()
    weight_copy = pltpu.make_async_copy(time_weight, weight, local.at[0])
    weight_copy.start()
    scalar_copies = [
        pltpu.make_async_copy(source, place, local.at[n])
        for n, (source, place) in enumerate(
            ((levels_in, levels), (timesteps_in, timesteps), (mask_in, cache_mask)), start=1
        )
    ]
    for copy in scalar_copies:
        copy.start()

    @pl.when(core == zh)
    def _():
        pltpu.make_async_copy(cache_keys, landed.at[1, 0], recv_kv.at[1, 0]).start()
        pltpu.make_async_copy(cache_values, landed.at[1, 1], recv_kv.at[1, 1]).start()

    barrier = pltpu.get_barrier_semaphore()
    partners = [sibling, across, right, left, far, to_up, to_down]
    partners += [device(y, (z + hop) % 8, x, core) for hop in HOPS[1:]]
    for partner in partners:
        pl.semaphore_signal(barrier, inc=1, device_id=partner, device_id_type=MESH)
    pl.semaphore_wait(barrier, len(partners))

    def cache_across(which):
        source = (cache_keys, cache_values)[which]
        return remote(source, landed.at[1, which], send_z.at[0, which], recv_kv.at[1, which], across)

    def query_over_z(j):
        to = (z + HOPS[j]) % 8
        return remote(
            query_in.at[:, group_columns(to)], query.at[j], send_z.at[j, 2], recv_q.at[j], device(y, to, x, core)
        )

    def kv_over_z(j, which):
        to = (z + HOPS[j]) % 8
        source = (key_in, value_in)[which].at[:, group_columns(to)]
        return remote(
            source, landed.at[j + 1, which], send_z.at[j, which], recv_kv.at[j + 1, which], device(y, to, x, core)
        )

    shared = slice((GROUP - 1) * HEAD_DIM, GROUP * HEAD_DIM)

    def chunk(i):
        return kv.at[PLACE[i]]

    def own_copies(i):
        return (
            pltpu.make_async_copy(landed.at[i, :, :, of_head(x)], chunk(i).at[:, 0, 0], own_x.at[i, 0]),
            pltpu.make_async_copy(landed.at[i, :, :, shared], chunk(i).at[:, 1, 0], own_x.at[i, 1]),
        )

    def x_copy(i, n):
        src, dst, to = (
            lambda: (landed.at[i, :, :, of_head(x_right)], chunk(i).at[:, 0, 1], right),
            lambda: (landed.at[i, :, :, shared], chunk(i).at[:, 1, 1], right),
            lambda: (landed.at[i, :, :, of_head(x_left)], chunk(i).at[:, 0, 3], left),
            lambda: (landed.at[i, :, :, shared], chunk(i).at[:, 1, 3], left),
            lambda: (landed.at[i, :, :, of_head(x_far)], chunk(i).at[:, 0, 2], far),
            lambda: (landed.at[i, :, :, shared], chunk(i).at[:, 1, 2], far),
            lambda: (chunk(i).at[:, :, 0:4], chunk(i).at[:, :, 4:8], sibling),
        )[n]()
        return remote(src, dst, send_x.at[i, n], recv_x.at[i, n], to)

    def y_copy(n):
        src, dst, to = (
            lambda: (chunk(1).at[:, :, 0:4], chunk(9).at[:, :, 0:4], to_up),
            lambda: (chunk(1).at[:, :, 0:4], chunk(10).at[:, :, 0:4], to_down),
            lambda: (chunk(9).at[0, :, 0:4], chunk(11).at[0, :, 0:4], to_up),
            lambda: (chunk(10).at[1, :, 0:4], chunk(11).at[1, :, 0:4], to_down),
            lambda: (chunk(9).at[:, :, 0:4], chunk(9).at[:, :, 4:8], sibling),
            lambda: (chunk(10).at[:, :, 0:4], chunk(10).at[:, :, 4:8], sibling),
            lambda: (chunk(11).at[:, :, 0:4], chunk(11).at[:, :, 4:8], sibling),
            lambda: (latent, shifted, to_down),
        )[n]()
        return remote(src, dst, send_y.at[n], recv_y.at[n], to)

    def query_over_x(n):
        to, slot = ((x_right, 1), (x_far, 2), (x_left, 3))[n]
        return remote(
            query.at[:, :, of_head(to)], row_query.at[slot], send_q.at[n], recv_rq.at[n], device(y, z, to, core)
        )

    def back(tile, j):
        to_x, of = (x, GROUP - 1) if tile == GROUP - 1 else ((x + (0, 3, 2, 1)[tile]) % 4, x)
        to = device(down, (z - HOPS[j] + 8) % 8, to_x, core)
        columns = pl.ds(pl.multiple_of(group_of(z) * WIDTH + of * HEAD_DIM, 128), HEAD_DIM)
        return remote(attended.at[tile, j], returned.at[:, columns], send_o.at[tile, j], recv_o.at[tile, j], to)

    def start_kv(j):
        kv_over_z(j, 0).start()
        kv_over_z(j, 1).start()

    @pl.when(core != zh)
    def _():
        cache_across(0).start()
        cache_across(1).start()

    for j in reversed(range(1, 8)):
        query_over_z(j).start()
    start_kv(1)
    start_kv(2)
    y_copy(7).start()

    def prepare():
        for copy in scalar_copies:
            copy.wait()
        slots = lax.broadcasted_iota(jnp.int32, (1, KEYS), 1) // ROWS
        for i in (1, 9, 10, 11):
            plane = {1: y, 9: down, 10: up, 11: (y + 2) % 4}[i]
            shown = jnp.zeros((1, KEYS), jnp.float32)
            for slot in range(8):
                side = core if slot < 4 else 1 - core
                block = plane * 8 + side * 4 + (x + (0, 3, 2, 1)[slot % 4]) % 4
                hidden = jnp.where(cache_mask[y, block] == 1, 0.0, HIDDEN).astype(jnp.float32)
                shown = jnp.where(slots == slot, hidden, shown)
            bias[PLACE[i]] = shown

        peak[...] = jnp.full_like(peak, HIDDEN)
        total[...] = jnp.zeros_like(total)
        summed[...] = jnp.zeros_like(summed)

    scale = LOG2E / math.sqrt(HEAD_DIM)

    def attend(c, cached, last=False):
        def tile_of(h):
            return slice(h * KEYS, (h + 1) * KEYS)

        keys = [kv[c, 0, n].reshape(KEYS, HEAD_DIM) for n in (0, 1)]
        values = [kv[c, 1, n].reshape(KEYS, HEAD_DIM) for n in (0, 1)]

        def score(h):
            if h < GROUP:
                scored[tile_of(h)] = lax.dot_general(
                    row_query[h].reshape(KEYS, HEAD_DIM),
                    keys[h // (GROUP - 1)],
                    (((1,), (1,)), ((), ())),
                    preferred_element_type=jnp.float32,
                )

        def softmax(h):
            for first in (h * KEYS, h * KEYS + 128):
                rows = slice(first, first + 128)
                sides = [scored[rows, 0:128], scored[rows, 128:256]]
                if cached:
                    sides = [sides[n] + bias[c, :, n * 128 : (n + 1) * 128] for n in (0, 1)]
                old = peak[rows]
                new = jnp.maximum(old, jnp.max(jnp.maximum(*sides), axis=1, keepdims=True) * scale)
                weights = [jnp.exp2(side * scale - new) for side in sides]
                shrink = jnp.exp2(old - new)
                peak[rows] = new
                factor[rows] = shrink
                total[rows] = shrink * total[rows] + (weights[0] + weights[1])
                weighed[rows, 0:128] = weights[0].astype(jnp.bfloat16)
                weighed[rows, 128:256] = weights[1].astype(jnp.bfloat16)

        def add_values(h):
            tile = tile_of(h)
            added = jnp.dot(weighed[tile], values[h // (GROUP - 1)], preferred_element_type=jnp.float32)
            sums = factor[tile] * summed[tile] + added
            if not last:
                summed[tile] = sums
                return
            result = sums * (1.0 / jnp.sum(total[tile], axis=1, keepdims=True))
            attended[h] = result.astype(jnp.bfloat16).reshape(8, ROWS, HEAD_DIM)
            for j in reversed(range(8)):
                back(h, j).start()

        score(0)
        score(1)
        for h in range(GROUP):
            softmax(h)
            score(h + 2)
            if h:
                add_values(h - 1)
        add_values(GROUP - 1)

    def arrived(*items):
        for i in items:
            for which in (0, 1):
                place = landed.at[i, which]
                pltpu.make_async_copy(place, place, recv_kv.at[i, which]).wait()
            for n in range(6):
                x_copy(i, n).start()
            for copy in own_copies(i):
                copy.start()

    def gathered(*items):
        for i in items:
            for copy in own_copies(i):
                copy.wait()
            for n in range(6):
                x_copy(i, n).wait_recv()
            x_copy(i, 6).start()

    def complete(i):
        if i >= X_CHUNKS:
            y_copy(i - 5).wait_recv()
        else:
            x_copy(i, 6).wait_recv()

    def before(c):
        if c == 0:
            arrived(0)
            prepare()
            arrived(1)
            start_kv(3)
            start_kv(4)
            gathered(0, 1)
            y_copy(0).start()
            y_copy(1).start()
            for j in (1, 2, 3, 4):
                query_over_z(j).wait_recv()
            start_kv(5)
            start_kv(6)
            own_query.wait()
            for j in (5, 6, 7):
                query_over_z(j).wait_recv()
            for n in range(3):
                query_over_x(n).start()
            start_kv(7)
            arrived(2, 3)
            row_query[0] = query[:, :, of_head(x)]
            row_query[4] = query[:, :, shared]
            for n in range(3):
                query_over_x(n).wait_recv()
        if c == 1:
            for n in (0, 1):
                y_copy(n).wait_recv()
                y_copy(n + 2).start()
                y_copy(n + 4).start()
        if c == 3:
            gathered(2, 3)
            arrived(4)
            arrived(5)
            y_copy(2).wait_recv()
            y_copy(3).wait_recv()
            y_copy(6).start()
        if c == 6:
            gathered(4, 5)
        if c == 7:
            arrived(6)
        if c == 8:
            arrived(7)
        if c == 9:
            gathered(6, 7)
            arrived(8)
        if c == 11:
            gathered(8)
        complete(ATTEND[c])

    def turn(c, carry):
        cached = False
        for now in range(CHUNKS - 1):
            pl.when(c == now)(functools.partial(before, now))
            if ATTEND[now] == 1 or ATTEND[now] >= X_CHUNKS:
                cached = cached | (c == now)
        pl.when(cached)(functools.partial(attend, c, True))
        pl.when(jnp.logical_not(cached))(functools.partial(attend, c, False))
        return carry

    lax.fori_loop(0, CHUNKS - 1, turn, 0)
    before(CHUNKS - 1)
    attend(CHUNKS - 1, False, True)

    stamp = timesteps[levels[up]].astype(jnp.float32)
    count = 128
    index = lax.broadcasted_iota(jnp.int32, (8, count), 1).astype(jnp.float32)
    phase = stamp * jnp.exp(-math.log(10000.0) * index / count)
    embed = jnp.concatenate([jnp.cos(phase), jnp.sin(phase)], axis=1).astype(jnp.bfloat16)
    weight_copy.wait()

    def gate_columns(c, carry):
        columns = pl.ds(pl.multiple_of(c * WIDTH, 128), WIDTH)
        gate[:, columns] = jnp.dot(embed, weight[:, columns], preferred_element_type=jnp.float32)[0:1]
        return carry

    lax.fori_loop(0, 8, gate_columns, 0)

    @pl.when(core != zh)
    def _():
        cache_across(0).wait_send()
        cache_across(1).wait_send()

    for j in range(1, 8):
        query_over_z(j).wait_send()
        kv_over_z(j, 0).wait_send()
        kv_over_z(j, 1).wait_send()

    for i in range(X_CHUNKS):
        for n in range(7):
            x_copy(i, n).wait_send()
    for n in range(8):
        y_copy(n).wait_send()
    for n in range(3):
        query_over_x(n).wait_send()

    y_copy(7).wait_recv()
    for tile in range(GROUP):
        for j in range(8):
            back(tile, j).wait_recv()
    for tile in range(GROUP):
        for j in range(8):
            back(tile, j).wait_send()


def shards(
    latent, query_in, key_in, value_in, cache_keys, cache_values, levels, timesteps, cache_mask, time_weight
):
    anywhere = pl.BlockSpec(memory_space=pl.ANY)
    bf16, f32, i32 = jnp.bfloat16, jnp.float32, jnp.int32
    dma = pltpu.SemaphoreType.DMA
    returned, shifted, gate = pl.pallas_call(
        kernel,
        out_shape=(
            jax.ShapeDtypeStruct(latent.shape, bf16),
            jax.ShapeDtypeStruct(latent.shape, bf16),
            jax.ShapeDtypeStruct((1, latent.shape[1]), f32),
        ),
        in_specs=[anywhere] * 10,
        out_specs=(anywhere, anywhere, pl.BlockSpec(memory_space=pltpu.VMEM)),
        scratch_shapes=[
            pltpu.SMEM(levels.shape, i32),
            pltpu.SMEM(timesteps.shape, i32),
            pltpu.SMEM(cache_mask.shape, i32),
            pltpu.VMEM((8, ROWS, WIDTH), bf16),
            pltpu.VMEM((GROUP, 8, ROWS, HEAD_DIM), bf16),
            pltpu.VMEM((X_CHUNKS, 2, ROWS, WIDTH), bf16),
            pltpu.VMEM((CHUNKS, 2, 2, 8, ROWS, HEAD_DIM), bf16),
            pltpu.VMEM((GROUP, 8, ROWS, HEAD_DIM), bf16),
            pltpu.VMEM(time_weight.shape, bf16),
            pltpu.VMEM((GROUP * KEYS, KEYS), f32),
            pltpu.VMEM((GROUP * KEYS, KEYS), bf16),
            pltpu.VMEM((GROUP * KEYS, HEAD_DIM), f32),
            pltpu.VMEM((GROUP * KEYS, HEAD_DIM), f32),
            pltpu.VMEM((GROUP * KEYS, HEAD_DIM), f32),
            pltpu.VMEM((GROUP * KEYS, HEAD_DIM), f32),
            pltpu.VMEM((CHUNKS, 1, KEYS), f32),
            dma((8, 3)),
            dma((X_CHUNKS, 7)),
            dma((8,)),
            dma((3,)),
            dma((GROUP, 8)),
            dma((8,)),
            dma((X_CHUNKS, 2)),
            dma((X_CHUNKS, 7)),
            dma((8,)),
            dma((3,)),
            dma((GROUP, 8)),
            dma((4,)),
            dma((X_CHUNKS, 2)),
        ],
        compiler_params=pltpu.CompilerParams(
            collective_id=0, has_side_effects=True, vmem_limit_bytes=64 * 1024 * 1024
        ),
        cost_estimate=pl.CostEstimate(flops=2 * 10**9, bytes_accessed=5 * 10**6, transcendentals=4 * 10**6),
    )(
        levels, timesteps, cache_mask, latent, query_in, key_in, value_in, cache_keys, cache_values, time_weight
    )
    return (shifted.astype(f32) + gate * returned.astype(f32)).astype(bf16)


def solution(mesh):
    return jax.shard_map(
        shards,
        mesh=mesh,
        in_specs=(
            P(("chain", "head"), None),
            P(("chain", "head"), None),
            P(("chain", "head"), None),
            P(("chain", "head"), None),
            P("chain", "head"),
            P("chain", "head"),
            P(),
            P(),
            P(),
            P(),
        ),
        out_specs=P(("chain", "head"), None),
        check_vma=False,
    )
```
